32 devices in a mesh: dp: 16 (over z, x, core), mp: 2 (over y).
Axes of the slice: x: 2, y: 2, z: 4, core: 2. Of those that a mesh axis runs over, the one named last changes fastest.
Arguments:
- history: bfloat16 [9, 2048, 6144], P(None, 'dp'), may hold values from -6 to 6
- mix_in: float32 [6144, 36], P('dp'), may hold values from -3 to 3
- doc_ids: int32 [16, 384], P('dp'), may hold values from 0 to 3, never falling along the last dimension, each value on 1 to 192 neighbouring positions
- group_ids: int32 [16, 384], P('dp'), may hold values from 0 to 7
- group_scale: float32 [8], replicated, may hold values from 0.5 to 2
- w_qkv: bfloat16 [3, 2048, 2048], P(None, 'dp', 'mp'), may hold values from -0.125 to 0.125
- w_out: bfloat16 [2048, 2048], P('dp', 'mp'), may hold values from -0.375 to 0.375
- w_up: bfloat16 [2048, 8192], P('dp', 'mp'), may hold values from -0.125 to 0.125
- w_down: bfloat16 [2048, 8192], P('dp', 'mp'), may hold values from -0.0625 to 0.0625
- w_mix1: bfloat16 [2048, 40], P('dp'), may hold values from -0.125 to 0.125
- w_mix2: bfloat16 [40, 40], replicated, may hold values from -1 to 1
- gains: bfloat16 [5, 2048], P(None, 'dp'), may hold values from 0.25 to 1.75
- cot_out: bfloat16 [2048, 6144], P('dp'), may hold values from -6 to 6
- cot_mix: bfloat16 [6144, 40], P('dp'), may hold values from -15 to 15
Outputs:
- block_out: bfloat16 [2048, 6144], P('dp')
- mix_out: float32 [6144, 40], P('dp')
- grad_history: bfloat16 [9, 2048, 6144], P(None, 'dp')
- grad_mix_in: float32 [6144, 36], P('dp')
- grad_qkv: float32 [3, 2048, 2048], P(None, 'dp', 'mp')
- grad_w_out: float32 [2048, 2048], P('dp', 'mp')
- grad_w_up: float32 [2048, 8192], P('dp', 'mp')
- grad_w_down: float32 [2048, 8192], P('dp', 'mp')
- grad_w_mix1: float32 [2048, 40], P('dp')
- grad_w_mix2: float32 [40, 40], replicated
- grad_gains: float32 [5, 2048], P(None, 'dp')
The draws below stay inside these ranges and needn't reach their ends.
Inputs may be any that keep to these rules, and one draw needn't show every extreme that they name: `doc_ids`: in each row the ids never fall; each document has 1 to 192 tokens, and one has exactly 192.
All inputs are finite; a program needn't handle non-finite values.
Results may differ from the reference program's by a relative error of at most 0.012.
Values may be sent and summed in bfloat16 or wider, within the bound.
A program may use at most 384 MiB of HBM per device.

```python
import math
from functools import partial
import jax
import jax.numpy as jnp
import numpy as np
from jax import lax

D = 2048
HEADS = 16
HEAD = 128
FF = 8192
ROT = 32
HIST = 9
STREAMS = 4
DOCS = 4
GROUPS = 8
TOK_DEV = 384
MIXH = 40
ROWS = 16
TOKENS = 6144


def touch_ends(array, key, least, top_value):
    longest = array.shape.index(max(array.shape))
    spots = []
    for shift in (0, 1):
        where = [jax.random.randint(jax.random.fold_in(key, axis), (), 0, length) for axis, length in enumerate(array.shape)]
        where[longest] = (where[longest] + shift) % array.shape[longest]
        spots.append(tuple(where))
    return array.at[spots[0]].set(least).at[spots[1]].set(top_value)


def shard_levels(key, dims, split, smallest, high):
    def one(axis_at, blocks):
        steps = jax.random.uniform(jax.random.fold_in(jax.random.fold_in(key, 6), axis_at), (blocks,), jnp.float32, smallest / len(split), high / len(split))
        return jnp.repeat(jnp.exp(steps), dims[axis_at] // blocks).reshape((-1,) + (1,) * (len(dims) - axis_at - 1))

    factor_of = one(*split[0])
    for cut in split[1:]:
        factor_of = factor_of * one(*cut)
    return factor_of


def length_profile(count, total, bound, lean):
    weights = [(1 << 20) // math.isqrt(rank ** lean) + 1 for rank in range(2, count + 1)]
    spare, given = total - bound - (count - 1), [1] * (count - 1)
    while spare > 0:
        free = [i for i in range(count - 1) if given[i] < bound]
        mass, left = sum([weights[i] for i in free]), spare
        for i in free:
            extra = min(bound - given[i], max(1, left * weights[i] // mass), spare)
            given[i] = given[i] + extra
            spare = spare - extra
    return np.array([bound] + given)


def ragged(stream_key, count, total, limit, lean):
    if count == 2:
        one = jax.random.randint(stream_key, (), max(1, total - limit), min(limit, total - 1) + 1)
        return jnp.stack([one, total - one])
    sizes = jnp.asarray(length_profile(count, total, limit, lean), jnp.int32)
    twos = (count - 1) // 2
    donor, receiver = sizes[1:1 + 2 * twos:2], sizes[2:2 + 2 * twos:2]
    room = jnp.minimum(donor - 1, limit - receiver)
    passed = jax.random.randint(jax.random.fold_in(stream_key, 1), (twos,), 0, 1 << 20) % (room + 1)
    sizes = sizes.at[1:1 + 2 * twos:2].set(donor - passed).at[2:2 + 2 * twos:2].set(receiver + passed)
    return sizes[jax.random.permutation(jax.random.fold_in(stream_key, 2), count)]


def noise(own_key, dims, spread, most, shards=(), held_as=jnp.bfloat16):
    array = jax.random.normal(own_key, dims, jnp.float32) * spread
    if len(shards) > 0:
        array = shard_levels(own_key, dims, shards, -0.22, 0.18) * array
    return jnp.clip(array, min=-most, max=most).astype(held_as)


def setup_inputs(seed: int = 0) -> dict:
    key_list = jax.random.split(jax.random.key(seed), 15)
    history = noise(key_list[0], (HIST, D, TOKENS), 1.0, 6.0, ((1, 16),))
    mix_in = noise(key_list[1], (TOKENS, STREAMS * HIST), 0.5, 3.0, ((0, 16),), jnp.float32)
    doc_ids = jax.vmap(lambda own: jnp.searchsorted(jnp.cumsum(ragged(own, DOCS, TOK_DEV, TOK_DEV // 2, 1)), jnp.arange(TOK_DEV), side="right"))(jax.random.split(key_list[2], ROWS)).reshape((ROWS, TOK_DEV)).astype(jnp.int32)
    group_ids = touch_ends(jax.random.randint(key_list[3], (ROWS, TOK_DEV), 0, GROUPS), jax.random.fold_in(key_list[3], 1), 0, GROUPS - 1).astype(jnp.int32)
    group_scale = jnp.clip(jnp.exp(jax.random.uniform(key_list[4], (GROUPS,), jnp.float32, math.log(0.5), math.log(2.0))), 0.5, 2.0)
    w_qkv = noise(key_list[5], (3, D, D), D ** -0.5, 0.125, ((1, 16), (2, 2)))
    w_out = noise(key_list[6], (D, D), (D // 8) ** -0.5, 0.375, ((0, 16), (1, 2)))
    w_up = noise(key_list[7], (D, FF), D ** -0.5, 0.125, ((0, 16), (1, 2)))
    w_down = noise(key_list[8], (D, FF), FF ** -0.5, 0.0625, ((0, 16), (1, 2)))
    w_mix1 = noise(key_list[9], (D, MIXH), D ** -0.5, 0.125, ((0, 16),))
    w_mix2 = noise(key_list[10], (MIXH, MIXH), MIXH ** -0.5, 1.0)
    gains = jnp.clip(1.0 + 0.15 * jax.random.normal(key_list[11], (5, D), jnp.float32), 0.25, 1.75).astype(jnp.bfloat16)
    cot_out = noise(key_list[12], (D, TOKENS), 1.0, 6.0, ((0, 16),))
    cot_mix = noise(key_list[13], (TOKENS, MIXH), 2.5, 15.0, ((0, 16),))
    return {"history": history, "mix_in": mix_in, "doc_ids": doc_ids, "group_ids": group_ids, "group_scale": group_scale, "w_qkv": w_qkv, "w_out": w_out, "w_up": w_up, "w_down": w_down, "w_mix1": w_mix1, "w_mix2": w_mix2, "gains": gains, "cot_out": cot_out, "cot_mix": cot_mix}


highest = lax.Precision.HIGHEST

@jax.custom_vjp
def low(v):
    return lax.optimization_barrier(v.astype(jnp.bfloat16)).astype(jnp.float32)

@jax.custom_vjp
def low_back(v):
    return v

def low_keep(v):
    return (low(v), None)

def low_pass(kept, grad):
    return (grad,)

def back_keep(v):
    return (v, None)

def back_low(kept, grad):
    return (low(grad),)
low.defvjp(low_keep, low_pass)
low_back.defvjp(back_keep, back_low)

def rms_norm(inputs, scales):
    return inputs * lax.rsqrt(lax.optimization_barrier(jnp.mean(inputs * inputs, axis=-1, keepdims=True)) + 1e-05) * scales

def rotary(heads_in, angles):
    halfway = ROT // 2
    cosine = jnp.cos(angles)[:, None, :]
    sine_part = jnp.sin(angles)[:, None, :]
    first_half = heads_in[..., :halfway]
    second_half = heads_in[..., halfway:ROT]
    return jnp.concatenate([first_half * cosine - second_half * sine_part, second_half * cosine + first_half * sine_part, heads_in[..., ROT:]], axis=-1)

def angle_table(length):
    halfway = ROT // 2
    frequency = jnp.exp(jnp.arange(halfway, dtype=jnp.float32) * (-2.0 * math.log(10000.0) / ROT))
    places = (jnp.arange(length) % TOK_DEV).astype(jnp.float32)
    return places[:, None] * frequency[None, :]

def gelu_exact(inputs):
    return jax.nn.gelu(inputs, approximate=False)

def attend_row(row_block):
    q_row, k_row, v_row, row_docs = row_block
    scores = low_back(jnp.einsum('qhd,khd->hqk', q_row, k_row, precision=highest) * HEAD ** (-0.5))
    positions = jnp.arange(TOK_DEV)
    allowed = (positions[:, None] >= positions[None, :]) & (row_docs[:, None] == row_docs[None, :])
    masked = jnp.where(allowed[None], scores, -1000000000.0)
    attn_probs = low(jax.nn.softmax(masked, axis=-1))
    return jnp.einsum('hqk,khd->qhd', attn_probs, v_row, precision=highest)

def layer(history, mix_in, w_qkv, w_out, w_up, w_down, w_mix1, w_mix2, gains, doc_ids):
    tokens_all = history.shape[2]
    mixing = mix_in.reshape(tokens_all, STREAMS, HIST)
    streams = jnp.einsum('tsj,jdt->tsd', mixing, history, precision=highest)
    normed = [low(rms_norm(streams[:, stream_num], gains[stream_num])) for stream_num in range(STREAMS)]
    angles = angle_table(tokens_all)

    def project(stream_num):
        return low_back(jnp.dot(normed[stream_num], w_qkv[stream_num], precision=highest)).reshape(tokens_all, HEADS, HEAD)
    queries = low(rotary(project(0), angles)).reshape(ROWS, TOK_DEV, HEADS, HEAD)
    key_heads = low(rotary(project(1), angles)).reshape(ROWS, TOK_DEV, HEADS, HEAD)
    values = low(project(2)).reshape(ROWS, TOK_DEV, HEADS, HEAD)
    attended = lax.map(jax.checkpoint(attend_row), (queries, key_heads, values, doc_ids))
    attended = low(low_back(attended.reshape(tokens_all, D)))
    up_pre = low_back(jnp.dot(normed[3], w_up, precision=highest))
    hidden = low(gelu_exact(up_pre))
    branch = low_back(jnp.dot(attended, w_out.T, precision=highest) + jnp.dot(hidden, w_down.T, precision=highest))
    out_full = streams[:, 3] + branch
    mix_normed = low(rms_norm(out_full, gains[4]))
    mix_pre = low_back(jnp.dot(mix_normed, w_mix1, precision=highest))
    mix_hidden = low(gelu_exact(mix_pre))
    mix_out = jnp.dot(mix_hidden, w_mix2, precision=highest)
    return (out_full.T, mix_out)

def reference(history, mix_in, doc_ids, group_ids, group_scale, w_qkv, w_out, w_up, w_down, w_mix1, w_mix2, gains, cot_out, cot_mix):
    floats = [array_in.astype(jnp.float32) for array_in in (history, mix_in, w_qkv, w_out, w_up, w_down, w_mix1, w_mix2, gains)]
    (out_full, mix_out), layer_pull = jax.vjp(partial(layer, doc_ids=doc_ids), *floats)
    row_scale = group_scale[group_ids.reshape(-1)]
    seeds = (cot_out.astype(jnp.float32) * row_scale[None, :], cot_mix.astype(jnp.float32))
    grads = layer_pull(seeds)
    return (out_full.astype(jnp.bfloat16), mix_out, grads[0].astype(jnp.bfloat16), grads[1], grads[2], grads[3], grads[4], grads[5], grads[6], grads[7], grads[8])
```

```python
import functools
import math

import jax
import jax.numpy as jnp
from jax import lax
from jax.experimental import pallas as pl
from jax.experimental.pallas import tpu as pltpu
from jax.sharding import PartitionSpec as P

HEAD = 128
ROT = 32
HIST = 9
STREAMS = 4
GROUPS = 8
TOK_DEV = 384


MESH = pl.DeviceIdType.MESH


def chip_at(pos, ring):
    far = pos // (ring // 2)
    return (1 - far) * 2 * pos + far * (2 * (ring - 1 - pos) + 1)


def place_of(chip, ring):
    odd = chip % 2
    return (1 - odd) * (chip // 2) + odd * (ring - 1 - chip // 2)


def ring_places(n):
    ring = n // 2
    me = lax.axis_index("dp")
    core = me % 2
    place = place_of(me // 2, ring)

    def owner(offset):
        return chip_at((place + offset + 2 * ring) % ring, ring) * 2 + core

    mate = me + 1 - 2 * core
    return me, mate, owner, ring


def greet(devices):
    barrier = pltpu.get_barrier_semaphore()
    for device in devices:
        pl.semaphore_signal(barrier, inc=1, device_id=device, device_id_type=MESH)
    pl.semaphore_wait(barrier, len(devices))


def rows_of(ref, start, count):
    if len(ref.shape) == 3:
        return ref.at[:, pl.ds(start, count), :]
    return ref.at[pl.ds(start, count), :]


def gather_kernel(n, count, *refs):
    shards, fulls = refs[:count], refs[count : 2 * count]
    local_sem, ring_send, ring_recv, core_send, core_recv = refs[2 * count :]
    me, mate, owner, ring = ring_places(n)
    ahead, behind = owner(1), owner(-1)
    size = shards[0].shape[-2]
    half = size // 2
    greet([{"dp": ahead}, {"dp": behind}, {"dp": mate}])
    local = []
    for i in range(count):
        local.append(
            pltpu.make_async_copy(shards[i], rows_of(fulls[i], me * size, size), local_sem.at[i])
        )

    def ring_copy(way, step, i, first=False):
        origin = owner(-step if way == 0 else step)
        start = pl.multiple_of(origin * size + way * half, half)
        there = rows_of(fulls[i], start, half)
        here = rows_of(shards[i], way * half, half) if first else there
        return pltpu.make_async_remote_copy(
            src_ref=here,
            dst_ref=there,
            send_sem=ring_send.at[way, step, i],
            recv_sem=ring_recv.at[way, step, i],
            device_id={"dp": ahead if way == 0 else behind},
            device_id_type=MESH,
        )

    def ring_arrival(way, step, i):
        origin = owner(-step - 1 if way == 0 else step + 1)
        start = pl.multiple_of(origin * size + way * half, half)
        there = rows_of(fulls[i], start, half)
        return pltpu.make_async_remote_copy(
            src_ref=there,
            dst_ref=there,
            send_sem=ring_send.at[way, step, i],
            recv_sem=ring_recv.at[way, step, i],
            device_id={"dp": ahead if way == 0 else behind},
            device_id_type=MESH,
        )

    def core_copy(way, step, i, first=False):
        origin = owner(-step if way == 0 else step)
        start = pl.multiple_of(origin * size + way * half, half)
        there = rows_of(fulls[i], start, half)
        here = rows_of(shards[i], way * half, half) if first else there
        return pltpu.make_async_remote_copy(
            src_ref=here,
            dst_ref=there,
            send_sem=core_send.at[way, step, i],
            recv_sem=core_recv.at[way, step, i],
            device_id={"dp": mate},
            device_id_type=MESH,
        )

    for i in range(count):
        for way in range(2):
            ring_copy(way, 0, i, True).start()
    for i in range(count):
        for way in range(2):
            core_copy(way, 0, i, True).start()
        local[i].start()

    @pl.loop(1, ring - 1)
    def _(step):
        for i in range(count):
            for way in range(2):
                ring_arrival(way, step - 1, i).wait_recv()
                ring_copy(way, step, i).start()
                core_copy(way, step, i).start()

    for i in range(count):
        for way in range(2):
            ring_arrival(way, ring - 2, i).wait_recv()
            core_copy(way, ring - 1, i).start()

    for i in range(count):
        local[i].wait()

    @pl.loop(0, ring)
    def _(step):
        for i in range(count):
            for way in range(2):
                core_copy(way, step, i).wait()

    @pl.loop(0, ring - 1)
    def _(step):
        for i in range(count):
            for way in range(2):
                ring_copy(way, step, i).wait_send()


def gather_rows(n, *shards):
    count, ring = len(shards), n // 2
    hbm = pl.BlockSpec(memory_space=pl.ANY)
    return pl.pallas_call(
        functools.partial(gather_kernel, n, count),
        out_shape=[
            jax.ShapeDtypeStruct(s.shape[:-2] + (s.shape[-2] * n, s.shape[-1]), s.dtype)
            for s in shards
        ],
        in_specs=[hbm] * count,
        out_specs=[hbm] * count,
        scratch_shapes=[
            pltpu.SemaphoreType.DMA((count,)),
            pltpu.SemaphoreType.DMA((2, ring - 1, count)),
            pltpu.SemaphoreType.DMA((2, ring - 1, count)),
            pltpu.SemaphoreType.DMA((2, ring, count)),
            pltpu.SemaphoreType.DMA((2, ring, count)),
        ],
        compiler_params=pltpu.CompilerParams(collective_id=0, has_side_effects=True),
    )(*shards)


def scatter_kernel(n, count, *refs):
    parts, sums, mates = refs[:count], refs[count : 2 * count], refs[2 * count : 3 * count]
    slots, own, other = (refs[(3 + k) * count : (4 + k) * count] for k in range(3))
    own_sem, other_sem, ring_send, ring_recv, core_send, core_recv = refs[6 * count :]
    me, mate, owner, ring = ring_places(n)
    ahead, behind = owner(1), owner(-1)
    size = sums[0].shape[-2]
    half = size // 2
    greet([{"dp": ahead}, {"dp": behind}, {"dp": mate}])

    def target(way, step):
        return -1 - step if way == 0 else 1 + step

    def core_copy(way, step, i):
        theirs = owner(target(way, step)) + (mate - me)
        start = pl.multiple_of(theirs * size + way * half, half)
        return pltpu.make_async_remote_copy(
            src_ref=rows_of(parts[i], start, half),
            dst_ref=mates[i].at[way, step],
            send_sem=core_send.at[way, step, i],
            recv_sem=core_recv.at[way, step, i],
            device_id={"dp": mate},
            device_id_type=MESH,
        )

    def own_copy(way, step, i):
        start = pl.multiple_of(owner(target(way, step)) * size + way * half, half)
        spot = step % 2
        return pltpu.make_async_copy(
            rows_of(parts[i], start, half), own[i].at[way, spot], own_sem.at[way, spot, i]
        )

    def other_copy(way, step, i):
        spot = step % 2
        return pltpu.make_async_copy(
            mates[i].at[way, step], other[i].at[way, spot], other_sem.at[way, spot, i]
        )

    def ring_copy(way, step, i):
        return pltpu.make_async_remote_copy(
            src_ref=slots[i].at[way, step],
            dst_ref=slots[i].at[way, step + 1],
            send_sem=ring_send.at[way, step, i],
            recv_sem=ring_recv.at[way, step, i],
            device_id={"dp": ahead if way == 0 else behind},
            device_id_type=MESH,
        )

    def stage(way, step, i):
        own_copy(way, step, i).start()
        core_copy(way, step, i).wait_recv()
        other_copy(way, step, i).start()

    def staged(way, step, i):
        own_copy(way, step, i).wait()
        other_copy(way, step, i).wait()

    def chunks(i):
        lead = parts[i].shape[0] if len(parts[i].shape) == 3 else 1
        return lead, half // 16

    def add(way, step, i, first):
        spot = step % 2
        lead, tall = chunks(i)
        deep = len(parts[i].shape) == 3
        slot, mine, theirs = slots[i].at[way, step], own[i].at[way, spot], other[i].at[way, spot]

        for k in range(lead):
            @pl.loop(0, tall)
            def _(r):
                rows = pl.ds(pl.multiple_of(r * 16, 16), 16)
                at = (k, rows) if deep else (rows,)
                total = mine[at].astype(jnp.float32) + theirs[at].astype(jnp.float32)
                if not first:
                    total = total + slot[at].astype(jnp.float32)
                slot[at] = total.astype(slot.dtype)

    def finish(way, step, i):
        spot = step % 2
        lead, tall = chunks(i)
        deep = len(parts[i].shape) == 3
        slot, mine, theirs = slots[i].at[way, step], own[i].at[way, spot], other[i].at[way, spot]

        for k in range(lead):
            @pl.loop(0, tall)
            def _(r):
                rows = pl.ds(pl.multiple_of(r * 16, 16), 16)
                into = pl.ds(pl.multiple_of(way * half + r * 16, 16), 16)
                at = (k, rows) if deep else (rows,)
                total = mine[at].astype(jnp.float32) + theirs[at].astype(jnp.float32)
                total = total + slot[at].astype(jnp.float32)
                sums[i][(k, into) if deep else (into,)] = total

    each = [(i, way) for i in range(count) for way in range(2)]
    for step in range(2):
        for i, way in each:
            core_copy(way, step, i).start()
    for i, way in each:
        stage(way, 0, i)
    for i, way in each:
        staged(way, 0, i)
        add(way, 0, i, True)
        ring_copy(way, 0, i).start()
        stage(way, 1, i)

    @pl.loop(1, ring - 1)
    def _(step):
        for i, way in each:
            core_copy(way, step + 1, i).start()
        for i, way in each:
            staged(way, step, i)
            ring_copy(way, step - 1, i).wait_recv()
            add(way, step, i, False)
            ring_copy(way, step, i).start()
            stage(way, step + 1, i)

    for i, way in each:
        staged(way, ring - 1, i)
        ring_copy(way, ring - 2, i).wait_recv()
        finish(way, ring - 1, i)

    @pl.loop(0, ring - 1)
    def _(step):
        for i, way in each:
            ring_copy(way, step, i).wait_send()

    @pl.loop(0, ring)
    def _(step):
        for i, way in each:
            core_copy(way, step, i).wait_send()


def scatter_rows(n, *parts):
    count, ring = len(parts), n // 2
    hbm = pl.BlockSpec(memory_space=pl.ANY)
    vmem = pl.BlockSpec(memory_space=pltpu.VMEM)
    bf16 = jnp.bfloat16

    def cut(s, rows):
        return s.shape[:-2] + (rows, s.shape[-1])

    half = parts[0].shape[-2] // n // 2
    found = pl.pallas_call(
        functools.partial(scatter_kernel, n, count),
        out_shape=[jax.ShapeDtypeStruct(cut(s, 2 * half), jnp.float32) for s in parts]
        + [jax.ShapeDtypeStruct((2, ring) + cut(s, half), bf16) for s in parts],
        in_specs=[hbm] * count,
        out_specs=[vmem] * count + [hbm] * count,
        scratch_shapes=[pltpu.VMEM((2, ring) + cut(s, half), bf16) for s in parts]
        + [pltpu.VMEM((2, 2) + cut(s, half), bf16) for s in parts]
        + [pltpu.VMEM((2, 2) + cut(s, half), bf16) for s in parts]
        + [
            pltpu.SemaphoreType.DMA((2, 2, count)),
            pltpu.SemaphoreType.DMA((2, 2, count)),
            pltpu.SemaphoreType.DMA((2, ring - 1, count)),
            pltpu.SemaphoreType.DMA((2, ring - 1, count)),
            pltpu.SemaphoreType.DMA((2, ring, count)),
            pltpu.SemaphoreType.DMA((2, ring, count)),
        ],
        compiler_params=pltpu.CompilerParams(
            collective_id=1, has_side_effects=True, vmem_limit_bytes=56 * 1024 * 1024
        ),
    )(*parts)
    return found[:count]


def rms_norm(inputs, scales):
    return inputs * lax.rsqrt(jnp.mean(inputs * inputs, axis=-1, keepdims=True) + 1e-05) * scales


def rotary(heads_in, angles):
    halfway = ROT // 2
    cosine = jnp.cos(angles)[:, None, :]
    sine_part = jnp.sin(angles)[:, None, :]
    first_half = heads_in[..., :halfway]
    second_half = heads_in[..., halfway:ROT]
    return jnp.concatenate(
        [
            first_half * cosine - second_half * sine_part,
            second_half * cosine + first_half * sine_part,
            heads_in[..., ROT:],
        ],
        axis=-1,
    )


def angle_table(length):
    halfway = ROT // 2
    frequency = jnp.exp(jnp.arange(halfway, dtype=jnp.float32) * (-2.0 * math.log(10000.0) / ROT))
    places = (jnp.arange(length) % TOK_DEV).astype(jnp.float32)
    return places[:, None] * frequency[None, :]


def gelu_exact(inputs):
    return jax.nn.gelu(inputs, approximate=False)


def outer_sum(left, right):
    return jnp.einsum("td,te->de", left, right, preferred_element_type=jnp.float32)


def right_product(left, matrix):
    return jnp.einsum("ti,oi->to", left, matrix, preferred_element_type=jnp.float32)


def masked_scores(queries, key_heads, allowed, scale_qk):
    scores = (
        jnp.einsum("hqd,hkd->hqk", queries, key_heads, preferred_element_type=jnp.float32)
        * scale_qk
    )
    return jnp.where(allowed[None], scores, -1000000000.0)


def body(
    history,
    mix_in,
    doc_ids,
    group_ids,
    group_scale,
    w_qkv,
    w_out,
    w_up,
    w_down,
    w_mix1,
    w_mix2,
    gains,
    cot_out,
    cot_mix,
):
    f32 = jnp.float32
    bf16 = jnp.bfloat16
    hist_tok, cot_tok = (
        lax.all_to_all(history, "dp", split_axis=2, concat_axis=1, tiled=True),
        lax.all_to_all(cot_out[None], "dp", split_axis=2, concat_axis=1, tiled=True),
    )
    n = lax.axis_size("dp")
    full_qkv, full_o, full_up, full_down = gather_rows(n, w_qkv, w_out, w_up, w_down)
    full_m1, full_gain = (
        lax.all_gather(w_mix1, "dp", axis=0, tiled=True),
        lax.all_gather(gains, "dp", axis=1, tiled=True),
    )
    gain_f = full_gain.astype(f32)
    tokens_here = hist_tok.shape[2]
    heads_here = full_qkv.shape[2] // HEAD
    width_here = heads_here * HEAD
    mixing = mix_in.reshape(tokens_here, STREAMS, HIST)
    streams = mixing[:, :, 0, None] * hist_tok[0].astype(f32).T[:, None, :]
    for entry_num in range(1, HIST):
        streams = (
            streams + mixing[:, :, entry_num, None] * hist_tok[entry_num].astype(f32).T[:, None, :]
        )
    normed = []
    norm_pulls = []
    for stream_num in range(STREAMS):
        normed_f, norm_pull = jax.vjp(rms_norm, streams[:, stream_num], gain_f[stream_num])
        normed.append(normed_f.astype(bf16))
        norm_pulls.append(norm_pull)
    angles = angle_table(tokens_here)

    def project(stream_num):
        return jnp.dot(
            normed[stream_num], full_qkv[stream_num], preferred_element_type=f32
        ).reshape(tokens_here, heads_here, HEAD)

    queries = rotary(project(0), angles).astype(bf16).transpose(1, 0, 2)
    key_heads = rotary(project(1), angles).astype(bf16).transpose(1, 0, 2)
    values = project(2).astype(bf16).transpose(1, 0, 2)
    scale_qk = HEAD ** (-0.5)
    positions = jnp.arange(tokens_here)
    doc_row = doc_ids[0]
    allowed = (positions[:, None] >= positions[None, :]) & (doc_row[:, None] == doc_row[None, :])
    scores = masked_scores(queries, key_heads, allowed, scale_qk)
    row_max = jnp.max(scores, axis=-1, keepdims=True)
    log_total = row_max + jnp.log(jnp.sum(jnp.exp(scores - row_max), axis=-1, keepdims=True))
    probs_low = jnp.exp(scores - log_total).astype(bf16)
    attended = jnp.einsum("hqk,hkd->hqd", probs_low, values, preferred_element_type=f32)
    attn_cat = attended.astype(bf16).transpose(1, 0, 2).reshape(tokens_here, width_here)
    up_pre = jnp.dot(normed[3], full_up, preferred_element_type=f32)
    hidden = gelu_exact(up_pre).astype(bf16)
    branch_part = right_product(attn_cat, full_o) + right_product(hidden, full_down)
    branch = lax.psum(branch_part, "mp")
    out_full = streams[:, 3] + branch
    out_low = out_full.astype(bf16)
    mix_norm_f, mix_pull = jax.vjp(rms_norm, out_full, gain_f[4])
    mix_normed = mix_norm_f.astype(bf16)
    mix_pre = jnp.dot(mix_normed, full_m1, preferred_element_type=f32)
    mix_hidden = gelu_exact(mix_pre).astype(bf16)
    mix_out = jnp.dot(mix_hidden, w_mix2, preferred_element_type=f32)
    out_hidden = lax.all_to_all(out_low.T[None], "dp", split_axis=1, concat_axis=2, tiled=True)[0]
    back_qkv, back_o, back_up, back_down, back_m1 = full_qkv, full_o, full_up, full_down, full_m1
    row_scale = jnp.sum(
        jnp.where(group_ids[0][:, None] == jnp.arange(GROUPS)[None, :], group_scale[None, :], 0.0),
        axis=1,
    )
    seed = cot_tok[0].astype(f32).T * row_scale[:, None]
    grad_mix2_part = outer_sum(mix_hidden, cot_mix)
    grad_mix_hidden = jnp.dot(cot_mix, w_mix2.T, preferred_element_type=f32)
    grad_mix_pre = jax.vjp(gelu_exact, mix_pre)[1](grad_mix_hidden)[0].astype(bf16)
    grad_m1_part = outer_sum(mix_normed, grad_mix_pre)
    grad_mix_normed = jnp.dot(grad_mix_pre, back_m1.T, preferred_element_type=f32)
    grad_from_mix, grad_gain_mix = mix_pull(grad_mix_normed)
    grad_out_full = seed + grad_from_mix
    grad_branch = grad_out_full.astype(bf16)
    grad_o_part = outer_sum(grad_branch, attn_cat)
    grad_down_part = outer_sum(grad_branch, hidden)
    grad_attended = jnp.dot(grad_branch, back_o, preferred_element_type=f32).astype(bf16)
    grad_attended = grad_attended.reshape(tokens_here, heads_here, HEAD).transpose(1, 0, 2)
    grad_hidden = jnp.dot(grad_branch, back_down, preferred_element_type=f32)
    grad_up_pre = jax.vjp(gelu_exact, up_pre)[1](grad_hidden)[0].astype(bf16)
    grad_up_part = outer_sum(normed[3], grad_up_pre)
    grad_normed_ff = jnp.dot(grad_up_pre, back_up.T, preferred_element_type=f32)
    scores_again = masked_scores(queries, key_heads, allowed, scale_qk)
    attn_probs = jnp.exp(scores_again - log_total)
    grad_probs = jnp.einsum("hqd,hkd->hqk", grad_attended, values, preferred_element_type=f32)
    grad_values = jnp.einsum(
        "hqk,hqd->hkd", attn_probs.astype(bf16), grad_attended, preferred_element_type=f32
    )
    inner = jnp.sum(attn_probs * grad_probs, axis=-1, keepdims=True)
    grad_scores = (attn_probs * (grad_probs - inner)).astype(bf16)
    grad_q_rot = (
        jnp.einsum("hqk,hkd->hqd", grad_scores, key_heads, preferred_element_type=f32) * scale_qk
    )
    grad_k_rot = (
        jnp.einsum("hqk,hqd->hkd", grad_scores, queries, preferred_element_type=f32) * scale_qk
    )
    grad_proj_q = (
        rotary(grad_q_rot.transpose(1, 0, 2), -angles).reshape(tokens_here, width_here).astype(bf16)
    )
    grad_proj_k = (
        rotary(grad_k_rot.transpose(1, 0, 2), -angles).reshape(tokens_here, width_here).astype(bf16)
    )
    grad_proj_v = grad_values.transpose(1, 0, 2).reshape(tokens_here, width_here).astype(bf16)
    grad_projs = (grad_proj_q, grad_proj_k, grad_proj_v)
    grad_qkv_part = jnp.stack(
        [outer_sum(normed[stream_num], grad_projs[stream_num]) for stream_num in range(3)]
    )
    norm_terms = tuple(
        (
            jnp.dot(grad_projs[stream_num], back_qkv[stream_num].T, preferred_element_type=f32)
            for stream_num in range(3)
        )
    )
    grad_normed = (
        lax.psum(norm_terms[0].astype(jnp.bfloat16), "mp").astype(jnp.float32),
        lax.psum(norm_terms[1].astype(jnp.bfloat16), "mp").astype(jnp.float32),
        lax.psum(norm_terms[2].astype(jnp.bfloat16), "mp").astype(jnp.float32),
        lax.psum(grad_normed_ff.astype(jnp.bfloat16), "mp").astype(jnp.float32),
    )
    stream_grads = []
    gain_grads = []
    for stream_num in range(STREAMS):
        grad_stream, grad_gain = norm_pulls[stream_num](grad_normed[stream_num])
        stream_grads.append(grad_stream)
        gain_grads.append(grad_gain)
    stream_grads[3] = stream_grads[3] + grad_out_full
    gain_grads.append(grad_gain_mix)
    grad_streams = jnp.stack(stream_grads, axis=1)
    grad_gain_part = jnp.stack(gain_grads)
    grad_mix_in = jnp.stack(
        [
            jnp.sum(grad_streams * hist_tok[entry_num].astype(f32).T[:, None, :], axis=-1)
            for entry_num in range(HIST)
        ],
        axis=-1,
    ).reshape(tokens_here, STREAMS * HIST)
    grad_hist_low = jnp.einsum(
        "tsj,tsd->jdt", mixing, grad_streams, precision=lax.Precision.HIGHEST
    ).astype(bf16)
    grad_history = lax.all_to_all(grad_hist_low, "dp", split_axis=1, concat_axis=2, tiled=True)
    grad_qkv, grad_w_out, grad_w_up, grad_w_down = scatter_rows(
        n,
        grad_qkv_part.astype(bf16),
        grad_o_part.astype(bf16),
        grad_up_part.astype(bf16),
        grad_down_part.astype(bf16),
    )
    grad_w_mix1, grad_gains = (
        lax.psum_scatter(grad_m1_part, "dp", scatter_dimension=0, tiled=True),
        lax.psum_scatter(grad_gain_part, "dp", scatter_dimension=1, tiled=True),
    )
    grad_w_mix2 = lax.psum(grad_mix2_part, "dp")
    return (
        out_hidden,
        mix_out,
        grad_history,
        grad_mix_in,
        grad_qkv,
        grad_w_out,
        grad_w_up,
        grad_w_down,
        grad_w_mix1,
        grad_w_mix2,
        grad_gains,
    )


def solution(mesh):
    return jax.shard_map(
        body,
        mesh=mesh,
        in_specs=(
            P(None, "dp", None),
            P("dp", None),
            P("dp", None),
            P("dp", None),
            P(),
            P(None, "dp", "mp"),
            P("dp", "mp"),
            P("dp", "mp"),
            P("dp", "mp"),
            P("dp", None),
            P(),
            P(None, "dp"),
            P("dp", None),
            P("dp", None),
        ),
        out_specs=(
            P("dp", None),
            P("dp", None),
            P(None, "dp", None),
            P("dp", None),
            P(None, "dp", "mp"),
            P("dp", "mp"),
            P("dp", "mp"),
            P("dp", "mp"),
            P("dp", None),
            P(),
            P(None, "dp"),
        ),
        check_vma=False,
    )
```

```python
import functools
import math

import jax
import jax.numpy as jnp
from jax import lax
from jax.experimental import pallas as pl
from jax.experimental.pallas import tpu as pltpu
from jax.sharding import PartitionSpec as P

HEAD = 128
ROT = 32
HIST = 9
STREAMS = 4
GROUPS = 8
TOK_DEV = 384
MIXH = 40
WIDE = 128
EPS = 1e-05
MESH = pl.DeviceIdType.MESH
DMA = pltpu.SemaphoreType.DMA
f32 = jnp.float32
bf16 = jnp.bfloat16


def chip_at(pos, ring):
    far = pos // (ring // 2)
    return (1 - far) * 2 * pos + far * (2 * (ring - 1 - pos) + 1)


def place_of(chip, ring):
    odd = chip % 2
    return (1 - odd) * (chip // 2) + odd * (ring - 1 - chip // 2)


def remote(src, dst, send, recv, device):
    return pltpu.make_async_remote_copy(
        src_ref=src,
        dst_ref=dst,
        send_sem=send,
        recv_sem=recv,
        device_id=device,
        device_id_type=MESH,
    )


def greet_plane(n, me, mp):
    barrier = pltpu.get_barrier_semaphore()

    @pl.loop(1, n)
    def _(k):
        pl.semaphore_signal(barrier, inc=1, device_id={"dp": (me + k) % n}, device_id_type=MESH)

    pl.semaphore_signal(barrier, inc=1, device_id={"mp": 1 - mp}, device_id_type=MESH)
    pl.semaphore_wait(barrier, n)


def rows_of(ref, start, count):
    if len(ref.shape) == 3:
        return ref.at[:, pl.ds(start, count), :]
    return ref.at[pl.ds(start, count), :]


class Ring:
    def __init__(self, n):
        self.n, self.ring = n, n // 2
        self.me = lax.axis_index("dp")
        self.core = self.me % 2
        self.place = place_of(self.me // 2, self.ring)
        self.mate = self.me + 1 - 2 * self.core
        self.next_of = ({"dp": self.owner(1)}, {"dp": self.owner(-1)})

    def owner(self, offset):
        return chip_at((self.place + offset + 2 * self.ring) % self.ring, self.ring) * 2 + self.core


def forward_kernel(n, count, *refs):
    hist, cot, mix, small = refs[:4]
    shards = refs[4 : 4 + count]
    inputs, mixes, smalls = refs[4 + count : 7 + count]
    fulls = refs[7 + count : 7 + 2 * count]
    (
        hist_buf,
        slots,
        hist_sem,
        cot_sem,
        own_sem,
        local_sem,
        mix_send,
        mix_recv,
        small_send,
        small_recv,
        a_send,
        a_recv,
        y_send,
        y_recv,
        ring_send,
        ring_recv,
        core_send,
        core_recv,
    ) = refs[7 + 2 * count :]
    where = Ring(n)
    me, ring, owner = where.me, where.ring, where.owner
    mp = lax.axis_index("mp")
    across = {"mp": 1 - mp}
    feat, tokens = hist.shape[1], mix.shape[1]
    h = feat // 2
    size = shards[0].shape[-2]
    half = size // 2
    greet_plane(n, me, mp)

    def origin_rows(offset, way):
        return pl.multiple_of(owner(offset) * size + way * half, half)

    def ring_copy(way, step, i, first=False):
        there = rows_of(fulls[i], origin_rows(-step if way == 0 else step, way), half)
        here = rows_of(shards[i], way * half, half) if first else there
        return remote(
            here, there, ring_send.at[way, step, i], ring_recv.at[way, step, i], where.next_of[way]
        )

    def ring_arrival(way, step, i):
        there = rows_of(fulls[i], origin_rows(-step - 1 if way == 0 else step + 1, way), half)
        return remote(
            there, there, ring_send.at[way, step, i], ring_recv.at[way, step, i], where.next_of[way]
        )

    def core_copy(way, step, i, first=False):
        there = rows_of(fulls[i], origin_rows(-step if way == 0 else step, way), half)
        here = rows_of(shards[i], way * half, half) if first else there
        return remote(
            here, there, core_send.at[way, step, i], core_recv.at[way, step, i], {"dp": where.mate}
        )

    def shard_copy(i):
        return pltpu.make_async_copy(shards[i], rows_of(fulls[i], me * size, size), local_sem.at[i])

    def turn(q):
        return (q + 1) % n

    def mix_copy(q):
        return remote(
            mix, mixes.at[me], mix_send.at[q], mix_recv.at[q], {"dp": (me + turn(q)) % n}
        )

    def small_copy(q):
        return remote(
            small,
            smalls.at[pl.ds(pl.multiple_of(me * feat, feat), feat)],
            small_send.at[q],
            small_recv.at[q],
            {"dp": (me + turn(q)) % n},
        )

    def lanes(peer):
        return pl.ds(pl.multiple_of(peer * tokens, 128), tokens)

    def hist_copy(q):
        peer = (me + turn(q)) % n
        return pltpu.make_async_copy(
            hist.at[:, pl.ds(pl.multiple_of(mp * h, h), h), lanes(peer)],
            hist_buf.at[q % 2],
            hist_sem.at[q % 2],
        )

    def cot_copy(q):
        peer = (me + turn(q)) % n
        return pltpu.make_async_copy(
            cot.at[pl.ds(pl.multiple_of(mp * h, h), h), lanes(peer)],
            slots.at[q, STREAMS],
            cot_sem.at[q],
        )

    def features(source, plane):
        return inputs.at[:, pl.ds(pl.multiple_of(source * feat + plane * h, h), h), :]

    def stream_copy(q):
        return remote(
            slots.at[q], features(me, mp), a_send.at[q], a_recv.at[q], {"dp": (me + turn(q)) % n}
        )

    def own_copy():
        return pltpu.make_async_copy(slots.at[n - 1], features(me, mp), own_sem)

    def across_copy(q, own=False):
        there = features((me - turn(q) + n) % n, mp)
        return remote(
            slots.at[n - 1] if own else there, there, y_send.at[q], y_recv.at[q], across
        )

    def mix_streams(q):
        peer = (me + turn(q)) % n

        @pl.loop(0, h // 16)
        def _(r):
            rows = pl.ds(pl.multiple_of(r * 16, 16), 16)
            sums = [None] * STREAMS
            for j in range(HIST):
                entry = hist_buf[q % 2, j, rows, :].astype(f32)
                for s in range(STREAMS):
                    term = mixes[peer, pl.ds(s * HIST + j, 1), :] * entry
                    sums[s] = term if j == 0 else sums[s] + term
            for s in range(STREAMS):
                slots[q, s, rows, :] = sums[s].astype(bf16)

    pieces = [(i, way) for i in range(count) for way in range(2)]

    @pl.loop(0, n - 1)
    def _(q):
        mix_copy(q).start()
        small_copy(q).start()
        cot_copy(q).start()

    cot_copy(n - 1).start()
    hist_copy(0).start()
    for i, way in pieces:
        ring_copy(way, 0, i, True).start()
    own_small = pltpu.make_async_copy(
        small, smalls.at[pl.ds(pl.multiple_of(me * feat, feat), feat)], local_sem.at[count]
    )
    own_small.start()
    mixes[me] = mix[...]

    @pl.loop(0, n - 1)
    def _(q):
        hist_copy(q).wait()
        hist_copy(q + 1).start()
        mix_copy(n - 2 - q).wait_recv()
        mix_streams(q)
        cot_copy(q).wait()
        stream_copy(q).start()

    hist_copy(n - 1).wait()
    mix_streams(n - 1)
    cot_copy(n - 1).wait()
    own_copy().start()
    across_copy(n - 1, True).start()
    for i, way in pieces:
        core_copy(way, 0, i, True).start()
    for i in range(count):
        shard_copy(i).start()

    @pl.loop(1, ring - 1)
    def _(step):
        for i, way in pieces:
            ring_arrival(way, step - 1, i).wait_recv()
            ring_copy(way, step, i).start()
            core_copy(way, step, i).start()
        for k in range(2):
            q = (step - 1) * 2 + k
            stream_copy(q).wait_recv()
            across_copy(q).start()

    @pl.loop((ring - 2) * 2, n - 1)
    def _(q):
        stream_copy(q).wait_recv()
        across_copy(q).start()

    for i, way in pieces:
        ring_arrival(way, ring - 2, i).wait_recv()
        core_copy(way, ring - 1, i).start()

    own_copy().wait()
    own_small.wait()
    for i in range(count):
        shard_copy(i).wait()

    @pl.loop(0, n - 1)
    def _(q):
        mix_copy(q).wait_send()
        small_copy(q).wait()
        stream_copy(q).wait_send()

    @pl.loop(0, n)
    def _(q):
        across_copy(q).wait()

    @pl.loop(0, ring)
    def _(step):
        for i, way in pieces:
            core_copy(way, step, i).wait()

    @pl.loop(0, ring - 1)
    def _(step):
        for i, way in pieces:
            ring_copy(way, step, i).wait_send()


def forward_exchange(n, history, cot_out, mix, small, shards):
    count, ring = len(shards), n // 2
    feat, tokens = history.shape[1], mix.shape[1]
    h = feat // 2
    hbm = pl.BlockSpec(memory_space=pl.ANY)
    vmem = pl.BlockSpec(memory_space=pltpu.VMEM)
    found = pl.pallas_call(
        functools.partial(forward_kernel, n, count),
        out_shape=[
            jax.ShapeDtypeStruct((STREAMS + 1, n * feat, tokens), bf16),
            jax.ShapeDtypeStruct((n,) + mix.shape, f32),
            jax.ShapeDtypeStruct((n * feat, WIDE), bf16),
        ]
        + [
            jax.ShapeDtypeStruct(s.shape[:-2] + (s.shape[-2] * n, s.shape[-1]), s.dtype)
            for s in shards
        ],
        in_specs=[hbm, hbm, vmem, hbm] + [hbm] * count,
        out_specs=[hbm, vmem, hbm] + [hbm] * count,
        scratch_shapes=[
            pltpu.VMEM((2, HIST, h, tokens), bf16),
            pltpu.VMEM((n, STREAMS + 1, h, tokens), bf16),
            DMA((2,)),
            DMA((n,)),
            DMA,
            DMA((count + 1,)),
        ]
        + [DMA((n,)) for _ in range(8)]
        + [DMA((2, ring - 1, count)) for _ in range(2)]
        + [DMA((2, ring, count)) for _ in range(2)],
        compiler_params=pltpu.CompilerParams(
            collective_id=0, has_side_effects=True, vmem_limit_bytes=32 * 1024 * 1024
        ),
    )(history, cot_out, mix, small, *shards)
    return found[0], found[1], found[2], found[3:]


def backward_kernel(n, count, *refs):
    grads, inner, scale, inputs, direct, output, smalls, little, second, hist, mixes = refs[:11]
    parts = refs[11 : 11 + count]
    refs = refs[11 + count :]
    across_land, feature_side, mix_sum, little_sum, second_sum = refs[:5]
    sums, mates = refs[5 : 5 + count], refs[5 + count : 5 + 2 * count]
    refs = refs[5 + 2 * count :]
    slots, own, other, final = (refs[k * count : (k + 1) * count] for k in range(4))
    (
        inner_land,
        d_buf,
        e_buf,
        x_buf,
        go_buf,
        g_buf,
        l_buf,
        g_slots,
        l_slots,
        l_land,
        second_land,
        f_buf,
        h_buf,
        m_slots,
        m_land,
        m_mine,
        m_other,
        l_sum,
        load_sem,
        out_sem,
        back_sem,
        own_sem,
        other_sem,
        final_sem,
        y_send,
        y_recv,
        p_sem,
        a_send,
        a_recv,
        l_send,
        l_recv,
        w_send,
        w_recv,
        fy_send,
        fy_recv,
        m_send,
        m_recv,
        end_sem,
        ring_send,
        ring_recv,
        core_send,
        core_recv,
    ) = refs[4 * count :]
    where = Ring(n)
    me, ring, owner = where.me, where.ring, where.owner
    mp = lax.axis_index("mp")
    across = {"mp": 1 - mp}
    feat, tokens = hist.shape[1], inner.shape[1]
    h = feat // 2
    size = sums[0].shape[-2]
    half = size // 2
    greet_plane(n, me, mp)

    def target(way, step):
        return -1 - step if way == 0 else 1 + step

    def core_copy(way, step, i):
        theirs = owner(target(way, step)) + (where.mate - me)
        start = pl.multiple_of(theirs * size + way * half, half)
        return remote(
            rows_of(parts[i], start, half),
            mates[i].at[way, step],
            core_send.at[way, step, i],
            core_recv.at[way, step, i],
            {"dp": where.mate},
        )

    def own_copy(way, step, i):
        start = pl.multiple_of(owner(target(way, step)) * size + way * half, half)
        spot = step % 2
        return pltpu.make_async_copy(
            rows_of(parts[i], start, half), own[i].at[way, spot], own_sem.at[way, spot, i]
        )

    def other_copy(way, step, i):
        spot = step % 2
        return pltpu.make_async_copy(
            mates[i].at[way, step], other[i].at[way, spot], other_sem.at[way, spot, i]
        )

    def ring_copy(way, step, i):
        return remote(
            slots[i].at[way, step],
            slots[i].at[way, step + 1],
            ring_send.at[way, step, i],
            ring_recv.at[way, step, i],
            where.next_of[way],
        )

    def final_copy(way, i):
        return pltpu.make_async_copy(
            final[i], rows_of(sums[i], way * half, half), final_sem.at[i]
        )

    def stage(way, step, i):
        own_copy(way, step, i).start()
        core_copy(way, step, i).wait_recv()
        other_copy(way, step, i).start()

    def staged(way, step, i):
        own_copy(way, step, i).wait()
        other_copy(way, step, i).wait()

    def add(way, step, i, first=False, last=False):
        spot = step % 2
        deep = len(parts[i].shape) == 3
        slot, mine, theirs = slots[i].at[way, step], own[i].at[way, spot], other[i].at[way, spot]
        for k in range(parts[i].shape[0] if deep else 1):

            @pl.loop(0, half // 16)
            def _(r):
                rows = pl.ds(pl.multiple_of(r * 16, 16), 16)
                at = (k, rows) if deep else (rows,)
                total = mine[at].astype(f32) + theirs[at].astype(f32)
                if not first:
                    total = total + slot[at].astype(f32)
                if last:
                    final[i][at] = total
                else:
                    slot[at] = total.astype(bf16)

    def turn(q):
        return (q + 1) % n

    def span(peer, plane):
        return pl.ds(pl.multiple_of(peer * feat + plane * h, h), h)

    def sum_copy(q):
        peer = (me + turn(q)) % n
        return remote(
            grads.at[:, span(peer, 1 - mp), :],
            across_land.at[q],
            y_send.at[q],
            y_recv.at[q],
            across,
        )

    def inner_copy():
        return remote(inner, inner_land, p_sem.at[0], p_sem.at[1], across)

    def loads(q):
        rows = span((me + turn(q)) % n, mp)
        spot = q % 2
        return [
            pltpu.make_async_copy(grads.at[:, rows, :], d_buf.at[spot], load_sem.at[spot, 0]),
            pltpu.make_async_copy(across_land.at[q], e_buf.at[spot], load_sem.at[spot, 1]),
            pltpu.make_async_copy(
                inputs.at[pl.ds(0, STREAMS), rows, :], x_buf.at[spot], load_sem.at[spot, 2]
            ),
            pltpu.make_async_copy(direct.at[rows, :], go_buf.at[spot], load_sem.at[spot, 3]),
            pltpu.make_async_copy(smalls.at[rows, :], g_buf.at[spot], load_sem.at[spot, 4]),
            pltpu.make_async_copy(little.at[rows, :], l_buf.at[spot], load_sem.at[spot, 5]),
        ]

    def out_copy(q):
        rows = span((me + turn(q)) % n, mp)
        return pltpu.make_async_copy(output.at[rows, :], g_slots.at[q, STREAMS], out_sem.at[q])

    def place(source, plane):
        return feature_side.at[source, :, pl.ds(pl.multiple_of(plane * h, h), h), :]

    def stream_copy(q):
        return remote(
            g_slots.at[q], place(me, mp), a_send.at[q], a_recv.at[q], {"dp": (me + turn(q)) % n}
        )

    def little_copy(q):
        return remote(
            l_slots.at[q], l_land.at[q], l_send.at[q], l_recv.at[q], {"dp": (me + turn(q)) % n}
        )

    def second_copy(q):
        return remote(
            second, second_land.at[me], w_send.at[q], w_recv.at[q], {"dp": (me + turn(q)) % n}
        )

    def home_copy():
        return pltpu.make_async_copy(g_slots.at[n - 1], place(me, mp), end_sem.at[0])

    def across_copy(q, own=False):
        there = place((me - turn(q) + n) % n, mp)
        return remote(
            g_slots.at[n - 1] if own else there, there, fy_send.at[q], fy_recv.at[q], across
        )

    def start_loads(q):
        sum_copy(q).wait_recv()
        for copy in loads(q):
            copy.start()

    def norm_backward(q):
        spot = q % 2
        for copy in loads(q):
            copy.wait()

        @pl.loop(0, h // 16)
        def _(r):
            rows = pl.ds(pl.multiple_of(r * 16, 16), 16)
            tail = l_buf[spot, rows, :]
            lane = lax.broadcasted_iota(jnp.int32, tail.shape, 1)
            for s in range(STREAMS):
                dy = d_buf[spot, s, rows, :].astype(f32) + e_buf[spot, s, rows, :].astype(f32)
                level = scale[pl.ds(s, 1), :]
                common = (inner[pl.ds(s, 1), :] + inner_land[pl.ds(s, 1), :]) * level
                common = common * (1.0 / (n * feat))
                unit = x_buf[spot, s, rows, :].astype(f32) * level
                gain = g_buf[spot, rows, :].astype(f32)[:, MIXH + s : MIXH + s + 1]
                grad = level * (gain * dy) - unit * common
                if s == STREAMS - 1:
                    grad = grad + go_buf[spot, rows, :]
                g_slots[q, s, rows, :] = grad.astype(bf16)
                gain_grad = jnp.sum(unit * dy, axis=1, keepdims=True)
                tail = jnp.where(lane == MIXH + s, gain_grad, tail)
            l_slots[q, rows, :] = tail

    def norm_turn(q, last=False):
        if not last:
            start_loads(q + 1)
        norm_backward(q)
        out_copy(q).wait()
        if last:
            home_copy().start()
            across_copy(q, True).start()
        else:
            stream_copy(q).start()
            little_copy(q).start()

    def hist_load(q):
        source = (me - turn(q) + n) % n
        return pltpu.make_async_copy(
            hist.at[
                :,
                pl.ds(pl.multiple_of(mp * h, h), h),
                pl.ds(pl.multiple_of(source * tokens, 128), tokens),
            ],
            h_buf.at[q % 2],
            back_sem.at[q % 2, 0],
        )

    def grad_load(q):
        source = (me - turn(q) + n) % n
        return pltpu.make_async_copy(
            feature_side.at[source, pl.ds(0, STREAMS), pl.ds(pl.multiple_of(mp * h, h), h), :],
            f_buf,
            back_sem.at[0, 1],
        )

    def mix_copy(q):
        return remote(
            m_slots.at[q],
            m_land.at[q],
            m_send.at[q],
            m_recv.at[q],
            {"dp": (me - turn(q) + n) % n},
        )

    def mix_backward(q):
        for s in range(STREAMS):
            totals = [None] * HIST
            for r in range(h // 16):
                grad = f_buf[s, r * 16 : r * 16 + 16, :].astype(f32)
                for j in range(HIST):
                    both = h_buf[q % 2, j, r * 16 : r * 16 + 16, :].astype(f32) * grad
                    both = both[0:8] + both[8:16]
                    totals[j] = both if r == 0 else totals[j] + both
            for j in range(HIST):
                m_slots[q, pl.ds(s * HIST + j, 1), :] = jnp.sum(totals[j], axis=0, keepdims=True)

    def mix_turn(q, last=False):
        if last:
            home_copy().wait()
        else:
            hist_load(q + 1).start()
            stream_copy(q).wait_recv()
            across_copy(q).start()
        grad_load(q).start()
        grad_load(q).wait()
        hist_load(q).wait()
        mix_backward(q)
        if not last:
            mix_copy(q).start()

    pieces = [(i, way) for i in range(count) for way in range(2)]
    units = len(pieces)

    inner_copy().start()
    for step in range(2):
        for i, way in pieces:
            core_copy(way, step, i).start()

    @pl.loop(0, n)
    def _(q):
        sum_copy(q).start()
        out_copy(q).start()

    second_land[me] = second[...]

    @pl.loop(0, n - 1)
    def _(q):
        second_copy(q).start()

    for i, way in pieces:
        stage(way, 0, i)
    for i, way in pieces:
        staged(way, 0, i)
        add(way, 0, i, first=True)
        ring_copy(way, 0, i).start()
        stage(way, 1, i)
    inner_copy().wait()
    start_loads(0)

    def ring_unit(step, i, way):
        staged(way, step, i)
        ring_copy(way, step - 1, i).wait_recv()
        add(way, step, i)
        ring_copy(way, step, i).start()
        stage(way, step + 1, i)

    def mates_ahead(step):
        for i, way in pieces:
            core_copy(way, step + 1, i).start()

    turns = n // units

    @pl.loop(1, 1 + turns)
    def _(step):
        mates_ahead(step)
        for u, (i, way) in enumerate(pieces):
            ring_unit(step, i, way)
            q = (step - 1) * units + u
            if u < units - 1:
                norm_turn(q)
            else:

                @pl.when(step < turns)
                def _():
                    norm_turn(q)

    norm_turn(n - 1, True)
    hist_load(0).start()

    @pl.loop(1 + turns, 1 + 2 * turns)
    def _(step):
        mates_ahead(step)
        for u, (i, way) in enumerate(pieces):
            ring_unit(step, i, way)
            q = (step - 1 - turns) * units + u
            if u < units - 1:
                mix_turn(q)
            else:

                @pl.when(step < 2 * turns)
                def _():
                    mix_turn(q)

    mix_turn(n - 1, True)

    @pl.loop(1 + 2 * turns, ring - 1)
    def _(step):
        mates_ahead(step)
        for i, way in pieces:
            ring_unit(step, i, way)

    @pl.loop(0, n - 1)
    def _(q):
        little_copy(q).wait_recv()
        second_copy(q).wait_recv()
        mix_copy(q).wait_recv()

    def sum_over(land, mine):
        return lax.fori_loop(0, n - 1, lambda q, total: total + land[q], mine)

    l_sum[...] = sum_over(l_land, l_slots[n - 1])
    m_mine[...] = sum_over(m_land, m_slots[n - 1])
    second_sum[...] = lax.fori_loop(
        1, n, lambda q, total: total + second_land[q], second_land[0]
    )
    here = pl.ds(pl.multiple_of(mp * h, h), h)
    little_home = pltpu.make_async_copy(l_sum, little_sum.at[here], end_sem.at[1])
    little_across = remote(l_sum, little_sum.at[here], end_sem.at[2], end_sem.at[3], across)
    mix_across = remote(m_mine, m_other, end_sem.at[4], end_sem.at[5], across)
    little_home.start()
    little_across.start()
    mix_across.start()

    for way in range(2):
        for i in range(count):
            staged(way, ring - 1, i)
            ring_copy(way, ring - 2, i).wait_recv()
            if way == 1:
                final_copy(0, i).wait()
            add(way, ring - 1, i, last=True)
            final_copy(way, i).start()

    mix_across.wait()
    mix_sum[...] = m_mine[...] + m_other[...]
    little_home.wait()
    little_across.wait()
    for i in range(count):
        final_copy(1, i).wait()

    @pl.loop(0, n - 1)
    def _(q):
        stream_copy(q).wait_send()
        little_copy(q).wait_send()
        second_copy(q).wait_send()
        mix_copy(q).wait_send()

    @pl.loop(0, n)
    def _(q):
        sum_copy(q).wait_send()
        across_copy(q).wait()

    @pl.loop(0, ring - 1)
    def _(step):
        for i, way in pieces:
            ring_copy(way, step, i).wait_send()

    @pl.loop(0, ring)
    def _(step):
        for i, way in pieces:
            core_copy(way, step, i).wait_send()


def backward_exchange(
    n, grads, inner, scale, inputs, direct, output, smalls, little, second, history, mixes, parts
):
    count, ring = len(parts), n // 2
    feat, tokens = history.shape[1], grads.shape[2]
    h = feat // 2
    hbm = pl.BlockSpec(memory_space=pl.ANY)
    vmem = pl.BlockSpec(memory_space=pltpu.VMEM)

    def cut(s, rows):
        return s.shape[:-2] + (rows, s.shape[-1])

    half = parts[0].shape[-2] // n // 2
    found = pl.pallas_call(
        functools.partial(backward_kernel, n, count),
        out_shape=[
            jax.ShapeDtypeStruct((n, STREAMS, h, tokens), bf16),
            jax.ShapeDtypeStruct((n, STREAMS + 1, feat, tokens), bf16),
            jax.ShapeDtypeStruct((STREAMS * HIST, tokens), f32),
            jax.ShapeDtypeStruct((feat, WIDE), f32),
            jax.ShapeDtypeStruct(second.shape, f32),
        ]
        + [jax.ShapeDtypeStruct(cut(s, 2 * half), f32) for s in parts]
        + [jax.ShapeDtypeStruct((2, ring) + cut(s, half), bf16) for s in parts],
        in_specs=[hbm, vmem, vmem, hbm, hbm, hbm, hbm, hbm, vmem, hbm, hbm] + [hbm] * count,
        out_specs=[hbm, hbm, vmem, hbm, vmem] + [hbm] * (2 * count),
        scratch_shapes=[pltpu.VMEM((2, ring) + cut(s, half), bf16) for s in parts]
        + [pltpu.VMEM((2, 2) + cut(s, half), bf16) for s in parts]
        + [pltpu.VMEM((2, 2) + cut(s, half), bf16) for s in parts]
        + [pltpu.VMEM(cut(s, half), f32) for s in parts]
        + [
            pltpu.VMEM(inner.shape, f32),
            pltpu.VMEM((2, STREAMS, h, tokens), bf16),
            pltpu.VMEM((2, STREAMS, h, tokens), bf16),
            pltpu.VMEM((2, STREAMS, h, tokens), bf16),
            pltpu.VMEM((2, h, tokens), f32),
            pltpu.VMEM((2, h, WIDE), bf16),
            pltpu.VMEM((2, h, WIDE), f32),
            pltpu.VMEM((n, STREAMS + 1, h, tokens), bf16),
            pltpu.VMEM((n, h, WIDE), f32),
            pltpu.VMEM((n, h, WIDE), f32),
            pltpu.VMEM((n,) + second.shape, f32),
            pltpu.VMEM((STREAMS, h, tokens), bf16),
            pltpu.VMEM((2, HIST, h, tokens), bf16),
            pltpu.VMEM((n, STREAMS * HIST, tokens), f32),
            pltpu.VMEM((n, STREAMS * HIST, tokens), f32),
            pltpu.VMEM((STREAMS * HIST, tokens), f32),
            pltpu.VMEM((STREAMS * HIST, tokens), f32),
            pltpu.VMEM((h, WIDE), f32),
            DMA((2, 6)),
            DMA((n,)),
            DMA((2, 2)),
            DMA((2, 2, count)),
            DMA((2, 2, count)),
            DMA((count,)),
            DMA((n,)),
            DMA((n,)),
            DMA((2,)),
        ]
        + [DMA((n,)) for _ in range(10)]
        + [DMA((6,))]
        + [DMA((2, ring - 1, count)) for _ in range(2)]
        + [DMA((2, ring, count)) for _ in range(2)],
        compiler_params=pltpu.CompilerParams(
            collective_id=1, has_side_effects=True, vmem_limit_bytes=60 * 1024 * 1024
        ),
    )(grads, inner, scale, inputs, direct, output, smalls, little, second, history, mixes, *parts)
    return found[1], found[2], found[3], found[4], found[5 : 5 + count]


def history_kernel(grads, mixes, grad_history, block_out):
    feat = grads.shape[2]

    @pl.loop(0, feat // 16)
    def _(r):
        rows = pl.ds(pl.multiple_of(r * 16, 16), 16)
        each = [grads[0, s, rows, :].astype(f32) for s in range(STREAMS)]
        for j in range(HIST):
            total = mixes[0, pl.ds(j, 1), :] * each[0]
            for s in range(1, STREAMS):
                total = total + mixes[0, pl.ds(s * HIST + j, 1), :] * each[s]
            grad_history[j, rows, :] = total.astype(bf16)

    block_out[...] = grads[0, STREAMS]


def history_gradient(feature_side, mixes):
    n, streams, feat, tokens = feature_side.shape
    return pl.pallas_call(
        history_kernel,
        grid=(n,),
        out_shape=[
            jax.ShapeDtypeStruct((HIST, feat, n * tokens), bf16),
            jax.ShapeDtypeStruct((feat, n * tokens), bf16),
        ],
        in_specs=[
            pl.BlockSpec((1, streams, feat, tokens), lambda i: (i, 0, 0, 0)),
            pl.BlockSpec((1,) + mixes.shape[1:], lambda i: (i, 0, 0)),
        ],
        out_specs=[
            pl.BlockSpec((HIST, feat, tokens), lambda i: (0, 0, i)),
            pl.BlockSpec((feat, tokens), lambda i: (0, i)),
        ],
        compiler_params=pltpu.CompilerParams(vmem_limit_bytes=32 * 1024 * 1024),
    )(feature_side, mixes)


def rotary(heads_in, angles):
    halfway = ROT // 2
    cosine = jnp.cos(angles)[:, None, :]
    sine_part = jnp.sin(angles)[:, None, :]
    first_half = heads_in[..., :halfway]
    second_half = heads_in[..., halfway:ROT]
    return jnp.concatenate(
        [
            first_half * cosine - second_half * sine_part,
            second_half * cosine + first_half * sine_part,
            heads_in[..., ROT:],
        ],
        axis=-1,
    )


def angle_table(length):
    halfway = ROT // 2
    frequency = jnp.exp(jnp.arange(halfway, dtype=f32) * (-2.0 * math.log(10000.0) / ROT))
    places = (jnp.arange(length) % TOK_DEV).astype(f32)
    return places[:, None] * frequency[None, :]


def gelu_exact(inputs):
    return jax.nn.gelu(inputs, approximate=False)


def product(spec, left, right):
    return jnp.einsum(spec, left, right, preferred_element_type=f32)


def body(
    history,
    mix_in,
    doc_ids,
    group_ids,
    group_scale,
    w_qkv,
    w_out,
    w_up,
    w_down,
    w_mix1,
    w_mix2,
    gains,
    cot_out,
    cot_mix,
):
    n = lax.axis_size("dp")
    tokens_here = mix_in.shape[0]
    width = n * history.shape[1]
    small = jnp.pad(
        jnp.concatenate([w_mix1, gains.T], axis=1), ((0, 0), (0, WIDE - MIXH - gains.shape[0]))
    )
    inputs, mixes, smalls, (full_qkv, full_o, full_up, full_down) = forward_exchange(
        n, history, cot_out, mix_in.T, small, (w_qkv, w_out, w_up, w_down)
    )
    full_m1 = smalls[:, :MIXH]
    gain_f = smalls[:, MIXH : MIXH + STREAMS + 1].astype(f32)
    heads_here = full_qkv.shape[2] // HEAD
    width_here = heads_here * HEAD
    streams = inputs[:STREAMS].astype(f32)
    level = lax.rsqrt(jnp.mean(streams * streams, axis=1) + EPS)
    normed = [
        (streams[s] * level[s][None, :] * gain_f[:, s : s + 1]).astype(bf16) for s in range(STREAMS)
    ]
    angles = angle_table(tokens_here)

    def project(s):
        return product("dt,dn->tn", normed[s], full_qkv[s]).reshape(tokens_here, heads_here, HEAD)

    queries = rotary(project(0), angles).astype(bf16).transpose(1, 0, 2)
    key_heads = rotary(project(1), angles).astype(bf16).transpose(1, 0, 2)
    values = project(2).astype(bf16).transpose(1, 0, 2)
    scale_qk = HEAD ** (-0.5)
    positions = jnp.arange(tokens_here)
    doc_row = doc_ids[0]
    allowed = (positions[:, None] >= positions[None, :]) & (doc_row[:, None] == doc_row[None, :])
    scores = product("hqd,hkd->hqk", queries, key_heads) * scale_qk
    scores = jnp.where(allowed[None], scores, -1000000000.0)
    row_max = jnp.max(scores, axis=-1, keepdims=True)
    log_total = row_max + jnp.log(jnp.sum(jnp.exp(scores - row_max), axis=-1, keepdims=True))
    attn_probs = jnp.exp(scores - log_total)
    probs_low = attn_probs.astype(bf16)
    attended = product("hqk,hkd->hqd", probs_low, values)
    attn_cat = attended.astype(bf16).transpose(1, 0, 2).reshape(tokens_here, width_here)
    up_pre = product("dt,dn->tn", normed[3], full_up)
    hidden = gelu_exact(up_pre).astype(bf16)
    branch_part = product("oi,ti->ot", full_o, attn_cat) + product("oi,ti->ot", full_down, hidden)
    branch_low = branch_part.astype(bf16)
    swap = [(0, 1), (1, 0)]
    branch = branch_low.astype(f32) + lax.ppermute(branch_low, "mp", swap).astype(f32)
    out_full = streams[3] + branch
    out_low = out_full.astype(bf16)
    mix_level = lax.rsqrt(jnp.mean(out_full * out_full, axis=0) + EPS)
    mix_unit = out_full * mix_level[None, :]
    mix_gain = gain_f[:, STREAMS : STREAMS + 1]
    mix_normed = (mix_unit * mix_gain).astype(bf16)
    mix_pre = product("dt,dm->tm", mix_normed, full_m1)
    mix_hidden = gelu_exact(mix_pre).astype(bf16)
    mix_out = product("tm,mo->to", mix_hidden, w_mix2)

    row_scale = jnp.sum(
        jnp.where(group_ids[0][:, None] == jnp.arange(GROUPS)[None, :], group_scale[None, :], 0.0),
        axis=1,
    )
    seed = inputs[STREAMS].astype(f32) * row_scale[None, :]
    grad_mix2_part = product("tm,to->mo", mix_hidden, cot_mix)
    grad_mix_hidden = product("to,mo->tm", cot_mix, w_mix2)
    grad_mix_pre = jax.vjp(gelu_exact, mix_pre)[1](grad_mix_hidden)[0].astype(bf16)
    grad_m1_part = product("dt,tm->dm", mix_normed, grad_mix_pre)
    grad_mix_normed = product("dm,tm->dt", full_m1, grad_mix_pre)
    grad_gain_mix = jnp.sum(mix_unit * grad_mix_normed, axis=1)
    mix_inner = jnp.mean(mix_unit * mix_gain * grad_mix_normed, axis=0)
    grad_out_full = seed + mix_level[None, :] * (
        mix_gain * grad_mix_normed - mix_unit * mix_inner[None, :]
    )
    grad_branch = grad_out_full.astype(bf16)
    grad_o_part = product("ot,ti->oi", grad_branch, attn_cat).astype(bf16)
    grad_down_part = product("ot,ti->oi", grad_branch, hidden).astype(bf16)
    grad_attended = product("ot,oi->ti", grad_branch, full_o).astype(bf16)
    grad_attended = grad_attended.reshape(tokens_here, heads_here, HEAD).transpose(1, 0, 2)
    grad_hidden = product("ot,oi->ti", grad_branch, full_down)
    grad_up_pre = jax.vjp(gelu_exact, up_pre)[1](grad_hidden)[0].astype(bf16)
    grad_up_part = product("dt,tn->dn", normed[3], grad_up_pre).astype(bf16)
    grad_normed_ff = product("dn,tn->dt", full_up, grad_up_pre)
    grad_probs = product("hqd,hkd->hqk", grad_attended, values)
    grad_values = product("hqk,hqd->hkd", probs_low, grad_attended)
    inner = jnp.sum(attn_probs * grad_probs, axis=-1, keepdims=True)
    grad_scores = (attn_probs * (grad_probs - inner)).astype(bf16)
    grad_q_rot = product("hqk,hkd->hqd", grad_scores, key_heads) * scale_qk
    grad_k_rot = product("hqk,hqd->hkd", grad_scores, queries) * scale_qk

    def flat(heads):
        return heads.reshape(tokens_here, width_here).astype(bf16)

    grad_projs = (
        flat(rotary(grad_q_rot.transpose(1, 0, 2), -angles)),
        flat(rotary(grad_k_rot.transpose(1, 0, 2), -angles)),
        flat(grad_values.transpose(1, 0, 2)),
    )
    grad_qkv_part = jnp.stack(
        [product("dt,tn->dn", normed[s], grad_projs[s]).astype(bf16) for s in range(3)]
    )
    grad_normed = jnp.stack(
        [product("dn,tn->dt", full_qkv[s], grad_projs[s]).astype(bf16) for s in range(3)]
        + [grad_normed_ff.astype(bf16)]
    )
    norm_inner = jnp.sum(jnp.stack(normed).astype(f32) * grad_normed.astype(f32), axis=1)

    def eight(rows):
        return jnp.pad(rows, ((0, 8 - rows.shape[0]), (0, 0)))

    little = jnp.concatenate(
        [
            grad_m1_part,
            jnp.zeros((width, STREAMS), f32),
            grad_gain_mix[:, None],
            jnp.zeros((width, WIDE - MIXH - STREAMS - 1), f32),
        ],
        axis=1,
    )
    second = jnp.pad(grad_mix2_part, ((0, 0), (0, WIDE - MIXH)))
    feature_side, mix_sum, little_sum, second_sum, sums = backward_exchange(
        n,
        grad_normed,
        eight(norm_inner),
        eight(level),
        inputs,
        grad_out_full,
        out_low,
        smalls,
        little,
        second,
        history,
        mixes,
        (grad_qkv_part, grad_o_part, grad_up_part, grad_down_part),
    )
    grad_history, block_out = history_gradient(feature_side, mixes)
    grad_qkv, grad_w_out, grad_w_up, grad_w_down = sums
    return (
        block_out,
        mix_out,
        grad_history,
        mix_sum.T,
        grad_qkv,
        grad_w_out,
        grad_w_up,
        grad_w_down,
        little_sum[:, :MIXH],
        second_sum[:, :MIXH],
        little_sum[:, MIXH : MIXH + STREAMS + 1].T,
    )


def solution(mesh):
    return jax.shard_map(
        body,
        mesh=mesh,
        in_specs=(
            P(None, "dp", None),
            P("dp", None),
            P("dp", None),
            P("dp", None),
            P(),
            P(None, "dp", "mp"),
            P("dp", "mp"),
            P("dp", "mp"),
            P("dp", "mp"),
            P("dp", None),
            P(),
            P(None, "dp"),
            P("dp", None),
            P("dp", None),
        ),
        out_specs=(
            P("dp", None),
            P("dp", None),
            P(None, "dp", None),
            P("dp", None),
            P(None, "dp", "mp"),
            P("dp", "mp"),
            P("dp", "mp"),
            P("dp", "mp"),
            P("dp", None),
            P(),
            P(None, "dp"),
        ),
        check_vma=False,
    )
```

```python
import functools
import math

import jax
import jax.numpy as jnp
from jax import lax
from jax.experimental import pallas as pl
from jax.experimental.pallas import tpu as pltpu
from jax.sharding import PartitionSpec as P

HEAD = 128
ROT = 32
HIST = 9
STREAMS = 4
GROUPS = 8
TOK_DEV = 384
MIXH = 40
WIDE = 128
EPS = 1e-05
AHEAD = 6
CUTS = (1, 1, 2, 2)
MESH = pl.DeviceIdType.MESH
DMA = pltpu.SemaphoreType.DMA
f32 = jnp.float32
bf16 = jnp.bfloat16


def chip_at(pos, ring):
    far = pos // (ring // 2)
    return (1 - far) * 2 * pos + far * (2 * (ring - 1 - pos) + 1)


def place_of(chip, ring):
    odd = chip % 2
    return (1 - odd) * (chip // 2) + odd * (ring - 1 - chip // 2)


def remote(src, dst, send, recv, device):
    return pltpu.make_async_remote_copy(
        src_ref=src,
        dst_ref=dst,
        send_sem=send,
        recv_sem=recv,
        device_id=device,
        device_id_type=MESH,
    )


def greet_plane(n, me, mp):
    barrier = pltpu.get_barrier_semaphore()

    @pl.loop(1, n)
    def _(k):
        pl.semaphore_signal(barrier, inc=1, device_id={"dp": (me + k) % n}, device_id_type=MESH)

    pl.semaphore_signal(barrier, inc=1, device_id={"mp": 1 - mp}, device_id_type=MESH)
    pl.semaphore_wait(barrier, n)


def rows_of(ref, start, count):
    if len(ref.shape) == 3:
        return ref.at[:, pl.ds(start, count), :]
    return ref.at[pl.ds(start, count), :]


def cuts_of(shards, cuts):
    pieces = []
    for i, shard in enumerate(shards):
        if len(shard.shape) == 3:
            pieces += [(i, s, 0) for s in range(shard.shape[0])]
        else:
            wide = shard.shape[1] // cuts[i]
            pieces += [(i, k * wide, wide) for k in range(cuts[i])]
    return pieces


def piece_of(refs, piece, start, count):
    i, first, wide = piece
    if wide == 0:
        return refs[i].at[first, pl.ds(start, count), :]
    return refs[i].at[pl.ds(start, count), pl.ds(first, wide)]


class Ring:
    def __init__(self, n):
        self.n, self.ring = n, n // 2
        self.me = lax.axis_index("dp")
        self.core = self.me % 2
        self.place = place_of(self.me // 2, self.ring)
        self.mate = self.me + 1 - 2 * self.core
        self.next_of = ({"dp": self.owner(1)}, {"dp": self.owner(-1)})

    def owner(self, offset):
        return chip_at((self.place + offset + 2 * self.ring) % self.ring, self.ring) * 2 + self.core


def forward_kernel(n, count, *refs):
    hist, cot, mix, small, tables, docs_row, docs_col = refs[:7]
    shards = refs[7 : 7 + count]
    refs = refs[7 + count :]
    inputs, mixes, smalls, normed_out, level, heads_out, attn_out, pre_out, hidden_out, total = refs[:10]
    fulls = refs[10 : 10 + count]
    (
        hist_buf,
        slots,
        streams,
        normed,
        tiles,
        heads,
        attn,
        pre_buf,
        hidden,
        down_buf,
        out_buf,
        branch,
        branch_land,
        hist_sem,
        cot_sem,
        own_sem,
        local_sem,
        keep_sem,
        tile_sem,
        pre_sem,
        row_sem,
        swap_send,
        swap_recv,
        mix_send,
        mix_recv,
        small_send,
        small_recv,
        a_send,
        a_recv,
        y_send,
        y_recv,
        ring_send,
        ring_recv,
        core_send,
        core_recv,
    ) = refs[10 + count :]
    where = Ring(n)
    me, ring, owner = where.me, where.ring, where.owner
    mp = lax.axis_index("mp")
    across = {"mp": 1 - mp}
    feat, tokens = hist.shape[1], mix.shape[1]
    h = feat // 2
    width = n * feat
    size = shards[0].shape[-2]
    half = size // 2
    w_qkv, w_out, w_up, w_down = fulls
    greet_plane(n, me, mp)

    pieces = cuts_of(shards, CUTS)

    def of(*arrays):
        return [p for p, piece in enumerate(pieces) if piece[0] in arrays]

    def origin_rows(offset, way):
        return pl.multiple_of(owner(offset) * size + way * half, half)

    def ring_copy(way, step, p, first=False):
        there = piece_of(fulls, pieces[p], origin_rows(-step if way == 0 else step, way), half)
        here = piece_of(shards, pieces[p], way * half, half) if first else there
        return remote(
            here, there, ring_send.at[way, step, p], ring_recv.at[way, step, p], where.next_of[way]
        )

    def ring_arrival(way, step, p):
        offset = -step - 1 if way == 0 else step + 1
        there = piece_of(fulls, pieces[p], origin_rows(offset, way), half)
        return remote(
            there, there, ring_send.at[way, step, p], ring_recv.at[way, step, p], where.next_of[way]
        )

    def core_copy(way, step, p, first=False):
        there = piece_of(fulls, pieces[p], origin_rows(-step if way == 0 else step, way), half)
        here = piece_of(shards, pieces[p], way * half, half) if first else there
        return remote(
            here, there, core_send.at[way, step, p], core_recv.at[way, step, p], {"dp": where.mate}
        )

    def shard_copy(i):
        return pltpu.make_async_copy(shards[i], rows_of(fulls[i], me * size, size), local_sem.at[i])

    def ring_begin(some):
        for p in some:
            for way in range(2):
                ring_copy(way, 0, p, True).start()

    def ring_step(step, some):
        for p in some:
            for way in range(2):
                ring_arrival(way, step - 1, p).wait_recv()
                ring_copy(way, step, p).start()
                core_copy(way, step, p).start()

    def ring_end(some):
        for p in some:
            for way in range(2):
                ring_arrival(way, ring - 2, p).wait_recv()
                core_copy(way, ring - 1, p).start()

    def ring_complete(*arrays):
        for i in arrays:
            shard_copy(i).wait()
        for p in of(*arrays):

            @pl.loop(0, ring)
            def _(step):
                for way in range(2):
                    core_copy(way, step, p).wait_recv()

    def mix_copy(q):
        return remote(
            mix, mixes.at[me], mix_send.at[q], mix_recv.at[q], {"dp": (me + q) % n}
        )

    def small_copy(q):
        return remote(
            small,
            smalls.at[pl.ds(pl.multiple_of(me * feat, feat), feat)],
            small_send.at[q],
            small_recv.at[q],
            {"dp": (me + q) % n},
        )

    def lanes(peer):
        return pl.ds(pl.multiple_of(peer * tokens, 128), tokens)

    def hist_copy(q):
        peer = (me + q) % n
        return pltpu.make_async_copy(
            hist.at[:, pl.ds(pl.multiple_of(mp * h, h), h), lanes(peer)],
            hist_buf.at[q % 2],
            hist_sem.at[q % 2],
        )

    def cot_copy(q):
        peer = (me + q) % n
        return pltpu.make_async_copy(
            cot.at[pl.ds(pl.multiple_of(mp * h, h), h), lanes(peer)],
            slots.at[q, STREAMS],
            cot_sem.at[q],
        )

    def features(source, plane):
        return streams.at[:, pl.ds(pl.multiple_of(source * feat + plane * h, h), h), :]

    def stream_copy(q):
        return remote(
            slots.at[q], features(me, mp), a_send.at[q], a_recv.at[q], {"dp": (me + q) % n}
        )

    def own_copy():
        return pltpu.make_async_copy(slots.at[0], features(me, mp), own_sem)

    def across_copy(q, own=False):
        there = features((me - q + n) % n, mp)
        return remote(
            slots.at[0] if own else there, there, y_send.at[q], y_recv.at[q], across
        )

    def mix_streams(q):
        peer = (me + q) % n

        @pl.loop(0, h // 16)
        def _(r):
            rows = pl.ds(pl.multiple_of(r * 16, 16), 16)
            sums = [None] * STREAMS
            for j in range(HIST):
                entry = hist_buf[q % 2, j, rows, :].astype(f32)
                for s in range(STREAMS):
                    term = mixes[peer, pl.ds(s * HIST + j, 1), :] * entry
                    sums[s] = term if j == 0 else sums[s] + term
            for s in range(STREAMS):
                slots[q, s, rows, :] = sums[s].astype(bf16)

    def normalise():
        level[...] = jnp.zeros_like(level)
        for s in range(STREAMS):

            def add(r, total):
                part = streams[s, pl.ds(pl.multiple_of(r * 32, 32), 32), :].astype(f32)
                part = part * part
                return total + (part[0:8] + part[8:16]) + (part[16:24] + part[24:32])

            squares = lax.fori_loop(0, width // 32, add, jnp.zeros((8, tokens), f32))
            mean = jnp.sum(squares, axis=0, keepdims=True) * (1.0 / width)
            level[pl.ds(s, 1), :] = lax.rsqrt(mean + EPS)

        @pl.loop(0, width // 32)
        def _(r):
            rows = pl.ds(pl.multiple_of(r * 32, 32), 32)
            gain = smalls[rows, :].astype(f32)
            for s in range(STREAMS):
                unit = streams[s, rows, :].astype(f32) * level[pl.ds(s, 1), :]
                normed[s, rows, :] = (unit * gain[:, MIXH + s : MIXH + s + 1]).astype(bf16)

    def head_tiles(pair, spot):
        columns = pl.ds(pl.multiple_of(pair * 2 * HEAD, 2 * HEAD), 2 * HEAD)
        return [
            pltpu.make_async_copy(
                w_qkv.at[s, :, columns], tiles.at[spot * 3 + s], tile_sem.at[spot * 3 + s]
            )
            for s in range(3)
        ]

    def first_dims(left, right):
        return lax.dot_general(left, right, (((0,), (0,)), ((), ())), preferred_element_type=f32)

    def last_dims(left, right):
        return lax.dot_general(left, right, (((1,), (1,)), ((), ())), preferred_element_type=f32)

    def attend(pair):
        spot = pair % 2
        for copy in head_tiles(pair, spot):
            copy.wait()

        @pl.when(pair < heads.shape[1] // 2 - 1)
        def _():
            for copy in head_tiles(pair + 1, 1 - spot):
                copy.start()

        for s in range(3):
            both = first_dims(normed[s], tiles[spot * 3 + s])
            for u in range(2):
                one = both[:, u * HEAD : (u + 1) * HEAD]
                if s < 2:
                    one = (
                        one * tables[0]
                        + pltpu.roll(one, HEAD - ROT // 2, 1) * tables[1]
                        + pltpu.roll(one, ROT // 2, 1) * tables[2]
                    )
                heads[s, pair * 2 + u] = one.astype(bf16)
        place = lax.broadcasted_iota(jnp.int32, (tokens, tokens), 0)
        other = lax.broadcasted_iota(jnp.int32, (tokens, tokens), 1)
        allowed = (place >= other) & (docs_col[...] == docs_row[...])
        for u in range(2):
            scores = last_dims(heads[0, pair * 2 + u], heads[1, pair * 2 + u]) * HEAD ** (-0.5)
            scores = jnp.where(allowed, scores, -1000000000.0)
            weight = jnp.exp(scores - jnp.max(scores, axis=1, keepdims=True))
            probs = weight * (1.0 / jnp.sum(weight, axis=1, keepdims=True))
            value = jnp.dot(
                probs.astype(bf16), heads[2, pair * 2 + u], preferred_element_type=f32
            )
            attn[:, pl.ds(pl.multiple_of((pair * 2 + u) * HEAD, HEAD), HEAD)] = value.astype(bf16)

    chunk = 512
    ups = hidden.shape[1] // chunk

    def up_tile(c, spot):
        return [
            pltpu.make_async_copy(
                w_up.at[:, pl.ds(pl.multiple_of(c * chunk + k * 256, 256), 256)],
                tiles.at[spot * 2 + k],
                tile_sem.at[spot * 2 + k],
            )
            for k in range(2)
        ]

    def pre_copy(c):
        return pltpu.make_async_copy(
            pre_buf.at[c % 2],
            pre_out.at[:, pl.ds(pl.multiple_of(c * chunk, chunk), chunk)],
            pre_sem.at[c % 2],
        )

    def feed(c, spot):
        for copy in up_tile(c, spot):
            copy.wait()

        @pl.when(c < ups - 1)
        def _():
            for copy in up_tile(c + 1, 1 - spot):
                copy.start()

        @pl.when(c >= 2)
        def _():
            pre_copy(c - 2).wait()

        for k in range(2):
            pre = first_dims(normed[STREAMS - 1], tiles[spot * 2 + k])
            pre_buf[c % 2, :, k * 256 : (k + 1) * 256] = pre
            low = (0.5 * pre * (1.0 + lax.erf(pre * math.sqrt(0.5)))).astype(bf16)
            hidden[:, pl.ds(pl.multiple_of(c * chunk + k * 256, 256), 256)] = low
        pre_copy(c).start()

    deep = down_buf.shape[1]

    def row_tiles(c):
        rows = pl.ds(c * deep, deep)
        return [
            pltpu.make_async_copy(w_down.at[rows, :], down_buf.at[c % 2], row_sem.at[c % 2, 0]),
            pltpu.make_async_copy(w_out.at[rows, :], out_buf.at[c % 2], row_sem.at[c % 2, 1]),
        ]

    def swap_copy(c):
        rows = pl.ds(c * deep, deep)
        return remote(
            branch.at[rows], branch_land.at[rows], swap_send.at[c], swap_recv.at[c], across
        )

    def keep(k):
        pairs = [
            (streams, inputs),
            (normed, normed_out),
            (heads, heads_out),
            (attn, attn_out),
            (hidden, hidden_out),
        ]
        return pltpu.make_async_copy(pairs[k][0], pairs[k][1], keep_sem.at[k])

    def stream_turn(q):
        hist_copy(q).wait()

        @pl.when(q < n - 1)
        def _():
            hist_copy(q + 1).start()

        mix_copy(n - q).wait_recv()
        mix_streams(q)
        cot_copy(q).wait()
        stream_copy(q).start()

    def forward_turn(q):
        stream_copy(q).wait_recv()
        across_copy(q).start()

    @pl.loop(1, n)
    def _(q):
        mix_copy(q).start()
        small_copy(q).start()

    @pl.loop(0, n)
    def _(q):
        cot_copy(q).start()

    hist_copy(0).start()
    ring_begin(of(0, 1))
    own_small = pltpu.make_async_copy(
        small, smalls.at[pl.ds(pl.multiple_of(me * feat, feat), feat)], local_sem.at[count]
    )
    own_small.start()
    mixes[me] = mix[...]
    hist_copy(0).wait()
    hist_copy(1).start()
    mix_streams(0)
    cot_copy(0).wait()
    own_copy().start()
    across_copy(0, True).start()

    @pl.loop(1, 4)
    def _(q):
        stream_turn(q)

    for p in range(len(pieces)):
        for way in range(2):
            core_copy(way, 0, p, True).start()
    for i in range(count):
        shard_copy(i).start()
    ring_begin(of(2))

    @pl.loop(1, ring - 1)
    def _(step):
        ring_step(step, of(0, 1))
        for u in range(2):
            stream_turn(2 + 2 * step + u)
        for u in range(2):
            forward_turn(2 * step - 1 + u)

    ring_end(of(0, 1))
    ring_begin(of(3))

    @pl.loop(n - 3, n)
    def _(q):
        forward_turn(q)

    own_copy().wait()
    own_small.wait()

    @pl.loop(1, n)
    def _(q):
        small_copy(q).wait_recv()

    @pl.loop(0, n)
    def _(q):
        across_copy(q).wait_recv()

    keep(0).start()
    ring_complete(0, 1)
    for copy in head_tiles(0, 0):
        copy.start()
    normalise()
    keep(1).start()
    pairs = heads.shape[1] // 2

    @pl.loop(1, ring - 1)
    def _(step):
        ring_step(step, of(2))

        @pl.when(step <= pairs)
        def _():
            attend(step - 1)

    keep(2).start()
    keep(3).start()
    ring_end(of(2))
    ring_complete(2)
    for copy in up_tile(0, 0):
        copy.start()

    @pl.loop(1, ring - 1)
    def _(step):
        ring_step(step, of(3))

        @pl.when(step <= ups - 2)
        def _():
            feed(step - 1, (step - 1) % 2)

    feed(ups - 2, (ups - 2) % 2)
    feed(ups - 1, (ups - 1) % 2)
    keep(4).start()
    ring_end(of(3))
    ring_complete(3)
    rounds = width // deep
    for copy in row_tiles(0):
        copy.start()
    for c in range(rounds):
        if c < rounds - 1:
            for copy in row_tiles(c + 1):
                copy.start()
        for copy in row_tiles(c):
            copy.wait()
        part = last_dims(down_buf[c % 2], hidden[...]) + last_dims(out_buf[c % 2], attn[...])
        branch[pl.ds(c * deep, deep)] = part.astype(bf16)
        swap_copy(c).start()
    for c in range(rounds):
        swap_copy(c).wait_recv()

        @pl.loop(0, deep // 32)
        def _(r):
            rows = pl.ds(pl.multiple_of(c * deep + r * 32, 32), 32)
            both = branch[rows, :].astype(f32) + branch_land[rows, :].astype(f32)
            total[rows, :] = streams[STREAMS - 1, rows, :].astype(f32) + both

    for c in range(ups - 2, ups):
        pre_copy(c).wait()
    for k in range(5):
        keep(k).wait()
    for c in range(rounds):
        swap_copy(c).wait_send()

    @pl.loop(1, n)
    def _(q):
        mix_copy(q).wait_send()
        small_copy(q).wait_send()
        stream_copy(q).wait_send()

    @pl.loop(0, n)
    def _(q):
        across_copy(q).wait_send()

    @pl.loop(0, ring)
    def _(step):
        for p in range(len(pieces)):
            for way in range(2):
                core_copy(way, step, p).wait_send()

    @pl.loop(0, ring - 1)
    def _(step):
        for p in range(len(pieces)):
            for way in range(2):
                ring_copy(way, step, p).wait_send()


def forward_exchange(n, history, cot_out, mix, small, tables, docs, shards):
    count, ring = len(shards), n // 2
    feat, tokens = history.shape[1], mix.shape[1]
    h, width = feat // 2, n * feat
    hbm = pl.BlockSpec(memory_space=pl.ANY)
    vmem = pl.BlockSpec(memory_space=pltpu.VMEM)
    columns, units = shards[0].shape[2], shards[2].shape[1]
    across = columns // HEAD
    deep = 512
    rounds = width // deep
    travel = len(cuts_of(shards, CUTS))
    found = pl.pallas_call(
        functools.partial(forward_kernel, n, count),
        out_shape=[
            jax.ShapeDtypeStruct((STREAMS + 1, width, tokens), bf16),
            jax.ShapeDtypeStruct((n,) + mix.shape, f32),
            jax.ShapeDtypeStruct((width, WIDE), bf16),
            jax.ShapeDtypeStruct((STREAMS, width, tokens), bf16),
            jax.ShapeDtypeStruct((8, tokens), f32),
            jax.ShapeDtypeStruct((3, across, tokens, HEAD), bf16),
            jax.ShapeDtypeStruct((tokens, columns), bf16),
            jax.ShapeDtypeStruct((tokens, units), f32),
            jax.ShapeDtypeStruct((tokens, units), bf16),
            jax.ShapeDtypeStruct((width, tokens), f32),
        ]
        + [
            jax.ShapeDtypeStruct(s.shape[:-2] + (s.shape[-2] * n, s.shape[-1]), s.dtype)
            for s in shards
        ],
        in_specs=[hbm, hbm, vmem, hbm, vmem, vmem, vmem] + [hbm] * count,
        out_specs=[hbm, vmem, vmem, hbm, vmem, hbm, hbm, hbm, hbm, vmem] + [hbm] * count,
        scratch_shapes=[
            pltpu.VMEM((2, HIST, h, tokens), bf16),
            pltpu.VMEM((n, STREAMS + 1, h, tokens), bf16),
            pltpu.VMEM((STREAMS + 1, width, tokens), bf16),
            pltpu.VMEM((STREAMS, width, tokens), bf16),
            pltpu.VMEM((6, width, 2 * HEAD), bf16),
            pltpu.VMEM((3, across, tokens, HEAD), bf16),
            pltpu.VMEM((tokens, columns), bf16),
            pltpu.VMEM((2, tokens, 512), f32),
            pltpu.VMEM((tokens, units), bf16),
            pltpu.VMEM((2, deep, units), bf16),
            pltpu.VMEM((2, deep, columns), bf16),
            pltpu.VMEM((width, tokens), bf16),
            pltpu.VMEM((width, tokens), bf16),
            DMA((2,)),
            DMA((n,)),
            DMA,
            DMA((count + 1,)),
            DMA((5,)),
            DMA((6,)),
            DMA((2,)),
            DMA((2, 2)),
            DMA((rounds,)),
            DMA((rounds,)),
        ]
        + [DMA((n,)) for _ in range(8)]
        + [DMA((2, ring - 1, travel)) for _ in range(2)]
        + [DMA((2, ring, travel)) for _ in range(2)],
        compiler_params=pltpu.CompilerParams(
            collective_id=0, has_side_effects=True, vmem_limit_bytes=60 * 1024 * 1024
        ),
    )(history, cot_out, mix, small, tables, docs, docs.T, *shards)
    return found[:10], found[10:]


def backward_kernel(n, count, *refs):
    grads, inner, scale, inputs, direct, output, smalls, little, second, hist, mixes = refs[:11]
    parts = refs[11 : 11 + count]
    refs = refs[11 + count :]
    across_land, feature_side, mix_sum, little_sum, second_sum = refs[:5]
    sums, mates = refs[5 : 5 + count], refs[5 + count : 5 + 2 * count]
    refs = refs[5 + 2 * count :]
    slots, own, other, final = (refs[k * count : (k + 1) * count] for k in range(4))
    (
        inner_land,
        d_buf,
        e_buf,
        x_buf,
        go_buf,
        g_buf,
        l_buf,
        g_slots,
        l_slots,
        l_land,
        second_land,
        f_buf,
        h_buf,
        m_slots,
        m_land,
        m_mine,
        m_other,
        l_sum,
        load_sem,
        out_sem,
        back_sem,
        own_sem,
        other_sem,
        final_sem,
        y_send,
        y_recv,
        p_sem,
        a_send,
        a_recv,
        l_send,
        l_recv,
        w_send,
        w_recv,
        fy_send,
        fy_recv,
        m_send,
        m_recv,
        end_sem,
        ring_send,
        ring_recv,
        core_send,
        core_recv,
    ) = refs[4 * count :]
    where = Ring(n)
    me, ring, owner = where.me, where.ring, where.owner
    mp = lax.axis_index("mp")
    across = {"mp": 1 - mp}
    feat, tokens = hist.shape[1], inner.shape[1]
    h = feat // 2
    size = sums[0].shape[-2]
    half = size // 2
    greet_plane(n, me, mp)

    def target(way, step):
        return -1 - step if way == 0 else 1 + step

    def core_copy(way, step, i):
        theirs = owner(target(way, step)) + (where.mate - me)
        start = pl.multiple_of(theirs * size + way * half, half)
        return remote(
            rows_of(parts[i], start, half),
            mates[i].at[way, step],
            core_send.at[way, step, i],
            core_recv.at[way, step, i],
            {"dp": where.mate},
        )

    def own_copy(way, step, i):
        start = pl.multiple_of(owner(target(way, step)) * size + way * half, half)
        spot = step % 2
        return pltpu.make_async_copy(
            rows_of(parts[i], start, half), own[i].at[way, spot], own_sem.at[way, spot, i]
        )

    def other_copy(way, step, i):
        spot = step % 2
        return pltpu.make_async_copy(
            mates[i].at[way, step], other[i].at[way, spot], other_sem.at[way, spot, i]
        )

    def ring_copy(way, step, i):
        return remote(
            slots[i].at[way, step],
            slots[i].at[way, step + 1],
            ring_send.at[way, step, i],
            ring_recv.at[way, step, i],
            where.next_of[way],
        )

    def final_copy(way, i):
        return pltpu.make_async_copy(
            final[i], rows_of(sums[i], way * half, half), final_sem.at[i]
        )

    def stage(way, step, i):
        own_copy(way, step, i).start()
        core_copy(way, step, i).wait_recv()
        other_copy(way, step, i).start()

    def staged(way, step, i):
        own_copy(way, step, i).wait()
        other_copy(way, step, i).wait()

    def add(way, step, i, first=False, last=False):
        spot = step % 2
        deep = len(parts[i].shape) == 3
        slot, mine, theirs = slots[i].at[way, step], own[i].at[way, spot], other[i].at[way, spot]
        for k in range(parts[i].shape[0] if deep else 1):

            @pl.loop(0, half // 16)
            def _(r):
                rows = pl.ds(pl.multiple_of(r * 16, 16), 16)
                at = (k, rows) if deep else (rows,)
                total = mine[at].astype(f32) + theirs[at].astype(f32)
                if not first:
                    total = total + slot[at].astype(f32)
                if last:
                    final[i][at] = total
                else:
                    slot[at] = total.astype(bf16)

    def span(peer, plane):
        return pl.ds(pl.multiple_of(peer * feat + plane * h, h), h)

    def sum_copy(q):
        peer = (me + q) % n
        return remote(
            grads.at[:, span(peer, 1 - mp), :],
            across_land.at[q],
            y_send.at[q],
            y_recv.at[q],
            across,
        )

    def inner_copy():
        return remote(inner, inner_land, p_sem.at[0], p_sem.at[1], across)

    def loads(q):
        rows = span((me + q) % n, mp)
        spot = q % 2
        return [
            pltpu.make_async_copy(grads.at[:, rows, :], d_buf.at[spot], load_sem.at[spot, 0]),
            pltpu.make_async_copy(across_land.at[q], e_buf.at[spot], load_sem.at[spot, 1]),
            pltpu.make_async_copy(
                inputs.at[pl.ds(0, STREAMS), rows, :], x_buf.at[spot], load_sem.at[spot, 2]
            ),
            pltpu.make_async_copy(direct.at[rows, :], go_buf.at[spot], load_sem.at[spot, 3]),
            pltpu.make_async_copy(smalls.at[rows, :], g_buf.at[spot], load_sem.at[spot, 4]),
            pltpu.make_async_copy(little.at[rows, :], l_buf.at[spot], load_sem.at[spot, 5]),
        ]

    def out_copy(q):
        rows = span((me + q) % n, mp)
        return pltpu.make_async_copy(output.at[rows, :], g_slots.at[q, STREAMS], out_sem.at[q])

    def place(source, plane):
        return feature_side.at[source, :, pl.ds(pl.multiple_of(plane * h, h), h), :]

    def stream_copy(q):
        return remote(
            g_slots.at[q], place(me, mp), a_send.at[q], a_recv.at[q], {"dp": (me + q) % n}
        )

    def little_copy(q):
        return remote(
            l_slots.at[q], l_land.at[q], l_send.at[q], l_recv.at[q], {"dp": (me + q) % n}
        )

    def second_copy(q):
        return remote(
            second, second_land.at[me], w_send.at[q], w_recv.at[q], {"dp": (me + q) % n}
        )

    def home_copy():
        return pltpu.make_async_copy(g_slots.at[0], place(me, mp), end_sem.at[0])

    def across_copy(q, own=False):
        there = place((me - q + n) % n, mp)
        return remote(
            g_slots.at[0] if own else there, there, fy_send.at[q], fy_recv.at[q], across
        )

    def start_loads(q):
        sum_copy(q).wait_recv()
        for copy in loads(q):
            copy.start()

    def norm_backward(q):
        spot = q % 2
        for copy in loads(q):
            copy.wait()

        @pl.loop(0, h // 16)
        def _(r):
            rows = pl.ds(pl.multiple_of(r * 16, 16), 16)
            tail = l_buf[spot, rows, :]
            lane = lax.broadcasted_iota(jnp.int32, tail.shape, 1)
            for s in range(STREAMS):
                dy = d_buf[spot, s, rows, :].astype(f32) + e_buf[spot, s, rows, :].astype(f32)
                level = scale[pl.ds(s, 1), :]
                common = (inner[pl.ds(s, 1), :] + inner_land[pl.ds(s, 1), :]) * level
                common = common * (1.0 / (n * feat))
                unit = x_buf[spot, s, rows, :].astype(f32) * level
                gain = g_buf[spot, rows, :].astype(f32)[:, MIXH + s : MIXH + s + 1]
                grad = level * (gain * dy) - unit * common
                if s == STREAMS - 1:
                    grad = grad + go_buf[spot, rows, :]
                g_slots[q, s, rows, :] = grad.astype(bf16)
                gain_grad = jnp.sum(unit * dy, axis=1, keepdims=True)
                tail = jnp.where(lane == MIXH + s, gain_grad, tail)
            l_slots[q, rows, :] = tail

    def norm_turn(q):
        @pl.when(q < n - 1)
        def _():
            start_loads(q + 1)

        @pl.when(q < n - AHEAD)
        def _():
            sum_copy(q + AHEAD).start()

        norm_backward(q)
        out_copy(q).wait()

        @pl.when(q == 0)
        def _():
            home_copy().start()
            across_copy(q, True).start()

        @pl.when(q > 0)
        def _():
            stream_copy(q).start()
            little_copy(q).start()

    def hist_load(q):
        source = (me - q + n) % n
        return pltpu.make_async_copy(
            hist.at[
                :,
                pl.ds(pl.multiple_of(mp * h, h), h),
                pl.ds(pl.multiple_of(source * tokens, 128), tokens),
            ],
            h_buf.at[q % 2],
            back_sem.at[q % 2, 0],
        )

    def grad_load(q):
        source = (me - q + n) % n
        return pltpu.make_async_copy(
            feature_side.at[source, pl.ds(0, STREAMS), pl.ds(pl.multiple_of(mp * h, h), h), :],
            f_buf,
            back_sem.at[0, 1],
        )

    def mix_copy(q):
        return remote(
            m_slots.at[q],
            m_land.at[q],
            m_send.at[q],
            m_recv.at[q],
            {"dp": (me - q + n) % n},
        )

    def mix_backward(q):
        for s in range(STREAMS):
            totals = [None] * HIST
            for r in range(h // 16):
                grad = f_buf[s, r * 16 : r * 16 + 16, :].astype(f32)
                for j in range(HIST):
                    both = h_buf[q % 2, j, r * 16 : r * 16 + 16, :].astype(f32) * grad
                    both = both[0:8] + both[8:16]
                    totals[j] = both if r == 0 else totals[j] + both
            for j in range(HIST):
                m_slots[q, pl.ds(s * HIST + j, 1), :] = jnp.sum(totals[j], axis=0, keepdims=True)

    def mix_turn(q):
        @pl.when(q < n - 1)
        def _():
            hist_load(q + 1).start()

        @pl.when(q == 0)
        def _():
            home_copy().wait()

        @pl.when(q > 0)
        def _():
            stream_copy(q).wait_recv()
            across_copy(q).start()

        grad_load(q).start()
        grad_load(q).wait()
        hist_load(q).wait()
        mix_backward(q)

        @pl.when(q > 0)
        def _():
            mix_copy(q).start()

    pieces = [(i, way) for i in range(count) for way in range(2)]

    inner_copy().start()
    for step in range(2):
        for i, way in pieces:
            core_copy(way, step, i).start()

    @pl.loop(0, AHEAD)
    def _(q):
        sum_copy(q).start()

    @pl.loop(0, n)
    def _(q):
        out_copy(q).start()

    second_land[me] = second[...]

    @pl.loop(1, n)
    def _(q):
        second_copy(q).start()

    for i, way in pieces:
        stage(way, 0, i)
    for i, way in pieces:
        staged(way, 0, i)
        add(way, 0, i, first=True)
        ring_copy(way, 0, i).start()
        stage(way, 1, i)
    inner_copy().wait()
    start_loads(0)

    def ring_unit(step, i, way):
        staged(way, step, i)
        ring_copy(way, step - 1, i).wait_recv()
        add(way, step, i)
        ring_copy(way, step, i).start()
        stage(way, step + 1, i)

    def mates_ahead(step):
        for i, way in pieces:
            core_copy(way, step + 1, i).start()

    hist_load(0).start()

    @pl.loop(1, ring - 1)
    def _(step):
        mates_ahead(step)
        for u, (i, way) in enumerate(pieces):
            ring_unit(step, i, way)
            if u % 2 == 0:

                @pl.when(step <= n // 4)
                def _():
                    norm_turn(4 * (step - 1) + u // 2)
            else:

                @pl.when((step >= 2) & (step <= n // 4 + 1))
                def _():
                    mix_turn(4 * (step - 2) + u // 2)

    @pl.loop(1, n)
    def _(q):
        little_copy(q).wait_recv()
        second_copy(q).wait_recv()
        mix_copy(q).wait_recv()

    def sum_over(land, mine):
        return lax.fori_loop(1, n, lambda q, total: total + land[q], mine)

    l_sum[...] = sum_over(l_land, l_slots[0])
    m_mine[...] = sum_over(m_land, m_slots[0])
    second_sum[...] = lax.fori_loop(
        1, n, lambda q, total: total + second_land[q], second_land[0]
    )
    here = pl.ds(pl.multiple_of(mp * h, h), h)
    little_home = pltpu.make_async_copy(l_sum, little_sum.at[here], end_sem.at[1])
    little_across = remote(l_sum, little_sum.at[here], end_sem.at[2], end_sem.at[3], across)
    mix_across = remote(m_mine, m_other, end_sem.at[4], end_sem.at[5], across)
    little_home.start()
    little_across.start()
    mix_across.start()

    for way in range(2):
        for i in range(count):
            staged(way, ring - 1, i)
            ring_copy(way, ring - 2, i).wait_recv()
            if way == 1:
                final_copy(0, i).wait()
            add(way, ring - 1, i, last=True)
            final_copy(way, i).start()

    mix_across.wait()
    mix_sum[...] = m_mine[...] + m_other[...]
    little_home.wait()
    little_across.wait()
    for i in range(count):
        final_copy(1, i).wait()

    @pl.loop(1, n)
    def _(q):
        stream_copy(q).wait_send()
        little_copy(q).wait_send()
        second_copy(q).wait_send()
        mix_copy(q).wait_send()

    @pl.loop(0, n)
    def _(q):
        sum_copy(q).wait_send()
        across_copy(q).wait()

    @pl.loop(0, ring - 1)
    def _(step):
        for i, way in pieces:
            ring_copy(way, step, i).wait_send()

    @pl.loop(0, ring)
    def _(step):
        for i, way in pieces:
            core_copy(way, step, i).wait_send()


def backward_exchange(
    n, grads, inner, scale, inputs, direct, output, smalls, little, second, history, mixes, parts
):
    count, ring = len(parts), n // 2
    feat, tokens = history.shape[1], grads.shape[2]
    h = feat // 2
    hbm = pl.BlockSpec(memory_space=pl.ANY)
    vmem = pl.BlockSpec(memory_space=pltpu.VMEM)

    def cut(s, rows):
        return s.shape[:-2] + (rows, s.shape[-1])

    half = parts[0].shape[-2] // n // 2
    found = pl.pallas_call(
        functools.partial(backward_kernel, n, count),
        out_shape=[
            jax.ShapeDtypeStruct((n, STREAMS, h, tokens), bf16),
            jax.ShapeDtypeStruct((n, STREAMS + 1, feat, tokens), bf16),
            jax.ShapeDtypeStruct((STREAMS * HIST, tokens), f32),
            jax.ShapeDtypeStruct((feat, WIDE), f32),
            jax.ShapeDtypeStruct(second.shape, f32),
        ]
        + [jax.ShapeDtypeStruct(cut(s, 2 * half), f32) for s in parts]
        + [jax.ShapeDtypeStruct((2, ring) + cut(s, half), bf16) for s in parts],
        in_specs=[hbm, vmem, vmem, hbm, hbm, hbm, hbm, hbm, vmem, hbm, hbm] + [hbm] * count,
        out_specs=[hbm, hbm, vmem, hbm, vmem] + [hbm] * (2 * count),
        scratch_shapes=[pltpu.VMEM((2, ring) + cut(s, half), bf16) for s in parts]
        + [pltpu.VMEM((2, 2) + cut(s, half), bf16) for s in parts]
        + [pltpu.VMEM((2, 2) + cut(s, half), bf16) for s in parts]
        + [pltpu.VMEM(cut(s, half), f32) for s in parts]
        + [
            pltpu.VMEM(inner.shape, f32),
            pltpu.VMEM((2, STREAMS, h, tokens), bf16),
            pltpu.VMEM((2, STREAMS, h, tokens), bf16),
            pltpu.VMEM((2, STREAMS, h, tokens), bf16),
            pltpu.VMEM((2, h, tokens), f32),
            pltpu.VMEM((2, h, WIDE), bf16),
            pltpu.VMEM((2, h, WIDE), f32),
            pltpu.VMEM((n, STREAMS + 1, h, tokens), bf16),
            pltpu.VMEM((n, h, WIDE), f32),
            pltpu.VMEM((n, h, WIDE), f32),
            pltpu.VMEM((n,) + second.shape, f32),
            pltpu.VMEM((STREAMS, h, tokens), bf16),
            pltpu.VMEM((2, HIST, h, tokens), bf16),
            pltpu.VMEM((n, STREAMS * HIST, tokens), f32),
            pltpu.VMEM((n, STREAMS * HIST, tokens), f32),
            pltpu.VMEM((STREAMS * HIST, tokens), f32),
            pltpu.VMEM((STREAMS * HIST, tokens), f32),
            pltpu.VMEM((h, WIDE), f32),
            DMA((2, 6)),
            DMA((n,)),
            DMA((2, 2)),
            DMA((2, 2, count)),
            DMA((2, 2, count)),
            DMA((count,)),
            DMA((n,)),
            DMA((n,)),
            DMA((2,)),
        ]
        + [DMA((n,)) for _ in range(10)]
        + [DMA((6,))]
        + [DMA((2, ring - 1, count)) for _ in range(2)]
        + [DMA((2, ring, count)) for _ in range(2)],
        compiler_params=pltpu.CompilerParams(
            collective_id=1, has_side_effects=True, vmem_limit_bytes=60 * 1024 * 1024
        ),
    )(grads, inner, scale, inputs, direct, output, smalls, little, second, history, mixes, *parts)
    return found[1], found[2], found[3], found[4], found[5 : 5 + count]


def history_kernel(grads, mixes, grad_history, block_out):
    feat = grads.shape[2]

    @pl.loop(0, feat // 16)
    def _(r):
        rows = pl.ds(pl.multiple_of(r * 16, 16), 16)
        each = [grads[0, s, rows, :].astype(f32) for s in range(STREAMS)]
        for j in range(HIST):
            total = mixes[0, pl.ds(j, 1), :] * each[0]
            for s in range(1, STREAMS):
                total = total + mixes[0, pl.ds(s * HIST + j, 1), :] * each[s]
            grad_history[j, rows, :] = total.astype(bf16)

    block_out[...] = grads[0, STREAMS]


def history_gradient(feature_side, mixes):
    n, streams, feat, tokens = feature_side.shape
    return pl.pallas_call(
        history_kernel,
        grid=(n,),
        out_shape=[
            jax.ShapeDtypeStruct((HIST, feat, n * tokens), bf16),
            jax.ShapeDtypeStruct((feat, n * tokens), bf16),
        ],
        in_specs=[
            pl.BlockSpec((1, streams, feat, tokens), lambda i: (i, 0, 0, 0)),
            pl.BlockSpec((1,) + mixes.shape[1:], lambda i: (i, 0, 0)),
        ],
        out_specs=[
            pl.BlockSpec((HIST, feat, tokens), lambda i: (0, 0, i)),
            pl.BlockSpec((feat, tokens), lambda i: (0, i)),
        ],
        compiler_params=pltpu.CompilerParams(vmem_limit_bytes=32 * 1024 * 1024),
    )(feature_side, mixes)


def rotary(heads_in, tables):
    ahead = jnp.roll(heads_in, -(ROT // 2), axis=-1)
    behind = jnp.roll(heads_in, ROT // 2, axis=-1)
    return heads_in * tables[0] + ahead * tables[1] + behind * tables[2]


def angle_tables(length):
    halfway = ROT // 2
    frequency = jnp.exp(jnp.arange(halfway, dtype=f32) * (-2.0 * math.log(10000.0) / ROT))
    places = (jnp.arange(length) % TOK_DEV).astype(f32)
    angles = places[:, None] * frequency[None, :]
    cosine, sine_part = jnp.cos(angles), jnp.sin(angles)
    rest = jnp.zeros((length, HEAD - ROT), f32)
    none = jnp.zeros((length, halfway), f32)
    return jnp.stack(
        [
            jnp.concatenate([cosine, cosine, rest + 1.0], axis=1),
            jnp.concatenate([-sine_part, none, rest], axis=1),
            jnp.concatenate([none, sine_part, rest], axis=1),
        ]
    )


def gelu_exact(inputs):
    return jax.nn.gelu(inputs, approximate=False)


def product(spec, left, right):
    return jnp.einsum(spec, left, right, preferred_element_type=f32)


def body(
    history,
    mix_in,
    doc_ids,
    group_ids,
    group_scale,
    w_qkv,
    w_out,
    w_up,
    w_down,
    w_mix1,
    w_mix2,
    gains,
    cot_out,
    cot_mix,
):
    n = lax.axis_size("dp")
    tokens_here = mix_in.shape[0]
    width = n * history.shape[1]
    small = jnp.pad(
        jnp.concatenate([w_mix1, gains.T], axis=1), ((0, 0), (0, WIDE - MIXH - gains.shape[0]))
    )
    tables = angle_tables(tokens_here)
    kept, (full_qkv, full_o, full_up, full_down) = forward_exchange(
        n, history, cot_out, mix_in.T, small, tables, doc_ids, (w_qkv, w_out, w_up, w_down)
    )
    inputs, mixes, smalls, normed, level, qkv_heads, attn_cat, up_pre, hidden, out_full = kept
    queries, key_heads, values = qkv_heads[0], qkv_heads[1], qkv_heads[2]
    heads_here = full_qkv.shape[2] // HEAD
    width_here = heads_here * HEAD
    full_m1 = smalls[:, :MIXH]
    gain_f = smalls[:, MIXH : MIXH + STREAMS + 1].astype(f32)
    scale_qk = HEAD ** (-0.5)
    positions = jnp.arange(tokens_here)
    doc_row = doc_ids[0]
    allowed = (positions[:, None] >= positions[None, :]) & (doc_row[:, None] == doc_row[None, :])
    scores = product("hqd,hkd->hqk", queries, key_heads) * scale_qk
    scores = jnp.where(allowed[None], scores, -1000000000.0)
    row_max = jnp.max(scores, axis=-1, keepdims=True)
    log_total = row_max + jnp.log(jnp.sum(jnp.exp(scores - row_max), axis=-1, keepdims=True))
    attn_probs = jnp.exp(scores - log_total)
    probs_low = attn_probs.astype(bf16)
    out_low = out_full.astype(bf16)
    mix_level = lax.rsqrt(jnp.mean(out_full * out_full, axis=0) + EPS)
    mix_unit = out_full * mix_level[None, :]
    mix_gain = gain_f[:, STREAMS : STREAMS + 1]
    mix_normed = (mix_unit * mix_gain).astype(bf16)
    mix_pre = product("dt,dm->tm", mix_normed, full_m1)
    mix_hidden = gelu_exact(mix_pre).astype(bf16)
    mix_out = product("tm,mo->to", mix_hidden, w_mix2)

    row_scale = jnp.sum(
        jnp.where(group_ids[0][:, None] == jnp.arange(GROUPS)[None, :], group_scale[None, :], 0.0),
        axis=1,
    )
    seed = inputs[STREAMS].astype(f32) * row_scale[None, :]
    grad_mix2_part = product("tm,to->mo", mix_hidden, cot_mix)
    grad_mix_hidden = product("to,mo->tm", cot_mix, w_mix2)
    grad_mix_pre = jax.vjp(gelu_exact, mix_pre)[1](grad_mix_hidden)[0].astype(bf16)
    grad_m1_part = product("dt,tm->dm", mix_normed, grad_mix_pre)
    grad_mix_normed = product("dm,tm->dt", full_m1, grad_mix_pre)
    grad_gain_mix = jnp.sum(mix_unit * grad_mix_normed, axis=1)
    mix_inner = jnp.mean(mix_unit * mix_gain * grad_mix_normed, axis=0)
    grad_out_full = seed + mix_level[None, :] * (
        mix_gain * grad_mix_normed - mix_unit * mix_inner[None, :]
    )
    grad_branch = grad_out_full.astype(bf16)
    grad_o_part = product("ot,ti->oi", grad_branch, attn_cat).astype(bf16)
    grad_down_part = product("ot,ti->oi", grad_branch, hidden).astype(bf16)
    grad_attended = product("ot,oi->ti", grad_branch, full_o).astype(bf16)
    grad_attended = grad_attended.reshape(tokens_here, heads_here, HEAD).transpose(1, 0, 2)
    grad_hidden = product("ot,oi->ti", grad_branch, full_down)
    grad_up_pre = jax.vjp(gelu_exact, up_pre)[1](grad_hidden)[0].astype(bf16)
    grad_up_part = product("dt,tn->dn", normed[3], grad_up_pre).astype(bf16)
    grad_normed_ff = product("dn,tn->dt", full_up, grad_up_pre)
    grad_probs = product("hqd,hkd->hqk", grad_attended, values)
    grad_values = product("hqk,hqd->hkd", probs_low, grad_attended)
    inner = jnp.sum(attn_probs * grad_probs, axis=-1, keepdims=True)
    grad_scores = (attn_probs * (grad_probs - inner)).astype(bf16)
    grad_q_rot = product("hqk,hkd->hqd", grad_scores, key_heads) * scale_qk
    grad_k_rot = product("hqk,hqd->hkd", grad_scores, queries) * scale_qk

    back_tables = (tables[0], -tables[1], -tables[2])

    def flat(heads):
        return heads.astype(bf16).transpose(1, 0, 2).reshape(tokens_here, width_here)

    grad_projs = (
        flat(rotary(grad_q_rot, back_tables)),
        flat(rotary(grad_k_rot, back_tables)),
        flat(grad_values),
    )
    grad_qkv_part = jnp.stack(
        [product("dt,tn->dn", normed[s], grad_projs[s]).astype(bf16) for s in range(3)]
    )
    grad_normed = jnp.stack(
        [product("dn,tn->dt", full_qkv[s], grad_projs[s]).astype(bf16) for s in range(3)]
        + [grad_normed_ff.astype(bf16)]
    )
    norm_inner = jnp.sum(normed.astype(f32) * grad_normed.astype(f32), axis=1)

    def eight(rows):
        return jnp.pad(rows, ((0, 8 - rows.shape[0]), (0, 0)))

    little = jnp.concatenate(
        [
            grad_m1_part,
            jnp.zeros((width, STREAMS), f32),
            grad_gain_mix[:, None],
            jnp.zeros((width, WIDE - MIXH - STREAMS - 1), f32),
        ],
        axis=1,
    )
    second = jnp.pad(grad_mix2_part, ((0, 0), (0, WIDE - MIXH)))
    feature_side, mix_sum, little_sum, second_sum, sums = backward_exchange(
        n,
        grad_normed,
        eight(norm_inner),
        level,
        inputs,
        grad_out_full,
        out_low,
        smalls,
        little,
        second,
        history,
        mixes,
        (grad_qkv_part, grad_o_part, grad_up_part, grad_down_part),
    )
    grad_history, block_out = history_gradient(feature_side, mixes)
    grad_qkv, grad_w_out, grad_w_up, grad_w_down = sums
    return (
        block_out,
        mix_out,
        grad_history,
        mix_sum.T,
        grad_qkv,
        grad_w_out,
        grad_w_up,
        grad_w_down,
        little_sum[:, :MIXH],
        second_sum[:, :MIXH],
        little_sum[:, MIXH : MIXH + STREAMS + 1].T,
    )


def solution(mesh):
    return jax.shard_map(
        body,
        mesh=mesh,
        in_specs=(
            P(None, "dp", None),
            P("dp", None),
            P("dp", None),
            P("dp", None),
            P(),
            P(None, "dp", "mp"),
            P("dp", "mp"),
            P("dp", "mp"),
            P("dp", "mp"),
            P("dp", None),
            P(),
            P(None, "dp"),
            P("dp", None),
            P("dp", None),
        ),
        out_specs=(
            P("dp", None),
            P("dp", None),
            P(None, "dp", None),
            P("dp", None),
            P(None, "dp", "mp"),
            P("dp", "mp"),
            P("dp", "mp"),
            P("dp", "mp"),
            P("dp", None),
            P(),
            P(None, "dp"),
        ),
        check_vma=False,
    )
```

```python
import functools
import math

import jax
import jax.numpy as jnp
from jax import lax
from jax.experimental import pallas as pl
from jax.experimental.pallas import tpu as pltpu
from jax.sharding import PartitionSpec as P

HEAD = 128
ROT = 32
HIST = 9
STREAMS = 4
GROUPS = 8
TOK_DEV = 384
MIXH = 40
WIDE = 128
MIXED = 48
EPS = 1e-05
CUTS = (1, 1, 2, 2, 1)
MESH = pl.DeviceIdType.MESH
DMA = pltpu.SemaphoreType.DMA
f32 = jnp.float32
bf16 = jnp.bfloat16


def chip_at(pos, ring):
    far = pos // (ring // 2)
    return (1 - far) * 2 * pos + far * (2 * (ring - 1 - pos) + 1)


def place_of(chip, ring):
    odd = chip % 2
    return (1 - odd) * (chip // 2) + odd * (ring - 1 - chip // 2)


def remote(src, dst, send, recv, device):
    return pltpu.make_async_remote_copy(
        src_ref=src,
        dst_ref=dst,
        send_sem=send,
        recv_sem=recv,
        device_id=device,
        device_id_type=MESH,
    )


def greet_plane(n, me, mp):
    barrier = pltpu.get_barrier_semaphore()

    @pl.loop(1, n)
    def _(k):
        pl.semaphore_signal(barrier, inc=1, device_id={"dp": (me + k) % n}, device_id_type=MESH)

    pl.semaphore_signal(barrier, inc=1, device_id={"mp": 1 - mp}, device_id_type=MESH)
    pl.semaphore_wait(barrier, n)


def rows_of(ref, start, count):
    if len(ref.shape) == 3:
        return ref.at[:, pl.ds(start, count), :]
    return ref.at[pl.ds(start, count), :]


def cuts_of(shards, cuts):
    pieces = []
    for i, shard in enumerate(shards):
        if len(shard.shape) == 3:
            pieces += [(i, s, 0) for s in range(shard.shape[0])]
        else:
            wide = shard.shape[1] // cuts[i]
            pieces += [(i, k * wide, wide) for k in range(cuts[i])]
    return pieces


def piece_of(refs, piece, start, count):
    i, first, wide = piece
    if wide == 0:
        return refs[i].at[first, pl.ds(start, count), :]
    return refs[i].at[pl.ds(start, count), pl.ds(first, wide)]


class Ring:
    def __init__(self, n):
        self.n, self.ring = n, n // 2
        self.me = lax.axis_index("dp")
        self.core = self.me % 2
        self.place = place_of(self.me // 2, self.ring)
        self.mate = self.me + 1 - 2 * self.core
        self.next_of = ({"dp": self.owner(1)}, {"dp": self.owner(-1)})

    def owner(self, offset):
        return chip_at((self.place + offset + 2 * self.ring) % self.ring, self.ring) * 2 + self.core


def forward_kernel(n, count, *refs):
    hist, cot, mix, tables, docs_row, docs_col = refs[:6]
    shards = refs[6 : 6 + count]
    refs = refs[6 + count :]
    inputs, mixes, normed_out, level, heads_out, attn_out, slope_out, hidden_out, total = refs[:9]
    fulls = refs[9 : 9 + count]
    (
        hist_buf,
        slots,
        streams,
        normed,
        tiles,
        heads,
        attn,
        slope_buf,
        hidden,
        down_buf,
        out_buf,
        branch,
        branch_land,
        smalls,
        hist_sem,
        cot_sem,
        own_sem,
        local_sem,
        keep_sem,
        tile_sem,
        slope_sem,
        row_sem,
        swap_send,
        swap_recv,
        mix_send,
        mix_recv,
        a_send,
        a_recv,
        y_send,
        y_recv,
        ring_send,
        ring_recv,
        core_send,
        core_recv,
    ) = refs[9 + count :]
    where = Ring(n)
    me, ring, owner = where.me, where.ring, where.owner
    mp = lax.axis_index("mp")
    across = {"mp": 1 - mp}
    feat, tokens = hist.shape[1], mix.shape[1]
    h = feat // 2
    width = n * feat
    size = shards[0].shape[-2]
    half = size // 2
    w_qkv, w_out, w_up, w_down, all_small = fulls
    greet_plane(n, me, mp)

    pieces = cuts_of(shards, CUTS)

    def of(*arrays):
        return [p for p, piece in enumerate(pieces) if piece[0] in arrays]

    def origin_rows(offset, way):
        return pl.multiple_of(owner(offset) * size + way * half, half)

    def ring_copy(way, step, p, first=False):
        there = piece_of(fulls, pieces[p], origin_rows(-step if way == 0 else step, way), half)
        here = piece_of(shards, pieces[p], way * half, half) if first else there
        return remote(
            here, there, ring_send.at[way, step, p], ring_recv.at[way, step, p], where.next_of[way]
        )

    def ring_arrival(way, step, p):
        offset = -step - 1 if way == 0 else step + 1
        there = piece_of(fulls, pieces[p], origin_rows(offset, way), half)
        return remote(
            there, there, ring_send.at[way, step, p], ring_recv.at[way, step, p], where.next_of[way]
        )

    def core_copy(way, step, p, first=False):
        there = piece_of(fulls, pieces[p], origin_rows(-step if way == 0 else step, way), half)
        here = piece_of(shards, pieces[p], way * half, half) if first else there
        return remote(
            here, there, core_send.at[way, step, p], core_recv.at[way, step, p], {"dp": where.mate}
        )

    def shard_copy(i):
        return pltpu.make_async_copy(shards[i], rows_of(fulls[i], me * size, size), local_sem.at[i])

    def ring_begin(some):
        for p in some:
            for way in range(2):
                ring_copy(way, 0, p, True).start()

    def ring_step(step, some):
        for p in some:
            for way in range(2):
                ring_arrival(way, step - 1, p).wait_recv()
                ring_copy(way, step, p).start()
                core_copy(way, step, p).start()

    def ring_end(some):
        for p in some:
            for way in range(2):
                ring_arrival(way, ring - 2, p).wait_recv()
                core_copy(way, ring - 1, p).start()

    def ring_complete(*arrays):
        for i in arrays:
            shard_copy(i).wait()
        for p in of(*arrays):

            @pl.loop(0, ring)
            def _(step):
                for way in range(2):
                    core_copy(way, step, p).wait_recv()

    def mix_copy(q):
        return remote(
            mix, mixes.at[me], mix_send.at[q], mix_recv.at[q], {"dp": (me + q) % n}
        )

    def lanes(peer):
        return pl.ds(pl.multiple_of(peer * tokens, 128), tokens)

    def hist_copy(q):
        peer = (me + q) % n
        return pltpu.make_async_copy(
            hist.at[:, pl.ds(pl.multiple_of(mp * h, h), h), lanes(peer)],
            hist_buf.at[q % 2],
            hist_sem.at[q % 2],
        )

    def cot_copy(q):
        peer = (me + q) % n
        return pltpu.make_async_copy(
            cot.at[pl.ds(pl.multiple_of(mp * h, h), h), lanes(peer)],
            slots.at[q, STREAMS],
            cot_sem.at[q],
        )

    def features(source, plane):
        return streams.at[:, pl.ds(pl.multiple_of(source * feat + plane * h, h), h), :]

    def stream_copy(q):
        return remote(
            slots.at[q], features(me, mp), a_send.at[q], a_recv.at[q], {"dp": (me + q) % n}
        )

    def own_copy():
        return pltpu.make_async_copy(slots.at[0], features(me, mp), own_sem)

    def across_copy(q, own=False):
        there = features((me - q + n) % n, mp)
        return remote(
            slots.at[0] if own else there, there, y_send.at[q], y_recv.at[q], across
        )

    def mix_streams(q):
        peer = (me + q) % n

        @pl.loop(0, h // 16)
        def _(r):
            rows = pl.ds(pl.multiple_of(r * 16, 16), 16)
            sums = [None] * STREAMS
            for j in range(HIST):
                entry = hist_buf[q % 2, j, rows, :].astype(f32)
                for s in range(STREAMS):
                    term = mixes[peer, pl.ds(s * HIST + j, 1), :] * entry
                    sums[s] = term if j == 0 else sums[s] + term
            for s in range(STREAMS):
                slots[q, s, rows, :] = sums[s].astype(bf16)

    def normalise():
        level[...] = jnp.zeros_like(level)
        for s in range(STREAMS):

            def add(r, total):
                part = streams[s, pl.ds(pl.multiple_of(r * 32, 32), 32), :].astype(f32)
                part = part * part
                return total + (part[0:8] + part[8:16]) + (part[16:24] + part[24:32])

            squares = lax.fori_loop(0, width // 32, add, jnp.zeros((8, tokens), f32))
            mean = jnp.sum(squares, axis=0, keepdims=True) * (1.0 / width)
            level[pl.ds(s, 1), :] = lax.rsqrt(mean + EPS)

        @pl.loop(0, width // 32)
        def _(r):
            rows = pl.ds(pl.multiple_of(r * 32, 32), 32)
            gain = smalls[rows, :].astype(f32)
            for s in range(STREAMS):
                unit = streams[s, rows, :].astype(f32) * level[pl.ds(s, 1), :]
                normed[s, rows, :] = (unit * gain[:, MIXH + s : MIXH + s + 1]).astype(bf16)

    def head_tiles(pair, spot):
        columns = pl.ds(pl.multiple_of(pair * 2 * HEAD, 2 * HEAD), 2 * HEAD)
        return [
            pltpu.make_async_copy(
                w_qkv.at[s, :, columns], tiles.at[spot * 3 + s], tile_sem.at[spot * 3 + s]
            )
            for s in range(3)
        ]

    def first_dims(left, right):
        return lax.dot_general(left, right, (((0,), (0,)), ((), ())), preferred_element_type=f32)

    def last_dims(left, right):
        return lax.dot_general(left, right, (((1,), (1,)), ((), ())), preferred_element_type=f32)

    def attend(pair):
        spot = pair % 2
        for copy in head_tiles(pair, spot):
            copy.wait()

        @pl.when(pair < heads.shape[1] // 2 - 1)
        def _():
            for copy in head_tiles(pair + 1, 1 - spot):
                copy.start()

        for s in range(3):
            both = first_dims(normed[s], tiles[spot * 3 + s])
            for u in range(2):
                one = both[:, u * HEAD : (u + 1) * HEAD]
                if s < 2:
                    one = (
                        one * tables[0]
                        + pltpu.roll(one, HEAD - ROT // 2, 1) * tables[1]
                        + pltpu.roll(one, ROT // 2, 1) * tables[2]
                    )
                heads[s, pair * 2 + u] = one.astype(bf16)
        place = lax.broadcasted_iota(jnp.int32, (tokens, tokens), 0)
        other = lax.broadcasted_iota(jnp.int32, (tokens, tokens), 1)
        allowed = (place >= other) & (docs_col[...] == docs_row[...])
        for u in range(2):
            scores = last_dims(heads[0, pair * 2 + u], heads[1, pair * 2 + u]) * HEAD ** (-0.5)
            scores = jnp.where(allowed, scores, -1000000000.0)
            weight = jnp.exp(scores - jnp.max(scores, axis=1, keepdims=True))
            probs = weight * (1.0 / jnp.sum(weight, axis=1, keepdims=True))
            value = jnp.dot(
                probs.astype(bf16), heads[2, pair * 2 + u], preferred_element_type=f32
            )
            attn[:, pl.ds(pl.multiple_of((pair * 2 + u) * HEAD, HEAD), HEAD)] = value.astype(bf16)

    chunk = 512
    ups = hidden.shape[1] // chunk

    def up_tile(c, spot):
        return [
            pltpu.make_async_copy(
                w_up.at[:, pl.ds(pl.multiple_of(c * chunk + k * 256, 256), 256)],
                tiles.at[spot * 2 + k],
                tile_sem.at[spot * 2 + k],
            )
            for k in range(2)
        ]

    def slope_copy(c):
        return pltpu.make_async_copy(
            slope_buf.at[c % 2],
            slope_out.at[:, pl.ds(pl.multiple_of(c * chunk, chunk), chunk)],
            slope_sem.at[c % 2],
        )

    def feed(c, spot):
        for copy in up_tile(c, spot):
            copy.wait()

        @pl.when(c < ups - 1)
        def _():
            for copy in up_tile(c + 1, 1 - spot):
                copy.start()

        @pl.when(c >= 2)
        def _():
            slope_copy(c - 2).wait()

        for k in range(2):
            pre = first_dims(normed[STREAMS - 1], tiles[spot * 2 + k])
            below = 0.5 + 0.5 * lax.erf(pre * math.sqrt(0.5))
            bell = jnp.exp(-0.5 * pre * pre) * (1.0 / math.sqrt(2.0 * math.pi))
            slope_buf[c % 2, :, k * 256 : (k + 1) * 256] = below + pre * bell
            low = (pre * below).astype(bf16)
            hidden[:, pl.ds(pl.multiple_of(c * chunk + k * 256, 256), 256)] = low
        slope_copy(c).start()

    deep = down_buf.shape[1]

    def row_tiles(c):
        rows = pl.ds(c * deep, deep)
        return [
            pltpu.make_async_copy(w_down.at[rows, :], down_buf.at[c % 2], row_sem.at[c % 2, 0]),
            pltpu.make_async_copy(w_out.at[rows, :], out_buf.at[c % 2], row_sem.at[c % 2, 1]),
        ]

    def swap_copy(c):
        rows = pl.ds(c * deep, deep)
        return remote(
            branch.at[rows], branch_land.at[rows], swap_send.at[c], swap_recv.at[c], across
        )

    def keep(k):
        pairs = [
            (streams, inputs),
            (normed, normed_out),
            (heads, heads_out),
            (attn, attn_out),
            (hidden, hidden_out),
        ]
        return pltpu.make_async_copy(pairs[k][0], pairs[k][1], keep_sem.at[k])

    def stream_turn(q):
        hist_copy(q).wait()

        @pl.when(q < n - 1)
        def _():
            hist_copy(q + 1).start()

        mix_copy(n - q).wait_recv()
        mix_streams(q)
        cot_copy(q).wait()
        stream_copy(q).start()

    def forward_turn(q):
        stream_copy(q).wait_recv()
        across_copy(q).start()

    @pl.loop(1, n)
    def _(q):
        mix_copy(q).start()

    @pl.loop(0, n)
    def _(q):
        cot_copy(q).start()

    hist_copy(0).start()
    ring_begin(of(0, 1, 4))
    mixes[me] = mix[...]
    hist_copy(0).wait()
    hist_copy(1).start()
    mix_streams(0)
    cot_copy(0).wait()
    own_copy().start()
    across_copy(0, True).start()

    @pl.loop(1, 4)
    def _(q):
        stream_turn(q)

    for p in range(len(pieces)):
        for way in range(2):
            core_copy(way, 0, p, True).start()
    for i in range(count):
        shard_copy(i).start()
    ring_begin(of(2))

    @pl.loop(1, ring - 1)
    def _(step):
        ring_step(step, of(0, 1, 4))
        for u in range(2):
            stream_turn(2 + 2 * step + u)
        for u in range(2):
            forward_turn(2 * step - 1 + u)

    ring_end(of(0, 1, 4))
    ring_begin(of(3))
    pairs = heads.shape[1] // 2
    last = ring - 2
    early = 3

    def streams_here():
        ring_complete(0, 1, 4)
        gains_copy = pltpu.make_async_copy(all_small, smalls, local_sem.at[count])
        gains_copy.start()
        for copy in head_tiles(0, 0):
            copy.start()
        own_copy().wait()

        @pl.loop(0, n)
        def _(q):
            across_copy(q).wait_recv()

        keep(0).start()
        gains_copy.wait()
        normalise()
        keep(1).start()

    @pl.loop(1, ring - 1)
    def _(step):
        ring_step(step, of(2))

        @pl.when(step == 1)
        def _():
            @pl.loop(n - 3, n)
            def _(q):
                forward_turn(q)

        @pl.when(step > last - early)
        def _():
            ring_step(step - (last - early), of(3))

        @pl.when(step == last - pairs)
        def _():
            streams_here()

        @pl.when(step > last - pairs)
        def _():
            attend(step - (last - pairs) - 1)

    keep(2).start()
    keep(3).start()
    ring_end(of(2))
    ring_complete(2)
    for copy in up_tile(0, 0):
        copy.start()

    @pl.loop(early + 1, ring - 1)
    def _(step):
        ring_step(step, of(3))

        @pl.when(2 * (step - early) <= ups - 2)
        def _():
            for u in range(2):
                feed(2 * (step - early - 1) + u, u)

    for c in range(ups - 2, ups):
        feed(c, c % 2)
    keep(4).start()
    ring_end(of(3))
    ring_complete(3)
    rounds = width // deep
    for copy in row_tiles(0):
        copy.start()
    for c in range(rounds):
        if c < rounds - 1:
            for copy in row_tiles(c + 1):
                copy.start()
        for copy in row_tiles(c):
            copy.wait()
        part = last_dims(down_buf[c % 2], hidden[...]) + last_dims(out_buf[c % 2], attn[...])
        branch[pl.ds(c * deep, deep)] = part.astype(bf16)
        swap_copy(c).start()
    for c in range(rounds):
        swap_copy(c).wait_recv()

        @pl.loop(0, deep // 32)
        def _(r):
            rows = pl.ds(pl.multiple_of(c * deep + r * 32, 32), 32)
            both = branch[rows, :].astype(f32) + branch_land[rows, :].astype(f32)
            total[rows, :] = streams[STREAMS - 1, rows, :].astype(f32) + both

    for c in range(ups - 2, ups):
        slope_copy(c).wait()
    for k in range(5):
        keep(k).wait()
    for c in range(rounds):
        swap_copy(c).wait_send()

    @pl.loop(1, n)
    def _(q):
        mix_copy(q).wait_send()
        stream_copy(q).wait_send()

    @pl.loop(0, n)
    def _(q):
        across_copy(q).wait_send()

    @pl.loop(0, ring)
    def _(step):
        for p in range(len(pieces)):
            for way in range(2):
                core_copy(way, step, p).wait_send()

    @pl.loop(0, ring - 1)
    def _(step):
        for p in range(len(pieces)):
            for way in range(2):
                ring_copy(way, step, p).wait_send()


def forward_exchange(n, history, cot_out, mix, tables, docs, shards):
    count, ring = len(shards), n // 2
    feat, tokens = history.shape[1], mix.shape[1]
    h, width = feat // 2, n * feat
    hbm = pl.BlockSpec(memory_space=pl.ANY)
    vmem = pl.BlockSpec(memory_space=pltpu.VMEM)
    columns, units = shards[0].shape[2], shards[2].shape[1]
    across = columns // HEAD
    deep = 512
    rounds = width // deep
    travel = len(cuts_of(shards, CUTS))
    found = pl.pallas_call(
        functools.partial(forward_kernel, n, count),
        out_shape=[
            jax.ShapeDtypeStruct((STREAMS + 1, width, tokens), bf16),
            jax.ShapeDtypeStruct((n,) + mix.shape, f32),
            jax.ShapeDtypeStruct((STREAMS, width, tokens), bf16),
            jax.ShapeDtypeStruct((8, tokens), f32),
            jax.ShapeDtypeStruct((3, across, tokens, HEAD), bf16),
            jax.ShapeDtypeStruct((tokens, columns), bf16),
            jax.ShapeDtypeStruct((tokens, units), f32),
            jax.ShapeDtypeStruct((tokens, units), bf16),
            jax.ShapeDtypeStruct((width, tokens), f32),
        ]
        + [
            jax.ShapeDtypeStruct(s.shape[:-2] + (s.shape[-2] * n, s.shape[-1]), s.dtype)
            for s in shards
        ],
        in_specs=[hbm, hbm, vmem, vmem, vmem, vmem] + [hbm] * count,
        out_specs=[hbm, vmem, hbm, vmem, hbm, hbm, hbm, hbm, vmem] + [hbm] * count,
        scratch_shapes=[
            pltpu.VMEM((2, HIST, h, tokens), bf16),
            pltpu.VMEM((n, STREAMS + 1, h, tokens), bf16),
            pltpu.VMEM((STREAMS + 1, width, tokens), bf16),
            pltpu.VMEM((STREAMS, width, tokens), bf16),
            pltpu.VMEM((6, width, 2 * HEAD), bf16),
            pltpu.VMEM((3, across, tokens, HEAD), bf16),
            pltpu.VMEM((tokens, columns), bf16),
            pltpu.VMEM((2, tokens, 512), f32),
            pltpu.VMEM((tokens, units), bf16),
            pltpu.VMEM((2, deep, units), bf16),
            pltpu.VMEM((2, deep, columns), bf16),
            pltpu.VMEM((width, tokens), bf16),
            pltpu.VMEM((width, tokens), bf16),
            pltpu.VMEM((width, WIDE), bf16),
            DMA((2,)),
            DMA((n,)),
            DMA,
            DMA((count + 1,)),
            DMA((5,)),
            DMA((6,)),
            DMA((2,)),
            DMA((2, 2)),
            DMA((rounds,)),
            DMA((rounds,)),
        ]
        + [DMA((n,)) for _ in range(6)]
        + [DMA((2, ring - 1, travel)) for _ in range(2)]
        + [DMA((2, ring, travel)) for _ in range(2)],
        compiler_params=pltpu.CompilerParams(
            collective_id=0, has_side_effects=True, vmem_limit_bytes=60 * 1024 * 1024
        ),
    )(history, cot_out, mix, tables, docs, docs.T, *shards)
    return found[:9], found[9:]


def backward_kernel(n, count, *refs):
    (
        normed,
        grad_branch,
        hidden,
        attn,
        grad_up,
        heads,
        grad_attended,
        w_qkv,
        w_up,
        tables,
        docs_row,
        docs_col,
        level,
        inputs,
        direct,
        output,
        smalls,
        little,
        second,
        hist,
        mixes,
    ) = refs[:21]
    across_land, feature_side, mix_sum, little_sum, second_sum = refs[21:26]
    sums, mates = refs[26 : 26 + count], refs[26 + count : 26 + 2 * count]
    refs = refs[26 + 2 * count :]
    slots, other, mine, final = (refs[k * count : (k + 1) * count] for k in range(4))
    (
        rows_buf,
        projs,
        grads,
        qkv_tile,
        up_tile,
        n_tile,
        inner,
        inner_land,
        e_buf,
        x_buf,
        go_buf,
        g_buf,
        l_buf,
        g_slots,
        l_slots,
        l_land,
        second_land,
        second_own,
        f_buf,
        h_buf,
        m_wide,
        m_slots,
        m_land,
        m_mine,
        m_other,
        l_sum,
        rows_sem,
        tile_sem,
        load_sem,
        out_sem,
        back_sem,
        other_sem,
        final_sem,
        y_send,
        y_recv,
        p_sem,
        a_send,
        a_recv,
        l_send,
        l_recv,
        w_send,
        w_recv,
        fy_send,
        fy_recv,
        m_send,
        m_recv,
        end_sem,
        ring_send,
        ring_recv,
        core_send,
        core_recv,
    ) = refs[4 * count :]
    where = Ring(n)
    me, ring, owner = where.me, where.ring, where.owner
    mp = lax.axis_index("mp")
    across = {"mp": 1 - mp}
    feat, tokens = hist.shape[1], level.shape[1]
    h = feat // 2
    width = n * feat
    size = sums[0].shape[-2]
    half = size // 2
    greet_plane(n, me, mp)

    def first_dims(left, right):
        return lax.dot_general(left, right, (((0,), (0,)), ((), ())), preferred_element_type=f32)

    def last_dims(left, right):
        return lax.dot_general(left, right, (((1,), (1,)), ((), ())), preferred_element_type=f32)

    def target(way, step):
        return -1 - step if way == 0 else 1 + step

    def rows_load(way, step):
        spot = step % 3
        copies = []
        for which in range(2):
            shard = owner(target(way, step)) + which * (where.mate - me)
            rows = pl.ds(pl.multiple_of(shard * size + way * half, half), half)
            copies += [
                pltpu.make_async_copy(
                    normed.at[:, rows, :],
                    rows_buf.at[way, spot, which, pl.ds(0, STREAMS)],
                    rows_sem.at[way, spot, 2 * which],
                ),
                pltpu.make_async_copy(
                    grad_branch.at[rows, :],
                    rows_buf.at[way, spot, which, STREAMS],
                    rows_sem.at[way, spot, 2 * which + 1],
                ),
            ]
        return copies

    def part(way, step, i, which, k, columns):
        source = (k, STREAMS, STREAMS - 1, STREAMS)[i]
        left = rows_buf[way, step % 3, which, source]
        right = (projs, attn, grad_up, hidden)[i]
        right = right[k, :, columns] if i == 0 else right[:, columns]
        return jnp.dot(left, right, preferred_element_type=f32)

    strip = 1024

    def strips(i, work):
        deep = len(sums[i].shape) == 3
        for k in range(sums[i].shape[0] if deep else 1):

            @pl.loop(0, sums[i].shape[-1] // strip)
            def _(c):
                columns = pl.ds(pl.multiple_of(c * strip, strip), strip)
                at = (k, slice(None), columns) if deep else (slice(None), columns)
                work(k, columns, at)

    def core_copy(way, step, i):
        return remote(
            mine[i].at[way],
            mates[i].at[way, step],
            core_send.at[way, step, i],
            core_recv.at[way, step, i],
            {"dp": where.mate},
        )

    def other_copy(way, step, i):
        return pltpu.make_async_copy(
            mates[i].at[way, step], other[i].at[way], other_sem.at[way, i]
        )

    def ring_copy(way, step, i):
        return remote(
            slots[i].at[way, step % 4],
            slots[i].at[way, (step + 1) % 4],
            ring_send.at[way, step, i],
            ring_recv.at[way, step, i],
            where.next_of[way],
        )

    def final_copy(way, i):
        return pltpu.make_async_copy(
            final[i], rows_of(sums[i], way * half, half), final_sem.at[i]
        )

    def give(way, step, i):
        def work(k, columns, at):
            mine[i][(way,) + at] = part(way, step, i, 1, k, columns).astype(bf16)

        strips(i, work)
        core_copy(way, step, i).start()

    def stage(way, step, i):
        core_copy(way, step, i).wait_recv()
        other_copy(way, step, i).start()

    def add(way, step, i, first=False, last=False):
        def work(k, columns, at):
            total = part(way, step, i, 0, k, columns) + other[i][(way,) + at].astype(f32)
            place = (way, step % 4) + at
            if not first:
                total = total + slots[i][place].astype(f32)
            if last:
                final[i][at] = total
            else:
                slots[i][place] = total.astype(bf16)

        strips(i, work)

    def ring_unit(step, i, way):
        other_copy(way, step, i).wait()
        ring_copy(way, step - 1, i).wait_recv()
        add(way, step, i)
        ring_copy(way, step, i).start()
        core_copy(way, step, i).wait_send()
        give(way, step + 1, i)

    def attend_back(head):
        lane = pl.ds(pl.multiple_of(head * HEAD, HEAD), HEAD)
        query, key, value = heads[0, head], heads[1, head], heads[2, head]
        grad = grad_attended[:, lane]
        place = lax.broadcasted_iota(jnp.int32, (tokens, tokens), 0)
        behind = lax.broadcasted_iota(jnp.int32, (tokens, tokens), 1)
        allowed = (place >= behind) & (docs_col[...] == docs_row[...])
        scores = jnp.where(allowed, last_dims(query, key) * HEAD ** (-0.5), -1000000000.0)
        weight = jnp.exp(scores - jnp.max(scores, axis=1, keepdims=True))
        probs = weight * (1.0 / jnp.sum(weight, axis=1, keepdims=True))
        grad_probs = last_dims(grad, value)
        inside = jnp.sum(probs * grad_probs, axis=1, keepdims=True)
        grad_scores = (probs * (grad_probs - inside)).astype(bf16)
        grad_value = first_dims(probs.astype(bf16), grad)
        grad_query = jnp.dot(grad_scores, key, preferred_element_type=f32) * HEAD ** (-0.5)
        grad_key = first_dims(grad_scores, query) * HEAD ** (-0.5)

        def turn_back(one):
            return (
                one * tables[0]
                - pltpu.roll(one, HEAD - ROT // 2, 1) * tables[1]
                - pltpu.roll(one, ROT // 2, 1) * tables[2]
            )

        projs[0, :, lane] = turn_back(grad_query).astype(bf16)
        projs[1, :, lane] = turn_back(grad_key).astype(bf16)
        projs[2, :, lane] = grad_value.astype(bf16)

    tall = n_tile.shape[2]
    tiles = width // tall
    per = tall // feat

    def tile_loads(t):
        rows = pl.ds(pl.multiple_of(((me // per + t) % tiles) * tall, tall), tall)
        spot = t % 2
        return [
            pltpu.make_async_copy(w_qkv.at[:, rows, :], qkv_tile.at[spot], tile_sem.at[spot, 0]),
            pltpu.make_async_copy(w_up.at[rows, :], up_tile.at[spot], tile_sem.at[spot, 1]),
            pltpu.make_async_copy(normed.at[:, rows, :], n_tile.at[spot], tile_sem.at[spot, 2]),
        ]

    def tile_turn(t):
        spot = t % 2
        for copy in tile_loads(t):
            copy.wait()

        @pl.when(t < tiles - 1)
        def _():
            for copy in tile_loads(t + 1):
                copy.start()

        base = ((me // per + t) % tiles) * per
        rows = pl.ds(pl.multiple_of(base * feat, tall), tall)
        for s in range(STREAMS):
            if s < 3:
                grad = last_dims(qkv_tile[spot, s], projs[s])
            else:
                grad = last_dims(up_tile[spot], grad_up[...])
            grads[s, rows, :] = grad.astype(bf16)
            products = jnp.sum(n_tile[spot, s].astype(f32) * grad, axis=0, keepdims=True)
            inner[pl.ds(s, 1), :] = inner[pl.ds(s, 1), :] + products
        for e in range(per):
            sum_copy((base + e - me + n) % n).start()

    def span(peer, plane):
        return pl.ds(pl.multiple_of(peer * feat + plane * h, h), h)

    def sum_copy(q):
        peer = (me + q) % n
        return remote(
            grads.at[:, span(peer, 1 - mp), :],
            across_land.at[q],
            y_send.at[q],
            y_recv.at[q],
            across,
        )

    def inner_copy():
        return remote(inner, inner_land, p_sem.at[0], p_sem.at[1], across)

    def loads(q):
        rows = span((me + q) % n, mp)
        spot = q % 2
        return [
            pltpu.make_async_copy(across_land.at[q], e_buf.at[spot], load_sem.at[spot, 0]),
            pltpu.make_async_copy(
                inputs.at[pl.ds(0, STREAMS), rows, :], x_buf.at[spot], load_sem.at[spot, 1]
            ),
            pltpu.make_async_copy(direct.at[rows, :], go_buf.at[spot], load_sem.at[spot, 2]),
            pltpu.make_async_copy(smalls.at[rows, :], g_buf.at[spot], load_sem.at[spot, 3]),
            pltpu.make_async_copy(little.at[rows, :], l_buf.at[spot], load_sem.at[spot, 4]),
        ]

    def out_copy(q):
        rows = span((me + q) % n, mp)
        return pltpu.make_async_copy(output.at[rows, :], g_slots.at[q, STREAMS], out_sem.at[q])

    def place_of_source(source, plane):
        return feature_side.at[source, :, pl.ds(pl.multiple_of(plane * h, h), h), :]

    def stream_copy(q):
        return remote(
            g_slots.at[q],
            place_of_source(me, mp),
            a_send.at[q],
            a_recv.at[q],
            {"dp": (me + q) % n},
        )

    def little_copy(q):
        return remote(
            l_slots.at[q], l_land.at[q], l_send.at[q], l_recv.at[q], {"dp": (me + q) % n}
        )

    bits = second_land.shape[0]

    def second_copy(b):
        bit = (me // 2**b) % 2
        return remote(
            second_own,
            second_land.at[b],
            w_send.at[b],
            w_recv.at[b],
            {"dp": me + 2**b * (1 - 2 * bit)},
        )

    def second_turn(b):
        second_copy(b).wait()
        second_own[...] = second_own[...] + second_land[b]

    def home_copy():
        return pltpu.make_async_copy(g_slots.at[0], place_of_source(me, mp), end_sem.at[0])

    def across_copy(q, own=False):
        there = place_of_source((me - q + n) % n, mp)
        return remote(
            g_slots.at[0] if own else there, there, fy_send.at[q], fy_recv.at[q], across
        )

    def start_loads(q):
        sum_copy(q).wait_recv()
        for copy in loads(q):
            copy.start()

    def norm_backward(q):
        spot = q % 2
        peer = (me + q) % n
        for copy in loads(q):
            copy.wait()

        @pl.loop(0, h // 16)
        def _(r):
            rows = pl.ds(pl.multiple_of(r * 16, 16), 16)
            full = pl.ds(pl.multiple_of(peer * feat + mp * h + r * 16, 16), 16)
            tail = l_buf[spot, rows, :]
            lane = lax.broadcasted_iota(jnp.int32, tail.shape, 1)
            for s in range(STREAMS):
                dy = grads[s, full, :].astype(f32) + e_buf[spot, s, rows, :].astype(f32)
                scale = level[pl.ds(s, 1), :]
                common = (inner[pl.ds(s, 1), :] + inner_land[pl.ds(s, 1), :]) * scale
                common = common * (1.0 / width)
                unit = x_buf[spot, s, rows, :].astype(f32) * scale
                gain = g_buf[spot, rows, :].astype(f32)[:, MIXH + s : MIXH + s + 1]
                grad = scale * (gain * dy) - unit * common
                if s == STREAMS - 1:
                    grad = grad + go_buf[spot, rows, :]
                g_slots[q, s, rows, :] = grad.astype(bf16)
                gain_grad = jnp.sum(unit * dy, axis=1, keepdims=True)
                tail = jnp.where(lane == MIXH + s, gain_grad, tail)
            l_slots[q, rows, :] = tail.astype(bf16)

    def norm_turn(q):
        @pl.when(q < n - 1)
        def _():
            start_loads(q + 1)

        norm_backward(q)
        out_copy(q).wait()

        @pl.when(q == 0)
        def _():
            home_copy().start()
            across_copy(q, True).start()

        @pl.when(q > 0)
        def _():
            stream_copy(q).start()
            little_copy(q).start()

    def hist_load(q):
        source = (me - q + n) % n
        return pltpu.make_async_copy(
            hist.at[
                :,
                pl.ds(pl.multiple_of(mp * h, h), h),
                pl.ds(pl.multiple_of(source * tokens, 128), tokens),
            ],
            h_buf.at[q % 2],
            back_sem.at[q % 2, 0],
        )

    def grad_load(q):
        source = (me - q + n) % n
        return pltpu.make_async_copy(
            feature_side.at[source, pl.ds(0, STREAMS), pl.ds(pl.multiple_of(mp * h, h), h), :],
            f_buf,
            back_sem.at[0, 1],
        )

    def mix_copy(q):
        return remote(
            m_slots.at[q], m_land.at[q], m_send.at[q], m_recv.at[q], {"dp": (me - q + n) % n}
        )

    def mix_backward(q):
        for s in range(STREAMS):
            totals = [None] * HIST
            for r in range(h // 16):
                grad = f_buf[s, r * 16 : r * 16 + 16, :].astype(f32)
                for j in range(HIST):
                    both = h_buf[q % 2, j, r * 16 : r * 16 + 16, :].astype(f32) * grad
                    both = both[0:8] + both[8:16]
                    totals[j] = both if r == 0 else totals[j] + both
            for j in range(HIST):
                m_wide[pl.ds(s * HIST + j, 1), :] = jnp.sum(totals[j], axis=0, keepdims=True)
        m_slots[q] = m_wide[...].astype(bf16)

    def mix_turn(q):
        @pl.when(q < n - 1)
        def _():
            hist_load(q + 1).start()

        @pl.when(q == 0)
        def _():
            home_copy().wait()

        @pl.when(q > 0)
        def _():
            stream_copy(q).wait_recv()
            across_copy(q).start()

        grad_load(q).start()
        grad_load(q).wait()
        hist_load(q).wait()
        mix_backward(q)

        @pl.when(q > 0)
        def _():
            mix_copy(q).start()

    early = [(i, way) for i in (3, 2, 1) for way in range(2)]
    late = [(0, way) for way in range(2)]

    for way in range(2):
        for step in range(3):
            for copy in rows_load(way, step):
                copy.start()

    @pl.loop(0, n)
    def _(q):
        out_copy(q).start()

    second_own[...] = second[...]
    for copy in tile_loads(0):
        copy.start()
    inner[...] = jnp.zeros_like(inner)
    m_wide[...] = jnp.zeros_like(m_wide)
    for way in range(2):
        slots[0][way, 0] = jnp.zeros_like(slots[0][way, 0])
        for copy in rows_load(way, 0) + rows_load(way, 1):
            copy.wait()
    for i, way in early:
        give(way, 0, i)
    for i, way in early:
        stage(way, 0, i)
    for i, way in early:
        other_copy(way, 0, i).wait()
        add(way, 0, i, first=True)
        ring_copy(way, 0, i).start()
        core_copy(way, 0, i).wait_send()
        give(way, 1, i)
    for i, way in early:
        stage(way, 1, i)

    @pl.loop(0, heads.shape[1])
    def _(head):
        attend_back(head)

    for i, way in late:
        give(way, 0, i)
    for i, way in late:
        stage(way, 0, i)
    hist_load(0).start()

    opening = 2

    @pl.loop(1, ring - 1)
    def _(step):
        for way in range(2):
            for copy in rows_load(way, step + 1):
                copy.wait()

        for b in range(bits):

            @pl.when(step == b + 1)
            def _():
                if b > 0:
                    second_turn(b - 1)
                second_copy(b).start()

        @pl.when(step == opening)
        def _():
            inner_copy().start()
            start_loads(0)
            inner_copy().wait()

        for u, (i, way) in enumerate(early + late):
            if i == 0:

                @pl.when(step > 1)
                def _():
                    if way == 0:
                        for w in range(2):
                            ring_copy(w, step - 2, i).wait_send()

                other_copy(way, step - 1, i).wait()

                @pl.when(step > 1)
                def _():
                    ring_copy(way, step - 2, i).wait_recv()

                add(way, step - 1, i)
                ring_copy(way, step - 1, i).start()
                core_copy(way, step - 1, i).wait_send()
                give(way, step, i)
            else:
                if way == 0:
                    for w in range(2):
                        ring_copy(w, step - 1, i).wait_send()
                ring_unit(step, i, way)
            if u % 2 == 0:

                @pl.when((step >= opening) & (step < opening + n // 4))
                def _():
                    norm_turn(4 * (step - opening) + u // 2)
            else:

                @pl.when((step > opening) & (step <= opening + n // 4))
                def _():
                    mix_turn(4 * (step - opening - 1) + u // 2)

            @pl.when(step == 1)
            def _():
                tile_turn(u)

            if u > 0:
                before, w = (early + late)[u - 1]
                stage(w, step if before == 0 else step + 1, before)
        stage(1, step, 0)

        @pl.when(step < ring - 2)
        def _():
            for way in range(2):
                for copy in rows_load(way, step + 2):
                    copy.start()

    @pl.loop(1, n)
    def _(q):
        little_copy(q).wait_recv()
        mix_copy(q).wait_recv()

    def sum_over(land, own):
        return lax.fori_loop(
            1, n, lambda q, total: total + land[q].astype(f32), own.astype(f32)
        )

    l_sum[...] = sum_over(l_land, l_slots[0])
    m_mine[...] = sum_over(m_land, m_slots[0])
    second_turn(bits - 1)
    second_sum[...] = second_own[...]
    here = pl.ds(pl.multiple_of(mp * h, h), h)
    little_home = pltpu.make_async_copy(l_sum, little_sum.at[here], end_sem.at[1])
    little_across = remote(l_sum, little_sum.at[here], end_sem.at[2], end_sem.at[3], across)
    mix_across = remote(m_mine, m_other, end_sem.at[4], end_sem.at[5], across)
    little_home.start()
    little_across.start()
    mix_across.start()

    for i, way in late:
        if way == 0:
            for w in range(2):
                ring_copy(w, ring - 3, i).wait_send()
        ring_unit(ring - 2, i, way)
    for i, way in late:
        stage(way, ring - 1, i)

    for i, way in early + late:
        other_copy(way, ring - 1, i).wait()
        ring_copy(way, ring - 2, i).wait_recv()
        if way == 1:
            final_copy(0, i).wait()
        add(way, ring - 1, i, last=True)
        final_copy(way, i).start()

    mix_across.wait()
    mix_sum[...] = m_mine[...] + m_other[...]
    little_home.wait()
    little_across.wait()
    for i in range(count):
        final_copy(1, i).wait()

    @pl.loop(1, n)
    def _(q):
        stream_copy(q).wait_send()
        little_copy(q).wait_send()
        mix_copy(q).wait_send()

    @pl.loop(0, n)
    def _(q):
        sum_copy(q).wait_send()
        across_copy(q).wait()

    for i, way in early + late:
        ring_copy(way, ring - 2, i).wait_send()
        core_copy(way, ring - 1, i).wait_send()


def backward_exchange(
    n,
    normed,
    grad_branch,
    hidden,
    attn,
    grad_up,
    heads,
    grad_attended,
    w_qkv,
    w_up,
    tables,
    docs,
    level,
    inputs,
    direct,
    output,
    smalls,
    little,
    second,
    history,
    mixes,
    shards,
):
    count, ring = len(shards), n // 2
    feat, tokens = history.shape[1], level.shape[1]
    h, width = feat // 2, n * feat
    units = grad_up.shape[1]
    hbm = pl.BlockSpec(memory_space=pl.ANY)
    vmem = pl.BlockSpec(memory_space=pltpu.VMEM)

    def cut(s, rows):
        return s.shape[:-2] + (rows, s.shape[-1])

    half = shards[0].shape[-2] // 2
    tall = 256
    columns = attn.shape[1]
    places = [hbm, hbm, vmem, vmem, vmem, vmem, vmem, hbm, hbm, vmem, vmem, vmem, vmem]
    places += [hbm, hbm, hbm, hbm, hbm, vmem, hbm, hbm]
    found = pl.pallas_call(
        functools.partial(backward_kernel, n, count),
        out_shape=[
            jax.ShapeDtypeStruct((n, STREAMS, h, tokens), bf16),
            jax.ShapeDtypeStruct((n, STREAMS + 1, feat, tokens), bf16),
            jax.ShapeDtypeStruct((MIXED, tokens), f32),
            jax.ShapeDtypeStruct((feat, WIDE), f32),
            jax.ShapeDtypeStruct(second.shape, f32),
        ]
        + [jax.ShapeDtypeStruct(s.shape, f32) for s in shards]
        + [jax.ShapeDtypeStruct((2, ring) + cut(s, half), bf16) for s in shards],
        in_specs=places,
        out_specs=[hbm, hbm, vmem, hbm, vmem] + [hbm] * (2 * count),
        scratch_shapes=[pltpu.VMEM((2, 4) + cut(s, half), bf16) for s in shards]
        + [pltpu.VMEM((2,) + cut(s, half), bf16) for s in shards]
        + [pltpu.VMEM((2,) + cut(s, half), bf16) for s in shards]
        + [pltpu.VMEM(cut(s, half), f32) for s in shards]
        + [
            pltpu.VMEM((2, 3, 2, STREAMS + 1, half, tokens), bf16),
            pltpu.VMEM((3, tokens, columns), bf16),
            pltpu.VMEM((STREAMS, width, tokens), bf16),
            pltpu.VMEM((2, 3, tall, columns), bf16),
            pltpu.VMEM((2, tall, units), bf16),
            pltpu.VMEM((2, STREAMS, tall, tokens), bf16),
            pltpu.VMEM((8, tokens), f32),
            pltpu.VMEM((8, tokens), f32),
            pltpu.VMEM((2, STREAMS, h, tokens), bf16),
            pltpu.VMEM((2, STREAMS, h, tokens), bf16),
            pltpu.VMEM((2, h, tokens), f32),
            pltpu.VMEM((2, h, WIDE), bf16),
            pltpu.VMEM((2, h, WIDE), f32),
            pltpu.VMEM((n, STREAMS + 1, h, tokens), bf16),
            pltpu.VMEM((n, h, WIDE), bf16),
            pltpu.VMEM((n, h, WIDE), bf16),
            pltpu.VMEM((n.bit_length() - 1,) + second.shape, f32),
            pltpu.VMEM(second.shape, f32),
            pltpu.VMEM((STREAMS, h, tokens), bf16),
            pltpu.VMEM((2, HIST, h, tokens), bf16),
            pltpu.VMEM((MIXED, tokens), f32),
            pltpu.VMEM((n, MIXED, tokens), bf16),
            pltpu.VMEM((n, MIXED, tokens), bf16),
            pltpu.VMEM((MIXED, tokens), f32),
            pltpu.VMEM((MIXED, tokens), f32),
            pltpu.VMEM((h, WIDE), f32),
            DMA((2, 3, 4)),
            DMA((2, 3)),
            DMA((2, 5)),
            DMA((n,)),
            DMA((2, 2)),
            DMA((2, count)),
            DMA((count,)),
            DMA((n,)),
            DMA((n,)),
            DMA((2,)),
        ]
        + [DMA((n,)) for _ in range(10)]
        + [DMA((6,))]
        + [DMA((2, ring - 1, count)) for _ in range(2)]
        + [DMA((2, ring, count)) for _ in range(2)],
        compiler_params=pltpu.CompilerParams(
            collective_id=1, has_side_effects=True, vmem_limit_bytes=62 * 1024 * 1024
        ),
    )(
        normed,
        grad_branch,
        hidden,
        attn,
        grad_up,
        heads,
        grad_attended,
        w_qkv,
        w_up,
        tables,
        docs,
        docs.T,
        level,
        inputs,
        direct,
        output,
        smalls,
        little,
        second,
        history,
        mixes,
    )
    return found[1], found[2], found[3], found[4], found[5 : 5 + count]


def history_kernel(grads, mixes, grad_history, block_out):
    feat = grads.shape[2]

    @pl.loop(0, feat // 16)
    def _(r):
        rows = pl.ds(pl.multiple_of(r * 16, 16), 16)
        each = [grads[0, s, rows, :].astype(f32) for s in range(STREAMS)]
        for j in range(HIST):
            total = mixes[0, pl.ds(j, 1), :] * each[0]
            for s in range(1, STREAMS):
                total = total + mixes[0, pl.ds(s * HIST + j, 1), :] * each[s]
            grad_history[j, rows, :] = total.astype(bf16)

    block_out[...] = grads[0, STREAMS]


def history_gradient(feature_side, mixes):
    n, streams, feat, tokens = feature_side.shape
    return pl.pallas_call(
        history_kernel,
        grid=(n,),
        out_shape=[
            jax.ShapeDtypeStruct((HIST, feat, n * tokens), bf16),
            jax.ShapeDtypeStruct((feat, n * tokens), bf16),
        ],
        in_specs=[
            pl.BlockSpec((1, streams, feat, tokens), lambda i: (i, 0, 0, 0)),
            pl.BlockSpec((1,) + mixes.shape[1:], lambda i: (i, 0, 0)),
        ],
        out_specs=[
            pl.BlockSpec((HIST, feat, tokens), lambda i: (0, 0, i)),
            pl.BlockSpec((feat, tokens), lambda i: (0, i)),
        ],
        compiler_params=pltpu.CompilerParams(vmem_limit_bytes=32 * 1024 * 1024),
    )(feature_side, mixes)


def angle_tables(length):
    halfway = ROT // 2
    frequency = jnp.exp(jnp.arange(halfway, dtype=f32) * (-2.0 * math.log(10000.0) / ROT))
    places = (jnp.arange(length) % TOK_DEV).astype(f32)
    angles = places[:, None] * frequency[None, :]
    cosine, sine_part = jnp.cos(angles), jnp.sin(angles)
    rest = jnp.zeros((length, HEAD - ROT), f32)
    none = jnp.zeros((length, halfway), f32)
    return jnp.stack(
        [
            jnp.concatenate([cosine, cosine, rest + 1.0], axis=1),
            jnp.concatenate([-sine_part, none, rest], axis=1),
            jnp.concatenate([none, sine_part, rest], axis=1),
        ]
    )


def gelu_exact(inputs):
    return jax.nn.gelu(inputs, approximate=False)


def product(spec, left, right):
    return jnp.einsum(spec, left, right, preferred_element_type=f32)


def body(
    history,
    mix_in,
    doc_ids,
    group_ids,
    group_scale,
    w_qkv,
    w_out,
    w_up,
    w_down,
    w_mix1,
    w_mix2,
    gains,
    cot_out,
    cot_mix,
):
    n = lax.axis_size("dp")
    tokens_here = mix_in.shape[0]
    width = n * history.shape[1]
    small = jnp.pad(
        jnp.concatenate([w_mix1, gains.T], axis=1), ((0, 0), (0, WIDE - MIXH - gains.shape[0]))
    )
    tables = angle_tables(tokens_here)
    kept, (full_qkv, full_o, full_up, full_down, smalls) = forward_exchange(
        n, history, cot_out, mix_in.T, tables, doc_ids, (w_qkv, w_out, w_up, w_down, small)
    )
    inputs, mixes, normed, level, qkv_heads, attn_cat, slope, hidden, out_full = kept
    full_m1 = smalls[:, :MIXH]
    gain_f = smalls[:, MIXH : MIXH + STREAMS + 1].astype(f32)
    out_low = out_full.astype(bf16)
    mix_level = lax.rsqrt(jnp.mean(out_full * out_full, axis=0) + EPS)
    mix_unit = out_full * mix_level[None, :]
    mix_gain = gain_f[:, STREAMS : STREAMS + 1]
    mix_normed = (mix_unit * mix_gain).astype(bf16)
    mix_pre = product("dt,dm->tm", mix_normed, full_m1)
    mix_hidden = gelu_exact(mix_pre).astype(bf16)
    mix_out = product("tm,mo->to", mix_hidden, w_mix2)

    row_scale = jnp.sum(
        jnp.where(group_ids[0][:, None] == jnp.arange(GROUPS)[None, :], group_scale[None, :], 0.0),
        axis=1,
    )
    seed = inputs[STREAMS].astype(f32) * row_scale[None, :]
    grad_mix2_part = product("tm,to->mo", mix_hidden, cot_mix)
    grad_mix_hidden = product("to,mo->tm", cot_mix, w_mix2)
    grad_mix_pre = jax.vjp(gelu_exact, mix_pre)[1](grad_mix_hidden)[0].astype(bf16)
    grad_m1_part = product("dt,tm->dm", mix_normed, grad_mix_pre)
    grad_mix_normed = product("dm,tm->dt", full_m1, grad_mix_pre)
    grad_gain_mix = jnp.sum(mix_unit * grad_mix_normed, axis=1)
    mix_inner = jnp.mean(mix_unit * mix_gain * grad_mix_normed, axis=0)
    grad_out_full = seed + mix_level[None, :] * (
        mix_gain * grad_mix_normed - mix_unit * mix_inner[None, :]
    )
    grad_branch = grad_out_full.astype(bf16)
    grad_attended = product("ot,oi->ti", grad_branch, full_o).astype(bf16)
    grad_hidden = product("ot,oi->ti", grad_branch, full_down)
    grad_up_pre = (slope * grad_hidden).astype(bf16)

    little = jnp.concatenate(
        [
            grad_m1_part,
            jnp.zeros((width, STREAMS), f32),
            grad_gain_mix[:, None],
            jnp.zeros((width, WIDE - MIXH - STREAMS - 1), f32),
        ],
        axis=1,
    )
    second = jnp.pad(grad_mix2_part, ((0, 0), (0, WIDE - MIXH)))
    feature_side, mix_sum, little_sum, second_sum, sums = backward_exchange(
        n,
        normed,
        grad_branch,
        hidden,
        attn_cat,
        grad_up_pre,
        qkv_heads,
        grad_attended,
        full_qkv,
        full_up,
        tables,
        doc_ids,
        level,
        inputs,
        grad_out_full,
        out_low,
        smalls,
        little,
        second,
        history,
        mixes,
        (w_qkv, w_out, w_up, w_down),
    )
    grad_history, block_out = history_gradient(feature_side, mixes)
    grad_qkv, grad_w_out, grad_w_up, grad_w_down = sums
    return (
        block_out,
        mix_out,
        grad_history,
        mix_sum[: STREAMS * HIST].T,
        grad_qkv,
        grad_w_out,
        grad_w_up,
        grad_w_down,
        little_sum[:, :MIXH],
        second_sum[:, :MIXH],
        little_sum[:, MIXH : MIXH + STREAMS + 1].T,
    )


def solution(mesh):
    return jax.shard_map(
        body,
        mesh=mesh,
        in_specs=(
            P(None, "dp", None),
            P("dp", None),
            P("dp", None),
            P("dp", None),
            P(),
            P(None, "dp", "mp"),
            P("dp", "mp"),
            P("dp", "mp"),
            P("dp", "mp"),
            P("dp", None),
            P(),
            P(None, "dp"),
            P("dp", None),
            P("dp", None),
        ),
        out_specs=(
            P("dp", None),
            P("dp", None),
            P(None, "dp", None),
            P("dp", None),
            P(None, "dp", "mp"),
            P("dp", "mp"),
            P("dp", "mp"),
            P("dp", "mp"),
            P("dp", None),
            P(),
            P(None, "dp"),
        ),
        check_vma=False,
    )
```

```python
import functools
import math

import jax
import jax.numpy as jnp
from jax import lax
from jax.experimental import pallas as pl
from jax.experimental.pallas import tpu as pltpu
from jax.sharding import PartitionSpec as P

HEAD = 128
ROT = 32
HIST = 9
STREAMS = 4
GROUPS = 8
TOK_DEV = 384
MIXH = 40
WIDE = 128
MIXED = 48
EPS = 1e-05
CUTS = (1, 1, 2, 2, 1)
MESH = pl.DeviceIdType.MESH
DMA = pltpu.SemaphoreType.DMA
f32 = jnp.float32
bf16 = jnp.bfloat16


def chip_at(pos, ring):
    far = pos // (ring // 2)
    return (1 - far) * 2 * pos + far * (2 * (ring - 1 - pos) + 1)


def place_of(chip, ring):
    odd = chip % 2
    return (1 - odd) * (chip // 2) + odd * (ring - 1 - chip // 2)


def remote(src, dst, send, recv, device):
    return pltpu.make_async_remote_copy(
        src_ref=src,
        dst_ref=dst,
        send_sem=send,
        recv_sem=recv,
        device_id=device,
        device_id_type=MESH,
    )


def greet_plane(n, me, mp):
    barrier = pltpu.get_barrier_semaphore()

    @pl.loop(1, n)
    def _(k):
        pl.semaphore_signal(barrier, inc=1, device_id={"dp": (me + k) % n}, device_id_type=MESH)

    pl.semaphore_signal(barrier, inc=1, device_id={"mp": 1 - mp}, device_id_type=MESH)
    pl.semaphore_wait(barrier, n)


def rows_of(ref, start, count):
    if len(ref.shape) == 3:
        return ref.at[:, pl.ds(start, count), :]
    return ref.at[pl.ds(start, count), :]


def cuts_of(shards, cuts):
    pieces = []
    for i, shard in enumerate(shards):
        if len(shard.shape) == 3:
            pieces += [(i, s, 0) for s in range(shard.shape[0])]
        else:
            wide = shard.shape[1] // cuts[i]
            pieces += [(i, k * wide, wide) for k in range(cuts[i])]
    return pieces


def piece_of(refs, piece, start, count):
    i, first, wide = piece
    if wide == 0:
        return refs[i].at[first, pl.ds(start, count), :]
    return refs[i].at[pl.ds(start, count), pl.ds(first, wide)]


class Ring:
    def __init__(self, n):
        self.n, self.ring = n, n // 2
        self.me = lax.axis_index("dp")
        self.core = self.me % 2
        self.place = place_of(self.me // 2, self.ring)
        self.mate = self.me + 1 - 2 * self.core
        self.next_of = ({"dp": self.owner(1)}, {"dp": self.owner(-1)})

    def owner(self, offset):
        return chip_at((self.place + offset + 2 * self.ring) % self.ring, self.ring) * 2 + self.core


def forward_kernel(n, count, *refs):
    hist, cot, mix, tables, docs_row, docs_col = refs[:6]
    shards = refs[6 : 6 + count]
    refs = refs[6 + count :]
    inputs, mixes, normed_out, level, heads_out, attn_out, slope_out, hidden_out, total = refs[:9]
    fulls = refs[9 : 9 + count]
    (
        hist_buf,
        slots,
        streams,
        normed,
        tiles,
        heads,
        attn,
        slope_buf,
        hidden,
        down_buf,
        out_buf,
        branch,
        branch_land,
        smalls,
        hist_sem,
        cot_sem,
        own_sem,
        local_sem,
        keep_sem,
        tile_sem,
        slope_sem,
        row_sem,
        swap_send,
        swap_recv,
        mix_send,
        mix_recv,
        a_send,
        a_recv,
        y_send,
        y_recv,
        ring_send,
        ring_recv,
        core_send,
        core_recv,
    ) = refs[9 + count :]
    where = Ring(n)
    me, ring, owner = where.me, where.ring, where.owner
    mp = lax.axis_index("mp")
    across = {"mp": 1 - mp}
    feat, tokens = hist.shape[1], mix.shape[1]
    h = feat // 2
    width = n * feat
    size = shards[0].shape[-2]
    half = size // 2
    w_qkv, w_out, w_up, w_down, all_small = fulls
    greet_plane(n, me, mp)

    pieces = cuts_of(shards, CUTS)

    def of(*arrays):
        return [p for p, piece in enumerate(pieces) if piece[0] in arrays]

    def origin_rows(offset, way):
        return pl.multiple_of(owner(offset) * size + way * half, half)

    def ring_copy(way, step, p, first=False):
        there = piece_of(fulls, pieces[p], origin_rows(-step if way == 0 else step, way), half)
        here = piece_of(shards, pieces[p], way * half, half) if first else there
        return remote(
            here, there, ring_send.at[way, step, p], ring_recv.at[way, step, p], where.next_of[way]
        )

    def ring_arrival(way, step, p):
        offset = -step - 1 if way == 0 else step + 1
        there = piece_of(fulls, pieces[p], origin_rows(offset, way), half)
        return remote(
            there, there, ring_send.at[way, step, p], ring_recv.at[way, step, p], where.next_of[way]
        )

    def core_copy(way, step, p, first=False):
        there = piece_of(fulls, pieces[p], origin_rows(-step if way == 0 else step, way), half)
        here = piece_of(shards, pieces[p], way * half, half) if first else there
        return remote(
            here, there, core_send.at[way, step, p], core_recv.at[way, step, p], {"dp": where.mate}
        )

    def shard_copy(i):
        return pltpu.make_async_copy(shards[i], rows_of(fulls[i], me * size, size), local_sem.at[i])

    def ring_begin(some):
        for p in some:
            for way in range(2):
                ring_copy(way, 0, p, True).start()

    def ring_step(step, some):
        for p in some:
            for way in range(2):
                ring_arrival(way, step - 1, p).wait_recv()
                ring_copy(way, step, p).start()
                core_copy(way, step, p).start()

    def ring_end(some):
        for p in some:
            for way in range(2):
                ring_arrival(way, ring - 2, p).wait_recv()
                core_copy(way, ring - 1, p).start()

    def ring_complete(*arrays):
        for i in arrays:
            shard_copy(i).wait()
        for p in of(*arrays):

            @pl.loop(0, ring)
            def _(step):
                for way in range(2):
                    core_copy(way, step, p).wait_recv()

    def mix_copy(q):
        return remote(
            mix, mixes.at[me], mix_send.at[q], mix_recv.at[q], {"dp": (me + q) % n}
        )

    def lanes(peer):
        return pl.ds(pl.multiple_of(peer * tokens, 128), tokens)

    def hist_copy(q):
        peer = (me + q) % n
        return pltpu.make_async_copy(
            hist.at[:, pl.ds(pl.multiple_of(mp * h, h), h), lanes(peer)],
            hist_buf.at[q % 2],
            hist_sem.at[q % 2],
        )

    def cot_copy(q):
        peer = (me + q) % n
        return pltpu.make_async_copy(
            cot.at[pl.ds(pl.multiple_of(mp * h, h), h), lanes(peer)],
            slots.at[q, STREAMS],
            cot_sem.at[q],
        )

    def features(source, plane):
        return streams.at[:, pl.ds(pl.multiple_of(source * feat + plane * h, h), h), :]

    def stream_copy(q):
        return remote(
            slots.at[q], features(me, mp), a_send.at[q], a_recv.at[q], {"dp": (me + q) % n}
        )

    def own_copy():
        return pltpu.make_async_copy(slots.at[0], features(me, mp), own_sem)

    def across_copy(q, own=False):
        there = features((me - q + n) % n, mp)
        return remote(
            slots.at[0] if own else there, there, y_send.at[q], y_recv.at[q], across
        )

    def mix_streams(q):
        peer = (me + q) % n

        @pl.loop(0, h // 16)
        def _(r):
            rows = pl.ds(pl.multiple_of(r * 16, 16), 16)
            sums = [None] * STREAMS
            for j in range(HIST):
                entry = hist_buf[q % 2, j, rows, :].astype(f32)
                for s in range(STREAMS):
                    term = mixes[peer, pl.ds(s * HIST + j, 1), :] * entry
                    sums[s] = term if j == 0 else sums[s] + term
            for s in range(STREAMS):
                slots[q, s, rows, :] = sums[s].astype(bf16)

    def normalise():
        level[...] = jnp.zeros_like(level)
        for s in range(STREAMS):

            def add(r, total):
                part = streams[s, pl.ds(pl.multiple_of(r * 32, 32), 32), :].astype(f32)
                part = part * part
                return total + (part[0:8] + part[8:16]) + (part[16:24] + part[24:32])

            squares = lax.fori_loop(0, width // 32, add, jnp.zeros((8, tokens), f32))
            mean = jnp.sum(squares, axis=0, keepdims=True) * (1.0 / width)
            level[pl.ds(s, 1), :] = lax.rsqrt(mean + EPS)

        @pl.loop(0, width // 32)
        def _(r):
            rows = pl.ds(pl.multiple_of(r * 32, 32), 32)
            gain = smalls[rows, :].astype(f32)
            for s in range(STREAMS):
                unit = streams[s, rows, :].astype(f32) * level[pl.ds(s, 1), :]
                normed[s, rows, :] = (unit * gain[:, MIXH + s : MIXH + s + 1]).astype(bf16)

    def head_tiles(pair, spot):
        columns = pl.ds(pl.multiple_of(pair * 2 * HEAD, 2 * HEAD), 2 * HEAD)
        return [
            pltpu.make_async_copy(
                w_qkv.at[s, :, columns], tiles.at[spot * 3 + s], tile_sem.at[spot * 3 + s]
            )
            for s in range(3)
        ]

    def first_dims(left, right):
        return lax.dot_general(left, right, (((0,), (0,)), ((), ())), preferred_element_type=f32)

    def last_dims(left, right):
        return lax.dot_general(left, right, (((1,), (1,)), ((), ())), preferred_element_type=f32)

    def attend(pair):
        spot = pair % 2
        for copy in head_tiles(pair, spot):
            copy.wait()

        @pl.when(pair < heads.shape[1] // 2 - 1)
        def _():
            for copy in head_tiles(pair + 1, 1 - spot):
                copy.start()

        for s in range(3):
            both = first_dims(normed[s], tiles[spot * 3 + s])
            for u in range(2):
                one = both[:, u * HEAD : (u + 1) * HEAD]
                if s < 2:
                    one = (
                        one * tables[0]
                        + pltpu.roll(one, HEAD - ROT // 2, 1) * tables[1]
                        + pltpu.roll(one, ROT // 2, 1) * tables[2]
                    )
                heads[s, pair * 2 + u] = one.astype(bf16)
        place = lax.broadcasted_iota(jnp.int32, (tokens, tokens), 0)
        other = lax.broadcasted_iota(jnp.int32, (tokens, tokens), 1)
        allowed = (place >= other) & (docs_col[...] == docs_row[...])
        for u in range(2):
            scores = last_dims(heads[0, pair * 2 + u], heads[1, pair * 2 + u]) * HEAD ** (-0.5)
            scores = jnp.where(allowed, scores, -1000000000.0)
            weight = jnp.exp(scores - jnp.max(scores, axis=1, keepdims=True))
            probs = weight * (1.0 / jnp.sum(weight, axis=1, keepdims=True))
            value = jnp.dot(
                probs.astype(bf16), heads[2, pair * 2 + u], preferred_element_type=f32
            )
            attn[:, pl.ds(pl.multiple_of((pair * 2 + u) * HEAD, HEAD), HEAD)] = value.astype(bf16)

    chunk = 512
    ups = hidden.shape[1] // chunk

    def up_tile(c, spot):
        return [
            pltpu.make_async_copy(
                w_up.at[:, pl.ds(pl.multiple_of(c * chunk + k * 256, 256), 256)],
                tiles.at[spot * 2 + k],
                tile_sem.at[spot * 2 + k],
            )
            for k in range(2)
        ]

    def slope_copy(c):
        return pltpu.make_async_copy(
            slope_buf.at[c % 2],
            slope_out.at[:, pl.ds(pl.multiple_of(c * chunk, chunk), chunk)],
            slope_sem.at[c % 2],
        )

    def feed(c, spot):
        for copy in up_tile(c, spot):
            copy.wait()

        @pl.when(c < ups - 1)
        def _():
            for copy in up_tile(c + 1, 1 - spot):
                copy.start()

        @pl.when(c >= 2)
        def _():
            slope_copy(c - 2).wait()

        for k in range(2):
            pre = first_dims(normed[STREAMS - 1], tiles[spot * 2 + k])
            below = 0.5 + 0.5 * lax.erf(pre * math.sqrt(0.5))
            bell = jnp.exp(-0.5 * pre * pre) * (1.0 / math.sqrt(2.0 * math.pi))
            slope_buf[c % 2, :, k * 256 : (k + 1) * 256] = below + pre * bell
            low = (pre * below).astype(bf16)
            hidden[:, pl.ds(pl.multiple_of(c * chunk + k * 256, 256), 256)] = low
        slope_copy(c).start()

    def blocks(c):
        starts = []
        for way in range(2):
            shard = owner(-c if way == 0 else c)
            for which in range(2):
                row = (shard + which * (where.mate - me)) * size + way * half
                starts.append(pl.multiple_of(row, half))
        return starts

    def row_tiles(c):
        copies = []
        for b, start in enumerate(blocks(c)):
            rows, there = pl.ds(start, half), pl.ds(b * half, half)
            copies.append(
                pltpu.make_async_copy(
                    w_down.at[rows, :], down_buf.at[c % 2, there], row_sem.at[c % 2, b]
                )
            )
            copies.append(
                pltpu.make_async_copy(
                    w_out.at[rows, :], out_buf.at[c % 2, there], row_sem.at[c % 2, 4 + b]
                )
            )
        return copies

    def rows_begin(c):
        for p in of(3):
            for way in range(2):
                core_copy(way, c, p).wait_recv()
        for copy in row_tiles(c):
            copy.start()

    def rows_product(c):
        for copy in row_tiles(c):
            copy.wait()
        part = last_dims(down_buf[c % 2], hidden[...]) + last_dims(out_buf[c % 2], attn[...])
        branch[c] = part.astype(bf16)
        swap_copy(c).start()

    def swap_copy(c):
        return remote(
            branch.at[c], branch_land.at[c], swap_send.at[c], swap_recv.at[c], across
        )

    def keep(k):
        pairs = [
            (streams, inputs),
            (normed, normed_out),
            (heads, heads_out),
            (attn, attn_out),
            (hidden, hidden_out),
        ]
        return pltpu.make_async_copy(pairs[k][0], pairs[k][1], keep_sem.at[k])

    def stream_turn(q):
        hist_copy(q).wait()

        @pl.when(q < n - 1)
        def _():
            hist_copy(q + 1).start()

        mix_copy(n - q).wait_recv()
        mix_streams(q)
        cot_copy(q).wait()
        stream_copy(q).start()

    def forward_turn(q):
        stream_copy(q).wait_recv()
        across_copy(q).start()

    @pl.loop(1, n)
    def _(q):
        mix_copy(q).start()

    @pl.loop(0, n)
    def _(q):
        cot_copy(q).start()

    hist_copy(0).start()
    ring_begin(of(2, 4))
    mixes[me] = mix[...]
    hist_copy(0).wait()
    hist_copy(1).start()
    mix_streams(0)
    cot_copy(0).wait()
    own_copy().start()
    across_copy(0, True).start()

    @pl.loop(1, 4)
    def _(q):
        stream_turn(q)

    for p in range(len(pieces)):
        for way in range(2):
            core_copy(way, 0, p, True).start()
    for i in range(count):
        shard_copy(i).start()
    ring_begin(of(0, 1))

    @pl.loop(1, ring - 1)
    def _(step):
        ring_step(step, of(2, 4))
        for u in range(2):
            stream_turn(2 + 2 * step + u)
        for u in range(2):
            forward_turn(2 * step - 1 + u)

    ring_end(of(2, 4))
    ring_begin(of(3))
    pairs = heads.shape[1] // 2
    last = ring - 2
    early = 2

    def streams_here():
        ring_complete(2, 4)
        gains_copy = pltpu.make_async_copy(all_small, smalls, local_sem.at[count])
        gains_copy.start()
        for copy in up_tile(0, 0):
            copy.start()
        own_copy().wait()

        @pl.loop(0, n)
        def _(q):
            across_copy(q).wait_recv()

        keep(0).start()
        gains_copy.wait()
        normalise()
        keep(1).start()

    @pl.loop(1, ring - 1)
    def _(step):
        ring_step(step, of(0, 1))

        @pl.when(step == 1)
        def _():
            @pl.loop(n - 3, n)
            def _(q):
                forward_turn(q)

        @pl.when(step > last - early)
        def _():
            ring_step(step - (last - early), of(3))

        @pl.when(step == last - ups // 2)
        def _():
            streams_here()

        @pl.when(step > last - ups // 2)
        def _():
            for u in range(2):
                feed(2 * (step - (last - ups // 2) - 1) + u, u)

    keep(4).start()
    ring_end(of(0, 1))
    ring_complete(0, 1)
    shard_copy(3).wait()
    for copy in head_tiles(0, 0):
        copy.start()

    @pl.loop(early + 1, ring - 1)
    def _(step):
        ring_step(step, of(3))

        @pl.when(step <= early + pairs // 2)
        def _():
            for u in range(2):
                attend(2 * (step - early - 1) + u)

        @pl.when(step == early + pairs // 2)
        def _():
            for c in range(2):
                rows_begin(c)

        for ahead in range(1, 3):

            @pl.when(step == early + pairs // 2 + ahead)
            def _():
                for u in range(2):
                    c = 2 * (ahead - 1) + u
                    rows_product(c)
                    rows_begin(c + 2)

    keep(2).start()
    keep(3).start()

    @pl.loop(4, ring - 3)
    def _(c):
        rows_product(c)
        rows_begin(c + 2)

    rows_product(ring - 3)
    ring_end(of(3))
    rows_begin(ring - 1)
    rows_product(ring - 2)
    rows_product(ring - 1)

    @pl.loop(0, ring)
    def _(c):
        swap_copy(c).wait_recv()
        for b, start in enumerate(blocks(c)):
            both = branch[c, b * half : (b + 1) * half].astype(f32)
            both = both + branch_land[c, b * half : (b + 1) * half].astype(f32)
            rows = pl.ds(start, half)
            total[rows, :] = streams[STREAMS - 1, rows, :].astype(f32) + both

    for c in range(ups - 2, ups):
        slope_copy(c).wait()
    for k in range(5):
        keep(k).wait()

    @pl.loop(0, ring)
    def _(c):
        swap_copy(c).wait_send()

    @pl.loop(1, n)
    def _(q):
        mix_copy(q).wait_send()
        stream_copy(q).wait_send()

    @pl.loop(0, n)
    def _(q):
        across_copy(q).wait_send()

    @pl.loop(0, ring)
    def _(step):
        for p in range(len(pieces)):
            for way in range(2):
                core_copy(way, step, p).wait_send()

    @pl.loop(0, ring - 1)
    def _(step):
        for p in range(len(pieces)):
            for way in range(2):
                ring_copy(way, step, p).wait_send()


def forward_exchange(n, history, cot_out, mix, tables, docs, shards):
    count, ring = len(shards), n // 2
    feat, tokens = history.shape[1], mix.shape[1]
    h, width = feat // 2, n * feat
    hbm = pl.BlockSpec(memory_space=pl.ANY)
    vmem = pl.BlockSpec(memory_space=pltpu.VMEM)
    columns, units = shards[0].shape[2], shards[2].shape[1]
    across = columns // HEAD
    deep = 2 * shards[0].shape[1]
    travel = len(cuts_of(shards, CUTS))
    found = pl.pallas_call(
        functools.partial(forward_kernel, n, count),
        out_shape=[
            jax.ShapeDtypeStruct((STREAMS + 1, width, tokens), bf16),
            jax.ShapeDtypeStruct((n,) + mix.shape, f32),
            jax.ShapeDtypeStruct((STREAMS, width, tokens), bf16),
            jax.ShapeDtypeStruct((8, tokens), f32),
            jax.ShapeDtypeStruct((3, across, tokens, HEAD), bf16),
            jax.ShapeDtypeStruct((tokens, columns), bf16),
            jax.ShapeDtypeStruct((tokens, units), f32),
            jax.ShapeDtypeStruct((tokens, units), bf16),
            jax.ShapeDtypeStruct((width, tokens), f32),
        ]
        + [
            jax.ShapeDtypeStruct(s.shape[:-2] + (s.shape[-2] * n, s.shape[-1]), s.dtype)
            for s in shards
        ],
        in_specs=[hbm, hbm, vmem, vmem, vmem, vmem] + [hbm] * count,
        out_specs=[hbm, vmem, hbm, vmem, hbm, hbm, hbm, hbm, vmem] + [hbm] * count,
        scratch_shapes=[
            pltpu.VMEM((2, HIST, h, tokens), bf16),
            pltpu.VMEM((n, STREAMS + 1, h, tokens), bf16),
            pltpu.VMEM((STREAMS + 1, width, tokens), bf16),
            pltpu.VMEM((STREAMS, width, tokens), bf16),
            pltpu.VMEM((6, width, 2 * HEAD), bf16),
            pltpu.VMEM((3, across, tokens, HEAD), bf16),
            pltpu.VMEM((tokens, columns), bf16),
            pltpu.VMEM((2, tokens, 512), f32),
            pltpu.VMEM((tokens, units), bf16),
            pltpu.VMEM((2, deep, units), bf16),
            pltpu.VMEM((2, deep, columns), bf16),
            pltpu.VMEM((ring, deep, tokens), bf16),
            pltpu.VMEM((ring, deep, tokens), bf16),
            pltpu.VMEM((width, WIDE), bf16),
            DMA((2,)),
            DMA((n,)),
            DMA,
            DMA((count + 1,)),
            DMA((5,)),
            DMA((6,)),
            DMA((2,)),
            DMA((2, 8)),
            DMA((ring,)),
            DMA((ring,)),
        ]
        + [DMA((n,)) for _ in range(6)]
        + [DMA((2, ring - 1, travel)) for _ in range(2)]
        + [DMA((2, ring, travel)) for _ in range(2)],
        compiler_params=pltpu.CompilerParams(
            collective_id=0, has_side_effects=True, vmem_limit_bytes=60 * 1024 * 1024
        ),
    )(history, cot_out, mix, tables, docs, docs.T, *shards)
    return found[:9], found[9:]


def backward_kernel(n, count, *refs):
    (
        normed,
        grad_branch,
        hidden,
        attn,
        grad_up,
        heads,
        grad_attended,
        w_qkv,
        w_up,
        tables,
        docs_row,
        docs_col,
        level,
        inputs,
        direct,
        output,
        smalls,
        little,
        second,
        hist,
        mixes,
    ) = refs[:21]
    across_land, feature_side, mix_sum, little_sum, second_sum = refs[21:26]
    sums, mates = refs[26 : 26 + count], refs[26 + count : 26 + 2 * count]
    refs = refs[26 + 2 * count :]
    slots, other, mine, final = (refs[k * count : (k + 1) * count] for k in range(4))
    (
        rows_buf,
        projs,
        grads,
        qkv_tile,
        up_tile,
        n_tile,
        inner,
        inner_land,
        e_buf,
        x_buf,
        go_buf,
        g_buf,
        l_buf,
        g_slots,
        l_slots,
        l_land,
        second_land,
        second_own,
        f_buf,
        h_buf,
        m_wide,
        m_slots,
        m_land,
        m_mine,
        m_other,
        l_sum,
        rows_sem,
        tile_sem,
        load_sem,
        back_sem,
        other_sem,
        final_sem,
        y_send,
        y_recv,
        p_sem,
        o_send,
        o_recv,
        a_send,
        a_recv,
        l_send,
        l_recv,
        w_send,
        w_recv,
        fy_send,
        fy_recv,
        m_send,
        m_recv,
        end_sem,
        ring_send,
        ring_recv,
        core_send,
        core_recv,
    ) = refs[4 * count :]
    where = Ring(n)
    me, ring, owner = where.me, where.ring, where.owner
    mp = lax.axis_index("mp")
    across = {"mp": 1 - mp}
    feat, tokens = hist.shape[1], level.shape[1]
    h = feat // 2
    width = n * feat
    size = sums[0].shape[-2]
    half = size // 2
    greet_plane(n, me, mp)

    def first_dims(left, right):
        return lax.dot_general(left, right, (((0,), (0,)), ((), ())), preferred_element_type=f32)

    def last_dims(left, right):
        return lax.dot_general(left, right, (((1,), (1,)), ((), ())), preferred_element_type=f32)

    def target(way, step):
        return -1 - step if way == 0 else 1 + step

    def rows_load(way, step):
        spot = step % 3
        copies = []
        for which in range(2):
            shard = owner(target(way, step)) + which * (where.mate - me)
            rows = pl.ds(pl.multiple_of(shard * size + way * half, half), half)
            copies += [
                pltpu.make_async_copy(
                    normed.at[:, rows, :],
                    rows_buf.at[way, spot, which, pl.ds(0, STREAMS)],
                    rows_sem.at[way, spot, 2 * which],
                ),
                pltpu.make_async_copy(
                    grad_branch.at[rows, :],
                    rows_buf.at[way, spot, which, STREAMS],
                    rows_sem.at[way, spot, 2 * which + 1],
                ),
            ]
        return copies

    def part(way, step, i, which, k, columns):
        source = (k, STREAMS, STREAMS - 1, STREAMS)[i]
        left = rows_buf[way, step % 3, which, source]
        right = (projs, attn, grad_up, hidden)[i]
        right = right[k, :, columns] if i == 0 else right[:, columns]
        return jnp.dot(left, right, preferred_element_type=f32)

    strip = 1024

    def strips(i, work):
        deep = len(sums[i].shape) == 3
        for k in range(sums[i].shape[0] if deep else 1):

            @pl.loop(0, sums[i].shape[-1] // strip)
            def _(c):
                columns = pl.ds(pl.multiple_of(c * strip, strip), strip)
                at = (k, slice(None), columns) if deep else (slice(None), columns)
                work(k, columns, at)

    def core_copy(way, step, i):
        return remote(
            mine[i].at[way],
            mates[i].at[way, step],
            core_send.at[way, step, i],
            core_recv.at[way, step, i],
            {"dp": where.mate},
        )

    def other_copy(way, step, i):
        return pltpu.make_async_copy(
            mates[i].at[way, step], other[i].at[way], other_sem.at[way, i]
        )

    def ring_copy(way, step, i):
        return remote(
            slots[i].at[way, step % 4],
            slots[i].at[way, (step + 1) % 4],
            ring_send.at[way, step, i],
            ring_recv.at[way, step, i],
            where.next_of[way],
        )

    def final_copy(way, i):
        return pltpu.make_async_copy(
            final[i], rows_of(sums[i], way * half, half), final_sem.at[i]
        )

    def give(way, step, i):
        def work(k, columns, at):
            mine[i][(way,) + at] = part(way, step, i, 1, k, columns).astype(bf16)

        strips(i, work)
        core_copy(way, step, i).start()

    def stage(way, step, i):
        core_copy(way, step, i).wait_recv()
        other_copy(way, step, i).start()

    def add(way, step, i, first=False, last=False):
        def work(k, columns, at):
            total = part(way, step, i, 0, k, columns) + other[i][(way,) + at].astype(f32)
            place = (way, step % 4) + at
            if not first:
                total = total + slots[i][place].astype(f32)
            if last:
                final[i][at] = total
            else:
                slots[i][place] = total.astype(bf16)

        strips(i, work)

    def ring_unit(step, i, way):
        other_copy(way, step, i).wait()
        ring_copy(way, step - 1, i).wait_recv()
        add(way, step, i)
        ring_copy(way, step, i).start()
        core_copy(way, step, i).wait_send()
        give(way, step + 1, i)

    def attend_back(head):
        lane = pl.ds(pl.multiple_of(head * HEAD, HEAD), HEAD)
        query, key, value = heads[0, head], heads[1, head], heads[2, head]
        grad = grad_attended[:, lane]
        place = lax.broadcasted_iota(jnp.int32, (tokens, tokens), 0)
        behind = lax.broadcasted_iota(jnp.int32, (tokens, tokens), 1)
        allowed = (place >= behind) & (docs_col[...] == docs_row[...])
        scores = jnp.where(allowed, last_dims(query, key) * HEAD ** (-0.5), -1000000000.0)
        weight = jnp.exp(scores - jnp.max(scores, axis=1, keepdims=True))
        probs = weight * (1.0 / jnp.sum(weight, axis=1, keepdims=True))
        grad_probs = last_dims(grad, value)
        inside = jnp.sum(probs * grad_probs, axis=1, keepdims=True)
        grad_scores = (probs * (grad_probs - inside)).astype(bf16)
        grad_value = first_dims(probs.astype(bf16), grad)
        grad_query = jnp.dot(grad_scores, key, preferred_element_type=f32) * HEAD ** (-0.5)
        grad_key = first_dims(grad_scores, query) * HEAD ** (-0.5)

        def turn_back(one):
            return (
                one * tables[0]
                - pltpu.roll(one, HEAD - ROT // 2, 1) * tables[1]
                - pltpu.roll(one, ROT // 2, 1) * tables[2]
            )

        projs[0, :, lane] = turn_back(grad_query).astype(bf16)
        projs[1, :, lane] = turn_back(grad_key).astype(bf16)
        projs[2, :, lane] = grad_value.astype(bf16)

    tall = n_tile.shape[2]
    tiles = width // tall
    per = tall // feat

    def tile_loads(t):
        rows = pl.ds(pl.multiple_of(((me // per + t) % tiles) * tall, tall), tall)
        spot = t % 2
        return [
            pltpu.make_async_copy(w_qkv.at[:, rows, :], qkv_tile.at[spot], tile_sem.at[spot, 0]),
            pltpu.make_async_copy(w_up.at[rows, :], up_tile.at[spot], tile_sem.at[spot, 1]),
            pltpu.make_async_copy(normed.at[:, rows, :], n_tile.at[spot], tile_sem.at[spot, 2]),
        ]

    def tile_turn(t):
        spot = t % 2
        for copy in tile_loads(t):
            copy.wait()

        @pl.when(t < tiles - 1)
        def _():
            for copy in tile_loads(t + 1):
                copy.start()

        base = ((me // per + t) % tiles) * per
        rows = pl.ds(pl.multiple_of(base * feat, tall), tall)
        for s in range(STREAMS):
            if s < 3:
                grad = last_dims(qkv_tile[spot, s], projs[s])
            else:
                grad = last_dims(up_tile[spot], grad_up[...])
            grads[s, rows, :] = grad.astype(bf16)
            products = jnp.sum(n_tile[spot, s].astype(f32) * grad, axis=0, keepdims=True)
            inner[pl.ds(s, 1), :] = inner[pl.ds(s, 1), :] + products
        for e in range(per):
            sum_copy((base + e - me + n) % n).start()

    def span(peer, plane):
        return pl.ds(pl.multiple_of(peer * feat + plane * h, h), h)

    def sum_copy(q):
        peer = (me + q) % n
        return remote(
            grads.at[:, span(peer, 1 - mp), :],
            across_land.at[q],
            y_send.at[q],
            y_recv.at[q],
            across,
        )

    def inner_copy():
        return remote(inner, inner_land, p_sem.at[0], p_sem.at[1], across)

    def loads(q):
        rows = span((me + q) % n, mp)
        spot = q % 2
        return [
            pltpu.make_async_copy(across_land.at[q], e_buf.at[spot], load_sem.at[spot, 0]),
            pltpu.make_async_copy(
                inputs.at[pl.ds(0, STREAMS), rows, :], x_buf.at[spot], load_sem.at[spot, 1]
            ),
            pltpu.make_async_copy(direct.at[rows, :], go_buf.at[spot], load_sem.at[spot, 2]),
            pltpu.make_async_copy(smalls.at[rows, :], g_buf.at[spot], load_sem.at[spot, 3]),
            pltpu.make_async_copy(little.at[rows, :], l_buf.at[spot], load_sem.at[spot, 4]),
        ]

    def place_of_source(source, plane):
        return feature_side.at[source, :, pl.ds(pl.multiple_of(plane * h, h), h), :]

    def grads_of_source(source, plane):
        rows = pl.ds(pl.multiple_of(plane * h, h), h)
        return feature_side.at[source, pl.ds(0, STREAMS), rows, :]

    def output_of_source(source, plane):
        return feature_side.at[source, STREAMS, pl.ds(pl.multiple_of(plane * h, h), h), :]

    def out_copy(q):
        peer = (me + q) % n
        return remote(
            output.at[span(peer, mp), :],
            output_of_source(me, mp),
            o_send.at[q],
            o_recv.at[q],
            {"dp": peer},
        )

    def stream_copy(q):
        return remote(
            g_slots.at[q], grads_of_source(me, mp), a_send.at[q], a_recv.at[q], {"dp": (me + q) % n}
        )

    def little_copy(q):
        return remote(
            l_slots.at[q], l_land.at[q], l_send.at[q], l_recv.at[q], {"dp": (me + q) % n}
        )

    bits = second_land.shape[0]

    def second_copy(b):
        bit = (me // 2**b) % 2
        return remote(
            second_own,
            second_land.at[b],
            w_send.at[b],
            w_recv.at[b],
            {"dp": me + 2**b * (1 - 2 * bit)},
        )

    def second_turn(b):
        second_copy(b).wait()
        second_own[...] = second_own[...] + second_land[b]

    def home_copy():
        return pltpu.make_async_copy(g_slots.at[0], grads_of_source(me, mp), end_sem.at[0])

    def home_output():
        return pltpu.make_async_copy(
            output.at[span(me, mp), :], output_of_source(me, mp), end_sem.at[6]
        )

    def across_copy(q):
        there = place_of_source((me - q + n) % n, mp)
        return remote(there, there, fy_send.at[q], fy_recv.at[q], across)

    def start_loads(q):
        sum_copy(q).wait_recv()
        for copy in loads(q):
            copy.start()

    def norm_backward(q):
        spot = q % 2
        peer = (me + q) % n
        for copy in loads(q):
            copy.wait()

        @pl.loop(0, h // 16)
        def _(r):
            rows = pl.ds(pl.multiple_of(r * 16, 16), 16)
            full = pl.ds(pl.multiple_of(peer * feat + mp * h + r * 16, 16), 16)
            tail = l_buf[spot, rows, :]
            lane = lax.broadcasted_iota(jnp.int32, tail.shape, 1)
            for s in range(STREAMS):
                dy = grads[s, full, :].astype(f32) + e_buf[spot, s, rows, :].astype(f32)
                scale = level[pl.ds(s, 1), :]
                common = (inner[pl.ds(s, 1), :] + inner_land[pl.ds(s, 1), :]) * scale
                common = common * (1.0 / width)
                unit = x_buf[spot, s, rows, :].astype(f32) * scale
                gain = g_buf[spot, rows, :].astype(f32)[:, MIXH + s : MIXH + s + 1]
                grad = scale * (gain * dy) - unit * common
                if s == STREAMS - 1:
                    grad = grad + go_buf[spot, rows, :]
                g_slots[q, s, rows, :] = grad.astype(bf16)
                gain_grad = jnp.sum(unit * dy, axis=1, keepdims=True)
                tail = jnp.where(lane == MIXH + s, gain_grad, tail)
            l_slots[q, rows, :] = tail.astype(bf16)

    def norm_turn(q):
        @pl.when(q < n - 1)
        def _():
            start_loads(q + 1)

        norm_backward(q)

        @pl.when(q == 0)
        def _():
            home_copy().start()

        @pl.when(q > 0)
        def _():
            stream_copy(q).start()
            little_copy(q).start()

    def hist_load(q):
        source = (me - q + n) % n
        return pltpu.make_async_copy(
            hist.at[
                :,
                pl.ds(pl.multiple_of(mp * h, h), h),
                pl.ds(pl.multiple_of(source * tokens, 128), tokens),
            ],
            h_buf.at[q % 2],
            back_sem.at[q % 2, 0],
        )

    def grad_load(q):
        source = (me - q + n) % n
        return pltpu.make_async_copy(
            feature_side.at[source, pl.ds(0, STREAMS), pl.ds(pl.multiple_of(mp * h, h), h), :],
            f_buf,
            back_sem.at[0, 1],
        )

    def mix_copy(q):
        return remote(
            m_slots.at[q], m_land.at[q], m_send.at[q], m_recv.at[q], {"dp": (me - q + n) % n}
        )

    def mix_backward(q):
        for s in range(STREAMS):
            totals = [None] * HIST
            for r in range(h // 16):
                grad = f_buf[s, r * 16 : r * 16 + 16, :].astype(f32)
                for j in range(HIST):
                    both = h_buf[q % 2, j, r * 16 : r * 16 + 16, :].astype(f32) * grad
                    both = both[0:8] + both[8:16]
                    totals[j] = both if r == 0 else totals[j] + both
            for j in range(HIST):
                m_wide[pl.ds(s * HIST + j, 1), :] = jnp.sum(totals[j], axis=0, keepdims=True)
        m_slots[q] = m_wide[...].astype(bf16)

    def mix_turn(q):
        @pl.when(q < n - 1)
        def _():
            hist_load(q + 1).start()

        @pl.when(q == 0)
        def _():
            home_copy().wait()
            home_output().wait()

        @pl.when(q > 0)
        def _():
            stream_copy(q).wait_recv()
            out_copy(q).wait_recv()

        across_copy(q).start()
        grad_load(q).start()
        grad_load(q).wait()
        hist_load(q).wait()
        mix_backward(q)

        @pl.when(q > 0)
        def _():
            mix_copy(q).start()

    early = [(i, way) for i in (3, 2, 1) for way in range(2)]
    late = [(0, way) for way in range(2)]

    for way in range(2):
        for step in range(3):
            for copy in rows_load(way, step):
                copy.start()

    home_output().start()

    @pl.loop(1, n)
    def _(q):
        out_copy(q).start()

    second_own[...] = second[...]
    for copy in tile_loads(0):
        copy.start()
    inner[...] = jnp.zeros_like(inner)
    m_wide[...] = jnp.zeros_like(m_wide)
    for way in range(2):
        slots[0][way, 0] = jnp.zeros_like(slots[0][way, 0])
        for copy in rows_load(way, 0) + rows_load(way, 1):
            copy.wait()
    for i, way in early[:2]:
        give(way, 0, i)
    for u, (i, way) in enumerate(early):
        if u + 2 < len(early):
            give(early[u + 2][1], 0, early[u + 2][0])
        stage(way, 0, i)
        other_copy(way, 0, i).wait()
        add(way, 0, i, first=True)
        ring_copy(way, 0, i).start()
    for i, way in early:
        core_copy(way, 0, i).wait_send()
        give(way, 1, i)
    for i, way in early:
        stage(way, 1, i)

    @pl.loop(0, heads.shape[1])
    def _(head):
        attend_back(head)

    for i, way in late:
        give(way, 0, i)
    for i, way in late:
        stage(way, 0, i)
    hist_load(0).start()

    opening = 2

    @pl.loop(1, ring - 1)
    def _(step):
        for way in range(2):
            for copy in rows_load(way, step + 1):
                copy.wait()

        for b in range(bits):

            @pl.when(step == b + 1)
            def _():
                if b > 0:
                    second_turn(b - 1)
                second_copy(b).start()

        @pl.when(step == opening)
        def _():
            inner_copy().start()
            start_loads(0)
            inner_copy().wait()

        for u, (i, way) in enumerate(early + late):
            if i == 0:

                @pl.when(step > 1)
                def _():
                    if way == 0:
                        for w in range(2):
                            ring_copy(w, step - 2, i).wait_send()

                other_copy(way, step - 1, i).wait()

                @pl.when(step > 1)
                def _():
                    ring_copy(way, step - 2, i).wait_recv()

                add(way, step - 1, i)
                ring_copy(way, step - 1, i).start()
                core_copy(way, step - 1, i).wait_send()
                give(way, step, i)
            else:
                if way == 0:
                    for w in range(2):
                        ring_copy(w, step - 1, i).wait_send()
                ring_unit(step, i, way)
            if u % 2 == 0:

                @pl.when((step >= opening) & (step < opening + n // 4))
                def _():
                    norm_turn(4 * (step - opening) + u // 2)
            else:

                @pl.when((step > opening) & (step <= opening + n // 4))
                def _():
                    mix_turn(4 * (step - opening - 1) + u // 2)

            @pl.when(step == 1)
            def _():
                tile_turn(u)

            if u > 0:
                before, w = (early + late)[u - 1]
                stage(w, step if before == 0 else step + 1, before)
        stage(1, step, 0)

        @pl.when(step < ring - 2)
        def _():
            for way in range(2):
                for copy in rows_load(way, step + 2):
                    copy.start()

    @pl.loop(1, n)
    def _(q):
        little_copy(q).wait_recv()
        mix_copy(q).wait_recv()

    def sum_over(land, own):
        return lax.fori_loop(
            1, n, lambda q, total: total + land[q].astype(f32), own.astype(f32)
        )

    l_sum[...] = sum_over(l_land, l_slots[0])
    m_mine[...] = sum_over(m_land, m_slots[0])
    second_turn(bits - 1)
    second_sum[...] = second_own[...]
    here = pl.ds(pl.multiple_of(mp * h, h), h)
    little_home = pltpu.make_async_copy(l_sum, little_sum.at[here], end_sem.at[1])
    little_across = remote(l_sum, little_sum.at[here], end_sem.at[2], end_sem.at[3], across)
    mix_across = remote(m_mine, m_other, end_sem.at[4], end_sem.at[5], across)
    little_home.start()
    little_across.start()
    mix_across.start()

    for i, way in late:
        if way == 0:
            for w in range(2):
                ring_copy(w, ring - 3, i).wait_send()
        ring_unit(ring - 2, i, way)
    for i, way in late:
        stage(way, ring - 1, i)

    for i, way in early + late:
        other_copy(way, ring - 1, i).wait()
        ring_copy(way, ring - 2, i).wait_recv()
        if way == 1:
            final_copy(0, i).wait()
        add(way, ring - 1, i, last=True)
        final_copy(way, i).start()

    mix_across.wait()
    mix_sum[...] = m_mine[...] + m_other[...]
    little_home.wait()
    little_across.wait()
    for i in range(count):
        final_copy(1, i).wait()

    @pl.loop(1, n)
    def _(q):
        stream_copy(q).wait_send()
        out_copy(q).wait_send()
        little_copy(q).wait_send()
        mix_copy(q).wait_send()

    @pl.loop(0, n)
    def _(q):
        sum_copy(q).wait_send()
        across_copy(q).wait()

    for i, way in early + late:
        ring_copy(way, ring - 2, i).wait_send()
        core_copy(way, ring - 1, i).wait_send()


def backward_exchange(
    n,
    normed,
    grad_branch,
    hidden,
    attn,
    grad_up,
    heads,
    grad_attended,
    w_qkv,
    w_up,
    tables,
    docs,
    level,
    inputs,
    direct,
    output,
    smalls,
    little,
    second,
    history,
    mixes,
    shards,
):
    count, ring = len(shards), n // 2
    feat, tokens = history.shape[1], level.shape[1]
    h, width = feat // 2, n * feat
    units = grad_up.shape[1]
    hbm = pl.BlockSpec(memory_space=pl.ANY)
    vmem = pl.BlockSpec(memory_space=pltpu.VMEM)

    def cut(s, rows):
        return s.shape[:-2] + (rows, s.shape[-1])

    half = shards[0].shape[-2] // 2
    tall = 256
    columns = attn.shape[1]
    places = [hbm, hbm, vmem, vmem, vmem, vmem, vmem, hbm, hbm, vmem, vmem, vmem, vmem]
    places += [hbm, hbm, hbm, hbm, hbm, vmem, hbm, hbm]
    found = pl.pallas_call(
        functools.partial(backward_kernel, n, count),
        out_shape=[
            jax.ShapeDtypeStruct((n, STREAMS, h, tokens), bf16),
            jax.ShapeDtypeStruct((n, STREAMS + 1, feat, tokens), bf16),
            jax.ShapeDtypeStruct((MIXED, tokens), f32),
            jax.ShapeDtypeStruct((feat, WIDE), f32),
            jax.ShapeDtypeStruct(second.shape, f32),
        ]
        + [jax.ShapeDtypeStruct(s.shape, f32) for s in shards]
        + [jax.ShapeDtypeStruct((2, ring) + cut(s, half), bf16) for s in shards],
        in_specs=places,
        out_specs=[hbm, hbm, vmem, hbm, vmem] + [hbm] * (2 * count),
        scratch_shapes=[pltpu.VMEM((2, 4) + cut(s, half), bf16) for s in shards]
        + [pltpu.VMEM((2,) + cut(s, half), bf16) for s in shards]
        + [pltpu.VMEM((2,) + cut(s, half), bf16) for s in shards]
        + [pltpu.VMEM(cut(s, half), f32) for s in shards]
        + [
            pltpu.VMEM((2, 3, 2, STREAMS + 1, half, tokens), bf16),
            pltpu.VMEM((3, tokens, columns), bf16),
            pltpu.VMEM((STREAMS, width, tokens), bf16),
            pltpu.VMEM((2, 3, tall, columns), bf16),
            pltpu.VMEM((2, tall, units), bf16),
            pltpu.VMEM((2, STREAMS, tall, tokens), bf16),
            pltpu.VMEM((8, tokens), f32),
            pltpu.VMEM((8, tokens), f32),
            pltpu.VMEM((2, STREAMS, h, tokens), bf16),
            pltpu.VMEM((2, STREAMS, h, tokens), bf16),
            pltpu.VMEM((2, h, tokens), f32),
            pltpu.VMEM((2, h, WIDE), bf16),
            pltpu.VMEM((2, h, WIDE), f32),
            pltpu.VMEM((n, STREAMS, h, tokens), bf16),
            pltpu.VMEM((n, h, WIDE), bf16),
            pltpu.VMEM((n, h, WIDE), bf16),
            pltpu.VMEM((n.bit_length() - 1,) + second.shape, f32),
            pltpu.VMEM(second.shape, f32),
            pltpu.VMEM((STREAMS, h, tokens), bf16),
            pltpu.VMEM((2, HIST, h, tokens), bf16),
            pltpu.VMEM((MIXED, tokens), f32),
            pltpu.VMEM((n, MIXED, tokens), bf16),
            pltpu.VMEM((n, MIXED, tokens), bf16),
            pltpu.VMEM((MIXED, tokens), f32),
            pltpu.VMEM((MIXED, tokens), f32),
            pltpu.VMEM((h, WIDE), f32),
            DMA((2, 3, 4)),
            DMA((2, 3)),
            DMA((2, 5)),
            DMA((2, 2)),
            DMA((2, count)),
            DMA((count,)),
            DMA((n,)),
            DMA((n,)),
            DMA((2,)),
        ]
        + [DMA((n,)) for _ in range(12)]
        + [DMA((7,))]
        + [DMA((2, ring - 1, count)) for _ in range(2)]
        + [DMA((2, ring, count)) for _ in range(2)],
        compiler_params=pltpu.CompilerParams(
            collective_id=1, has_side_effects=True, vmem_limit_bytes=62 * 1024 * 1024
        ),
    )(
        normed,
        grad_branch,
        hidden,
        attn,
        grad_up,
        heads,
        grad_attended,
        w_qkv,
        w_up,
        tables,
        docs,
        docs.T,
        level,
        inputs,
        direct,
        output,
        smalls,
        little,
        second,
        history,
        mixes,
    )
    return found[1], found[2], found[3], found[4], found[5 : 5 + count]


def history_kernel(grads, mixes, grad_history, block_out):
    feat = grads.shape[2]

    @pl.loop(0, feat // 16)
    def _(r):
        rows = pl.ds(pl.multiple_of(r * 16, 16), 16)
        each = [grads[0, s, rows, :].astype(f32) for s in range(STREAMS)]
        for j in range(HIST):
            total = mixes[0, pl.ds(j, 1), :] * each[0]
            for s in range(1, STREAMS):
                total = total + mixes[0, pl.ds(s * HIST + j, 1), :] * each[s]
            grad_history[j, rows, :] = total.astype(bf16)

    block_out[...] = grads[0, STREAMS]


def history_gradient(feature_side, mixes):
    n, streams, feat, tokens = feature_side.shape
    return pl.pallas_call(
        history_kernel,
        grid=(n,),
        out_shape=[
            jax.ShapeDtypeStruct((HIST, feat, n * tokens), bf16),
            jax.ShapeDtypeStruct((feat, n * tokens), bf16),
        ],
        in_specs=[
            pl.BlockSpec((1, streams, feat, tokens), lambda i: (i, 0, 0, 0)),
            pl.BlockSpec((1,) + mixes.shape[1:], lambda i: (i, 0, 0)),
        ],
        out_specs=[
            pl.BlockSpec((HIST, feat, tokens), lambda i: (0, 0, i)),
            pl.BlockSpec((feat, tokens), lambda i: (0, i)),
        ],
        compiler_params=pltpu.CompilerParams(vmem_limit_bytes=32 * 1024 * 1024),
    )(feature_side, mixes)


def angle_tables(length):
    halfway = ROT // 2
    frequency = jnp.exp(jnp.arange(halfway, dtype=f32) * (-2.0 * math.log(10000.0) / ROT))
    places = (jnp.arange(length) % TOK_DEV).astype(f32)
    angles = places[:, None] * frequency[None, :]
    cosine, sine_part = jnp.cos(angles), jnp.sin(angles)
    rest = jnp.zeros((length, HEAD - ROT), f32)
    none = jnp.zeros((length, halfway), f32)
    return jnp.stack(
        [
            jnp.concatenate([cosine, cosine, rest + 1.0], axis=1),
            jnp.concatenate([-sine_part, none, rest], axis=1),
            jnp.concatenate([none, sine_part, rest], axis=1),
        ]
    )


def gelu_exact(inputs):
    return jax.nn.gelu(inputs, approximate=False)


def product(spec, left, right):
    return jnp.einsum(spec, left, right, preferred_element_type=f32)


def body(
    history,
    mix_in,
    doc_ids,
    group_ids,
    group_scale,
    w_qkv,
    w_out,
    w_up,
    w_down,
    w_mix1,
    w_mix2,
    gains,
    cot_out,
    cot_mix,
):
    n = lax.axis_size("dp")
    tokens_here = mix_in.shape[0]
    width = n * history.shape[1]
    small = jnp.pad(
        jnp.concatenate([w_mix1, gains.T], axis=1), ((0, 0), (0, WIDE - MIXH - gains.shape[0]))
    )
    tables = angle_tables(tokens_here)
    kept, (full_qkv, full_o, full_up, full_down, smalls) = forward_exchange(
        n, history, cot_out, mix_in.T, tables, doc_ids, (w_qkv, w_out, w_up, w_down, small)
    )
    inputs, mixes, normed, level, qkv_heads, attn_cat, slope, hidden, out_full = kept
    full_m1 = smalls[:, :MIXH]
    gain_f = smalls[:, MIXH : MIXH + STREAMS + 1].astype(f32)
    out_low = out_full.astype(bf16)
    mix_level = lax.rsqrt(jnp.mean(out_full * out_full, axis=0) + EPS)
    mix_unit = out_full * mix_level[None, :]
    mix_gain = gain_f[:, STREAMS : STREAMS + 1]
    mix_normed = (mix_unit * mix_gain).astype(bf16)
    mix_pre = product("dt,dm->tm", mix_normed, full_m1)
    mix_hidden = gelu_exact(mix_pre).astype(bf16)
    mix_out = product("tm,mo->to", mix_hidden, w_mix2)

    row_scale = jnp.sum(
        jnp.where(group_ids[0][:, None] == jnp.arange(GROUPS)[None, :], group_scale[None, :], 0.0),
        axis=1,
    )
    seed = inputs[STREAMS].astype(f32) * row_scale[None, :]
    grad_mix2_part = product("tm,to->mo", mix_hidden, cot_mix)
    grad_mix_hidden = product("to,mo->tm", cot_mix, w_mix2)
    grad_mix_pre = jax.vjp(gelu_exact, mix_pre)[1](grad_mix_hidden)[0].astype(bf16)
    grad_m1_part = product("dt,tm->dm", mix_normed, grad_mix_pre)
    grad_mix_normed = product("dm,tm->dt", full_m1, grad_mix_pre)
    grad_gain_mix = jnp.sum(mix_unit * grad_mix_normed, axis=1)
    mix_inner = jnp.mean(mix_unit * mix_gain * grad_mix_normed, axis=0)
    grad_out_full = seed + mix_level[None, :] * (
        mix_gain * grad_mix_normed - mix_unit * mix_inner[None, :]
    )
    grad_branch = grad_out_full.astype(bf16)
    grad_attended = product("ot,oi->ti", grad_branch, full_o).astype(bf16)
    grad_hidden = product("ot,oi->ti", grad_branch, full_down)
    grad_up_pre = (slope * grad_hidden).astype(bf16)

    little = jnp.concatenate(
        [
            grad_m1_part,
            jnp.zeros((width, STREAMS), f32),
            grad_gain_mix[:, None],
            jnp.zeros((width, WIDE - MIXH - STREAMS - 1), f32),
        ],
        axis=1,
    )
    second = jnp.pad(grad_mix2_part, ((0, 0), (0, WIDE - MIXH)))
    feature_side, mix_sum, little_sum, second_sum, sums = backward_exchange(
        n,
        normed,
        grad_branch,
        hidden,
        attn_cat,
        grad_up_pre,
        qkv_heads,
        grad_attended,
        full_qkv,
        full_up,
        tables,
        doc_ids,
        level,
        inputs,
        grad_out_full,
        out_low,
        smalls,
        little,
        second,
        history,
        mixes,
        (w_qkv, w_out, w_up, w_down),
    )
    grad_history, block_out = history_gradient(feature_side, mixes)
    grad_qkv, grad_w_out, grad_w_up, grad_w_down = sums
    return (
        block_out,
        mix_out,
        grad_history,
        mix_sum[: STREAMS * HIST].T,
        grad_qkv,
        grad_w_out,
        grad_w_up,
        grad_w_down,
        little_sum[:, :MIXH],
        second_sum[:, :MIXH],
        little_sum[:, MIXH : MIXH + STREAMS + 1].T,
    )


def solution(mesh):
    return jax.shard_map(
        body,
        mesh=mesh,
        in_specs=(
            P(None, "dp", None),
            P("dp", None),
            P("dp", None),
            P("dp", None),
            P(),
            P(None, "dp", "mp"),
            P("dp", "mp"),
            P("dp", "mp"),
            P("dp", "mp"),
            P("dp", None),
            P(),
            P(None, "dp"),
            P("dp", None),
            P("dp", None),
        ),
        out_specs=(
            P("dp", None),
            P("dp", None),
            P(None, "dp", None),
            P("dp", None),
            P(None, "dp", "mp"),
            P("dp", "mp"),
            P("dp", "mp"),
            P("dp", "mp"),
            P("dp", None),
            P(),
            P(None, "dp"),
        ),
        check_vma=False,
    )
```

```python
import functools
import math

import jax
import jax.numpy as jnp
import numpy as np
from jax import lax
from jax.experimental import pallas as pl
from jax.experimental.pallas import tpu as pltpu
from jax.sharding import PartitionSpec as P

HEAD = 128
ROT = 32
HIST = 9
STREAMS = 4
GROUPS = 8
TOK_DEV = 384
MIXH = 40
WIDE = 128
MIXED = 48
EPS = 1e-05
CUTS = (1, 1, 2, 2, 1)
MESH = pl.DeviceIdType.MESH
DMA = pltpu.SemaphoreType.DMA
f32 = jnp.float32
bf16 = jnp.bfloat16


def chip_at(pos, ring):
    far = pos // (ring // 2)
    return (1 - far) * 2 * pos + far * (2 * (ring - 1 - pos) + 1)


def place_of(chip, ring):
    odd = chip % 2
    return (1 - odd) * (chip // 2) + odd * (ring - 1 - chip // 2)


def remote(src, dst, send, recv, device):
    return pltpu.make_async_remote_copy(
        src_ref=src,
        dst_ref=dst,
        send_sem=send,
        recv_sem=recv,
        device_id=device,
        device_id_type=MESH,
    )


def greet_plane(n, me, mp):
    barrier = pltpu.get_barrier_semaphore()

    @pl.loop(1, n)
    def _(k):
        pl.semaphore_signal(barrier, inc=1, device_id={"dp": (me + k) % n}, device_id_type=MESH)

    pl.semaphore_signal(barrier, inc=1, device_id={"mp": 1 - mp}, device_id_type=MESH)
    pl.semaphore_wait(barrier, n)


def rows_of(ref, start, count):
    if len(ref.shape) == 3:
        return ref.at[:, pl.ds(start, count), :]
    return ref.at[pl.ds(start, count), :]


def cuts_of(shards, cuts):
    pieces = []
    for i, shard in enumerate(shards):
        if len(shard.shape) == 3:
            pieces += [(i, s, 0) for s in range(shard.shape[0])]
        else:
            wide = shard.shape[1] // cuts[i]
            pieces += [(i, k * wide, wide) for k in range(cuts[i])]
    return pieces


def piece_of(refs, piece, start, count):
    i, first, wide = piece
    if wide == 0:
        return refs[i].at[first, pl.ds(start, count), :]
    return refs[i].at[pl.ds(start, count), pl.ds(first, wide)]


class Ring:
    def __init__(self, n):
        self.n, self.ring = n, n // 2
        self.me = lax.axis_index("dp")
        self.core = self.me % 2
        self.place = place_of(self.me // 2, self.ring)
        self.mate = self.me + 1 - 2 * self.core
        self.next_of = ({"dp": self.owner(1)}, {"dp": self.owner(-1)})

    def owner(self, offset):
        return chip_at((self.place + offset + 2 * self.ring) % self.ring, self.ring) * 2 + self.core


def forward_kernel(n, count, *refs):
    hist, cot, mix, tables, docs_row, docs_col, groups, weights, cot_in, mix2_in = refs[:10]
    shards = refs[10 : 10 + count]
    refs = refs[10 + count :]
    inputs, mixes, normed_out, level, heads_out, attn_out, slope_out, hidden_out = refs[:8]
    direct, grad_branch, out_low, little, mix_out, second = refs[8:14]
    fulls = refs[14 : 14 + count]
    (
        hist_buf,
        slots,
        streams,
        normed,
        tiles,
        heads,
        attn,
        slope_buf,
        hidden,
        down_buf,
        out_buf,
        branch,
        branch_land,
        smalls,
        total,
        token_scale,
        cot_mix,
        w_mix2,
        hist_sem,
        cot_sem,
        own_sem,
        local_sem,
        keep_sem,
        tile_sem,
        slope_sem,
        row_sem,
        swap_send,
        swap_recv,
        mix_send,
        mix_recv,
        a_send,
        a_recv,
        y_send,
        y_recv,
        ring_send,
        ring_recv,
        core_send,
        core_recv,
    ) = refs[14 + count :]
    where = Ring(n)
    me, ring, owner = where.me, where.ring, where.owner
    mp = lax.axis_index("mp")
    across = {"mp": 1 - mp}
    feat, tokens = hist.shape[1], mix.shape[1]
    h = feat // 2
    width = n * feat
    size = shards[0].shape[-2]
    half = size // 2
    w_qkv, w_out, w_up, w_down, all_small = fulls
    greet_plane(n, me, mp)

    pieces = cuts_of(shards, CUTS)

    def of(*arrays):
        return [p for p, piece in enumerate(pieces) if piece[0] in arrays]

    def origin_rows(offset, way):
        return pl.multiple_of(owner(offset) * size + way * half, half)

    def ring_copy(way, step, p, first=False):
        there = piece_of(fulls, pieces[p], origin_rows(-step if way == 0 else step, way), half)
        here = piece_of(shards, pieces[p], way * half, half) if first else there
        return remote(
            here, there, ring_send.at[way, step, p], ring_recv.at[way, step, p], where.next_of[way]
        )

    def ring_arrival(way, step, p):
        offset = -step - 1 if way == 0 else step + 1
        there = piece_of(fulls, pieces[p], origin_rows(offset, way), half)
        return remote(
            there, there, ring_send.at[way, step, p], ring_recv.at[way, step, p], where.next_of[way]
        )

    def core_copy(way, step, p, first=False):
        there = piece_of(fulls, pieces[p], origin_rows(-step if way == 0 else step, way), half)
        here = piece_of(shards, pieces[p], way * half, half) if first else there
        return remote(
            here, there, core_send.at[way, step, p], core_recv.at[way, step, p], {"dp": where.mate}
        )

    def shard_copy(i):
        return pltpu.make_async_copy(shards[i], rows_of(fulls[i], me * size, size), local_sem.at[i])

    def ring_begin(some):
        for p in some:
            for way in range(2):
                ring_copy(way, 0, p, True).start()

    def ring_step(step, some):
        for p in some:
            for way in range(2):
                ring_arrival(way, step - 1, p).wait_recv()
                ring_copy(way, step, p).start()
                core_copy(way, step, p).start()

    def ring_end(some):
        for p in some:
            for way in range(2):
                ring_arrival(way, ring - 2, p).wait_recv()
                core_copy(way, ring - 1, p).start()

    def ring_complete(*arrays):
        for i in arrays:
            shard_copy(i).wait()
        for p in of(*arrays):

            @pl.loop(0, ring)
            def _(step):
                for way in range(2):
                    core_copy(way, step, p).wait_recv()

    def mix_copy(q):
        return remote(
            mix, mixes.at[me], mix_send.at[q], mix_recv.at[q], {"dp": (me + q) % n}
        )

    def lanes(peer):
        return pl.ds(pl.multiple_of(peer * tokens, 128), tokens)

    def hist_copy(q):
        peer = (me + q) % n
        return pltpu.make_async_copy(
            hist.at[:, pl.ds(pl.multiple_of(mp * h, h), h), lanes(peer)],
            hist_buf.at[q % 2],
            hist_sem.at[q % 2],
        )

    def cot_copy(q):
        peer = (me + q) % n
        return pltpu.make_async_copy(
            cot.at[pl.ds(pl.multiple_of(mp * h, h), h), lanes(peer)],
            slots.at[q, STREAMS],
            cot_sem.at[q],
        )

    def features(source, plane):
        return streams.at[:, pl.ds(pl.multiple_of(source * feat + plane * h, h), h), :]

    def stream_copy(q):
        return remote(
            slots.at[q], features(me, mp), a_send.at[q], a_recv.at[q], {"dp": (me + q) % n}
        )

    def own_copy():
        return pltpu.make_async_copy(slots.at[0], features(me, mp), own_sem)

    def across_copy(q, own=False):
        there = features((me - q + n) % n, mp)
        return remote(
            slots.at[0] if own else there, there, y_send.at[q], y_recv.at[q], across
        )

    def mix_streams(q):
        peer = (me + q) % n

        @pl.loop(0, h // 16)
        def _(r):
            rows = pl.ds(pl.multiple_of(r * 16, 16), 16)
            sums = [None] * STREAMS
            for j in range(HIST):
                entry = hist_buf[q % 2, j, rows, :].astype(f32)
                for s in range(STREAMS):
                    term = mixes[peer, pl.ds(s * HIST + j, 1), :] * entry
                    sums[s] = term if j == 0 else sums[s] + term
            for s in range(STREAMS):
                slots[q, s, rows, :] = sums[s].astype(bf16)

    def normalise():
        level[...] = jnp.zeros_like(level)
        for s in range(STREAMS):

            def add(r, total):
                part = streams[s, pl.ds(pl.multiple_of(r * 32, 32), 32), :].astype(f32)
                part = part * part
                return total + (part[0:8] + part[8:16]) + (part[16:24] + part[24:32])

            squares = lax.fori_loop(0, width // 32, add, jnp.zeros((8, tokens), f32))
            mean = jnp.sum(squares, axis=0, keepdims=True) * (1.0 / width)
            level[pl.ds(s, 1), :] = lax.rsqrt(mean + EPS)

        @pl.loop(0, width // 32)
        def _(r):
            rows = pl.ds(pl.multiple_of(r * 32, 32), 32)
            gain = smalls[rows, :].astype(f32)
            for s in range(STREAMS):
                unit = streams[s, rows, :].astype(f32) * level[pl.ds(s, 1), :]
                normed[s, rows, :] = (unit * gain[:, MIXH + s : MIXH + s + 1]).astype(bf16)

    def head_tiles(pair, spot):
        columns = pl.ds(pl.multiple_of(pair * 2 * HEAD, 2 * HEAD), 2 * HEAD)
        return [
            pltpu.make_async_copy(
                w_qkv.at[s, :, columns], tiles.at[spot * 3 + s], tile_sem.at[spot * 3 + s]
            )
            for s in range(3)
        ]

    def first_dims(left, right):
        return lax.dot_general(left, right, (((0,), (0,)), ((), ())), preferred_element_type=f32)

    def last_dims(left, right):
        return lax.dot_general(left, right, (((1,), (1,)), ((), ())), preferred_element_type=f32)

    def attend(pair):
        spot = pair % 2
        for copy in head_tiles(pair, spot):
            copy.wait()

        @pl.when(pair < heads.shape[1] // 2 - 1)
        def _():
            for copy in head_tiles(pair + 1, 1 - spot):
                copy.start()

        for s in range(3):
            both = first_dims(normed[s], tiles[spot * 3 + s])
            for u in range(2):
                one = both[:, u * HEAD : (u + 1) * HEAD]
                if s < 2:
                    one = (
                        one * tables[0]
                        + pltpu.roll(one, HEAD - ROT // 2, 1) * tables[1]
                        + pltpu.roll(one, ROT // 2, 1) * tables[2]
                    )
                heads[s, pair * 2 + u] = one.astype(bf16)
        place = lax.broadcasted_iota(jnp.int32, (tokens, tokens), 0)
        other = lax.broadcasted_iota(jnp.int32, (tokens, tokens), 1)
        allowed = (place >= other) & (docs_col[...] == docs_row[...])
        for u in range(2):
            scores = last_dims(heads[0, pair * 2 + u], heads[1, pair * 2 + u]) * HEAD ** (-0.5)
            scores = jnp.where(allowed, scores, -1000000000.0)
            weight = jnp.exp(scores - jnp.max(scores, axis=1, keepdims=True))
            probs = weight * (1.0 / jnp.sum(weight, axis=1, keepdims=True))
            value = jnp.dot(
                probs.astype(bf16), heads[2, pair * 2 + u], preferred_element_type=f32
            )
            attn[:, pl.ds(pl.multiple_of((pair * 2 + u) * HEAD, HEAD), HEAD)] = value.astype(bf16)

    chunk = 512
    ups = hidden.shape[1] // chunk

    def up_tile(c, spot):
        return [
            pltpu.make_async_copy(
                w_up.at[:, pl.ds(pl.multiple_of(c * chunk + k * 256, 256), 256)],
                tiles.at[spot * 2 + k],
                tile_sem.at[spot * 2 + k],
            )
            for k in range(2)
        ]

    def slope_copy(c):
        return pltpu.make_async_copy(
            slope_buf.at[c % 2],
            slope_out.at[:, pl.ds(pl.multiple_of(c * chunk, chunk), chunk)],
            slope_sem.at[c % 2],
        )

    def feed(c, spot):
        for copy in up_tile(c, spot):
            copy.wait()

        @pl.when(c < ups - 1)
        def _():
            for copy in up_tile(c + 1, 1 - spot):
                copy.start()

        @pl.when(c >= 2)
        def _():
            slope_copy(c - 2).wait()

        for k in range(2):
            pre = first_dims(normed[STREAMS - 1], tiles[spot * 2 + k])
            below = 0.5 + 0.5 * lax.erf(pre * math.sqrt(0.5))
            bell = jnp.exp(-0.5 * pre * pre) * (1.0 / math.sqrt(2.0 * math.pi))
            slope_buf[c % 2, :, k * 256 : (k + 1) * 256] = (below + pre * bell).astype(bf16)
            low = (pre * below).astype(bf16)
            hidden[:, pl.ds(pl.multiple_of(c * chunk + k * 256, 256), 256)] = low
        slope_copy(c).start()

    def blocks(c):
        starts = []
        for way in range(2):
            shard = owner(-c if way == 0 else c)
            for which in range(2):
                row = (shard + which * (where.mate - me)) * size + way * half
                starts.append(pl.multiple_of(row, half))
        return starts

    def row_tiles(c):
        copies = []
        for b, start in enumerate(blocks(c)):
            rows, there = pl.ds(start, half), pl.ds(b * half, half)
            copies.append(
                pltpu.make_async_copy(
                    w_down.at[rows, :], down_buf.at[c % 2, there], row_sem.at[c % 2, b]
                )
            )
            copies.append(
                pltpu.make_async_copy(
                    w_out.at[rows, :], out_buf.at[c % 2, there], row_sem.at[c % 2, 4 + b]
                )
            )
        return copies

    def rows_begin(c):
        for p in of(3):
            for way in range(2):
                core_copy(way, c, p).wait_recv()
        for copy in row_tiles(c):
            copy.start()

    def rows_product(c):
        for copy in row_tiles(c):
            copy.wait()
        part = last_dims(down_buf[c % 2], hidden[...]) + last_dims(out_buf[c % 2], attn[...])
        branch[c] = part.astype(bf16)
        swap_copy(c).start()

    def swap_copy(c):
        return remote(
            branch.at[c], branch_land.at[c], swap_send.at[c], swap_recv.at[c], across
        )

    def mixing_network(squares):
        columns = lax.broadcasted_iota(jnp.int32, (tokens, WIDE), 1)
        plain = normed.at[0]
        gain_at = slice(MIXH + STREAMS, MIXH + STREAMS + 1)
        scale = lax.rsqrt(jnp.sum(squares, axis=0, keepdims=True) * (1.0 / width) + EPS)

        @pl.loop(0, width // 64)
        def _(r):
            rows = pl.ds(pl.multiple_of(r * 64, 64), 64)
            value = total[rows, :]
            out_low[rows, :] = value.astype(bf16)
            plain[rows, :] = (value * scale * smalls[rows, :].astype(f32)[:, gain_at]).astype(bf16)

        pre = first_dims(plain[...], smalls[...])
        below = 0.5 + 0.5 * lax.erf(pre * math.sqrt(0.5))
        bell = jnp.exp(-0.5 * pre * pre) * (1.0 / math.sqrt(2.0 * math.pi))
        low = jnp.where(columns < MIXH, pre * below, 0.0).astype(bf16)
        mix_out[...] = jnp.dot(low, w_mix2[...], preferred_element_type=f32)[:, :MIXH]
        grad = last_dims(cot_mix[...], w_mix2[...])
        grad = jnp.where(columns < MIXH, (below + pre * bell) * grad, 0.0).astype(bf16)
        second[...] = first_dims(low, cot_mix[...])[:MIXH]
        product = grad.astype(f32) * pre
        high = product.astype(bf16)
        ones = jnp.ones((8, WIDE), bf16)
        inner = last_dims(ones, high) + last_dims(ones, (product - high.astype(f32)).astype(bf16))
        inner = inner[0:1] * (1.0 / width)
        step = 256

        @pl.loop(0, width // step)
        def _(r):
            rows = pl.ds(pl.multiple_of(r * step, step), step)
            first = smalls[rows, :]
            gain = first.astype(f32)[:, gain_at]
            sums = jnp.dot(plain[rows, :], grad, preferred_element_type=f32)
            lane = lax.broadcasted_iota(jnp.int32, sums.shape, 1)
            gain_grad = jnp.sum(first.astype(f32) * sums, axis=1, keepdims=True) / gain
            little[rows, :] = jnp.where(lane == MIXH + STREAMS, gain_grad, sums)
            grad_normed = last_dims(first, grad)
            seed = streams[STREAMS, rows, :].astype(f32) * token_scale[0:1, :]
            value = seed + scale * (gain * grad_normed - total[rows, :] * (scale * inner))
            direct[rows, :] = value
            grad_branch[rows, :] = value.astype(bf16)

    def keep(k):
        pairs = [
            (streams, inputs),
            (normed, normed_out),
            (heads, heads_out),
            (attn, attn_out),
            (hidden, hidden_out),
        ]
        return pltpu.make_async_copy(pairs[k][0], pairs[k][1], keep_sem.at[k])

    def stream_turn(q):
        hist_copy(q).wait()

        @pl.when(q < n - 1)
        def _():
            hist_copy(q + 1).start()

        mix_copy(n - q).wait_recv()
        mix_streams(q)
        cot_copy(q).wait()
        stream_copy(q).start()

    def forward_turn(q):
        stream_copy(q).wait_recv()
        across_copy(q).start()

    @pl.loop(1, n)
    def _(q):
        mix_copy(q).start()

    @pl.loop(0, n)
    def _(q):
        cot_copy(q).start()

    hist_copy(0).start()
    ring_begin(of(2, 4))
    mixes[me] = mix[...]
    row = jnp.zeros((1, tokens), f32)
    for g in range(GROUPS):
        row = row + jnp.where(groups[...] == g, weights[g], 0.0)
    token_scale[...] = jnp.broadcast_to(row, token_scale.shape)
    cot_mix[...] = jnp.zeros_like(cot_mix)
    cot_mix[:, 0:MIXH] = cot_in[...]
    w_mix2[...] = jnp.zeros_like(w_mix2)
    w_mix2[0:MIXH, 0:MIXH] = mix2_in[...]
    hist_copy(0).wait()
    hist_copy(1).start()
    mix_streams(0)
    cot_copy(0).wait()
    own_copy().start()
    across_copy(0, True).start()

    @pl.loop(1, 4)
    def _(q):
        stream_turn(q)

    for p in range(len(pieces)):
        for way in range(2):
            core_copy(way, 0, p, True).start()
    for i in range(count):
        shard_copy(i).start()
    ring_begin(of(0, 1))

    @pl.loop(1, ring - 1)
    def _(step):
        ring_step(step, of(2, 4))
        for u in range(2):
            stream_turn(2 + 2 * step + u)
        for u in range(2):
            forward_turn(2 * step - 1 + u)

    ring_end(of(2, 4))
    ring_begin(of(3))
    pairs = heads.shape[1] // 2
    last = ring - 2
    early = 2

    def streams_here():
        ring_complete(2, 4)
        gains_copy = pltpu.make_async_copy(all_small, smalls, local_sem.at[count])
        gains_copy.start()
        for copy in up_tile(0, 0):
            copy.start()
        own_copy().wait()

        @pl.loop(0, n)
        def _(q):
            across_copy(q).wait_recv()

        keep(0).start()
        gains_copy.wait()
        normalise()
        keep(1).start()

    @pl.loop(1, ring - 1)
    def _(step):
        ring_step(step, of(0, 1))

        @pl.when(step == 1)
        def _():
            @pl.loop(n - 3, n)
            def _(q):
                forward_turn(q)

        @pl.when(step > last - early)
        def _():
            ring_step(step - (last - early), of(3))

        @pl.when(step == last - ups // 2)
        def _():
            streams_here()

        @pl.when(step > last - ups // 2)
        def _():
            for u in range(2):
                feed(2 * (step - (last - ups // 2) - 1) + u, u)

    keep(4).start()
    ring_end(of(0, 1))
    ring_complete(0, 1)
    shard_copy(3).wait()
    for copy in head_tiles(0, 0):
        copy.start()

    @pl.loop(early + 1, ring - 1)
    def _(step):
        ring_step(step, of(3))

        @pl.when(step <= early + pairs // 2)
        def _():
            for u in range(2):
                attend(2 * (step - early - 1) + u)

        @pl.when(step == early + pairs // 2)
        def _():
            for c in range(2):
                rows_begin(c)

        for ahead in range(1, 3):

            @pl.when(step == early + pairs // 2 + ahead)
            def _():
                for u in range(2):
                    c = 2 * (ahead - 1) + u
                    rows_product(c)
                    rows_begin(c + 2)

    keep(2).start()
    keep(3).start()

    @pl.loop(4, ring - 3)
    def _(c):
        rows_product(c)
        rows_begin(c + 2)

    rows_product(ring - 3)
    ring_end(of(3))
    rows_begin(ring - 1)
    rows_product(ring - 2)
    rows_product(ring - 1)

    def add_up(c, squares):
        swap_copy(c).wait_recv()
        for b, start in enumerate(blocks(c)):
            both = branch[c, b * half : (b + 1) * half].astype(f32)
            both = both + branch_land[c, b * half : (b + 1) * half].astype(f32)
            rows = pl.ds(start, half)
            value = streams[STREAMS - 1, rows, :].astype(f32) + both
            total[rows, :] = value
            value = value * value
            for k in range(half // 8):
                squares = squares + value[k * 8 : (k + 1) * 8]
        return squares

    squares = lax.fori_loop(0, ring, add_up, jnp.zeros((8, tokens), f32))

    for c in range(ups - 2, ups):
        slope_copy(c).wait()
    for k in range(5):
        keep(k).wait()
    mixing_network(squares)

    @pl.loop(0, ring)
    def _(c):
        swap_copy(c).wait_send()

    @pl.loop(1, n)
    def _(q):
        mix_copy(q).wait_send()
        stream_copy(q).wait_send()

    @pl.loop(0, n)
    def _(q):
        across_copy(q).wait_send()

    @pl.loop(0, ring)
    def _(step):
        for p in range(len(pieces)):
            for way in range(2):
                core_copy(way, step, p).wait_send()

    @pl.loop(0, ring - 1)
    def _(step):
        for p in range(len(pieces)):
            for way in range(2):
                ring_copy(way, step, p).wait_send()


def forward_exchange(
    n, history, cot_out, mix, tables, docs, groups, weights, cot_mix, w_mix2, shards
):
    count, ring = len(shards), n // 2
    feat, tokens = history.shape[1], mix.shape[1]
    h, width = feat // 2, n * feat
    hbm = pl.BlockSpec(memory_space=pl.ANY)
    vmem = pl.BlockSpec(memory_space=pltpu.VMEM)
    smem = pl.BlockSpec(memory_space=pltpu.SMEM)
    columns, units = shards[0].shape[2], shards[2].shape[1]
    across = columns // HEAD
    deep = 2 * shards[0].shape[1]
    travel = len(cuts_of(shards, CUTS))
    found = pl.pallas_call(
        functools.partial(forward_kernel, n, count),
        out_shape=[
            jax.ShapeDtypeStruct((STREAMS + 1, width, tokens), bf16),
            jax.ShapeDtypeStruct((n,) + mix.shape, f32),
            jax.ShapeDtypeStruct((STREAMS, width, tokens), bf16),
            jax.ShapeDtypeStruct((8, tokens), f32),
            jax.ShapeDtypeStruct((3, across, tokens, HEAD), bf16),
            jax.ShapeDtypeStruct((tokens, columns), bf16),
            jax.ShapeDtypeStruct((tokens, units), bf16),
            jax.ShapeDtypeStruct((tokens, units), bf16),
            jax.ShapeDtypeStruct((width, tokens), f32),
            jax.ShapeDtypeStruct((width, tokens), bf16),
            jax.ShapeDtypeStruct((width, tokens), bf16),
            jax.ShapeDtypeStruct((width, WIDE), f32),
            jax.ShapeDtypeStruct((tokens, MIXH), f32),
            jax.ShapeDtypeStruct((MIXH, WIDE), f32),
        ]
        + [
            jax.ShapeDtypeStruct(s.shape[:-2] + (s.shape[-2] * n, s.shape[-1]), s.dtype)
            for s in shards
        ],
        in_specs=[hbm, hbm] + [vmem] * 5 + [smem] + [vmem] * 2 + [hbm] * count,
        out_specs=[hbm, vmem, hbm, vmem, hbm, hbm, hbm, hbm] + [vmem] * 6 + [hbm] * count,
        scratch_shapes=[
            pltpu.VMEM((2, HIST, h, tokens), bf16),
            pltpu.VMEM((n, STREAMS + 1, h, tokens), bf16),
            pltpu.VMEM((STREAMS + 1, width, tokens), bf16),
            pltpu.VMEM((STREAMS, width, tokens), bf16),
            pltpu.VMEM((6, width, 2 * HEAD), bf16),
            pltpu.VMEM((3, across, tokens, HEAD), bf16),
            pltpu.VMEM((tokens, columns), bf16),
            pltpu.VMEM((2, tokens, 512), bf16),
            pltpu.VMEM((tokens, units), bf16),
            pltpu.VMEM((2, deep, units), bf16),
            pltpu.VMEM((2, deep, columns), bf16),
            pltpu.VMEM((ring, deep, tokens), bf16),
            pltpu.VMEM((ring, deep, tokens), bf16),
            pltpu.VMEM((width, WIDE), bf16),
            pltpu.VMEM((width, tokens), f32),
            pltpu.VMEM((8, tokens), f32),
            pltpu.VMEM((tokens, WIDE), bf16),
            pltpu.VMEM((WIDE, WIDE), bf16),
            DMA((2,)),
            DMA((n,)),
            DMA,
            DMA((count + 1,)),
            DMA((5,)),
            DMA((6,)),
            DMA((2,)),
            DMA((2, 8)),
            DMA((ring,)),
            DMA((ring,)),
        ]
        + [DMA((n,)) for _ in range(6)]
        + [DMA((2, ring - 1, travel)) for _ in range(2)]
        + [DMA((2, ring, travel)) for _ in range(2)],
        compiler_params=pltpu.CompilerParams(
            collective_id=0, has_side_effects=True, vmem_limit_bytes=60 * 1024 * 1024
        ),
    )(history, cot_out, mix, tables, docs, docs.T, groups, weights, cot_mix, w_mix2, *shards)
    return found[:14], found[14:]


def backward_kernel(n, count, *refs):
    (
        normed,
        grad_branch,
        hidden,
        attn,
        slope,
        heads,
        w_qkv,
        w_out,
        w_up,
        w_down,
        tables,
        docs_row,
        docs_col,
        level,
        inputs,
        direct,
        output,
        smalls,
        little,
        second,
        hist,
        mixes,
    ) = refs[:22]
    across_land, feature_side, mix_sum, little_sum, second_sum = refs[22:27]
    sums, mates = refs[27 : 27 + count], refs[27 + count : 27 + 2 * count]
    refs = refs[27 + 2 * count :]
    slots, other, mine, final = (refs[k * count : (k + 1) * count] for k in range(4))
    (
        rows_buf,
        branch_buf,
        grad_up,
        grad_attended,
        projs,
        grads,
        qkv_tile,
        up_tile,
        n_tile,
        inner,
        inner_land,
        e_buf,
        x_buf,
        go_buf,
        g_buf,
        l_buf,
        g_slots,
        l_slots,
        l_land,
        second_land,
        second_own,
        f_buf,
        h_buf,
        m_wide,
        m_slots,
        m_land,
        m_mine,
        m_other,
        l_sum,
        rows_sem,
        branch_sem,
        back_tile,
        tile_sem,
        load_sem,
        back_sem,
        other_sem,
        final_sem,
        y_send,
        y_recv,
        p_sem,
        o_send,
        o_recv,
        a_send,
        a_recv,
        l_send,
        l_recv,
        w_send,
        w_recv,
        fy_send,
        fy_recv,
        m_send,
        m_recv,
        end_sem,
        ring_send,
        ring_recv,
        core_send,
        core_recv,
    ) = refs[4 * count :]
    where = Ring(n)
    me, ring, owner = where.me, where.ring, where.owner
    mp = lax.axis_index("mp")
    across = {"mp": 1 - mp}
    feat, tokens = hist.shape[1], level.shape[1]
    h = feat // 2
    width = n * feat
    size = sums[0].shape[-2]
    half = size // 2
    greet_plane(n, me, mp)

    def first_dims(left, right):
        return lax.dot_general(left, right, (((0,), (0,)), ((), ())), preferred_element_type=f32)

    def last_dims(left, right):
        return lax.dot_general(left, right, (((1,), (1,)), ((), ())), preferred_element_type=f32)

    def target(way, step):
        return -1 - step if way == 0 else 1 + step

    def rows_load(way, step, branch):
        spot = step % 3
        copies = []
        for which in range(2):
            shard = owner(target(way, step)) + which * (where.mate - me)
            rows = pl.ds(pl.multiple_of(shard * size + way * half, half), half)
            if branch:
                here, there, sem = grad_branch.at[rows, :], branch_buf, branch_sem
            else:
                here, there, sem = normed.at[:, rows, :], rows_buf, rows_sem
            copies.append(
                pltpu.make_async_copy(here, there.at[way, spot, which], sem.at[way, spot, which])
            )
        return copies

    def rows_begin(step, branch):
        for way in range(2):
            for copy in rows_load(way, step, branch):
                copy.start()

    def rows_wait(step, branch):
        for way in range(2):
            for copy in rows_load(way, step, branch):
                copy.wait()

    def part(way, step, i, which, k, columns):
        if i in (1, 3):
            left = branch_buf[way, step % 3, which]
        else:
            left = rows_buf[way, step % 3, which, k if i == 0 else STREAMS - 1]
        right = (projs, attn, grad_up, hidden)[i]
        right = right[k, :, columns] if i == 0 else right[:, columns]
        return jnp.dot(left, right, preferred_element_type=f32)

    strip = 1024

    def strips(i, work):
        deep = len(sums[i].shape) == 3
        for k in range(sums[i].shape[0] if deep else 1):

            @pl.loop(0, sums[i].shape[-1] // strip)
            def _(c):
                columns = pl.ds(pl.multiple_of(c * strip, strip), strip)
                at = (k, slice(None), columns) if deep else (slice(None), columns)
                work(k, columns, at)

    def core_copy(way, step, i):
        return remote(
            mine[i].at[way],
            mates[i].at[way, step],
            core_send.at[way, step, i],
            core_recv.at[way, step, i],
            {"dp": where.mate},
        )

    def other_copy(way, step, i):
        return pltpu.make_async_copy(
            mates[i].at[way, step], other[i].at[way], other_sem.at[way, i]
        )

    def ring_copy(way, step, i):
        return remote(
            slots[i].at[way, step % 4],
            slots[i].at[way, (step + 1) % 4],
            ring_send.at[way, step, i],
            ring_recv.at[way, step, i],
            where.next_of[way],
        )

    def final_copy(way, i):
        return pltpu.make_async_copy(
            final[i], rows_of(sums[i], way * half, half), final_sem.at[i]
        )

    def give(way, step, i):
        def work(k, columns, at):
            mine[i][(way,) + at] = part(way, step, i, 1, k, columns).astype(bf16)

        strips(i, work)
        core_copy(way, step, i).start()

    def stage(way, step, i):
        core_copy(way, step, i).wait_recv()
        other_copy(way, step, i).start()

    def add(way, step, i, first=False, last=False):
        def work(k, columns, at):
            total = part(way, step, i, 0, k, columns) + other[i][(way,) + at].astype(f32)
            place = (way, step % 4) + at
            if not first:
                total = total + slots[i][place].astype(f32)
            if last:
                final[i][at] = total
            else:
                slots[i][place] = total.astype(bf16)

        strips(i, work)

    def ring_unit(step, i, way):
        other_copy(way, step, i).wait()
        ring_copy(way, step - 1, i).wait_recv()
        add(way, step, i)
        ring_copy(way, step, i).start()
        core_copy(way, step, i).wait_send()
        give(way, step + 1, i)

    broad = tokens

    def back_loads(c, wide, source, sloped):
        columns = pl.ds(pl.multiple_of(c * broad, 128), wide)
        spot = c % 2
        copies = [
            pltpu.make_async_copy(
                source.at[:, columns], grads.at[1 + spot, :, pl.ds(0, wide)], back_tile.at[spot, 0]
            )
        ]
        if sloped:
            copies.append(
                pltpu.make_async_copy(
                    slope.at[:, columns],
                    grads.at[3, pl.ds(pl.multiple_of(spot * tokens, 128), tokens), pl.ds(0, wide)],
                    back_tile.at[spot, 1],
                )
            )
        return copies

    def back_turn(c, wide, source, sloped):
        columns = pl.ds(pl.multiple_of(c * broad, 128), wide)
        spot = c % 2
        for copy in back_loads(c, wide, source, sloped):
            copy.wait()
        value = first_dims(grads[0], grads[1 + spot, :, 0:wide])
        if sloped:
            rows = pl.ds(pl.multiple_of(spot * tokens, 128), tokens)
            value = value * grads[3, rows, 0:wide].astype(f32)
            grad_up[:, columns] = value.astype(bf16)
        else:
            grad_attended[:, columns] = value.astype(bf16)

    def back_all(source, units, sloped):
        full, rest = units // broad, units % broad
        for copy in back_loads(0, broad, source, sloped):
            copy.start()

        @pl.loop(0, full - 1)
        def _(c):
            for copy in back_loads(c + 1, broad, source, sloped):
                copy.start()
            back_turn(c, broad, source, sloped)

        if rest:
            for copy in back_loads(full, rest, source, sloped):
                copy.start()
        back_turn(full - 1, broad, source, sloped)
        if rest:
            back_turn(full, rest, source, sloped)

    def attend_back(head):
        lane = pl.ds(pl.multiple_of(head * HEAD, HEAD), HEAD)
        query, key, value = heads[0, head], heads[1, head], heads[2, head]
        grad = grad_attended[:, lane]
        place = lax.broadcasted_iota(jnp.int32, (tokens, tokens), 0)
        behind = lax.broadcasted_iota(jnp.int32, (tokens, tokens), 1)
        allowed = (place >= behind) & (docs_col[...] == docs_row[...])
        scores = jnp.where(allowed, last_dims(query, key) * HEAD ** (-0.5), -1000000000.0)
        weight = jnp.exp(scores - jnp.max(scores, axis=1, keepdims=True))
        probs = weight * (1.0 / jnp.sum(weight, axis=1, keepdims=True))
        grad_probs = last_dims(grad, value)
        inside = jnp.sum(probs * grad_probs, axis=1, keepdims=True)
        grad_scores = (probs * (grad_probs - inside)).astype(bf16)
        grad_value = first_dims(probs.astype(bf16), grad)
        grad_query = jnp.dot(grad_scores, key, preferred_element_type=f32) * HEAD ** (-0.5)
        grad_key = first_dims(grad_scores, query) * HEAD ** (-0.5)

        def turn_back(one):
            return (
                one * tables[0]
                - pltpu.roll(one, HEAD - ROT // 2, 1) * tables[1]
                - pltpu.roll(one, ROT // 2, 1) * tables[2]
            )

        projs[0, :, lane] = turn_back(grad_query).astype(bf16)
        projs[1, :, lane] = turn_back(grad_key).astype(bf16)
        projs[2, :, lane] = grad_value.astype(bf16)

    tall = n_tile.shape[2]
    tiles = width // tall
    per = tall // feat

    def tile_loads(t):
        rows = pl.ds(pl.multiple_of(((me // per + t) % tiles) * tall, tall), tall)
        spot = t % 2
        return [
            pltpu.make_async_copy(w_qkv.at[:, rows, :], qkv_tile.at[spot], tile_sem.at[spot, 0]),
            pltpu.make_async_copy(w_up.at[rows, :], up_tile.at[spot], tile_sem.at[spot, 1]),
            pltpu.make_async_copy(normed.at[:, rows, :], n_tile.at[spot], tile_sem.at[spot, 2]),
        ]

    def tile_turn(t):
        spot = t % 2
        for copy in tile_loads(t):
            copy.wait()

        @pl.when(t < tiles - 1)
        def _():
            for copy in tile_loads(t + 1):
                copy.start()

        base = ((me // per + t) % tiles) * per
        rows = pl.ds(pl.multiple_of(base * feat, tall), tall)
        for s in range(STREAMS):
            if s < 3:
                grad = last_dims(qkv_tile[spot, s], projs[s])
            else:
                grad = last_dims(up_tile[spot], grad_up[...])
            grads[s, rows, :] = grad.astype(bf16)
            products = jnp.sum(n_tile[spot, s].astype(f32) * grad, axis=0, keepdims=True)
            inner[pl.ds(s, 1), :] = inner[pl.ds(s, 1), :] + products
        for e in range(per):
            sum_copy((base + e - me + n) % n).start()

    def span(peer, plane):
        return pl.ds(pl.multiple_of(peer * feat + plane * h, h), h)

    def sum_copy(q):
        peer = (me + q) % n
        return remote(
            grads.at[:, span(peer, 1 - mp), :],
            across_land.at[q],
            y_send.at[q],
            y_recv.at[q],
            across,
        )

    def inner_copy():
        return remote(inner, inner_land, p_sem.at[0], p_sem.at[1], across)

    def loads(q):
        rows = span((me + q) % n, mp)
        spot = q % 2
        return [
            pltpu.make_async_copy(across_land.at[q], e_buf.at[spot], load_sem.at[spot, 0]),
            pltpu.make_async_copy(
                inputs.at[pl.ds(0, STREAMS), rows, :], x_buf.at[spot], load_sem.at[spot, 1]
            ),
            pltpu.make_async_copy(direct.at[rows, :], go_buf.at[spot], load_sem.at[spot, 2]),
            pltpu.make_async_copy(smalls.at[rows, :], g_buf.at[spot], load_sem.at[spot, 3]),
            pltpu.make_async_copy(little.at[rows, :], l_buf.at[spot], load_sem.at[spot, 4]),
        ]

    def place_of_source(source, plane):
        return feature_side.at[source, :, pl.ds(pl.multiple_of(plane * h, h), h), :]

    def grads_of_source(source, plane):
        rows = pl.ds(pl.multiple_of(plane * h, h), h)
        return feature_side.at[source, pl.ds(0, STREAMS), rows, :]

    def output_of_source(source, plane):
        return feature_side.at[source, STREAMS, pl.ds(pl.multiple_of(plane * h, h), h), :]

    def out_copy(q):
        peer = (me + q) % n
        return remote(
            output.at[span(peer, mp), :],
            output_of_source(me, mp),
            o_send.at[q],
            o_recv.at[q],
            {"dp": peer},
        )

    def stream_copy(q):
        return remote(
            g_slots.at[q], grads_of_source(me, mp), a_send.at[q], a_recv.at[q], {"dp": (me + q) % n}
        )

    def little_copy(q):
        return remote(
            l_slots.at[q], l_land.at[q], l_send.at[q], l_recv.at[q], {"dp": (me + q) % n}
        )

    bits = second_land.shape[0]

    def second_copy(b):
        bit = (me // 2**b) % 2
        return remote(
            second_own,
            second_land.at[b],
            w_send.at[b],
            w_recv.at[b],
            {"dp": me + 2**b * (1 - 2 * bit)},
        )

    def second_turn(b):
        second_copy(b).wait()
        second_own[...] = second_own[...] + second_land[b]

    def home_copy():
        return pltpu.make_async_copy(g_slots.at[0], grads_of_source(me, mp), end_sem.at[0])

    def home_output():
        return pltpu.make_async_copy(
            output.at[span(me, mp), :], output_of_source(me, mp), end_sem.at[6]
        )

    def across_copy(q):
        there = place_of_source((me - q + n) % n, mp)
        return remote(there, there, fy_send.at[q], fy_recv.at[q], across)

    def start_loads(q):
        sum_copy(q).wait_recv()
        for copy in loads(q):
            copy.start()

    def norm_backward(q):
        spot = q % 2
        peer = (me + q) % n
        for copy in loads(q):
            copy.wait()

        @pl.loop(0, h // 16)
        def _(r):
            rows = pl.ds(pl.multiple_of(r * 16, 16), 16)
            full = pl.ds(pl.multiple_of(peer * feat + mp * h + r * 16, 16), 16)
            tail = l_buf[spot, rows, :]
            lane = lax.broadcasted_iota(jnp.int32, tail.shape, 1)
            for s in range(STREAMS):
                dy = grads[s, full, :].astype(f32) + e_buf[spot, s, rows, :].astype(f32)
                scale = level[pl.ds(s, 1), :]
                common = (inner[pl.ds(s, 1), :] + inner_land[pl.ds(s, 1), :]) * scale
                common = common * (1.0 / width)
                unit = x_buf[spot, s, rows, :].astype(f32) * scale
                gain = g_buf[spot, rows, :].astype(f32)[:, MIXH + s : MIXH + s + 1]
                grad = scale * (gain * dy) - unit * common
                if s == STREAMS - 1:
                    grad = grad + go_buf[spot, rows, :]
                g_slots[q, s, rows, :] = grad.astype(bf16)
                gain_grad = jnp.sum(unit * dy, axis=1, keepdims=True)
                tail = jnp.where(lane == MIXH + s, gain_grad, tail)
            l_slots[q, rows, :] = tail.astype(bf16)

    def norm_turn(q):
        @pl.when(q < n - 1)
        def _():
            start_loads(q + 1)

        norm_backward(q)

        @pl.when(q == 0)
        def _():
            home_copy().start()

        @pl.when(q > 0)
        def _():
            stream_copy(q).start()
            little_copy(q).start()

    def hist_load(q):
        source = (me - q + n) % n
        return pltpu.make_async_copy(
            hist.at[
                :,
                pl.ds(pl.multiple_of(mp * h, h), h),
                pl.ds(pl.multiple_of(source * tokens, 128), tokens),
            ],
            h_buf.at[q % 2],
            back_sem.at[q % 2, 0],
        )

    def grad_load(q):
        source = (me - q + n) % n
        return pltpu.make_async_copy(
            feature_side.at[source, pl.ds(0, STREAMS), pl.ds(pl.multiple_of(mp * h, h), h), :],
            f_buf.at[q % 2],
            back_sem.at[q % 2, 1],
        )

    def mix_copy(q):
        return remote(
            m_slots.at[q], m_land.at[q], m_send.at[q], m_recv.at[q], {"dp": (me - q + n) % n}
        )

    def mix_backward(q):
        for s in range(STREAMS):
            totals = [None] * HIST
            for r in range(h // 16):
                grad = f_buf[q % 2, s, r * 16 : r * 16 + 16, :].astype(f32)
                for j in range(HIST):
                    both = h_buf[q % 2, j, r * 16 : r * 16 + 16, :].astype(f32) * grad
                    both = both[0:8] + both[8:16]
                    totals[j] = both if r == 0 else totals[j] + both
            for j in range(HIST):
                m_wide[pl.ds(s * HIST + j, 1), :] = jnp.sum(totals[j], axis=0, keepdims=True)
        m_slots[q] = m_wide[...].astype(bf16)

    def arrive(q):
        @pl.when(q == 0)
        def _():
            home_copy().wait()
            home_output().wait()

        @pl.when(q > 0)
        def _():
            stream_copy(q).wait_recv()
            out_copy(q).wait_recv()

        across_copy(q).start()
        grad_load(q).start()
        hist_load(q).start()

    def mix_turn(q):
        @pl.when(q == 0)
        def _():
            arrive(q)

        @pl.when(q < n - 1)
        def _():
            arrive(q + 1)

        grad_load(q).wait()
        hist_load(q).wait()
        mix_backward(q)

        @pl.when(q > 0)
        def _():
            mix_copy(q).start()

    ahead = [(i, way) for i in (3, 1) for way in range(2)]
    middle = [(2, way) for way in range(2)]
    late = [(0, way) for way in range(2)]
    lead = 3

    def unit(step, i, way):
        if way == 0:
            for w in range(2):
                ring_copy(w, step - 1, i).wait_send()
        ring_unit(step, i, way)

    def first_blocks(some):
        for i, way in some:
            give(way, 0, i)
        for i, way in some:
            stage(way, 0, i)
            other_copy(way, 0, i).wait()
            add(way, 0, i, first=True)
            ring_copy(way, 0, i).start()
        for i, way in some:
            core_copy(way, 0, i).wait_send()
            give(way, 1, i)
        for i, way in some:
            stage(way, 1, i)

    def ahead_units(step):
        for i, way in ahead:
            unit(step, i, way)
        for i, way in ahead:
            stage(way, step + 1, i)

    def finish(i, way):
        other_copy(way, ring - 1, i).wait()
        ring_copy(way, ring - 2, i).wait_recv()
        if way == 1:
            final_copy(0, i).wait()
        add(way, ring - 1, i, last=True)
        final_copy(way, i).start()

    branch_copy = pltpu.make_async_copy(grad_branch, grads.at[0], end_sem.at[7])
    for step in range(2):
        rows_begin(step, True)
    branch_copy.start()
    for step in range(3):
        rows_begin(step, False)
    rows_begin(2, True)
    home_output().start()

    @pl.loop(1, n)
    def _(q):
        out_copy(q).start()

    second_own[...] = second[...]
    for copy in tile_loads(0):
        copy.start()
    inner[...] = jnp.zeros_like(inner)
    m_wide[...] = jnp.zeros_like(m_wide)
    for way in range(2):
        slots[0][way, 0] = jnp.zeros_like(slots[0][way, 0])
    rows_wait(0, True)
    rows_wait(1, True)
    first_blocks(ahead[:2])
    first_blocks(ahead[2:])
    branch_copy.wait()
    back_all(w_down, grad_up.shape[1], True)
    rows_wait(2, True)
    ahead_units(1)
    rows_begin(3, True)
    rows_wait(0, False)
    rows_wait(1, False)
    first_blocks(middle)
    rows_wait(3, True)
    ahead_units(2)
    rows_begin(4, True)
    back_all(w_out, grad_attended.shape[1], False)
    heads_here = heads.shape[1]

    @pl.loop(0, heads_here // 2)
    def _(head):
        attend_back(head)

    rows_wait(4, True)
    ahead_units(3)
    rows_begin(5, True)

    @pl.loop(heads_here // 2, heads_here)
    def _(head):
        attend_back(head)

    for i, way in late:
        give(way, 0, i)
    for i, way in late:
        stage(way, 0, i)

    opening = 2
    order = middle + ahead + late

    @pl.loop(1, ring - 1)
    def _(step):
        rows_wait(step + 1, False)

        @pl.when(step + lead <= ring - 2)
        def _():
            rows_wait(step + lead + 1, True)

        for b in range(bits):

            @pl.when(step == b + 1)
            def _():
                if b > 0:
                    second_turn(b - 1)
                second_copy(b).start()

        @pl.when(step == opening)
        def _():
            inner_copy().start()
            start_loads(0)
            inner_copy().wait()

        for u, (i, way) in enumerate(order):
            if i == 0:

                @pl.when(step > 1)
                def _():
                    if way == 0:
                        for w in range(2):
                            ring_copy(w, step - 2, i).wait_send()

                other_copy(way, step - 1, i).wait()

                @pl.when(step > 1)
                def _():
                    ring_copy(way, step - 2, i).wait_recv()

                add(way, step - 1, i)
                ring_copy(way, step - 1, i).start()
                core_copy(way, step - 1, i).wait_send()
                give(way, step, i)
            elif i == 2:
                unit(step, i, way)
            else:

                @pl.when(step + lead <= ring - 2)
                def _():
                    unit(step + lead, i, way)

                @pl.when(step == ring - 1 - lead)
                def _():
                    finish(i, way)

            if u % 2 == 0:

                @pl.when((step >= opening) & (step < opening + n // 4))
                def _():
                    norm_turn(4 * (step - opening) + u // 2)
            else:

                @pl.when((step > opening) & (step <= opening + n // 4))
                def _():
                    mix_turn(4 * (step - opening - 1) + u // 2)

            @pl.when(step == 1)
            def _():
                tile_turn(u)

            if u > 0:
                before, w = order[u - 1]
                if before in (1, 3):

                    @pl.when(step + lead <= ring - 2)
                    def _():
                        stage(w, step + lead + 1, before)
                else:
                    stage(w, step if before == 0 else step + 1, before)
        stage(1, step, 0)

        @pl.when(step < ring - 2)
        def _():
            rows_begin(step + 2, False)

        @pl.when(step + lead < ring - 2)
        def _():
            rows_begin(step + lead + 2, True)

    @pl.loop(1, n)
    def _(q):
        little_copy(q).wait_recv()
        mix_copy(q).wait_recv()

    def sum_over(land, own):
        return lax.fori_loop(
            1, n, lambda q, total: total + land[q].astype(f32), own.astype(f32)
        )

    l_sum[...] = sum_over(l_land, l_slots[0])
    m_mine[...] = sum_over(m_land, m_slots[0])
    second_turn(bits - 1)
    second_sum[...] = second_own[...]
    here = pl.ds(pl.multiple_of(mp * h, h), h)
    little_home = pltpu.make_async_copy(l_sum, little_sum.at[here], end_sem.at[1])
    little_across = remote(l_sum, little_sum.at[here], end_sem.at[2], end_sem.at[3], across)
    mix_across = remote(m_mine, m_other, end_sem.at[4], end_sem.at[5], across)
    little_home.start()
    little_across.start()
    mix_across.start()

    for i, way in late:
        unit(ring - 2, i, way)
    for i, way in late:
        stage(way, ring - 1, i)
    for i, way in middle + late:
        finish(i, way)

    mix_across.wait()
    mix_sum[...] = m_mine[...] + m_other[...]
    little_home.wait()
    little_across.wait()
    for i in range(count):
        final_copy(1, i).wait()

    @pl.loop(1, n)
    def _(q):
        stream_copy(q).wait_send()
        out_copy(q).wait_send()
        little_copy(q).wait_send()
        mix_copy(q).wait_send()

    @pl.loop(0, n)
    def _(q):
        sum_copy(q).wait_send()
        across_copy(q).wait()

    for i, way in order:
        ring_copy(way, ring - 2, i).wait_send()
        core_copy(way, ring - 1, i).wait_send()


def backward_exchange(
    n,
    normed,
    grad_branch,
    hidden,
    attn,
    slope,
    heads,
    w_qkv,
    w_out,
    w_up,
    w_down,
    tables,
    docs,
    level,
    inputs,
    direct,
    output,
    smalls,
    little,
    second,
    history,
    mixes,
    shards,
):
    count, ring = len(shards), n // 2
    feat, tokens = history.shape[1], level.shape[1]
    h, width = feat // 2, n * feat
    units = slope.shape[1]
    hbm = pl.BlockSpec(memory_space=pl.ANY)
    vmem = pl.BlockSpec(memory_space=pltpu.VMEM)

    def cut(s, rows):
        return s.shape[:-2] + (rows, s.shape[-1])

    half = shards[0].shape[-2] // 2
    tall = 256
    columns = attn.shape[1]
    places = [hbm, hbm, vmem, vmem, hbm, vmem, hbm, hbm, hbm, hbm, vmem, vmem, vmem, vmem]
    places += [hbm, hbm, hbm, hbm, hbm, vmem, hbm, hbm]
    found = pl.pallas_call(
        functools.partial(backward_kernel, n, count),
        out_shape=[
            jax.ShapeDtypeStruct((n, STREAMS, h, tokens), bf16),
            jax.ShapeDtypeStruct((n, STREAMS + 1, feat, tokens), bf16),
            jax.ShapeDtypeStruct((MIXED, tokens), f32),
            jax.ShapeDtypeStruct((feat, WIDE), f32),
            jax.ShapeDtypeStruct(second.shape, f32),
        ]
        + [jax.ShapeDtypeStruct(s.shape, f32) for s in shards]
        + [jax.ShapeDtypeStruct((2, ring) + cut(s, half), bf16) for s in shards],
        in_specs=places,
        out_specs=[hbm, hbm, vmem, hbm, vmem] + [hbm] * (2 * count),
        scratch_shapes=[pltpu.VMEM((2, 4) + cut(s, half), bf16) for s in shards]
        + [pltpu.VMEM((2,) + cut(s, half), bf16) for s in shards]
        + [pltpu.VMEM((2,) + cut(s, half), bf16) for s in shards]
        + [pltpu.VMEM(cut(s, half), f32) for s in shards]
        + [
            pltpu.VMEM((2, 3, 2, STREAMS, half, tokens), bf16),
            pltpu.VMEM((2, 3, 2, half, tokens), bf16),
            pltpu.VMEM((tokens, units), bf16),
            pltpu.VMEM((tokens, columns), bf16),
            pltpu.VMEM((3, tokens, columns), bf16),
            pltpu.VMEM((STREAMS, width, tokens), bf16),
            pltpu.VMEM((2, 3, tall, columns), bf16),
            pltpu.VMEM((2, tall, units), bf16),
            pltpu.VMEM((2, STREAMS, tall, tokens), bf16),
            pltpu.VMEM((8, tokens), f32),
            pltpu.VMEM((8, tokens), f32),
            pltpu.VMEM((2, STREAMS, h, tokens), bf16),
            pltpu.VMEM((2, STREAMS, h, tokens), bf16),
            pltpu.VMEM((2, h, tokens), f32),
            pltpu.VMEM((2, h, WIDE), bf16),
            pltpu.VMEM((2, h, WIDE), f32),
            pltpu.VMEM((n, STREAMS, h, tokens), bf16),
            pltpu.VMEM((n, h, WIDE), bf16),
            pltpu.VMEM((n, h, WIDE), bf16),
            pltpu.VMEM((n.bit_length() - 1,) + second.shape, f32),
            pltpu.VMEM(second.shape, f32),
            pltpu.VMEM((2, STREAMS, h, tokens), bf16),
            pltpu.VMEM((2, HIST, h, tokens), bf16),
            pltpu.VMEM((MIXED, tokens), f32),
            pltpu.VMEM((n, MIXED, tokens), bf16),
            pltpu.VMEM((n, MIXED, tokens), bf16),
            pltpu.VMEM((MIXED, tokens), f32),
            pltpu.VMEM((MIXED, tokens), f32),
            pltpu.VMEM((h, WIDE), f32),
            DMA((2, 3, 2)),
            DMA((2, 3, 2)),
            DMA((2, 2)),
            DMA((2, 3)),
            DMA((2, 5)),
            DMA((2, 2)),
            DMA((2, count)),
            DMA((count,)),
            DMA((n,)),
            DMA((n,)),
            DMA((2,)),
        ]
        + [DMA((n,)) for _ in range(12)]
        + [DMA((8,))]
        + [DMA((2, ring - 1, count)) for _ in range(2)]
        + [DMA((2, ring, count)) for _ in range(2)],
        compiler_params=pltpu.CompilerParams(
            collective_id=1, has_side_effects=True, vmem_limit_bytes=62 * 1024 * 1024
        ),
    )(
        normed,
        grad_branch,
        hidden,
        attn,
        slope,
        heads,
        w_qkv,
        w_out,
        w_up,
        w_down,
        tables,
        docs,
        docs.T,
        level,
        inputs,
        direct,
        output,
        smalls,
        little,
        second,
        history,
        mixes,
    )
    return found[1], found[2], found[3], found[4], found[5 : 5 + count]


def history_kernel(count, *refs):
    grads, mixes = refs[:2]
    sums = refs[2 : 2 + count]
    grad_history, block_out = refs[2 + count : 4 + count]
    outs, kept = refs[4 + count : 4 + 2 * count], refs[4 + 2 * count : 4 + 3 * count]
    sems = refs[4 + 3 * count]
    feat = grads.shape[2]
    came = [pltpu.make_async_copy(sums[i], kept[i], sems.at[0, i]) for i in range(count)]
    left = [pltpu.make_async_copy(kept[i], outs[i], sems.at[1, i]) for i in range(count)]

    @pl.when(pl.program_id(0) == 0)
    def _():
        for copy in came:
            copy.start()

    @pl.when(pl.program_id(0) == pl.num_programs(0) // 2)
    def _():
        for copy in came:
            copy.wait()
        for copy in left:
            copy.start()

    tokens = grads.shape[3]
    for i in range(grads.shape[0]):
        lanes = pl.ds(i * tokens, tokens)

        @pl.loop(0, feat // 32)
        def _(r):
            rows = pl.ds(pl.multiple_of(r * 32, 32), 32)
            each = [grads[i, s, rows, :].astype(f32) for s in range(STREAMS)]
            for j in range(HIST):
                total = mixes[i, pl.ds(j, 1), :] * each[0]
                for s in range(1, STREAMS):
                    total = total + mixes[i, pl.ds(s * HIST + j, 1), :] * each[s]
                grad_history[j, rows, lanes] = total.astype(bf16)

        block_out[:, lanes] = grads[i, STREAMS]

    @pl.when(pl.program_id(0) == pl.num_programs(0) - 1)
    def _():
        for copy in left:
            copy.wait()


def history_gradient(feature_side, mixes, sums):
    n, streams, feat, tokens = feature_side.shape
    count, group = len(sums), 4
    hbm = pl.BlockSpec(memory_space=pl.ANY)
    found = pl.pallas_call(
        functools.partial(history_kernel, count),
        grid=(n // group,),
        out_shape=[
            jax.ShapeDtypeStruct((HIST, feat, n * tokens), bf16),
            jax.ShapeDtypeStruct((feat, n * tokens), bf16),
        ]
        + [jax.ShapeDtypeStruct(s.shape, s.dtype) for s in sums],
        in_specs=[
            pl.BlockSpec((group, streams, feat, tokens), lambda i: (i, 0, 0, 0)),
            pl.BlockSpec((group,) + mixes.shape[1:], lambda i: (i, 0, 0)),
        ]
        + [hbm] * count,
        out_specs=[
            pl.BlockSpec((HIST, feat, group * tokens), lambda i: (0, 0, i)),
            pl.BlockSpec((feat, group * tokens), lambda i: (0, i)),
        ]
        + [hbm] * count,
        scratch_shapes=[pltpu.VMEM(s.shape, s.dtype) for s in sums] + [DMA((2, count))],
        compiler_params=pltpu.CompilerParams(vmem_limit_bytes=62 * 1024 * 1024),
    )(feature_side, mixes, *sums)
    return found[0], found[1], found[2:]


def angle_tables(length):
    halfway = ROT // 2
    frequency = np.exp(np.arange(halfway) * (-2.0 * math.log(10000.0) / ROT))
    angles = (np.arange(length) % TOK_DEV)[:, None] * frequency[None, :]
    tables = np.zeros((3, length, HEAD), np.float32)
    tables[0] = 1.0
    tables[0, :, :halfway] = tables[0, :, halfway:ROT] = np.cos(angles)
    tables[1, :, :halfway] = -np.sin(angles)
    tables[2, :, halfway:ROT] = np.sin(angles)
    return jnp.asarray(tables)


def body(
    history,
    mix_in,
    doc_ids,
    group_ids,
    group_scale,
    w_qkv,
    w_out,
    w_up,
    w_down,
    w_mix1,
    w_mix2,
    gains,
    cot_out,
    cot_mix,
):
    n = lax.axis_size("dp")
    tokens_here = mix_in.shape[0]
    small = jnp.pad(
        jnp.concatenate([w_mix1, gains.T], axis=1), ((0, 0), (0, WIDE - MIXH - gains.shape[0]))
    )
    tables = angle_tables(tokens_here)
    kept, (full_qkv, full_o, full_up, full_down, smalls) = forward_exchange(
        n,
        history,
        cot_out,
        mix_in.T,
        tables,
        doc_ids,
        group_ids,
        group_scale,
        cot_mix,
        w_mix2,
        (w_qkv, w_out, w_up, w_down, small),
    )
    inputs, mixes, normed, level, qkv_heads, attn_cat, slope, hidden = kept[:8]
    grad_out_full, grad_branch, out_low, little, mix_out, second = kept[8:]
    feature_side, mix_sum, little_sum, second_sum, sums = backward_exchange(
        n,
        normed,
        grad_branch,
        hidden,
        attn_cat,
        slope,
        qkv_heads,
        full_qkv,
        full_o,
        full_up,
        full_down,
        tables,
        doc_ids,
        level,
        inputs,
        grad_out_full,
        out_low,
        smalls,
        little,
        second,
        history,
        mixes,
        (w_qkv, w_out, w_up, w_down),
    )
    grad_history, block_out, sums = history_gradient(feature_side, mixes, sums)
    grad_qkv, grad_w_out, grad_w_up, grad_w_down = sums
    return (
        block_out,
        mix_out,
        grad_history,
        mix_sum[: STREAMS * HIST].T,
        grad_qkv,
        grad_w_out,
        grad_w_up,
        grad_w_down,
        little_sum[:, :MIXH],
        second_sum[:, :MIXH],
        little_sum[:, MIXH : MIXH + STREAMS + 1].T,
    )


def solution(mesh):
    return jax.shard_map(
        body,
        mesh=mesh,
        in_specs=(
            P(None, "dp", None),
            P("dp", None),
            P("dp", None),
            P("dp", None),
            P(),
            P(None, "dp", "mp"),
            P("dp", "mp"),
            P("dp", "mp"),
            P("dp", "mp"),
            P("dp", None),
            P(),
            P(None, "dp"),
            P("dp", None),
            P("dp", None),
        ),
        out_specs=(
            P("dp", None),
            P("dp", None),
            P(None, "dp", None),
            P("dp", None),
            P(None, "dp", "mp"),
            P("dp", "mp"),
            P("dp", "mp"),
            P("dp", "mp"),
            P("dp", None),
            P(),
            P(None, "dp"),
        ),
        check_vma=False,
    )
```

```python
import functools
import math

import jax
import jax.numpy as jnp
import numpy as np
from jax import lax
from jax.experimental import pallas as pl
from jax.experimental.pallas import tpu as pltpu
from jax.sharding import PartitionSpec as P

HEAD = 128
ROT = 32
HIST = 9
STREAMS = 4
GROUPS = 8
TOK_DEV = 384
MIXH = 40
WIDE = 128
MIXED = 48
EPS = 1e-05
CUTS = (1, 1, 2, 2, 1)
MESH = pl.DeviceIdType.MESH
DMA = pltpu.SemaphoreType.DMA
f32 = jnp.float32
bf16 = jnp.bfloat16


def chip_at(pos, ring):
    far = pos // (ring // 2)
    return (1 - far) * 2 * pos + far * (2 * (ring - 1 - pos) + 1)


def place_of(chip, ring):
    odd = chip % 2
    return (1 - odd) * (chip // 2) + odd * (ring - 1 - chip // 2)


def remote(src, dst, send, recv, device):
    return pltpu.make_async_remote_copy(
        src_ref=src,
        dst_ref=dst,
        send_sem=send,
        recv_sem=recv,
        device_id=device,
        device_id_type=MESH,
    )


def greet_plane(n, me, mp):
    barrier = pltpu.get_barrier_semaphore()

    @pl.loop(1, n)
    def _(k):
        pl.semaphore_signal(barrier, inc=1, device_id={"dp": (me + k) % n}, device_id_type=MESH)

    pl.semaphore_signal(barrier, inc=1, device_id={"mp": 1 - mp}, device_id_type=MESH)
    pl.semaphore_wait(barrier, n)


def rows_of(ref, start, count):
    if len(ref.shape) == 3:
        return ref.at[:, pl.ds(start, count), :]
    return ref.at[pl.ds(start, count), :]


def cuts_of(shards, cuts):
    pieces = []
    for i, shard in enumerate(shards):
        if len(shard.shape) == 3:
            pieces += [(i, s, 0) for s in range(shard.shape[0])]
        else:
            wide = shard.shape[1] // cuts[i]
            pieces += [(i, k * wide, wide) for k in range(cuts[i])]
    return pieces


def piece_of(refs, piece, start, count):
    i, first, wide = piece
    if wide == 0:
        return refs[i].at[first, pl.ds(start, count), :]
    return refs[i].at[pl.ds(start, count), pl.ds(first, wide)]


class Ring:
    def __init__(self, n):
        self.n, self.ring = n, n // 2
        self.me = lax.axis_index("dp")
        self.core = self.me % 2
        self.place = place_of(self.me // 2, self.ring)
        self.mate = self.me + 1 - 2 * self.core
        self.next_of = ({"dp": self.owner(1)}, {"dp": self.owner(-1)})

    def owner(self, offset):
        return chip_at((self.place + offset + 2 * self.ring) % self.ring, self.ring) * 2 + self.core


def forward_kernel(n, count, *refs):
    hist, cot, mix, tables, docs_row, docs_col, groups, weights, cot_in, mix2_in = refs[:10]
    shards = refs[10 : 10 + count]
    refs = refs[10 + count :]
    inputs, mixes, normed_out, level, heads_out, attn_out, slope_out, hidden_out = refs[:8]
    direct, grad_branch, out_low, little, mix_out, second = refs[8:14]
    fulls = refs[14 : 14 + count]
    (
        hist_buf,
        slots,
        streams,
        normed,
        tiles,
        heads,
        attn,
        slope_buf,
        hidden,
        down_buf,
        out_buf,
        branch,
        branch_land,
        smalls,
        total,
        token_scale,
        cot_mix,
        w_mix2,
        hist_sem,
        cot_sem,
        own_sem,
        local_sem,
        keep_sem,
        tile_sem,
        slope_sem,
        row_sem,
        swap_send,
        swap_recv,
        mix_send,
        mix_recv,
        a_send,
        a_recv,
        y_send,
        y_recv,
        ring_send,
        ring_recv,
        core_send,
        core_recv,
    ) = refs[14 + count :]
    where = Ring(n)
    me, ring, owner = where.me, where.ring, where.owner
    mp = lax.axis_index("mp")
    across = {"mp": 1 - mp}
    feat, tokens = hist.shape[1], mix.shape[1]
    h = feat // 2
    width = n * feat
    size = shards[0].shape[-2]
    half = size // 2
    w_qkv, w_out, w_up, w_down, all_small = fulls
    greet_plane(n, me, mp)

    pieces = cuts_of(shards, CUTS)

    def of(*arrays):
        return [p for p, piece in enumerate(pieces) if piece[0] in arrays]

    def origin_rows(offset, way):
        return pl.multiple_of(owner(offset) * size + way * half, half)

    def ring_copy(way, step, p, first=False):
        there = piece_of(fulls, pieces[p], origin_rows(-step if way == 0 else step, way), half)
        here = piece_of(shards, pieces[p], way * half, half) if first else there
        return remote(
            here, there, ring_send.at[way, step, p], ring_recv.at[way, step, p], where.next_of[way]
        )

    def ring_arrival(way, step, p):
        offset = -step - 1 if way == 0 else step + 1
        there = piece_of(fulls, pieces[p], origin_rows(offset, way), half)
        return remote(
            there, there, ring_send.at[way, step, p], ring_recv.at[way, step, p], where.next_of[way]
        )

    def core_copy(way, step, p, first=False):
        there = piece_of(fulls, pieces[p], origin_rows(-step if way == 0 else step, way), half)
        here = piece_of(shards, pieces[p], way * half, half) if first else there
        return remote(
            here, there, core_send.at[way, step, p], core_recv.at[way, step, p], {"dp": where.mate}
        )

    def shard_copy(i):
        return pltpu.make_async_copy(shards[i], rows_of(fulls[i], me * size, size), local_sem.at[i])

    def ring_begin(some):
        for p in some:
            for way in range(2):
                ring_copy(way, 0, p, True).start()

    def ring_step(step, some):
        for p in some:
            for way in range(2):
                ring_arrival(way, step - 1, p).wait_recv()
                ring_copy(way, step, p).start()
                core_copy(way, step, p).start()

    def ring_end(some):
        for p in some:
            for way in range(2):
                ring_arrival(way, ring - 2, p).wait_recv()
                core_copy(way, ring - 1, p).start()

    def ring_complete(*arrays):
        for i in arrays:
            shard_copy(i).wait()
        for p in of(*arrays):

            @pl.loop(0, ring)
            def _(step):
                for way in range(2):
                    core_copy(way, step, p).wait_recv()

    def mix_copy(q):
        return remote(
            mix, mixes.at[me], mix_send.at[q], mix_recv.at[q], {"dp": (me + q) % n}
        )

    def lanes(peer):
        return pl.ds(pl.multiple_of(peer * tokens, 128), tokens)

    def hist_copy(q):
        peer = (me + q) % n
        return pltpu.make_async_copy(
            hist.at[:, pl.ds(pl.multiple_of(mp * h, h), h), lanes(peer)],
            hist_buf.at[q % 2],
            hist_sem.at[q % 2],
        )

    def cot_copy(q):
        peer = (me + q) % n
        return pltpu.make_async_copy(
            cot.at[pl.ds(pl.multiple_of(mp * h, h), h), lanes(peer)],
            slots.at[q, STREAMS],
            cot_sem.at[q],
        )

    def features(source, plane):
        return streams.at[:, pl.ds(pl.multiple_of(source * feat + plane * h, h), h), :]

    def stream_copy(q):
        return remote(
            slots.at[q], features(me, mp), a_send.at[q], a_recv.at[q], {"dp": (me + q) % n}
        )

    def own_copy():
        return pltpu.make_async_copy(slots.at[0], features(me, mp), own_sem)

    def across_copy(q, own=False):
        there = features((me - q + n) % n, mp)
        return remote(
            slots.at[0] if own else there, there, y_send.at[q], y_recv.at[q], across
        )

    def mix_streams(q):
        peer = (me + q) % n

        @pl.loop(0, h // 16)
        def _(r):
            rows = pl.ds(pl.multiple_of(r * 16, 16), 16)
            sums = [None] * STREAMS
            for j in range(HIST):
                entry = hist_buf[q % 2, j, rows, :].astype(f32)
                for s in range(STREAMS):
                    term = mixes[peer, pl.ds(s * HIST + j, 1), :] * entry
                    sums[s] = term if j == 0 else sums[s] + term
            for s in range(STREAMS):
                slots[q, s, rows, :] = sums[s].astype(bf16)

    def normalise():
        level[...] = jnp.zeros_like(level)
        for s in range(STREAMS):

            def add(r, total):
                part = streams[s, pl.ds(pl.multiple_of(r * 32, 32), 32), :].astype(f32)
                part = part * part
                return total + (part[0:8] + part[8:16]) + (part[16:24] + part[24:32])

            squares = lax.fori_loop(0, width // 32, add, jnp.zeros((8, tokens), f32))
            mean = jnp.sum(squares, axis=0, keepdims=True) * (1.0 / width)
            level[pl.ds(s, 1), :] = lax.rsqrt(mean + EPS)

        @pl.loop(0, width // 32)
        def _(r):
            rows = pl.ds(pl.multiple_of(r * 32, 32), 32)
            gain = smalls[rows, :].astype(f32)
            for s in range(STREAMS):
                unit = streams[s, rows, :].astype(f32) * level[pl.ds(s, 1), :]
                normed[s, rows, :] = (unit * gain[:, MIXH + s : MIXH + s + 1]).astype(bf16)

    def head_tiles(pair, spot):
        columns = pl.ds(pl.multiple_of(pair * 2 * HEAD, 2 * HEAD), 2 * HEAD)
        return [
            pltpu.make_async_copy(
                w_qkv.at[s, :, columns], tiles.at[spot * 3 + s], tile_sem.at[spot * 3 + s]
            )
            for s in range(3)
        ]

    def first_dims(left, right):
        return lax.dot_general(left, right, (((0,), (0,)), ((), ())), preferred_element_type=f32)

    def last_dims(left, right):
        return lax.dot_general(left, right, (((1,), (1,)), ((), ())), preferred_element_type=f32)

    def attend(pair):
        spot = pair % 2
        for copy in head_tiles(pair, spot):
            copy.wait()

        @pl.when(pair < heads.shape[1] // 2 - 1)
        def _():
            for copy in head_tiles(pair + 1, 1 - spot):
                copy.start()

        for s in range(3):
            both = first_dims(normed[s], tiles[spot * 3 + s])
            for u in range(2):
                one = both[:, u * HEAD : (u + 1) * HEAD]
                if s < 2:
                    one = (
                        one * tables[0]
                        + pltpu.roll(one, HEAD - ROT // 2, 1) * tables[1]
                        + pltpu.roll(one, ROT // 2, 1) * tables[2]
                    )
                heads[s, pair * 2 + u] = one.astype(bf16)
        place = lax.broadcasted_iota(jnp.int32, (tokens, tokens), 0)
        other = lax.broadcasted_iota(jnp.int32, (tokens, tokens), 1)
        allowed = (place >= other) & (docs_col[...] == docs_row[...])
        for u in range(2):
            scores = last_dims(heads[0, pair * 2 + u], heads[1, pair * 2 + u]) * HEAD ** (-0.5)
            scores = jnp.where(allowed, scores, -1000000000.0)
            weight = jnp.exp(scores - jnp.max(scores, axis=1, keepdims=True))
            probs = weight * (1.0 / jnp.sum(weight, axis=1, keepdims=True))
            value = jnp.dot(
                probs.astype(bf16), heads[2, pair * 2 + u], preferred_element_type=f32
            )
            attn[:, pl.ds(pl.multiple_of((pair * 2 + u) * HEAD, HEAD), HEAD)] = value.astype(bf16)

    chunk = 512
    ups = hidden.shape[1] // chunk

    def up_tile(c, spot):
        return [
            pltpu.make_async_copy(
                w_up.at[:, pl.ds(pl.multiple_of(c * chunk + k * 256, 256), 256)],
                tiles.at[spot * 2 + k],
                tile_sem.at[spot * 2 + k],
            )
            for k in range(2)
        ]

    def slope_copy(c):
        return pltpu.make_async_copy(
            slope_buf.at[c % 2],
            slope_out.at[:, pl.ds(pl.multiple_of(c * chunk, chunk), chunk)],
            slope_sem.at[c % 2],
        )

    def feed(c, spot):
        for copy in up_tile(c, spot):
            copy.wait()

        @pl.when(c < ups - 1)
        def _():
            for copy in up_tile(c + 1, 1 - spot):
                copy.start()

        @pl.when(c >= 2)
        def _():
            slope_copy(c - 2).wait()

        for k in range(2):
            pre = first_dims(normed[STREAMS - 1], tiles[spot * 2 + k])
            below = 0.5 + 0.5 * lax.erf(pre * math.sqrt(0.5))
            bell = jnp.exp(-0.5 * pre * pre) * (1.0 / math.sqrt(2.0 * math.pi))
            slope_buf[c % 2, :, k * 256 : (k + 1) * 256] = (below + pre * bell).astype(bf16)
            low = (pre * below).astype(bf16)
            hidden[:, pl.ds(pl.multiple_of(c * chunk + k * 256, 256), 256)] = low
        slope_copy(c).start()

    def blocks(c):
        starts = []
        for way in range(2):
            shard = owner(-c if way == 0 else c)
            for which in range(2):
                row = (shard + which * (where.mate - me)) * size + way * half
                starts.append(pl.multiple_of(row, half))
        return starts

    def row_tiles(c):
        copies = []
        for b, start in enumerate(blocks(c)):
            rows, there = pl.ds(start, half), pl.ds(b * half, half)
            copies.append(
                pltpu.make_async_copy(
                    w_down.at[rows, :], down_buf.at[c % 2, there], row_sem.at[c % 2, b]
                )
            )
            copies.append(
                pltpu.make_async_copy(
                    w_out.at[rows, :], out_buf.at[c % 2, there], row_sem.at[c % 2, 4 + b]
                )
            )
        return copies

    def rows_begin(c):
        for p in of(3):
            for way in range(2):
                core_copy(way, c, p).wait_recv()
        for copy in row_tiles(c):
            copy.start()

    def rows_product(c):
        for copy in row_tiles(c):
            copy.wait()
        part = last_dims(down_buf[c % 2], hidden[...]) + last_dims(out_buf[c % 2], attn[...])
        branch[c] = part.astype(bf16)
        swap_copy(c).start()

    def swap_copy(c):
        return remote(
            branch.at[c], branch_land.at[c], swap_send.at[c], swap_recv.at[c], across
        )

    def mixing_network(squares):
        columns = lax.broadcasted_iota(jnp.int32, (tokens, WIDE), 1)
        plain = normed.at[0]
        gain_at = slice(MIXH + STREAMS, MIXH + STREAMS + 1)
        scale = lax.rsqrt(jnp.sum(squares, axis=0, keepdims=True) * (1.0 / width) + EPS)

        @pl.loop(0, width // 64)
        def _(r):
            rows = pl.ds(pl.multiple_of(r * 64, 64), 64)
            value = total[rows, :]
            out_low[rows, :] = value.astype(bf16)
            plain[rows, :] = (value * scale * smalls[rows, :].astype(f32)[:, gain_at]).astype(bf16)

        pre = first_dims(plain[...], smalls[...])
        below = 0.5 + 0.5 * lax.erf(pre * math.sqrt(0.5))
        bell = jnp.exp(-0.5 * pre * pre) * (1.0 / math.sqrt(2.0 * math.pi))
        low = jnp.where(columns < MIXH, pre * below, 0.0).astype(bf16)
        mix_out[...] = jnp.dot(low, w_mix2[...], preferred_element_type=f32)[:, :MIXH]
        grad = last_dims(cot_mix[...], w_mix2[...])
        grad = jnp.where(columns < MIXH, (below + pre * bell) * grad, 0.0).astype(bf16)
        second[...] = first_dims(low, cot_mix[...])[:MIXH]
        product = grad.astype(f32) * pre
        high = product.astype(bf16)
        ones = jnp.ones((8, WIDE), bf16)
        inner = last_dims(ones, high) + last_dims(ones, (product - high.astype(f32)).astype(bf16))
        inner = inner[0:1] * (1.0 / width)
        step = 256

        @pl.loop(0, width // step)
        def _(r):
            rows = pl.ds(pl.multiple_of(r * step, step), step)
            first = smalls[rows, :]
            gain = first.astype(f32)[:, gain_at]
            sums = jnp.dot(plain[rows, :], grad, preferred_element_type=f32)
            lane = lax.broadcasted_iota(jnp.int32, sums.shape, 1)
            gain_grad = jnp.sum(first.astype(f32) * sums, axis=1, keepdims=True) / gain
            little[rows, :] = jnp.where(lane == MIXH + STREAMS, gain_grad, sums)
            grad_normed = last_dims(first, grad)
            seed = streams[STREAMS, rows, :].astype(f32) * token_scale[0:1, :]
            value = seed + scale * (gain * grad_normed - total[rows, :] * (scale * inner))
            direct[rows, :] = value
            grad_branch[rows, :] = value.astype(bf16)

    def keep(k):
        pairs = [
            (streams, inputs),
            (normed, normed_out),
            (heads, heads_out),
            (attn, attn_out),
            (hidden, hidden_out),
        ]
        return pltpu.make_async_copy(pairs[k][0], pairs[k][1], keep_sem.at[k])

    def stream_turn(q):
        hist_copy(q).wait()

        @pl.when(q < n - 1)
        def _():
            hist_copy(q + 1).start()

        mix_copy(n - q).wait_recv()
        mix_streams(q)
        cot_copy(q).wait()
        stream_copy(q).start()

    def forward_turn(q):
        stream_copy(q).wait_recv()
        across_copy(q).start()

    @pl.loop(1, n)
    def _(q):
        mix_copy(q).start()

    @pl.loop(0, n)
    def _(q):
        cot_copy(q).start()

    hist_copy(0).start()
    ring_begin(of(2, 4))
    mixes[me] = mix[...]
    row = jnp.zeros((1, tokens), f32)
    for g in range(GROUPS):
        row = row + jnp.where(groups[...] == g, weights[g], 0.0)
    token_scale[...] = jnp.broadcast_to(row, token_scale.shape)
    cot_mix[...] = jnp.zeros_like(cot_mix)
    cot_mix[:, 0:MIXH] = cot_in[...]
    w_mix2[...] = jnp.zeros_like(w_mix2)
    w_mix2[0:MIXH, 0:MIXH] = mix2_in[...]
    hist_copy(0).wait()
    hist_copy(1).start()
    mix_streams(0)
    cot_copy(0).wait()
    own_copy().start()
    across_copy(0, True).start()

    @pl.loop(1, 4)
    def _(q):
        stream_turn(q)

    for p in range(len(pieces)):
        for way in range(2):
            core_copy(way, 0, p, True).start()
    for i in range(count):
        shard_copy(i).start()
    ring_begin(of(0, 1))

    @pl.loop(1, ring - 1)
    def _(step):
        ring_step(step, of(2, 4))
        for u in range(2):
            stream_turn(2 + 2 * step + u)
        for u in range(2):
            forward_turn(2 * step - 1 + u)

    ring_end(of(2, 4))
    ring_begin(of(3))
    pairs = heads.shape[1] // 2
    last = ring - 2
    early = 1

    def streams_here():
        ring_complete(2, 4)
        gains_copy = pltpu.make_async_copy(all_small, smalls, local_sem.at[count])
        gains_copy.start()
        for copy in up_tile(0, 0):
            copy.start()
        own_copy().wait()

        @pl.loop(0, n)
        def _(q):
            across_copy(q).wait_recv()

        keep(0).start()
        gains_copy.wait()
        normalise()
        keep(1).start()

    @pl.loop(1, ring - 1)
    def _(step):
        ring_step(step, of(0, 1))

        @pl.when(step == 1)
        def _():
            @pl.loop(n - 3, n)
            def _(q):
                forward_turn(q)

        @pl.when(step > last - early)
        def _():
            ring_step(step - (last - early), of(3))

        @pl.when(step == last - ups // 2)
        def _():
            streams_here()

        @pl.when(step > last - ups // 2)
        def _():
            for u in range(2):
                feed(2 * (step - (last - ups // 2) - 1) + u, u)

    keep(4).start()
    ring_end(of(0, 1))
    ring_complete(0, 1)
    shard_copy(3).wait()
    for copy in head_tiles(0, 0):
        copy.start()

    @pl.loop(early + 1, ring - 1)
    def _(step):
        ring_step(step, of(3))

        @pl.when(step <= early + pairs // 2)
        def _():
            for u in range(2):
                attend(2 * (step - early - 1) + u)

        @pl.when(step == early + pairs // 2)
        def _():
            for c in range(2):
                rows_begin(c)

        for ahead in range(1, 3):

            @pl.when(step == early + pairs // 2 + ahead)
            def _():
                for u in range(2):
                    c = 2 * (ahead - 1) + u
                    rows_product(c)
                    rows_begin(c + 2)

    keep(2).start()
    keep(3).start()

    @pl.loop(4, ring - 3)
    def _(c):
        rows_product(c)
        rows_begin(c + 2)

    rows_product(ring - 3)
    ring_end(of(3))
    rows_begin(ring - 1)
    rows_product(ring - 2)
    rows_product(ring - 1)

    def add_up(c, squares):
        swap_copy(c).wait_recv()
        for b, start in enumerate(blocks(c)):
            both = branch[c, b * half : (b + 1) * half].astype(f32)
            both = both + branch_land[c, b * half : (b + 1) * half].astype(f32)
            rows = pl.ds(start, half)
            value = streams[STREAMS - 1, rows, :].astype(f32) + both
            total[rows, :] = value
            value = value * value
            for k in range(half // 8):
                squares = squares + value[k * 8 : (k + 1) * 8]
        return squares

    squares = lax.fori_loop(0, ring, add_up, jnp.zeros((8, tokens), f32))

    for c in range(ups - 2, ups):
        slope_copy(c).wait()
    for k in range(5):
        keep(k).wait()
    mixing_network(squares)

    @pl.loop(0, ring)
    def _(c):
        swap_copy(c).wait_send()

    @pl.loop(1, n)
    def _(q):
        mix_copy(q).wait_send()
        stream_copy(q).wait_send()

    @pl.loop(0, n)
    def _(q):
        across_copy(q).wait_send()

    @pl.loop(0, ring)
    def _(step):
        for p in range(len(pieces)):
            for way in range(2):
                core_copy(way, step, p).wait_send()

    @pl.loop(0, ring - 1)
    def _(step):
        for p in range(len(pieces)):
            for way in range(2):
                ring_copy(way, step, p).wait_send()


def forward_exchange(
    n, history, cot_out, mix, tables, docs, groups, weights, cot_mix, w_mix2, shards
):
    count, ring = len(shards), n // 2
    feat, tokens = history.shape[1], mix.shape[1]
    h, width = feat // 2, n * feat
    hbm = pl.BlockSpec(memory_space=pl.ANY)
    vmem = pl.BlockSpec(memory_space=pltpu.VMEM)
    smem = pl.BlockSpec(memory_space=pltpu.SMEM)
    columns, units = shards[0].shape[2], shards[2].shape[1]
    across = columns // HEAD
    deep = 2 * shards[0].shape[1]
    travel = len(cuts_of(shards, CUTS))
    found = pl.pallas_call(
        functools.partial(forward_kernel, n, count),
        out_shape=[
            jax.ShapeDtypeStruct((STREAMS + 1, width, tokens), bf16),
            jax.ShapeDtypeStruct((n,) + mix.shape, f32),
            jax.ShapeDtypeStruct((STREAMS, width, tokens), bf16),
            jax.ShapeDtypeStruct((8, tokens), f32),
            jax.ShapeDtypeStruct((3, across, tokens, HEAD), bf16),
            jax.ShapeDtypeStruct((tokens, columns), bf16),
            jax.ShapeDtypeStruct((tokens, units), bf16),
            jax.ShapeDtypeStruct((tokens, units), bf16),
            jax.ShapeDtypeStruct((width, tokens), f32),
            jax.ShapeDtypeStruct((width, tokens), bf16),
            jax.ShapeDtypeStruct((width, tokens), bf16),
            jax.ShapeDtypeStruct((width, WIDE), f32),
            jax.ShapeDtypeStruct((tokens, MIXH), f32),
            jax.ShapeDtypeStruct((MIXH, WIDE), f32),
        ]
        + [
            jax.ShapeDtypeStruct(s.shape[:-2] + (s.shape[-2] * n, s.shape[-1]), s.dtype)
            for s in shards
        ],
        in_specs=[hbm, hbm] + [vmem] * 5 + [smem] + [vmem] * 2 + [hbm] * count,
        out_specs=[hbm, vmem, hbm, vmem, hbm, hbm, hbm, hbm] + [vmem] * 6 + [hbm] * count,
        scratch_shapes=[
            pltpu.VMEM((2, HIST, h, tokens), bf16),
            pltpu.VMEM((n, STREAMS + 1, h, tokens), bf16),
            pltpu.VMEM((STREAMS + 1, width, tokens), bf16),
            pltpu.VMEM((STREAMS, width, tokens), bf16),
            pltpu.VMEM((6, width, 2 * HEAD), bf16),
            pltpu.VMEM((3, across, tokens, HEAD), bf16),
            pltpu.VMEM((tokens, columns), bf16),
            pltpu.VMEM((2, tokens, 512), bf16),
            pltpu.VMEM((tokens, units), bf16),
            pltpu.VMEM((2, deep, units), bf16),
            pltpu.VMEM((2, deep, columns), bf16),
            pltpu.VMEM((ring, deep, tokens), bf16),
            pltpu.VMEM((ring, deep, tokens), bf16),
            pltpu.VMEM((width, WIDE), bf16),
            pltpu.VMEM((width, tokens), f32),
            pltpu.VMEM((8, tokens), f32),
            pltpu.VMEM((tokens, WIDE), bf16),
            pltpu.VMEM((WIDE, WIDE), bf16),
            DMA((2,)),
            DMA((n,)),
            DMA,
            DMA((count + 1,)),
            DMA((5,)),
            DMA((6,)),
            DMA((2,)),
            DMA((2, 8)),
            DMA((ring,)),
            DMA((ring,)),
        ]
        + [DMA((n,)) for _ in range(6)]
        + [DMA((2, ring - 1, travel)) for _ in range(2)]
        + [DMA((2, ring, travel)) for _ in range(2)],
        compiler_params=pltpu.CompilerParams(
            collective_id=0, has_side_effects=True, vmem_limit_bytes=60 * 1024 * 1024
        ),
    )(history, cot_out, mix, tables, docs, docs.T, groups, weights, cot_mix, w_mix2, *shards)
    return found[:14], found[14:]


def backward_kernel(n, count, *refs):
    (
        normed,
        grad_branch,
        hidden,
        attn,
        slope,
        heads,
        w_qkv,
        w_out,
        w_up,
        w_down,
        tables,
        docs_row,
        docs_col,
        level,
        inputs,
        direct,
        output,
        smalls,
        little,
        second,
        hist,
        mixes,
    ) = refs[:22]
    across_land, feature_side, mix_sum, little_sum, second_sum = refs[22:27]
    sums, mates = refs[27 : 27 + count], refs[27 + count : 27 + 2 * count]
    refs = refs[27 + 2 * count :]
    slots, other, mine, final = (refs[k * count : (k + 1) * count] for k in range(4))
    (
        rows_buf,
        branch_buf,
        grad_up,
        grad_attended,
        projs,
        grads,
        qkv_tile,
        up_tile,
        n_tile,
        inner,
        inner_land,
        e_buf,
        x_buf,
        go_buf,
        g_buf,
        l_buf,
        g_slots,
        l_slots,
        l_land,
        second_land,
        second_own,
        f_buf,
        h_buf,
        m_wide,
        m_slots,
        m_land,
        m_mine,
        m_other,
        l_sum,
        rows_sem,
        branch_sem,
        back_tile,
        tile_sem,
        load_sem,
        back_sem,
        other_sem,
        final_sem,
        y_send,
        y_recv,
        p_sem,
        o_send,
        o_recv,
        a_send,
        a_recv,
        l_send,
        l_recv,
        w_send,
        w_recv,
        fy_send,
        fy_recv,
        m_send,
        m_recv,
        end_sem,
        ring_send,
        ring_recv,
        core_send,
        core_recv,
    ) = refs[4 * count :]
    where = Ring(n)
    me, ring, owner = where.me, where.ring, where.owner
    mp = lax.axis_index("mp")
    across = {"mp": 1 - mp}
    feat, tokens = hist.shape[1], level.shape[1]
    h = feat // 2
    width = n * feat
    size = sums[0].shape[-2]
    half = size // 2
    greet_plane(n, me, mp)

    def first_dims(left, right):
        return lax.dot_general(left, right, (((0,), (0,)), ((), ())), preferred_element_type=f32)

    def last_dims(left, right):
        return lax.dot_general(left, right, (((1,), (1,)), ((), ())), preferred_element_type=f32)

    def target(way, step):
        return -1 - step if way == 0 else 1 + step

    def rows_load(way, step, branch):
        spot = step % 3
        copies = []
        for which in range(2):
            shard = owner(target(way, step)) + which * (where.mate - me)
            rows = pl.ds(pl.multiple_of(shard * size + way * half, half), half)
            if branch:
                here, there, sem = grad_branch.at[rows, :], branch_buf, branch_sem
            else:
                here, there, sem = normed.at[:, rows, :], rows_buf, rows_sem
            copies.append(
                pltpu.make_async_copy(here, there.at[way, spot, which], sem.at[way, spot, which])
            )
        return copies

    def rows_begin(step, branch):
        for way in range(2):
            for copy in rows_load(way, step, branch):
                copy.start()

    def rows_wait(step, branch):
        for way in range(2):
            for copy in rows_load(way, step, branch):
                copy.wait()

    def part(way, step, i, which, k, columns):
        if i in (1, 3):
            left = branch_buf[way, step % 3, which]
        else:
            left = rows_buf[way, step % 3, which, k if i == 0 else STREAMS - 1]
        right = (projs, attn, grad_up, hidden)[i]
        right = right[k, :, columns] if i == 0 else right[:, columns]
        return jnp.dot(left, right, preferred_element_type=f32)

    strip = 1024

    def strips(i, work):
        deep = len(sums[i].shape) == 3
        for k in range(sums[i].shape[0] if deep else 1):

            @pl.loop(0, sums[i].shape[-1] // strip)
            def _(c):
                columns = pl.ds(pl.multiple_of(c * strip, strip), strip)
                at = (k, slice(None), columns) if deep else (slice(None), columns)
                work(k, columns, at)

    def core_copy(way, step, i):
        return remote(
            mine[i].at[way],
            mates[i].at[way, step],
            core_send.at[way, step, i],
            core_recv.at[way, step, i],
            {"dp": where.mate},
        )

    def other_copy(way, step, i):
        return pltpu.make_async_copy(
            mates[i].at[way, step], other[i].at[way], other_sem.at[way, i]
        )

    def ring_copy(way, step, i):
        return remote(
            slots[i].at[way, step % 4],
            slots[i].at[way, (step + 1) % 4],
            ring_send.at[way, step, i],
            ring_recv.at[way, step, i],
            where.next_of[way],
        )

    def final_copy(way, i):
        return pltpu.make_async_copy(
            final[i], rows_of(sums[i], way * half, half), final_sem.at[i]
        )

    def give(way, step, i):
        def work(k, columns, at):
            mine[i][(way,) + at] = part(way, step, i, 1, k, columns).astype(bf16)

        strips(i, work)
        core_copy(way, step, i).start()

    def stage(way, step, i):
        core_copy(way, step, i).wait_recv()
        other_copy(way, step, i).start()

    def add(way, step, i, first=False, last=False):
        def work(k, columns, at):
            total = part(way, step, i, 0, k, columns) + other[i][(way,) + at].astype(f32)
            place = (way, step % 4) + at
            if not first:
                total = total + slots[i][place].astype(f32)
            if last:
                final[i][at] = total
            else:
                slots[i][place] = total.astype(bf16)

        strips(i, work)

    def ring_unit(step, i, way):
        other_copy(way, step, i).wait()
        ring_copy(way, step - 1, i).wait_recv()
        add(way, step, i)
        ring_copy(way, step, i).start()
        core_copy(way, step, i).wait_send()
        give(way, step + 1, i)

    broad = tokens

    def back_loads(c, wide, source, sloped):
        columns = pl.ds(pl.multiple_of(c * broad, 128), wide)
        spot = c % 2
        copies = [
            pltpu.make_async_copy(
                source.at[:, columns], grads.at[1 + spot, :, pl.ds(0, wide)], back_tile.at[spot, 0]
            )
        ]
        if sloped:
            copies.append(
                pltpu.make_async_copy(
                    slope.at[:, columns],
                    grads.at[3, pl.ds(pl.multiple_of(spot * tokens, 128), tokens), pl.ds(0, wide)],
                    back_tile.at[spot, 1],
                )
            )
        return copies

    def back_turn(c, wide, source, sloped):
        columns = pl.ds(pl.multiple_of(c * broad, 128), wide)
        spot = c % 2
        for copy in back_loads(c, wide, source, sloped):
            copy.wait()
        value = first_dims(grads[0], grads[1 + spot, :, 0:wide])
        if sloped:
            rows = pl.ds(pl.multiple_of(spot * tokens, 128), tokens)
            value = value * grads[3, rows, 0:wide].astype(f32)
            grad_up[:, columns] = value.astype(bf16)
        else:
            grad_attended[:, columns] = value.astype(bf16)

    def back_all(source, units, sloped):
        full, rest = units // broad, units % broad
        for copy in back_loads(0, broad, source, sloped):
            copy.start()

        @pl.loop(0, full - 1)
        def _(c):
            for copy in back_loads(c + 1, broad, source, sloped):
                copy.start()
            back_turn(c, broad, source, sloped)

        if rest:
            for copy in back_loads(full, rest, source, sloped):
                copy.start()
        back_turn(full - 1, broad, source, sloped)
        if rest:
            back_turn(full, rest, source, sloped)

    def attend_back(head):
        lane = pl.ds(pl.multiple_of(head * HEAD, HEAD), HEAD)
        query, key, value = heads[0, head], heads[1, head], heads[2, head]
        grad = grad_attended[:, lane]
        place = lax.broadcasted_iota(jnp.int32, (tokens, tokens), 0)
        behind = lax.broadcasted_iota(jnp.int32, (tokens, tokens), 1)
        allowed = (place >= behind) & (docs_col[...] == docs_row[...])
        scores = jnp.where(allowed, last_dims(query, key) * HEAD ** (-0.5), -1000000000.0)
        weight = jnp.exp(scores - jnp.max(scores, axis=1, keepdims=True))
        probs = weight * (1.0 / jnp.sum(weight, axis=1, keepdims=True))
        grad_probs = last_dims(grad, value)
        inside = jnp.sum(probs * grad_probs, axis=1, keepdims=True)
        grad_scores = (probs * (grad_probs - inside)).astype(bf16)
        grad_value = first_dims(probs.astype(bf16), grad)
        grad_query = jnp.dot(grad_scores, key, preferred_element_type=f32) * HEAD ** (-0.5)
        grad_key = first_dims(grad_scores, query) * HEAD ** (-0.5)

        def turn_back(one):
            return (
                one * tables[0]
                - pltpu.roll(one, HEAD - ROT // 2, 1) * tables[1]
                - pltpu.roll(one, ROT // 2, 1) * tables[2]
            )

        projs[0, :, lane] = turn_back(grad_query).astype(bf16)
        projs[1, :, lane] = turn_back(grad_key).astype(bf16)
        projs[2, :, lane] = grad_value.astype(bf16)

    tall = n_tile.shape[2]
    tiles = width // tall
    per = tall // feat

    def tile_loads(t):
        rows = pl.ds(pl.multiple_of(((me // per + t) % tiles) * tall, tall), tall)
        spot = t % 2
        return [
            pltpu.make_async_copy(w_qkv.at[:, rows, :], qkv_tile.at[spot], tile_sem.at[spot, 0]),
            pltpu.make_async_copy(w_up.at[rows, :], up_tile.at[spot], tile_sem.at[spot, 1]),
            pltpu.make_async_copy(normed.at[:, rows, :], n_tile.at[spot], tile_sem.at[spot, 2]),
        ]

    def tile_turn(t):
        spot = t % 2
        for copy in tile_loads(t):
            copy.wait()

        @pl.when(t < tiles - 1)
        def _():
            for copy in tile_loads(t + 1):
                copy.start()

        base = ((me // per + t) % tiles) * per
        rows = pl.ds(pl.multiple_of(base * feat, tall), tall)
        for s in range(STREAMS):
            if s < 3:
                grad = last_dims(qkv_tile[spot, s], projs[s])
            else:
                grad = last_dims(up_tile[spot], grad_up[...])
            grads[s, rows, :] = grad.astype(bf16)
            products = jnp.sum(n_tile[spot, s].astype(f32) * grad, axis=0, keepdims=True)
            inner[pl.ds(s, 1), :] = inner[pl.ds(s, 1), :] + products
        for e in range(per):
            sum_copy((base + e - me + n) % n).start()

    def span(peer, plane):
        return pl.ds(pl.multiple_of(peer * feat + plane * h, h), h)

    def sum_copy(q):
        peer = (me + q) % n
        return remote(
            grads.at[:, span(peer, 1 - mp), :],
            across_land.at[q],
            y_send.at[q],
            y_recv.at[q],
            across,
        )

    def inner_copy():
        return remote(inner, inner_land, p_sem.at[0], p_sem.at[1], across)

    def loads(q):
        rows = span((me + q) % n, mp)
        spot = q % 2
        return [
            pltpu.make_async_copy(across_land.at[q], e_buf.at[spot], load_sem.at[spot, 0]),
            pltpu.make_async_copy(
                inputs.at[pl.ds(0, STREAMS), rows, :], x_buf.at[spot], load_sem.at[spot, 1]
            ),
            pltpu.make_async_copy(direct.at[rows, :], go_buf.at[spot], load_sem.at[spot, 2]),
            pltpu.make_async_copy(smalls.at[rows, :], g_buf.at[spot], load_sem.at[spot, 3]),
            pltpu.make_async_copy(little.at[rows, :], l_buf.at[spot], load_sem.at[spot, 4]),
        ]

    def place_of_source(source, plane):
        return feature_side.at[source, :, pl.ds(pl.multiple_of(plane * h, h), h), :]

    def grads_of_source(source, plane):
        rows = pl.ds(pl.multiple_of(plane * h, h), h)
        return feature_side.at[source, pl.ds(0, STREAMS), rows, :]

    def output_of_source(source, plane):
        return feature_side.at[source, STREAMS, pl.ds(pl.multiple_of(plane * h, h), h), :]

    def out_copy(q):
        peer = (me + q) % n
        return remote(
            output.at[span(peer, mp), :],
            output_of_source(me, mp),
            o_send.at[q],
            o_recv.at[q],
            {"dp": peer},
        )

    def stream_copy(q):
        return remote(
            g_slots.at[q], grads_of_source(me, mp), a_send.at[q], a_recv.at[q], {"dp": (me + q) % n}
        )

    def little_copy(q):
        return remote(
            l_slots.at[q], l_land.at[q], l_send.at[q], l_recv.at[q], {"dp": (me + q) % n}
        )

    bits = second_land.shape[0]

    def second_copy(b):
        bit = (me // 2**b) % 2
        return remote(
            second_own,
            second_land.at[b],
            w_send.at[b],
            w_recv.at[b],
            {"dp": me + 2**b * (1 - 2 * bit)},
        )

    def second_turn(b):
        second_copy(b).wait()
        second_own[...] = second_own[...] + second_land[b]

    def home_copy():
        return pltpu.make_async_copy(g_slots.at[0], grads_of_source(me, mp), end_sem.at[0])

    def home_output():
        return pltpu.make_async_copy(
            output.at[span(me, mp), :], output_of_source(me, mp), end_sem.at[6]
        )

    def across_copy(q):
        there = place_of_source((me - q + n) % n, mp)
        return remote(there, there, fy_send.at[q], fy_recv.at[q], across)

    def start_loads(q):
        sum_copy(q).wait_recv()
        for copy in loads(q):
            copy.start()

    def norm_backward(q):
        spot = q % 2
        peer = (me + q) % n
        for copy in loads(q):
            copy.wait()

        @pl.loop(0, h // 16)
        def _(r):
            rows = pl.ds(pl.multiple_of(r * 16, 16), 16)
            full = pl.ds(pl.multiple_of(peer * feat + mp * h + r * 16, 16), 16)
            tail = l_buf[spot, rows, :]
            lane = lax.broadcasted_iota(jnp.int32, tail.shape, 1)
            for s in range(STREAMS):
                dy = grads[s, full, :].astype(f32) + e_buf[spot, s, rows, :].astype(f32)
                scale = level[pl.ds(s, 1), :]
                common = (inner[pl.ds(s, 1), :] + inner_land[pl.ds(s, 1), :]) * scale
                common = common * (1.0 / width)
                unit = x_buf[spot, s, rows, :].astype(f32) * scale
                gain = g_buf[spot, rows, :].astype(f32)[:, MIXH + s : MIXH + s + 1]
                grad = scale * (gain * dy) - unit * common
                if s == STREAMS - 1:
                    grad = grad + go_buf[spot, rows, :]
                g_slots[q, s, rows, :] = grad.astype(bf16)
                gain_grad = jnp.sum(unit * dy, axis=1, keepdims=True)
                tail = jnp.where(lane == MIXH + s, gain_grad, tail)
            l_slots[q, rows, :] = tail.astype(bf16)

    def norm_turn(q):
        @pl.when(q < n - 1)
        def _():
            start_loads(q + 1)

        norm_backward(q)

        @pl.when(q == 0)
        def _():
            home_copy().start()

        @pl.when(q > 0)
        def _():
            stream_copy(q).start()
            little_copy(q).start()

    def hist_load(q):
        source = (me - q + n) % n
        return pltpu.make_async_copy(
            hist.at[
                :,
                pl.ds(pl.multiple_of(mp * h, h), h),
                pl.ds(pl.multiple_of(source * tokens, 128), tokens),
            ],
            h_buf.at[q % 2],
            back_sem.at[q % 2, 0],
        )

    def grad_load(q):
        source = (me - q + n) % n
        return pltpu.make_async_copy(
            feature_side.at[source, pl.ds(0, STREAMS), pl.ds(pl.multiple_of(mp * h, h), h), :],
            f_buf.at[q % 2],
            back_sem.at[q % 2, 1],
        )

    def mix_copy(q):
        return remote(
            m_slots.at[q], m_land.at[q], m_send.at[q], m_recv.at[q], {"dp": (me - q + n) % n}
        )

    def mix_backward(q):
        for s in range(STREAMS):
            totals = [None] * HIST
            for r in range(h // 16):
                grad = f_buf[q % 2, s, r * 16 : r * 16 + 16, :].astype(f32)
                for j in range(HIST):
                    both = h_buf[q % 2, j, r * 16 : r * 16 + 16, :].astype(f32) * grad
                    both = both[0:8] + both[8:16]
                    totals[j] = both if r == 0 else totals[j] + both
            for j in range(HIST):
                m_wide[pl.ds(s * HIST + j, 1), :] = jnp.sum(totals[j], axis=0, keepdims=True)
        m_slots[q] = m_wide[...].astype(bf16)

    def arrive(q):
        @pl.when(q == 0)
        def _():
            home_copy().wait()
            home_output().wait()

        @pl.when(q > 0)
        def _():
            stream_copy(q).wait_recv()
            out_copy(q).wait_recv()

        across_copy(q).start()
        grad_load(q).start()
        hist_load(q).start()

    def mix_turn(q):
        @pl.when(q == 0)
        def _():
            arrive(q)

        @pl.when(q < n - 1)
        def _():
            arrive(q + 1)

        grad_load(q).wait()
        hist_load(q).wait()
        mix_backward(q)

        @pl.when(q > 0)
        def _():
            mix_copy(q).start()

    ahead = [(i, way) for i in (3, 1) for way in range(2)]
    middle = [(2, way) for way in range(2)]
    late = [(0, way) for way in range(2)]
    lead = 3

    def unit(step, i, way):
        if way == 0:
            for w in range(2):
                ring_copy(w, step - 1, i).wait_send()
        ring_unit(step, i, way)

    def first_blocks(some):
        for i, way in some:
            give(way, 0, i)
        for i, way in some:
            stage(way, 0, i)
            other_copy(way, 0, i).wait()
            add(way, 0, i, first=True)
            ring_copy(way, 0, i).start()
        for i, way in some:
            core_copy(way, 0, i).wait_send()
            give(way, 1, i)
        for i, way in some:
            stage(way, 1, i)

    def ahead_units(step):
        for i, way in ahead:
            unit(step, i, way)
        for i, way in ahead:
            stage(way, step + 1, i)

    def finish(i, way):
        other_copy(way, ring - 1, i).wait()
        ring_copy(way, ring - 2, i).wait_recv()
        if way == 1:
            final_copy(0, i).wait()
        add(way, ring - 1, i, last=True)
        final_copy(way, i).start()

    branch_copy = pltpu.make_async_copy(grad_branch, grads.at[0], end_sem.at[7])
    for step in range(2):
        rows_begin(step, True)
    branch_copy.start()
    for step in range(3):
        rows_begin(step, False)
    rows_begin(2, True)
    home_output().start()

    @pl.loop(1, n)
    def _(q):
        out_copy(q).start()

    second_own[...] = second[...]
    for copy in tile_loads(0):
        copy.start()
    inner[...] = jnp.zeros_like(inner)
    m_wide[...] = jnp.zeros_like(m_wide)
    for way in range(2):
        slots[0][way, 0] = jnp.zeros_like(slots[0][way, 0])
    rows_wait(0, True)
    rows_wait(1, True)
    first_blocks(ahead[:2])
    first_blocks(ahead[2:])
    branch_copy.wait()
    back_all(w_down, grad_up.shape[1], True)
    rows_wait(2, True)
    ahead_units(1)
    rows_begin(3, True)
    rows_wait(0, False)
    rows_wait(1, False)
    first_blocks(middle)
    rows_wait(3, True)
    ahead_units(2)
    rows_begin(4, True)
    back_all(w_out, grad_attended.shape[1], False)
    heads_here = heads.shape[1]

    @pl.loop(0, heads_here // 2)
    def _(head):
        attend_back(head)

    rows_wait(4, True)
    ahead_units(3)
    rows_begin(5, True)

    @pl.loop(heads_here // 2, heads_here)
    def _(head):
        attend_back(head)

    for i, way in late:
        give(way, 0, i)
    for i, way in late:
        stage(way, 0, i)

    opening = 2
    order = ahead + middle + late

    @pl.loop(1, ring - 1)
    def _(step):
        rows_wait(step + 1, False)

        @pl.when(step + lead <= ring - 2)
        def _():
            rows_wait(step + lead + 1, True)

        for b in range(bits):

            @pl.when(step == b + 1)
            def _():
                if b > 0:
                    second_turn(b - 1)
                second_copy(b).start()

        @pl.when(step == opening)
        def _():
            inner_copy().start()
            start_loads(0)
            inner_copy().wait()

        for u, (i, way) in enumerate(order):
            if i == 0:

                @pl.when(step > 1)
                def _():
                    if way == 0:
                        for w in range(2):
                            ring_copy(w, step - 2, i).wait_send()

                other_copy(way, step - 1, i).wait()

                @pl.when(step > 1)
                def _():
                    ring_copy(way, step - 2, i).wait_recv()

                add(way, step - 1, i)
                ring_copy(way, step - 1, i).start()
                core_copy(way, step - 1, i).wait_send()
                give(way, step, i)
            elif i == 2:
                unit(step, i, way)
            else:

                @pl.when(step + lead <= ring - 2)
                def _():
                    unit(step + lead, i, way)

                @pl.when(step == ring - 1 - lead)
                def _():
                    finish(i, way)

            if u % 2 == 0:

                @pl.when((step >= opening) & (step < opening + n // 4))
                def _():
                    norm_turn(4 * (step - opening) + u // 2)
            else:

                @pl.when((step > opening) & (step <= opening + n // 4))
                def _():
                    mix_turn(4 * (step - opening - 1) + u // 2)

            @pl.when(step == 1)
            def _():
                tile_turn(u)

            if u > 0:
                before, w = order[u - 1]
                if before in (1, 3):

                    @pl.when(step + lead <= ring - 2)
                    def _():
                        stage(w, step + lead + 1, before)
                else:
                    stage(w, step if before == 0 else step + 1, before)
        stage(1, step, 0)

        @pl.when(step < ring - 2)
        def _():
            rows_begin(step + 2, False)

        @pl.when(step + lead < ring - 2)
        def _():
            rows_begin(step + lead + 2, True)

    @pl.loop(1, n)
    def _(q):
        little_copy(q).wait_recv()
        mix_copy(q).wait_recv()

    def sum_over(land, own):
        return lax.fori_loop(
            1, n, lambda q, total: total + land[q].astype(f32), own.astype(f32)
        )

    l_sum[...] = sum_over(l_land, l_slots[0])
    m_mine[...] = sum_over(m_land, m_slots[0])
    second_turn(bits - 1)
    second_sum[...] = second_own[...]
    here = pl.ds(pl.multiple_of(mp * h, h), h)
    little_home = pltpu.make_async_copy(l_sum, little_sum.at[here], end_sem.at[1])
    little_across = remote(l_sum, little_sum.at[here], end_sem.at[2], end_sem.at[3], across)
    mix_across = remote(m_mine, m_other, end_sem.at[4], end_sem.at[5], across)
    little_home.start()
    little_across.start()
    mix_across.start()

    for i, way in late:
        unit(ring - 2, i, way)
    for i, way in late:
        stage(way, ring - 1, i)
    for i, way in middle + late:
        finish(i, way)

    mix_across.wait()
    mix_sum[...] = m_mine[...] + m_other[...]
    little_home.wait()
    little_across.wait()
    for i in range(count):
        final_copy(1, i).wait()

    @pl.loop(1, n)
    def _(q):
        stream_copy(q).wait_send()
        out_copy(q).wait_send()
        little_copy(q).wait_send()
        mix_copy(q).wait_send()

    @pl.loop(0, n)
    def _(q):
        sum_copy(q).wait_send()
        across_copy(q).wait()

    for i, way in order:
        ring_copy(way, ring - 2, i).wait_send()
        core_copy(way, ring - 1, i).wait_send()


def backward_exchange(
    n,
    normed,
    grad_branch,
    hidden,
    attn,
    slope,
    heads,
    w_qkv,
    w_out,
    w_up,
    w_down,
    tables,
    docs,
    level,
    inputs,
    direct,
    output,
    smalls,
    little,
    second,
    history,
    mixes,
    shards,
):
    count, ring = len(shards), n // 2
    feat, tokens = history.shape[1], level.shape[1]
    h, width = feat // 2, n * feat
    units = slope.shape[1]
    hbm = pl.BlockSpec(memory_space=pl.ANY)
    vmem = pl.BlockSpec(memory_space=pltpu.VMEM)

    def cut(s, rows):
        return s.shape[:-2] + (rows, s.shape[-1])

    half = shards[0].shape[-2] // 2
    tall = 256
    columns = attn.shape[1]
    places = [hbm, hbm, vmem, vmem, hbm, vmem, hbm, hbm, hbm, hbm, vmem, vmem, vmem, vmem]
    places += [hbm, hbm, hbm, hbm, hbm, vmem, hbm, hbm]
    found = pl.pallas_call(
        functools.partial(backward_kernel, n, count),
        out_shape=[
            jax.ShapeDtypeStruct((n, STREAMS, h, tokens), bf16),
            jax.ShapeDtypeStruct((n, STREAMS + 1, feat, tokens), bf16),
            jax.ShapeDtypeStruct((MIXED, tokens), f32),
            jax.ShapeDtypeStruct((feat, WIDE), f32),
            jax.ShapeDtypeStruct(second.shape, f32),
        ]
        + [jax.ShapeDtypeStruct(s.shape, f32) for s in shards]
        + [jax.ShapeDtypeStruct((2, ring) + cut(s, half), bf16) for s in shards],
        in_specs=places,
        out_specs=[hbm, hbm, vmem, hbm, vmem] + [hbm] * (2 * count),
        scratch_shapes=[pltpu.VMEM((2, 4) + cut(s, half), bf16) for s in shards]
        + [pltpu.VMEM((2,) + cut(s, half), bf16) for s in shards]
        + [pltpu.VMEM((2,) + cut(s, half), bf16) for s in shards]
        + [pltpu.VMEM(cut(s, half), f32) for s in shards]
        + [
            pltpu.VMEM((2, 3, 2, STREAMS, half, tokens), bf16),
            pltpu.VMEM((2, 3, 2, half, tokens), bf16),
            pltpu.VMEM((tokens, units), bf16),
            pltpu.VMEM((tokens, columns), bf16),
            pltpu.VMEM((3, tokens, columns), bf16),
            pltpu.VMEM((STREAMS, width, tokens), bf16),
            pltpu.VMEM((2, 3, tall, columns), bf16),
            pltpu.VMEM((2, tall, units), bf16),
            pltpu.VMEM((2, STREAMS, tall, tokens), bf16),
            pltpu.VMEM((8, tokens), f32),
            pltpu.VMEM((8, tokens), f32),
            pltpu.VMEM((2, STREAMS, h, tokens), bf16),
            pltpu.VMEM((2, STREAMS, h, tokens), bf16),
            pltpu.VMEM((2, h, tokens), f32),
            pltpu.VMEM((2, h, WIDE), bf16),
            pltpu.VMEM((2, h, WIDE), f32),
            pltpu.VMEM((n, STREAMS, h, tokens), bf16),
            pltpu.VMEM((n, h, WIDE), bf16),
            pltpu.VMEM((n, h, WIDE), bf16),
            pltpu.VMEM((n.bit_length() - 1,) + second.shape, f32),
            pltpu.VMEM(second.shape, f32),
            pltpu.VMEM((2, STREAMS, h, tokens), bf16),
            pltpu.VMEM((2, HIST, h, tokens), bf16),
            pltpu.VMEM((MIXED, tokens), f32),
            pltpu.VMEM((n, MIXED, tokens), bf16),
            pltpu.VMEM((n, MIXED, tokens), bf16),
            pltpu.VMEM((MIXED, tokens), f32),
            pltpu.VMEM((MIXED, tokens), f32),
            pltpu.VMEM((h, WIDE), f32),
            DMA((2, 3, 2)),
            DMA((2, 3, 2)),
            DMA((2, 2)),
            DMA((2, 3)),
            DMA((2, 5)),
            DMA((2, 2)),
            DMA((2, count)),
            DMA((count,)),
            DMA((n,)),
            DMA((n,)),
            DMA((2,)),
        ]
        + [DMA((n,)) for _ in range(12)]
        + [DMA((8,))]
        + [DMA((2, ring - 1, count)) for _ in range(2)]
        + [DMA((2, ring, count)) for _ in range(2)],
        compiler_params=pltpu.CompilerParams(
            collective_id=1, has_side_effects=True, vmem_limit_bytes=62 * 1024 * 1024
        ),
    )(
        normed,
        grad_branch,
        hidden,
        attn,
        slope,
        heads,
        w_qkv,
        w_out,
        w_up,
        w_down,
        tables,
        docs,
        docs.T,
        level,
        inputs,
        direct,
        output,
        smalls,
        little,
        second,
        history,
        mixes,
    )
    return found[1], found[2], found[3], found[4], found[5 : 5 + count]


def history_kernel(count, *refs):
    grads, mixes = refs[:2]
    sums = refs[2 : 2 + count]
    grad_history, block_out = refs[2 + count : 4 + count]
    outs, kept = refs[4 + count : 4 + 2 * count], refs[4 + 2 * count : 4 + 3 * count]
    sems = refs[4 + 3 * count]
    feat = grads.shape[2]
    came = [pltpu.make_async_copy(sums[i], kept[i], sems.at[0, i]) for i in range(count)]
    left = [pltpu.make_async_copy(kept[i], outs[i], sems.at[1, i]) for i in range(count)]

    @pl.when(pl.program_id(0) == 0)
    def _():
        for copy in came:
            copy.start()

    @pl.when(pl.program_id(0) == pl.num_programs(0) // 2)
    def _():
        for copy in came:
            copy.wait()
        for copy in left:
            copy.start()

    tokens = grads.shape[3]
    for i in range(grads.shape[0]):
        lanes = pl.ds(i * tokens, tokens)

        @pl.loop(0, feat // 32)
        def _(r):
            rows = pl.ds(pl.multiple_of(r * 32, 32), 32)
            each = [grads[i, s, rows, :].astype(f32) for s in range(STREAMS)]
            for j in range(HIST):
                total = mixes[i, pl.ds(j, 1), :] * each[0]
                for s in range(1, STREAMS):
                    total = total + mixes[i, pl.ds(s * HIST + j, 1), :] * each[s]
                grad_history[j, rows, lanes] = total.astype(bf16)

        block_out[:, lanes] = grads[i, STREAMS]

    @pl.when(pl.program_id(0) == pl.num_programs(0) - 1)
    def _():
        for copy in left:
            copy.wait()


def history_gradient(feature_side, mixes, sums):
    n, streams, feat, tokens = feature_side.shape
    count, group = len(sums), 4
    hbm = pl.BlockSpec(memory_space=pl.ANY)
    found = pl.pallas_call(
        functools.partial(history_kernel, count),
        grid=(n // group,),
        out_shape=[
            jax.ShapeDtypeStruct((HIST, feat, n * tokens), bf16),
            jax.ShapeDtypeStruct((feat, n * tokens), bf16),
        ]
        + [jax.ShapeDtypeStruct(s.shape, s.dtype) for s in sums],
        in_specs=[
            pl.BlockSpec((group, streams, feat, tokens), lambda i: (i, 0, 0, 0)),
            pl.BlockSpec((group,) + mixes.shape[1:], lambda i: (i, 0, 0)),
        ]
        + [hbm] * count,
        out_specs=[
            pl.BlockSpec((HIST, feat, group * tokens), lambda i: (0, 0, i)),
            pl.BlockSpec((feat, group * tokens), lambda i: (0, i)),
        ]
        + [hbm] * count,
        scratch_shapes=[pltpu.VMEM(s.shape, s.dtype) for s in sums] + [DMA((2, count))],
        compiler_params=pltpu.CompilerParams(vmem_limit_bytes=62 * 1024 * 1024),
    )(feature_side, mixes, *sums)
    return found[0], found[1], found[2:]


def angle_tables(length):
    halfway = ROT // 2
    frequency = np.exp(np.arange(halfway) * (-2.0 * math.log(10000.0) / ROT))
    angles = (np.arange(length) % TOK_DEV)[:, None] * frequency[None, :]
    tables = np.zeros((3, length, HEAD), np.float32)
    tables[0] = 1.0
    tables[0, :, :halfway] = tables[0, :, halfway:ROT] = np.cos(angles)
    tables[1, :, :halfway] = -np.sin(angles)
    tables[2, :, halfway:ROT] = np.sin(angles)
    return jnp.asarray(tables)


def body(
    history,
    mix_in,
    doc_ids,
    group_ids,
    group_scale,
    w_qkv,
    w_out,
    w_up,
    w_down,
    w_mix1,
    w_mix2,
    gains,
    cot_out,
    cot_mix,
):
    n = lax.axis_size("dp")
    tokens_here = mix_in.shape[0]
    small = jnp.pad(
        jnp.concatenate([w_mix1, gains.T], axis=1), ((0, 0), (0, WIDE - MIXH - gains.shape[0]))
    )
    tables = angle_tables(tokens_here)
    kept, (full_qkv, full_o, full_up, full_down, smalls) = forward_exchange(
        n,
        history,
        cot_out,
        mix_in.T,
        tables,
        doc_ids,
        group_ids,
        group_scale,
        cot_mix,
        w_mix2,
        (w_qkv, w_out, w_up, w_down, small),
    )
    inputs, mixes, normed, level, qkv_heads, attn_cat, slope, hidden = kept[:8]
    grad_out_full, grad_branch, out_low, little, mix_out, second = kept[8:]
    feature_side, mix_sum, little_sum, second_sum, sums = backward_exchange(
        n,
        normed,
        grad_branch,
        hidden,
        attn_cat,
        slope,
        qkv_heads,
        full_qkv,
        full_o,
        full_up,
        full_down,
        tables,
        doc_ids,
        level,
        inputs,
        grad_out_full,
        out_low,
        smalls,
        little,
        second,
        history,
        mixes,
        (w_qkv, w_out, w_up, w_down),
    )
    grad_history, block_out, sums = history_gradient(feature_side, mixes, sums)
    grad_qkv, grad_w_out, grad_w_up, grad_w_down = sums
    return (
        block_out,
        mix_out,
        grad_history,
        mix_sum[: STREAMS * HIST].T,
        grad_qkv,
        grad_w_out,
        grad_w_up,
        grad_w_down,
        little_sum[:, :MIXH],
        second_sum[:, :MIXH],
        little_sum[:, MIXH : MIXH + STREAMS + 1].T,
    )


def solution(mesh):
    return jax.shard_map(
        body,
        mesh=mesh,
        in_specs=(
            P(None, "dp", None),
            P("dp", None),
            P("dp", None),
            P("dp", None),
            P(),
            P(None, "dp", "mp"),
            P("dp", "mp"),
            P("dp", "mp"),
            P("dp", "mp"),
            P("dp", None),
            P(),
            P(None, "dp"),
            P("dp", None),
            P("dp", None),
        ),
        out_specs=(
            P("dp", None),
            P("dp", None),
            P(None, "dp", None),
            P("dp", None),
            P(None, "dp", "mp"),
            P("dp", "mp"),
            P("dp", "mp"),
            P("dp", "mp"),
            P("dp", None),
            P(),
            P(None, "dp"),
        ),
        check_vma=False,
    )
```

```python
import functools
import math

import jax
import jax.numpy as jnp
import numpy as np
from jax import lax
from jax.experimental import pallas as pl
from jax.experimental.pallas import tpu as pltpu
from jax.sharding import PartitionSpec as P

HEAD = 128
ROT = 32
HIST = 9
STREAMS = 4
GROUPS = 8
TOK_DEV = 384
MIXH = 40
WIDE = 128
MIXED = 48
EPS = 1e-05
CUTS = (1, 1, 2, 2, 1)
MESH = pl.DeviceIdType.MESH
DMA = pltpu.SemaphoreType.DMA
f32 = jnp.float32
bf16 = jnp.bfloat16


def chip_at(pos, ring):
    far = pos // (ring // 2)
    return (1 - far) * 2 * pos + far * (2 * (ring - 1 - pos) + 1)


def place_of(chip, ring):
    odd = chip % 2
    return (1 - odd) * (chip // 2) + odd * (ring - 1 - chip // 2)


def remote(src, dst, send, recv, device):
    return pltpu.make_async_remote_copy(
        src_ref=src,
        dst_ref=dst,
        send_sem=send,
        recv_sem=recv,
        device_id=device,
        device_id_type=MESH,
    )


def greet_plane(n, me, mp):
    barrier = pltpu.get_barrier_semaphore()

    @pl.loop(1, n)
    def _(k):
        pl.semaphore_signal(barrier, inc=1, device_id={"dp": (me + k) % n}, device_id_type=MESH)

    pl.semaphore_signal(barrier, inc=1, device_id={"mp": 1 - mp}, device_id_type=MESH)
    pl.semaphore_wait(barrier, n)


def rows_of(ref, start, count):
    if len(ref.shape) == 3:
        return ref.at[:, pl.ds(start, count), :]
    return ref.at[pl.ds(start, count), :]


def cuts_of(shards, cuts):
    pieces = []
    for i, shard in enumerate(shards):
        if len(shard.shape) == 3:
            pieces += [(i, s, 0) for s in range(shard.shape[0])]
        else:
            wide = shard.shape[1] // cuts[i]
            pieces += [(i, k * wide, wide) for k in range(cuts[i])]
    return pieces


def piece_of(refs, piece, start, count):
    i, first, wide = piece
    if wide == 0:
        return refs[i].at[first, pl.ds(start, count), :]
    return refs[i].at[pl.ds(start, count), pl.ds(first, wide)]


class Ring:
    def __init__(self, n):
        self.n, self.ring = n, n // 2
        self.me = lax.axis_index("dp")
        self.core = self.me % 2
        self.place = place_of(self.me // 2, self.ring)
        self.mate = self.me + 1 - 2 * self.core
        self.next_of = ({"dp": self.owner(1)}, {"dp": self.owner(-1)})

    def owner(self, offset):
        return chip_at((self.place + offset + 2 * self.ring) % self.ring, self.ring) * 2 + self.core


def forward_kernel(n, count, *refs):
    hist, cot, mix, tables, docs_row, docs_col, groups, weights, cot_in, mix2_in = refs[:10]
    shards = refs[10 : 10 + count]
    refs = refs[10 + count :]
    inputs, mixes, normed_out, level, heads_out, attn_out, slope_out, hidden_out = refs[:8]
    direct, grad_branch, out_low, little, mix_out, second = refs[8:14]
    fulls = refs[14 : 14 + count]
    (
        hist_buf,
        slots,
        streams,
        normed,
        tiles,
        heads,
        attn,
        slope_buf,
        hidden,
        down_buf,
        out_buf,
        branch,
        branch_land,
        smalls,
        total,
        token_scale,
        cot_mix,
        w_mix2,
        hist_sem,
        cot_sem,
        own_sem,
        local_sem,
        keep_sem,
        tile_sem,
        slope_sem,
        row_sem,
        swap_send,
        swap_recv,
        mix_send,
        mix_recv,
        half_send,
        half_recv,
        a_send,
        a_recv,
        y_send,
        y_recv,
        ring_send,
        ring_recv,
        core_send,
        core_recv,
    ) = refs[14 + count :]
    where = Ring(n)
    me, ring, owner = where.me, where.ring, where.owner
    mp = lax.axis_index("mp")
    across = {"mp": 1 - mp}
    feat, tokens = hist.shape[1], mix.shape[1]
    h = feat // 2
    width = n * feat
    size = shards[0].shape[-2]
    half = size // 2
    w_qkv, w_out, w_up, w_down, all_small = fulls
    greet_plane(n, me, mp)

    pieces = cuts_of(shards, CUTS)

    def of(*arrays):
        return [p for p, piece in enumerate(pieces) if piece[0] in arrays]

    def origin_rows(offset, way):
        return pl.multiple_of(owner(offset) * size + way * half, half)

    def ring_copy(way, step, p, first=False):
        there = piece_of(fulls, pieces[p], origin_rows(-step if way == 0 else step, way), half)
        here = piece_of(shards, pieces[p], way * half, half) if first else there
        return remote(
            here, there, ring_send.at[way, step, p], ring_recv.at[way, step, p], where.next_of[way]
        )

    def ring_arrival(way, step, p):
        offset = -step - 1 if way == 0 else step + 1
        there = piece_of(fulls, pieces[p], origin_rows(offset, way), half)
        return remote(
            there, there, ring_send.at[way, step, p], ring_recv.at[way, step, p], where.next_of[way]
        )

    def core_copy(way, step, p, first=False):
        there = piece_of(fulls, pieces[p], origin_rows(-step if way == 0 else step, way), half)
        here = piece_of(shards, pieces[p], way * half, half) if first else there
        return remote(
            here, there, core_send.at[way, step, p], core_recv.at[way, step, p], {"dp": where.mate}
        )

    def shard_copy(i):
        return pltpu.make_async_copy(shards[i], rows_of(fulls[i], me * size, size), local_sem.at[i])

    def ring_begin(some):
        for p in some:
            for way in range(2):
                ring_copy(way, 0, p, True).start()

    def ring_step(step, some):
        for p in some:
            for way in range(2):
                ring_arrival(way, step - 1, p).wait_recv()
                ring_copy(way, step, p).start()
                core_copy(way, step, p).start()

    def ring_end(some):
        for p in some:
            for way in range(2):
                ring_arrival(way, ring - 2, p).wait_recv()
                core_copy(way, ring - 1, p).start()

    def ring_complete(*arrays):
        for i in arrays:
            shard_copy(i).wait()
        for p in of(*arrays):

            @pl.loop(0, ring)
            def _(step):
                for way in range(2):
                    core_copy(way, step, p).wait_recv()

    def mix_half():
        return pl.ds(pl.multiple_of(mp * (MIXED // 2), 8), MIXED // 2)

    def mix_copy(q):
        return remote(
            mix.at[mix_half()],
            mixes.at[me, mix_half()],
            mix_send.at[q],
            mix_recv.at[q],
            {"dp": (me + q) % n},
        )

    def half_copy(q):
        there = mixes.at[(me + q) % n, mix_half()]
        return remote(there, there, half_send.at[q], half_recv.at[q], across)

    def half_turn(q):
        mix_copy(n - q).wait_recv()
        half_copy(q).start()

    def lanes(peer):
        return pl.ds(pl.multiple_of(peer * tokens, 128), tokens)

    def hist_copy(q):
        peer = (me + q) % n
        return pltpu.make_async_copy(
            hist.at[:, pl.ds(pl.multiple_of(mp * h, h), h), lanes(peer)],
            hist_buf.at[q % 2],
            hist_sem.at[q % 2],
        )

    def cot_copy(q):
        peer = (me + q) % n
        return pltpu.make_async_copy(
            cot.at[pl.ds(pl.multiple_of(mp * h, h), h), lanes(peer)],
            slots.at[q, STREAMS],
            cot_sem.at[q],
        )

    def features(source, plane):
        return streams.at[:, pl.ds(pl.multiple_of(source * feat + plane * h, h), h), :]

    def stream_copy(q):
        return remote(
            slots.at[q], features(me, mp), a_send.at[q], a_recv.at[q], {"dp": (me + q) % n}
        )

    def own_copy():
        return pltpu.make_async_copy(slots.at[0], features(me, mp), own_sem)

    def across_copy(q, own=False):
        there = features((me - q + n) % n, mp)
        return remote(
            slots.at[0] if own else there, there, y_send.at[q], y_recv.at[q], across
        )

    def mix_streams(q):
        peer = (me + q) % n

        @pl.loop(0, h // 16)
        def _(r):
            rows = pl.ds(pl.multiple_of(r * 16, 16), 16)
            sums = [None] * STREAMS
            for j in range(HIST):
                entry = hist_buf[q % 2, j, rows, :].astype(f32)
                for s in range(STREAMS):
                    term = mixes[peer, pl.ds(s * HIST + j, 1), :] * entry
                    sums[s] = term if j == 0 else sums[s] + term
            for s in range(STREAMS):
                slots[q, s, rows, :] = sums[s].astype(bf16)

    def normalise():
        level[...] = jnp.zeros_like(level)
        for s in range(STREAMS):

            def add(r, total):
                part = streams[s, pl.ds(pl.multiple_of(r * 32, 32), 32), :].astype(f32)
                part = part * part
                return total + (part[0:8] + part[8:16]) + (part[16:24] + part[24:32])

            squares = lax.fori_loop(0, width // 32, add, jnp.zeros((8, tokens), f32))
            mean = jnp.sum(squares, axis=0, keepdims=True) * (1.0 / width)
            level[pl.ds(s, 1), :] = lax.rsqrt(mean + EPS)

        @pl.loop(0, width // 32)
        def _(r):
            rows = pl.ds(pl.multiple_of(r * 32, 32), 32)
            gain = smalls[rows, :].astype(f32)
            for s in range(STREAMS):
                unit = streams[s, rows, :].astype(f32) * level[pl.ds(s, 1), :]
                normed[s, rows, :] = (unit * gain[:, MIXH + s : MIXH + s + 1]).astype(bf16)

    def head_tiles(pair, spot):
        columns = pl.ds(pl.multiple_of(pair * 2 * HEAD, 2 * HEAD), 2 * HEAD)
        return [
            pltpu.make_async_copy(
                w_qkv.at[s, :, columns], tiles.at[spot * 3 + s], tile_sem.at[spot * 3 + s]
            )
            for s in range(3)
        ]

    def first_dims(left, right):
        return lax.dot_general(left, right, (((0,), (0,)), ((), ())), preferred_element_type=f32)

    def last_dims(left, right):
        return lax.dot_general(left, right, (((1,), (1,)), ((), ())), preferred_element_type=f32)

    def attend(pair):
        spot = pair % 2
        for copy in head_tiles(pair, spot):
            copy.wait()

        @pl.when(pair < heads.shape[1] // 2 - 1)
        def _():
            for copy in head_tiles(pair + 1, 1 - spot):
                copy.start()

        for s in range(3):
            both = first_dims(normed[s], tiles[spot * 3 + s])
            for u in range(2):
                one = both[:, u * HEAD : (u + 1) * HEAD]
                if s < 2:
                    one = (
                        one * tables[0]
                        + pltpu.roll(one, HEAD - ROT // 2, 1) * tables[1]
                        + pltpu.roll(one, ROT // 2, 1) * tables[2]
                    )
                heads[s, pair * 2 + u] = one.astype(bf16)
        place = lax.broadcasted_iota(jnp.int32, (tokens, tokens), 0)
        other = lax.broadcasted_iota(jnp.int32, (tokens, tokens), 1)
        allowed = (place >= other) & (docs_col[...] == docs_row[...])
        for u in range(2):
            scores = last_dims(heads[0, pair * 2 + u], heads[1, pair * 2 + u]) * HEAD ** (-0.5)
            scores = jnp.where(allowed, scores, -1000000000.0)
            weight = jnp.exp(scores - jnp.max(scores, axis=1, keepdims=True))
            probs = weight * (1.0 / jnp.sum(weight, axis=1, keepdims=True))
            value = jnp.dot(
                probs.astype(bf16), heads[2, pair * 2 + u], preferred_element_type=f32
            )
            attn[:, pl.ds(pl.multiple_of((pair * 2 + u) * HEAD, HEAD), HEAD)] = value.astype(bf16)

    chunk = 512
    ups = hidden.shape[1] // chunk

    def up_tile(c, spot):
        return [
            pltpu.make_async_copy(
                w_up.at[:, pl.ds(pl.multiple_of(c * chunk + k * 256, 256), 256)],
                tiles.at[spot * 2 + k],
                tile_sem.at[spot * 2 + k],
            )
            for k in range(2)
        ]

    def slope_copy(c):
        return pltpu.make_async_copy(
            slope_buf.at[c % 2],
            slope_out.at[:, pl.ds(pl.multiple_of(c * chunk, chunk), chunk)],
            slope_sem.at[c % 2],
        )

    def feed(c, spot):
        for copy in up_tile(c, spot):
            copy.wait()

        @pl.when(c < ups - 1)
        def _():
            for copy in up_tile(c + 1, 1 - spot):
                copy.start()

        @pl.when(c >= 2)
        def _():
            slope_copy(c - 2).wait()

        for k in range(2):
            pre = first_dims(normed[STREAMS - 1], tiles[spot * 2 + k])
            below = 0.5 + 0.5 * lax.erf(pre * math.sqrt(0.5))
            bell = jnp.exp(-0.5 * pre * pre) * (1.0 / math.sqrt(2.0 * math.pi))
            slope_buf[c % 2, :, k * 256 : (k + 1) * 256] = (below + pre * bell).astype(bf16)
            low = (pre * below).astype(bf16)
            hidden[:, pl.ds(pl.multiple_of(c * chunk + k * 256, 256), 256)] = low
        slope_copy(c).start()

    def blocks(c):
        starts = []
        for way in range(2):
            shard = owner(-c if way == 0 else c)
            for which in range(2):
                row = (shard + which * (where.mate - me)) * size + way * half
                starts.append(pl.multiple_of(row, half))
        return starts

    def row_tiles(c):
        copies = []
        for b, start in enumerate(blocks(c)):
            rows, there = pl.ds(start, half), pl.ds(b * half, half)
            copies.append(
                pltpu.make_async_copy(
                    w_down.at[rows, :], down_buf.at[c % 2, there], row_sem.at[c % 2, b]
                )
            )
            copies.append(
                pltpu.make_async_copy(
                    w_out.at[rows, :], out_buf.at[c % 2, there], row_sem.at[c % 2, 4 + b]
                )
            )
        return copies

    def rows_begin(c):
        for p in of(3):
            for way in range(2):
                core_copy(way, c, p).wait_recv()
        for copy in row_tiles(c):
            copy.start()

    def rows_product(c):
        for copy in row_tiles(c):
            copy.wait()
        part = last_dims(down_buf[c % 2], hidden[...]) + last_dims(out_buf[c % 2], attn[...])
        branch[c] = part.astype(bf16)
        swap_copy(c).start()

    def swap_copy(c):
        return remote(
            branch.at[c], branch_land.at[c], swap_send.at[c], swap_recv.at[c], across
        )

    def mixing_network(squares):
        columns = lax.broadcasted_iota(jnp.int32, (tokens, WIDE), 1)
        plain = normed.at[0]
        gain_at = slice(MIXH + STREAMS, MIXH + STREAMS + 1)
        scale = lax.rsqrt(jnp.sum(squares, axis=0, keepdims=True) * (1.0 / width) + EPS)

        @pl.loop(0, width // 64)
        def _(r):
            rows = pl.ds(pl.multiple_of(r * 64, 64), 64)
            value = total[rows, :]
            out_low[rows, :] = value.astype(bf16)
            plain[rows, :] = (value * scale * smalls[rows, :].astype(f32)[:, gain_at]).astype(bf16)

        pre = first_dims(plain[...], smalls[...])
        below = 0.5 + 0.5 * lax.erf(pre * math.sqrt(0.5))
        bell = jnp.exp(-0.5 * pre * pre) * (1.0 / math.sqrt(2.0 * math.pi))
        low = jnp.where(columns < MIXH, pre * below, 0.0).astype(bf16)
        mix_out[...] = jnp.dot(low, w_mix2[...], preferred_element_type=f32)[:, :MIXH]
        grad = last_dims(cot_mix[...], w_mix2[...])
        grad = jnp.where(columns < MIXH, (below + pre * bell) * grad, 0.0).astype(bf16)
        second[...] = first_dims(low, cot_mix[...])[:MIXH]
        product = grad.astype(f32) * pre
        high = product.astype(bf16)
        ones = jnp.ones((8, WIDE), bf16)
        inner = last_dims(ones, high) + last_dims(ones, (product - high.astype(f32)).astype(bf16))
        inner = inner[0:1] * (1.0 / width)
        step = 256

        @pl.loop(0, width // step)
        def _(r):
            rows = pl.ds(pl.multiple_of(r * step, step), step)
            first = smalls[rows, :]
            gain = first.astype(f32)[:, gain_at]
            sums = jnp.dot(plain[rows, :], grad, preferred_element_type=f32)
            lane = lax.broadcasted_iota(jnp.int32, sums.shape, 1)
            gain_grad = jnp.sum(first.astype(f32) * sums, axis=1, keepdims=True) / gain
            little[rows, :] = jnp.where(lane == MIXH + STREAMS, gain_grad, sums)
            grad_normed = last_dims(first, grad)
            seed = streams[STREAMS, rows, :].astype(f32) * token_scale[0:1, :]
            value = seed + scale * (gain * grad_normed - total[rows, :] * (scale * inner))
            direct[rows, :] = value
            grad_branch[rows, :] = value.astype(bf16)

    def keep(k):
        pairs = [
            (streams, inputs),
            (normed, normed_out),
            (heads, heads_out),
            (attn, attn_out),
            (hidden, hidden_out),
        ]
        return pltpu.make_async_copy(pairs[k][0], pairs[k][1], keep_sem.at[k])

    def stream_turn(q):
        hist_copy(q).wait()

        @pl.when(q < n - 1)
        def _():
            hist_copy(q + 1).start()

        @pl.when(q < n - 1)
        def _():
            half_turn(q + 1)

        half_copy(q).wait_recv()
        mix_streams(q)
        cot_copy(q).wait()
        stream_copy(q).start()

    def forward_turn(q):
        stream_copy(q).wait_recv()
        across_copy(q).start()

    @pl.loop(1, n)
    def _(q):
        mix_copy(q).start()

    @pl.loop(0, n)
    def _(q):
        cot_copy(q).start()

    hist_copy(0).start()
    ring_begin(of(2, 4))
    mixes[me] = mix[...]
    row = jnp.zeros((1, tokens), f32)
    for g in range(GROUPS):
        row = row + jnp.where(groups[...] == g, weights[g], 0.0)
    token_scale[...] = jnp.broadcast_to(row, token_scale.shape)
    cot_mix[...] = jnp.zeros_like(cot_mix)
    cot_mix[:, 0:MIXH] = cot_in[...]
    w_mix2[...] = jnp.zeros_like(w_mix2)
    w_mix2[0:MIXH, 0:MIXH] = mix2_in[...]
    hist_copy(0).wait()
    hist_copy(1).start()
    mix_streams(0)
    cot_copy(0).wait()
    own_copy().start()
    across_copy(0, True).start()
    half_turn(1)

    @pl.loop(1, 4)
    def _(q):
        stream_turn(q)

    for p in range(len(pieces)):
        for way in range(2):
            core_copy(way, 0, p, True).start()
    for i in range(count):
        shard_copy(i).start()
    ring_begin(of(0, 1))

    @pl.loop(1, ring - 1)
    def _(step):
        ring_step(step, of(2, 4))
        for u in range(2):
            stream_turn(2 + 2 * step + u)
        for u in range(2):
            forward_turn(2 * step - 1 + u)

    ring_end(of(2, 4))
    ring_begin(of(3))
    pairs = heads.shape[1] // 2
    last = ring - 2
    early = 1

    def streams_here():
        ring_complete(2, 4)
        gains_copy = pltpu.make_async_copy(all_small, smalls, local_sem.at[count])
        gains_copy.start()
        for copy in up_tile(0, 0):
            copy.start()
        own_copy().wait()

        @pl.loop(0, n)
        def _(q):
            across_copy(q).wait_recv()

        keep(0).start()
        gains_copy.wait()
        normalise()
        keep(1).start()

    @pl.loop(1, ring - 1)
    def _(step):
        ring_step(step, of(0, 1))

        @pl.when(step == 1)
        def _():
            @pl.loop(n - 3, n)
            def _(q):
                forward_turn(q)

        @pl.when(step > last - early)
        def _():
            ring_step(step - (last - early), of(3))

        @pl.when(step == last - ups // 2)
        def _():
            streams_here()

        @pl.when(step > last - ups // 2)
        def _():
            for u in range(2):
                feed(2 * (step - (last - ups // 2) - 1) + u, u)

    keep(4).start()
    ring_end(of(0, 1))
    ring_complete(0, 1)
    shard_copy(3).wait()
    for copy in head_tiles(0, 0):
        copy.start()

    @pl.loop(early + 1, ring - 1)
    def _(step):
        ring_step(step, of(3))

        @pl.when(step <= early + pairs // 2)
        def _():
            for u in range(2):
                attend(2 * (step - early - 1) + u)

        @pl.when(step == early + pairs // 2)
        def _():
            for c in range(2):
                rows_begin(c)

        for ahead in range(1, 3):

            @pl.when(step == early + pairs // 2 + ahead)
            def _():
                for u in range(2):
                    c = 2 * (ahead - 1) + u
                    rows_product(c)
                    rows_begin(c + 2)

    keep(2).start()
    keep(3).start()

    @pl.loop(4, ring - 3)
    def _(c):
        rows_product(c)
        rows_begin(c + 2)

    rows_product(ring - 3)
    ring_end(of(3))
    rows_begin(ring - 1)
    rows_product(ring - 2)
    rows_product(ring - 1)

    def add_up(c, squares):
        swap_copy(c).wait_recv()
        for b, start in enumerate(blocks(c)):
            both = branch[c, b * half : (b + 1) * half].astype(f32)
            both = both + branch_land[c, b * half : (b + 1) * half].astype(f32)
            rows = pl.ds(start, half)
            value = streams[STREAMS - 1, rows, :].astype(f32) + both
            total[rows, :] = value
            value = value * value
            for k in range(half // 8):
                squares = squares + value[k * 8 : (k + 1) * 8]
        return squares

    squares = lax.fori_loop(0, ring, add_up, jnp.zeros((8, tokens), f32))

    for c in range(ups - 2, ups):
        slope_copy(c).wait()
    for k in range(5):
        keep(k).wait()
    mixing_network(squares)

    @pl.loop(0, ring)
    def _(c):
        swap_copy(c).wait_send()

    @pl.loop(1, n)
    def _(q):
        mix_copy(q).wait_send()
        half_copy(q).wait_send()
        stream_copy(q).wait_send()

    @pl.loop(0, n)
    def _(q):
        across_copy(q).wait_send()

    @pl.loop(0, ring)
    def _(step):
        for p in range(len(pieces)):
            for way in range(2):
                core_copy(way, step, p).wait_send()

    @pl.loop(0, ring - 1)
    def _(step):
        for p in range(len(pieces)):
            for way in range(2):
                ring_copy(way, step, p).wait_send()


def forward_exchange(
    n, history, cot_out, mix, tables, docs, groups, weights, cot_mix, w_mix2, shards
):
    count, ring = len(shards), n // 2
    feat, tokens = history.shape[1], mix.shape[1]
    h, width = feat // 2, n * feat
    hbm = pl.BlockSpec(memory_space=pl.ANY)
    vmem = pl.BlockSpec(memory_space=pltpu.VMEM)
    smem = pl.BlockSpec(memory_space=pltpu.SMEM)
    columns, units = shards[0].shape[2], shards[2].shape[1]
    across = columns // HEAD
    deep = 2 * shards[0].shape[1]
    travel = len(cuts_of(shards, CUTS))
    found = pl.pallas_call(
        functools.partial(forward_kernel, n, count),
        out_shape=[
            jax.ShapeDtypeStruct((STREAMS + 1, width, tokens), bf16),
            jax.ShapeDtypeStruct((n,) + mix.shape, f32),
            jax.ShapeDtypeStruct((STREAMS, width, tokens), bf16),
            jax.ShapeDtypeStruct((8, tokens), f32),
            jax.ShapeDtypeStruct((3, across, tokens, HEAD), bf16),
            jax.ShapeDtypeStruct((tokens, columns), bf16),
            jax.ShapeDtypeStruct((tokens, units), bf16),
            jax.ShapeDtypeStruct((tokens, units), bf16),
            jax.ShapeDtypeStruct((width, tokens), f32),
            jax.ShapeDtypeStruct((width, tokens), bf16),
            jax.ShapeDtypeStruct((width, tokens), bf16),
            jax.ShapeDtypeStruct((width, WIDE), f32),
            jax.ShapeDtypeStruct((tokens, MIXH), f32),
            jax.ShapeDtypeStruct((MIXH, WIDE), f32),
        ]
        + [
            jax.ShapeDtypeStruct(s.shape[:-2] + (s.shape[-2] * n, s.shape[-1]), s.dtype)
            for s in shards
        ],
        in_specs=[hbm, hbm] + [vmem] * 5 + [smem] + [vmem] * 2 + [hbm] * count,
        out_specs=[hbm, vmem, hbm, vmem, hbm, hbm, hbm, hbm] + [vmem] * 6 + [hbm] * count,
        scratch_shapes=[
            pltpu.VMEM((2, HIST, h, tokens), bf16),
            pltpu.VMEM((n, STREAMS + 1, h, tokens), bf16),
            pltpu.VMEM((STREAMS + 1, width, tokens), bf16),
            pltpu.VMEM((STREAMS, width, tokens), bf16),
            pltpu.VMEM((6, width, 2 * HEAD), bf16),
            pltpu.VMEM((3, across, tokens, HEAD), bf16),
            pltpu.VMEM((tokens, columns), bf16),
            pltpu.VMEM((2, tokens, 512), bf16),
            pltpu.VMEM((tokens, units), bf16),
            pltpu.VMEM((2, deep, units), bf16),
            pltpu.VMEM((2, deep, columns), bf16),
            pltpu.VMEM((ring, deep, tokens), bf16),
            pltpu.VMEM((ring, deep, tokens), bf16),
            pltpu.VMEM((width, WIDE), bf16),
            pltpu.VMEM((width, tokens), f32),
            pltpu.VMEM((8, tokens), f32),
            pltpu.VMEM((tokens, WIDE), bf16),
            pltpu.VMEM((WIDE, WIDE), bf16),
            DMA((2,)),
            DMA((n,)),
            DMA,
            DMA((count + 1,)),
            DMA((5,)),
            DMA((6,)),
            DMA((2,)),
            DMA((2, 8)),
            DMA((ring,)),
            DMA((ring,)),
        ]
        + [DMA((n,)) for _ in range(8)]
        + [DMA((2, ring - 1, travel)) for _ in range(2)]
        + [DMA((2, ring, travel)) for _ in range(2)],
        compiler_params=pltpu.CompilerParams(
            collective_id=0, has_side_effects=True, vmem_limit_bytes=60 * 1024 * 1024
        ),
    )(history, cot_out, mix, tables, docs, docs.T, groups, weights, cot_mix, w_mix2, *shards)
    return found[:14], found[14:]


def backward_kernel(n, count, *refs):
    (
        normed,
        grad_branch,
        hidden,
        attn,
        slope,
        heads,
        w_qkv,
        w_out,
        w_up,
        w_down,
        tables,
        docs_row,
        docs_col,
        level,
        inputs,
        direct,
        output,
        smalls,
        little,
        second,
        hist,
        mixes,
    ) = refs[:22]
    across_land, feature_side, mix_sum, little_sum, second_sum = refs[22:27]
    sums, mates = refs[27 : 27 + count], refs[27 + count : 27 + 2 * count]
    refs = refs[27 + 2 * count :]
    slots, other, mine, final = (refs[k * count : (k + 1) * count] for k in range(4))
    (
        rows_buf,
        branch_buf,
        grad_up,
        grad_attended,
        projs,
        grads,
        qkv_tile,
        up_tile,
        n_tile,
        inner,
        inner_land,
        e_buf,
        x_buf,
        go_buf,
        g_buf,
        l_buf,
        g_slots,
        l_slots,
        l_land,
        second_land,
        second_own,
        f_buf,
        h_buf,
        m_wide,
        m_slots,
        m_land,
        m_mine,
        m_other,
        l_sum,
        rows_sem,
        branch_sem,
        back_tile,
        tile_sem,
        load_sem,
        back_sem,
        other_sem,
        final_sem,
        y_send,
        y_recv,
        p_sem,
        o_send,
        o_recv,
        a_send,
        a_recv,
        l_send,
        l_recv,
        w_send,
        w_recv,
        fy_send,
        fy_recv,
        m_send,
        m_recv,
        end_sem,
        ring_send,
        ring_recv,
        core_send,
        core_recv,
    ) = refs[4 * count :]
    where = Ring(n)
    me, ring, owner = where.me, where.ring, where.owner
    mp = lax.axis_index("mp")
    across = {"mp": 1 - mp}
    feat, tokens = hist.shape[1], level.shape[1]
    h = feat // 2
    width = n * feat
    size = sums[0].shape[-2]
    half = size // 2
    greet_plane(n, me, mp)

    def first_dims(left, right):
        return lax.dot_general(left, right, (((0,), (0,)), ((), ())), preferred_element_type=f32)

    def last_dims(left, right):
        return lax.dot_general(left, right, (((1,), (1,)), ((), ())), preferred_element_type=f32)

    def target(way, step):
        return -1 - step if way == 0 else 1 + step

    def rows_load(way, step, branch):
        spot = step % 3
        copies = []
        for which in range(2):
            shard = owner(target(way, step)) + which * (where.mate - me)
            rows = pl.ds(pl.multiple_of(shard * size + way * half, half), half)
            if branch:
                here, there, sem = grad_branch.at[rows, :], branch_buf, branch_sem
            else:
                here, there, sem = normed.at[:, rows, :], rows_buf, rows_sem
            copies.append(
                pltpu.make_async_copy(here, there.at[way, spot, which], sem.at[way, spot, which])
            )
        return copies

    def rows_begin(step, branch):
        for way in range(2):
            for copy in rows_load(way, step, branch):
                copy.start()

    def rows_wait(step, branch):
        for way in range(2):
            for copy in rows_load(way, step, branch):
                copy.wait()

    def part(way, step, i, which, k, columns):
        if i in (1, 3):
            left = branch_buf[way, step % 3, which]
        else:
            left = rows_buf[way, step % 3, which, k if i == 0 else STREAMS - 1]
        right = (projs, attn, grad_up, hidden)[i]
        right = right[k, :, columns] if i == 0 else right[:, columns]
        return jnp.dot(left, right, preferred_element_type=f32)

    strip = 1024

    def strips(i, work):
        deep = len(sums[i].shape) == 3
        for k in range(sums[i].shape[0] if deep else 1):

            @pl.loop(0, sums[i].shape[-1] // strip)
            def _(c):
                columns = pl.ds(pl.multiple_of(c * strip, strip), strip)
                at = (k, slice(None), columns) if deep else (slice(None), columns)
                work(k, columns, at)

    def core_copy(way, step, i):
        return remote(
            mine[i].at[way],
            mates[i].at[way, step],
            core_send.at[way, step, i],
            core_recv.at[way, step, i],
            {"dp": where.mate},
        )

    def other_copy(way, step, i):
        return pltpu.make_async_copy(
            mates[i].at[way, step], other[i].at[way], other_sem.at[way, i]
        )

    def ring_copy(way, step, i):
        return remote(
            slots[i].at[way, step % 4],
            slots[i].at[way, (step + 1) % 4],
            ring_send.at[way, step, i],
            ring_recv.at[way, step, i],
            where.next_of[way],
        )

    def final_copy(way, i):
        return pltpu.make_async_copy(
            final[i], rows_of(sums[i], way * half, half), final_sem.at[i]
        )

    def give(way, step, i):
        def work(k, columns, at):
            mine[i][(way,) + at] = part(way, step, i, 1, k, columns).astype(bf16)

        strips(i, work)
        core_copy(way, step, i).start()

    def stage(way, step, i):
        core_copy(way, step, i).wait_recv()
        other_copy(way, step, i).start()

    def add(way, step, i, first=False, last=False):
        def work(k, columns, at):
            total = part(way, step, i, 0, k, columns) + other[i][(way,) + at].astype(f32)
            place = (way, step % 4) + at
            if not first:
                total = total + slots[i][place].astype(f32)
            if last:
                final[i][at] = total
            else:
                slots[i][place] = total.astype(bf16)

        strips(i, work)

    def ring_unit(step, i, way):
        other_copy(way, step, i).wait()
        ring_copy(way, step - 1, i).wait_recv()
        add(way, step, i)
        ring_copy(way, step, i).start()
        core_copy(way, step, i).wait_send()
        give(way, step + 1, i)

    broad = tokens

    def back_loads(c, wide, source, sloped):
        columns = pl.ds(pl.multiple_of(c * broad, 128), wide)
        spot = c % 2
        copies = [
            pltpu.make_async_copy(
                source.at[:, columns], grads.at[1 + spot, :, pl.ds(0, wide)], back_tile.at[spot, 0]
            )
        ]
        if sloped:
            copies.append(
                pltpu.make_async_copy(
                    slope.at[:, columns],
                    grads.at[3, pl.ds(pl.multiple_of(spot * tokens, 128), tokens), pl.ds(0, wide)],
                    back_tile.at[spot, 1],
                )
            )
        return copies

    def back_turn(c, wide, source, sloped):
        columns = pl.ds(pl.multiple_of(c * broad, 128), wide)
        spot = c % 2
        for copy in back_loads(c, wide, source, sloped):
            copy.wait()
        value = first_dims(grads[0], grads[1 + spot, :, 0:wide])
        if sloped:
            rows = pl.ds(pl.multiple_of(spot * tokens, 128), tokens)
            value = value * grads[3, rows, 0:wide].astype(f32)
            grad_up[:, columns] = value.astype(bf16)
        else:
            grad_attended[:, columns] = value.astype(bf16)

    def back_all(source, units, sloped):
        full, rest = units // broad, units % broad
        for copy in back_loads(0, broad, source, sloped):
            copy.start()

        @pl.loop(0, full - 1)
        def _(c):
            for copy in back_loads(c + 1, broad, source, sloped):
                copy.start()
            back_turn(c, broad, source, sloped)

        if rest:
            for copy in back_loads(full, rest, source, sloped):
                copy.start()
        back_turn(full - 1, broad, source, sloped)
        if rest:
            back_turn(full, rest, source, sloped)

    def attend_back(head):
        lane = pl.ds(pl.multiple_of(head * HEAD, HEAD), HEAD)
        query, key, value = heads[0, head], heads[1, head], heads[2, head]
        grad = grad_attended[:, lane]
        place = lax.broadcasted_iota(jnp.int32, (tokens, tokens), 0)
        behind = lax.broadcasted_iota(jnp.int32, (tokens, tokens), 1)
        allowed = (place >= behind) & (docs_col[...] == docs_row[...])
        scores = jnp.where(allowed, last_dims(query, key) * HEAD ** (-0.5), -1000000000.0)
        weight = jnp.exp(scores - jnp.max(scores, axis=1, keepdims=True))
        probs = weight * (1.0 / jnp.sum(weight, axis=1, keepdims=True))
        grad_probs = last_dims(grad, value)
        inside = jnp.sum(probs * grad_probs, axis=1, keepdims=True)
        grad_scores = (probs * (grad_probs - inside)).astype(bf16)
        grad_value = first_dims(probs.astype(bf16), grad)
        grad_query = jnp.dot(grad_scores, key, preferred_element_type=f32) * HEAD ** (-0.5)
        grad_key = first_dims(grad_scores, query) * HEAD ** (-0.5)

        def turn_back(one):
            return (
                one * tables[0]
                - pltpu.roll(one, HEAD - ROT // 2, 1) * tables[1]
                - pltpu.roll(one, ROT // 2, 1) * tables[2]
            )

        projs[0, :, lane] = turn_back(grad_query).astype(bf16)
        projs[1, :, lane] = turn_back(grad_key).astype(bf16)
        projs[2, :, lane] = grad_value.astype(bf16)

    tall = n_tile.shape[2]
    tiles = width // tall
    per = tall // feat

    def tile_loads(t):
        rows = pl.ds(pl.multiple_of(((me // per + t) % tiles) * tall, tall), tall)
        spot = t % 2
        return [
            pltpu.make_async_copy(w_qkv.at[:, rows, :], qkv_tile.at[spot], tile_sem.at[spot, 0]),
            pltpu.make_async_copy(w_up.at[rows, :], up_tile.at[spot], tile_sem.at[spot, 1]),
            pltpu.make_async_copy(normed.at[:, rows, :], n_tile.at[spot], tile_sem.at[spot, 2]),
        ]

    def tile_turn(t):
        spot = t % 2
        for copy in tile_loads(t):
            copy.wait()

        @pl.when(t < tiles - 1)
        def _():
            for copy in tile_loads(t + 1):
                copy.start()

        base = ((me // per + t) % tiles) * per
        rows = pl.ds(pl.multiple_of(base * feat, tall), tall)
        for s in range(STREAMS):
            if s < 3:
                grad = last_dims(qkv_tile[spot, s], projs[s])
            else:
                grad = last_dims(up_tile[spot], grad_up[...])
            grads[s, rows, :] = grad.astype(bf16)
            products = jnp.sum(n_tile[spot, s].astype(f32) * grad, axis=0, keepdims=True)
            inner[pl.ds(s, 1), :] = inner[pl.ds(s, 1), :] + products
        for e in range(per):
            sum_copy((base + e - me + n) % n).start()

    def span(peer, plane):
        return pl.ds(pl.multiple_of(peer * feat + plane * h, h), h)

    def sum_copy(q):
        peer = (me + q) % n
        return remote(
            grads.at[:, span(peer, 1 - mp), :],
            across_land.at[q],
            y_send.at[q],
            y_recv.at[q],
            across,
        )

    def inner_copy():
        return remote(inner, inner_land, p_sem.at[0], p_sem.at[1], across)

    def loads(q):
        rows = span((me + q) % n, mp)
        spot = q % 2
        return [
            pltpu.make_async_copy(across_land.at[q], e_buf.at[spot], load_sem.at[spot, 0]),
            pltpu.make_async_copy(
                inputs.at[pl.ds(0, STREAMS), rows, :], x_buf.at[spot], load_sem.at[spot, 1]
            ),
            pltpu.make_async_copy(direct.at[rows, :], go_buf.at[spot], load_sem.at[spot, 2]),
            pltpu.make_async_copy(smalls.at[rows, :], g_buf.at[spot], load_sem.at[spot, 3]),
            pltpu.make_async_copy(little.at[rows, :], l_buf.at[spot], load_sem.at[spot, 4]),
        ]

    def place_of_source(source, plane):
        return feature_side.at[source, :, pl.ds(pl.multiple_of(plane * h, h), h), :]

    def grads_of_source(source, plane):
        rows = pl.ds(pl.multiple_of(plane * h, h), h)
        return feature_side.at[source, pl.ds(0, STREAMS), rows, :]

    def output_of_source(source, plane):
        return feature_side.at[source, STREAMS, pl.ds(pl.multiple_of(plane * h, h), h), :]

    def out_copy(q):
        peer = (me + q) % n
        return remote(
            output.at[span(peer, mp), :],
            output_of_source(me, mp),
            o_send.at[q],
            o_recv.at[q],
            {"dp": peer},
        )

    def stream_copy(q):
        return remote(
            g_slots.at[q], grads_of_source(me, mp), a_send.at[q], a_recv.at[q], {"dp": (me + q) % n}
        )

    def little_copy(q):
        return remote(
            l_slots.at[q], l_land.at[q], l_send.at[q], l_recv.at[q], {"dp": (me + q) % n}
        )

    bits = second_land.shape[0]

    def second_copy(b):
        bit = (me // 2**b) % 2
        return remote(
            second_own,
            second_land.at[b],
            w_send.at[b],
            w_recv.at[b],
            {"dp": me + 2**b * (1 - 2 * bit)},
        )

    def second_turn(b):
        second_copy(b).wait()
        second_own[...] = second_own[...] + second_land[b]

    def home_copy():
        return pltpu.make_async_copy(g_slots.at[0], grads_of_source(me, mp), end_sem.at[0])

    def home_output():
        return pltpu.make_async_copy(
            output.at[span(me, mp), :], output_of_source(me, mp), end_sem.at[6]
        )

    def across_copy(q):
        there = place_of_source((me - q + n) % n, mp)
        return remote(there, there, fy_send.at[q], fy_recv.at[q], across)

    def start_loads(q):
        sum_copy(q).wait_recv()
        for copy in loads(q):
            copy.start()

    def norm_backward(q):
        spot = q % 2
        peer = (me + q) % n
        for copy in loads(q):
            copy.wait()

        @pl.loop(0, h // 16)
        def _(r):
            rows = pl.ds(pl.multiple_of(r * 16, 16), 16)
            full = pl.ds(pl.multiple_of(peer * feat + mp * h + r * 16, 16), 16)
            tail = l_buf[spot, rows, :]
            lane = lax.broadcasted_iota(jnp.int32, tail.shape, 1)
            for s in range(STREAMS):
                dy = grads[s, full, :].astype(f32) + e_buf[spot, s, rows, :].astype(f32)
                scale = level[pl.ds(s, 1), :]
                common = (inner[pl.ds(s, 1), :] + inner_land[pl.ds(s, 1), :]) * scale
                common = common * (1.0 / width)
                unit = x_buf[spot, s, rows, :].astype(f32) * scale
                gain = g_buf[spot, rows, :].astype(f32)[:, MIXH + s : MIXH + s + 1]
                grad = scale * (gain * dy) - unit * common
                if s == STREAMS - 1:
                    grad = grad + go_buf[spot, rows, :]
                g_slots[q, s, rows, :] = grad.astype(bf16)
                gain_grad = jnp.sum(unit * dy, axis=1, keepdims=True)
                tail = jnp.where(lane == MIXH + s, gain_grad, tail)
            l_slots[q, rows, :] = tail.astype(bf16)

    def norm_turn(q):
        @pl.when(q < n - 1)
        def _():
            start_loads(q + 1)

        norm_backward(q)

        @pl.when(q == 0)
        def _():
            home_copy().start()

        @pl.when(q > 0)
        def _():
            stream_copy(q).start()
            little_copy(q).start()

    def hist_load(q):
        source = (me - q + n) % n
        return pltpu.make_async_copy(
            hist.at[
                :,
                pl.ds(pl.multiple_of(mp * h, h), h),
                pl.ds(pl.multiple_of(source * tokens, 128), tokens),
            ],
            h_buf.at[q % 2],
            back_sem.at[q % 2, 0],
        )

    def grad_load(q):
        source = (me - q + n) % n
        return pltpu.make_async_copy(
            feature_side.at[source, pl.ds(0, STREAMS), pl.ds(pl.multiple_of(mp * h, h), h), :],
            f_buf.at[q % 2],
            back_sem.at[q % 2, 1],
        )

    def mix_copy(q):
        return remote(
            m_slots.at[q], m_land.at[q], m_send.at[q], m_recv.at[q], {"dp": (me - q + n) % n}
        )

    def mix_backward(q):
        for s in range(STREAMS):
            totals = [None] * HIST
            for r in range(h // 16):
                grad = f_buf[q % 2, s, r * 16 : r * 16 + 16, :].astype(f32)
                for j in range(HIST):
                    both = h_buf[q % 2, j, r * 16 : r * 16 + 16, :].astype(f32) * grad
                    both = both[0:8] + both[8:16]
                    totals[j] = both if r == 0 else totals[j] + both
            for j in range(HIST):
                m_wide[pl.ds(s * HIST + j, 1), :] = jnp.sum(totals[j], axis=0, keepdims=True)
        m_slots[q] = m_wide[...].astype(bf16)

    def arrive(q):
        @pl.when(q == 0)
        def _():
            home_copy().wait()
            home_output().wait()

        @pl.when(q > 0)
        def _():
            stream_copy(q).wait_recv()
            out_copy(q).wait_recv()

        across_copy(q).start()
        grad_load(q).start()
        hist_load(q).start()

    def mix_turn(q):
        @pl.when(q == 0)
        def _():
            arrive(q)

        @pl.when(q < n - 1)
        def _():
            arrive(q + 1)

        grad_load(q).wait()
        hist_load(q).wait()
        mix_backward(q)

        @pl.when(q > 0)
        def _():
            mix_copy(q).start()

    ahead = [(i, way) for i in (3, 1) for way in range(2)]
    middle = [(2, way) for way in range(2)]
    late = [(0, way) for way in range(2)]
    lead = 3

    def unit(step, i, way):
        if way == 0:
            for w in range(2):
                ring_copy(w, step - 1, i).wait_send()
        ring_unit(step, i, way)

    def first_blocks(some):
        for i, way in some:
            give(way, 0, i)
        for i, way in some:
            stage(way, 0, i)
            other_copy(way, 0, i).wait()
            add(way, 0, i, first=True)
            ring_copy(way, 0, i).start()
        for i, way in some:
            core_copy(way, 0, i).wait_send()
            give(way, 1, i)
        for i, way in some:
            stage(way, 1, i)

    def ahead_units(step):
        for i, way in ahead:
            unit(step, i, way)
        for i, way in ahead:
            stage(way, step + 1, i)

    def finish(i, way):
        other_copy(way, ring - 1, i).wait()
        ring_copy(way, ring - 2, i).wait_recv()
        if way == 1:
            final_copy(0, i).wait()
        add(way, ring - 1, i, last=True)
        final_copy(way, i).start()

    branch_copy = pltpu.make_async_copy(grad_branch, grads.at[0], end_sem.at[7])
    for step in range(2):
        rows_begin(step, True)
    branch_copy.start()
    for step in range(3):
        rows_begin(step, False)
    rows_begin(2, True)
    home_output().start()

    @pl.loop(1, n)
    def _(q):
        out_copy(q).start()

    second_own[...] = second[...]
    for copy in tile_loads(0):
        copy.start()
    inner[...] = jnp.zeros_like(inner)
    m_wide[...] = jnp.zeros_like(m_wide)
    for way in range(2):
        slots[0][way, 0] = jnp.zeros_like(slots[0][way, 0])
    rows_wait(0, True)
    rows_wait(1, True)
    first_blocks(ahead[:2])
    first_blocks(ahead[2:])
    branch_copy.wait()
    back_all(w_down, grad_up.shape[1], True)
    rows_wait(2, True)
    ahead_units(1)
    rows_begin(3, True)
    rows_wait(0, False)
    rows_wait(1, False)
    first_blocks(middle)
    rows_wait(3, True)
    ahead_units(2)
    rows_begin(4, True)
    back_all(w_out, grad_attended.shape[1], False)
    heads_here = heads.shape[1]

    @pl.loop(0, heads_here // 2)
    def _(head):
        attend_back(head)

    rows_wait(4, True)
    ahead_units(3)
    rows_begin(5, True)

    @pl.loop(heads_here // 2, heads_here)
    def _(head):
        attend_back(head)

    for i, way in late:
        give(way, 0, i)
    for i, way in late:
        stage(way, 0, i)

    opening = 2
    order = ahead + middle + late

    @pl.loop(1, ring - 1)
    def _(step):
        rows_wait(step + 1, False)

        @pl.when(step + lead <= ring - 2)
        def _():
            rows_wait(step + lead + 1, True)

        for b in range(bits):

            @pl.when(step == b + 1)
            def _():
                if b > 0:
                    second_turn(b - 1)
                second_copy(b).start()

        @pl.when(step == opening)
        def _():
            inner_copy().start()
            start_loads(0)
            inner_copy().wait()

        for u, (i, way) in enumerate(order):
            if i == 0:

                @pl.when(step > 1)
                def _():
                    if way == 0:
                        for w in range(2):
                            ring_copy(w, step - 2, i).wait_send()

                other_copy(way, step - 1, i).wait()

                @pl.when(step > 1)
                def _():
                    ring_copy(way, step - 2, i).wait_recv()

                add(way, step - 1, i)
                ring_copy(way, step - 1, i).start()
                core_copy(way, step - 1, i).wait_send()
                give(way, step, i)
            elif i == 2:
                unit(step, i, way)
            else:

                @pl.when(step + lead <= ring - 2)
                def _():
                    unit(step + lead, i, way)

                @pl.when(step == ring - 1 - lead)
                def _():
                    finish(i, way)

            if u % 2 == 0:

                @pl.when((step >= opening) & (step < opening + n // 4))
                def _():
                    norm_turn(4 * (step - opening) + u // 2)
            else:

                @pl.when((step > opening) & (step <= opening + n // 4))
                def _():
                    mix_turn(4 * (step - opening - 1) + u // 2)

            @pl.when(step == 1)
            def _():
                tile_turn(u)

            if u > 0:
                before, w = order[u - 1]
                if before in (1, 3):

                    @pl.when(step + lead <= ring - 2)
                    def _():
                        stage(w, step + lead + 1, before)
                else:
                    stage(w, step if before == 0 else step + 1, before)
        stage(1, step, 0)

        @pl.when(step < ring - 2)
        def _():
            rows_begin(step + 2, False)

        @pl.when(step + lead < ring - 2)
        def _():
            rows_begin(step + lead + 2, True)

    @pl.loop(1, n)
    def _(q):
        little_copy(q).wait_recv()
        mix_copy(q).wait_recv()

    def sum_over(land, own):
        return lax.fori_loop(
            1, n, lambda q, total: total + land[q].astype(f32), own.astype(f32)
        )

    l_sum[...] = sum_over(l_land, l_slots[0])
    m_mine[...] = sum_over(m_land, m_slots[0])
    second_turn(bits - 1)
    second_sum[...] = second_own[...]
    here = pl.ds(pl.multiple_of(mp * h, h), h)
    little_home = pltpu.make_async_copy(l_sum, little_sum.at[here], end_sem.at[1])
    little_across = remote(l_sum, little_sum.at[here], end_sem.at[2], end_sem.at[3], across)
    mix_across = remote(m_mine, m_other, end_sem.at[4], end_sem.at[5], across)
    little_home.start()
    little_across.start()
    mix_across.start()

    for i, way in late:
        unit(ring - 2, i, way)
    for i, way in late:
        stage(way, ring - 1, i)
    for i, way in middle + late:
        finish(i, way)

    mix_across.wait()
    mix_sum[...] = m_mine[...] + m_other[...]
    little_home.wait()
    little_across.wait()
    for i in range(count):
        final_copy(1, i).wait()

    @pl.loop(1, n)
    def _(q):
        stream_copy(q).wait_send()
        out_copy(q).wait_send()
        little_copy(q).wait_send()
        mix_copy(q).wait_send()

    @pl.loop(0, n)
    def _(q):
        sum_copy(q).wait_send()
        across_copy(q).wait()

    for i, way in order:
        ring_copy(way, ring - 2, i).wait_send()
        core_copy(way, ring - 1, i).wait_send()


def backward_exchange(
    n,
    normed,
    grad_branch,
    hidden,
    attn,
    slope,
    heads,
    w_qkv,
    w_out,
    w_up,
    w_down,
    tables,
    docs,
    level,
    inputs,
    direct,
    output,
    smalls,
    little,
    second,
    history,
    mixes,
    shards,
):
    count, ring = len(shards), n // 2
    feat, tokens = history.shape[1], level.shape[1]
    h, width = feat // 2, n * feat
    units = slope.shape[1]
    hbm = pl.BlockSpec(memory_space=pl.ANY)
    vmem = pl.BlockSpec(memory_space=pltpu.VMEM)

    def cut(s, rows):
        return s.shape[:-2] + (rows, s.shape[-1])

    half = shards[0].shape[-2] // 2
    tall = 256
    columns = attn.shape[1]
    places = [hbm, hbm, vmem, vmem, hbm, vmem, hbm, hbm, hbm, hbm, vmem, vmem, vmem, vmem]
    places += [hbm, hbm, hbm, hbm, hbm, vmem, hbm, hbm]
    found = pl.pallas_call(
        functools.partial(backward_kernel, n, count),
        out_shape=[
            jax.ShapeDtypeStruct((n, STREAMS, h, tokens), bf16),
            jax.ShapeDtypeStruct((n, STREAMS + 1, feat, tokens), bf16),
            jax.ShapeDtypeStruct((MIXED, tokens), f32),
            jax.ShapeDtypeStruct((feat, WIDE), f32),
            jax.ShapeDtypeStruct(second.shape, f32),
        ]
        + [jax.ShapeDtypeStruct(s.shape, f32) for s in shards]
        + [jax.ShapeDtypeStruct((2, ring) + cut(s, half), bf16) for s in shards],
        in_specs=places,
        out_specs=[hbm, hbm, vmem, hbm, vmem] + [hbm] * (2 * count),
        scratch_shapes=[pltpu.VMEM((2, 4) + cut(s, half), bf16) for s in shards]
        + [pltpu.VMEM((2,) + cut(s, half), bf16) for s in shards]
        + [pltpu.VMEM((2,) + cut(s, half), bf16) for s in shards]
        + [pltpu.VMEM(cut(s, half), f32) for s in shards]
        + [
            pltpu.VMEM((2, 3, 2, STREAMS, half, tokens), bf16),
            pltpu.VMEM((2, 3, 2, half, tokens), bf16),
            pltpu.VMEM((tokens, units), bf16),
            pltpu.VMEM((tokens, columns), bf16),
            pltpu.VMEM((3, tokens, columns), bf16),
            pltpu.VMEM((STREAMS, width, tokens), bf16),
            pltpu.VMEM((2, 3, tall, columns), bf16),
            pltpu.VMEM((2, tall, units), bf16),
            pltpu.VMEM((2, STREAMS, tall, tokens), bf16),
            pltpu.VMEM((8, tokens), f32),
            pltpu.VMEM((8, tokens), f32),
            pltpu.VMEM((2, STREAMS, h, tokens), bf16),
            pltpu.VMEM((2, STREAMS, h, tokens), bf16),
            pltpu.VMEM((2, h, tokens), f32),
            pltpu.VMEM((2, h, WIDE), bf16),
            pltpu.VMEM((2, h, WIDE), f32),
            pltpu.VMEM((n, STREAMS, h, tokens), bf16),
            pltpu.VMEM((n, h, WIDE), bf16),
            pltpu.VMEM((n, h, WIDE), bf16),
            pltpu.VMEM((n.bit_length() - 1,) + second.shape, f32),
            pltpu.VMEM(second.shape, f32),
            pltpu.VMEM((2, STREAMS, h, tokens), bf16),
            pltpu.VMEM((2, HIST, h, tokens), bf16),
            pltpu.VMEM((MIXED, tokens), f32),
            pltpu.VMEM((n, MIXED, tokens), bf16),
            pltpu.VMEM((n, MIXED, tokens), bf16),
            pltpu.VMEM((MIXED, tokens), f32),
            pltpu.VMEM((MIXED, tokens), f32),
            pltpu.VMEM((h, WIDE), f32),
            DMA((2, 3, 2)),
            DMA((2, 3, 2)),
            DMA((2, 2)),
            DMA((2, 3)),
            DMA((2, 5)),
            DMA((2, 2)),
            DMA((2, count)),
            DMA((count,)),
            DMA((n,)),
            DMA((n,)),
            DMA((2,)),
        ]
        + [DMA((n,)) for _ in range(12)]
        + [DMA((8,))]
        + [DMA((2, ring - 1, count)) for _ in range(2)]
        + [DMA((2, ring, count)) for _ in range(2)],
        compiler_params=pltpu.CompilerParams(
            collective_id=1, has_side_effects=True, vmem_limit_bytes=62 * 1024 * 1024
        ),
    )(
        normed,
        grad_branch,
        hidden,
        attn,
        slope,
        heads,
        w_qkv,
        w_out,
        w_up,
        w_down,
        tables,
        docs,
        docs.T,
        level,
        inputs,
        direct,
        output,
        smalls,
        little,
        second,
        history,
        mixes,
    )
    return found[1], found[2], found[3], found[4], found[5 : 5 + count]


def history_kernel(count, *refs):
    grads, mixes = refs[:2]
    sums = refs[2 : 2 + count]
    grad_history, block_out = refs[2 + count : 4 + count]
    outs, kept = refs[4 + count : 4 + 2 * count], refs[4 + 2 * count : 4 + 3 * count]
    sems = refs[4 + 3 * count]
    feat = grads.shape[2]
    came = [pltpu.make_async_copy(sums[i], kept[i], sems.at[0, i]) for i in range(count)]
    left = [pltpu.make_async_copy(kept[i], outs[i], sems.at[1, i]) for i in range(count)]

    @pl.when(pl.program_id(0) == 0)
    def _():
        for copy in came:
            copy.start()

    @pl.when(pl.program_id(0) == pl.num_programs(0) // 2)
    def _():
        for copy in came:
            copy.wait()
        for copy in left:
            copy.start()

    tokens = grads.shape[3]
    for i in range(grads.shape[0]):
        lanes = pl.ds(i * tokens, tokens)

        @pl.loop(0, feat // 32)
        def _(r):
            rows = pl.ds(pl.multiple_of(r * 32, 32), 32)
            each = [grads[i, s, rows, :].astype(f32) for s in range(STREAMS)]
            for j in range(HIST):
                total = mixes[i, pl.ds(j, 1), :] * each[0]
                for s in range(1, STREAMS):
                    total = total + mixes[i, pl.ds(s * HIST + j, 1), :] * each[s]
                grad_history[j, rows, lanes] = total.astype(bf16)

        block_out[:, lanes] = grads[i, STREAMS]

    @pl.when(pl.program_id(0) == pl.num_programs(0) - 1)
    def _():
        for copy in left:
            copy.wait()


def history_gradient(feature_side, mixes, sums):
    n, streams, feat, tokens = feature_side.shape
    count, group = len(sums), 4
    hbm = pl.BlockSpec(memory_space=pl.ANY)
    found = pl.pallas_call(
        functools.partial(history_kernel, count),
        grid=(n // group,),
        out_shape=[
            jax.ShapeDtypeStruct((HIST, feat, n * tokens), bf16),
            jax.ShapeDtypeStruct((feat, n * tokens), bf16),
        ]
        + [jax.ShapeDtypeStruct(s.shape, s.dtype) for s in sums],
        in_specs=[
            pl.BlockSpec((group, streams, feat, tokens), lambda i: (i, 0, 0, 0)),
            pl.BlockSpec((group,) + mixes.shape[1:], lambda i: (i, 0, 0)),
        ]
        + [hbm] * count,
        out_specs=[
            pl.BlockSpec((HIST, feat, group * tokens), lambda i: (0, 0, i)),
            pl.BlockSpec((feat, group * tokens), lambda i: (0, i)),
        ]
        + [hbm] * count,
        scratch_shapes=[pltpu.VMEM(s.shape, s.dtype) for s in sums] + [DMA((2, count))],
        compiler_params=pltpu.CompilerParams(vmem_limit_bytes=62 * 1024 * 1024),
    )(feature_side, mixes, *sums)
    return found[0], found[1], found[2:]


def angle_tables(length):
    halfway = ROT // 2
    frequency = np.exp(np.arange(halfway) * (-2.0 * math.log(10000.0) / ROT))
    angles = (np.arange(length) % TOK_DEV)[:, None] * frequency[None, :]
    tables = np.zeros((3, length, HEAD), np.float32)
    tables[0] = 1.0
    tables[0, :, :halfway] = tables[0, :, halfway:ROT] = np.cos(angles)
    tables[1, :, :halfway] = -np.sin(angles)
    tables[2, :, halfway:ROT] = np.sin(angles)
    return jnp.asarray(tables)


def body(
    history,
    mix_in,
    doc_ids,
    group_ids,
    group_scale,
    w_qkv,
    w_out,
    w_up,
    w_down,
    w_mix1,
    w_mix2,
    gains,
    cot_out,
    cot_mix,
):
    n = lax.axis_size("dp")
    tokens_here = mix_in.shape[0]
    small = jnp.pad(
        jnp.concatenate([w_mix1, gains.T], axis=1), ((0, 0), (0, WIDE - MIXH - gains.shape[0]))
    )
    tables = angle_tables(tokens_here)
    kept, (full_qkv, full_o, full_up, full_down, smalls) = forward_exchange(
        n,
        history,
        cot_out,
        jnp.pad(mix_in.T, ((0, MIXED - STREAMS * HIST), (0, 0))),
        tables,
        doc_ids,
        group_ids,
        group_scale,
        cot_mix,
        w_mix2,
        (w_qkv, w_out, w_up, w_down, small),
    )
    inputs, mixes, normed, level, qkv_heads, attn_cat, slope, hidden = kept[:8]
    grad_out_full, grad_branch, out_low, little, mix_out, second = kept[8:]
    feature_side, mix_sum, little_sum, second_sum, sums = backward_exchange(
        n,
        normed,
        grad_branch,
        hidden,
        attn_cat,
        slope,
        qkv_heads,
        full_qkv,
        full_o,
        full_up,
        full_down,
        tables,
        doc_ids,
        level,
        inputs,
        grad_out_full,
        out_low,
        smalls,
        little,
        second,
        history,
        mixes,
        (w_qkv, w_out, w_up, w_down),
    )
    grad_history, block_out, sums = history_gradient(feature_side, mixes, sums)
    grad_qkv, grad_w_out, grad_w_up, grad_w_down = sums
    return (
        block_out,
        mix_out,
        grad_history,
        mix_sum[: STREAMS * HIST].T,
        grad_qkv,
        grad_w_out,
        grad_w_up,
        grad_w_down,
        little_sum[:, :MIXH],
        second_sum[:, :MIXH],
        little_sum[:, MIXH : MIXH + STREAMS + 1].T,
    )


def solution(mesh):
    return jax.shard_map(
        body,
        mesh=mesh,
        in_specs=(
            P(None, "dp", None),
            P("dp", None),
            P("dp", None),
            P("dp", None),
            P(),
            P(None, "dp", "mp"),
            P("dp", "mp"),
            P("dp", "mp"),
            P("dp", "mp"),
            P("dp", None),
            P(),
            P(None, "dp"),
            P("dp", None),
            P("dp", None),
        ),
        out_specs=(
            P("dp", None),
            P("dp", None),
            P(None, "dp", None),
            P("dp", None),
            P(None, "dp", "mp"),
            P("dp", "mp"),
            P("dp", "mp"),
            P("dp", "mp"),
            P("dp", None),
            P(),
            P(None, "dp"),
        ),
        check_vma=False,
    )
```
